32 devices in a mesh: dp: 8 (over z, x), tensor: 4 (over y, core).
Axes of the slice: x: 2, y: 2, z: 4, core: 2. Of those that a mesh axis runs over, the one named last changes fastest.
Arguments:
- byte_ids: int32 [32, 512], P(('dp', 'tensor')), may hold values from 0 to 255
- targets: int32 [32, 512], P(('dp', 'tensor')), may hold values from 0 to 255
- boundaries: int32 [32, 512], P(('dp', 'tensor')), may hold values from 0 to 1, as said below
- lengths: int32 [32], P(('dp', 'tensor')), may hold values from 1 to 512, as said below
- tables: float32 [2, 256, 1024], P(None, ('dp', 'tensor'))
- tables_first: float32 [2, 256, 1024], P(None, ('dp', 'tensor')), may hold values from -9.536743e-07 to 9.536743e-07
- tables_second: float32 [2, 256, 1024], P(None, ('dp', 'tensor')), may hold values from 5.753581e-14 to 9.294246e-13
- mamba_in: float32 [2, 1024, 4384], P(None, ('dp', 'tensor')), may hold values from -0.1875 to 0.1875
- mamba_in_first: float32 [2, 1024, 4384], P(None, ('dp', 'tensor')), may hold values from -9.536743e-07 to 9.536743e-07
- mamba_in_second: float32 [2, 1024, 4384], P(None, ('dp', 'tensor')), may hold values from 5.753581e-14 to 9.294246e-13
- mamba_out: float32 [2, 2048, 1024], P(None, ('dp', 'tensor')), may hold values from -0.125 to 0.125
- mamba_out_first: float32 [2, 2048, 1024], P(None, ('dp', 'tensor')), may hold values from -9.536743e-07 to 9.536743e-07
- mamba_out_second: float32 [2, 2048, 1024], P(None, ('dp', 'tensor')), may hold values from 5.753581e-14 to 9.294246e-13
- route_proj: float32 [1024, 3072], P(('dp', 'tensor'))
- route_proj_first: float32 [1024, 3072], P(('dp', 'tensor')), may hold values from -9.536743e-07 to 9.536743e-07
- route_proj_second: float32 [1024, 3072], P(('dp', 'tensor')), may hold values from 5.753581e-14 to 9.294246e-13
- small_params: float32 [34944], P(('dp', 'tensor'))
- small_params_first: float32 [34944], P(('dp', 'tensor')), may hold values from -3.8146973e-06 to 3.8146973e-06
- small_params_second: float32 [34944], P(('dp', 'tensor')), may hold values from 9.294246e-13 to 1.4826536e-11
- heed_triple_matrix: float32 [1536, 3, 1536], P('dp', None, 'tensor'), may hold values from -0.15625 to 0.15625
- attn_qkv_first: float32 [1536, 3, 1536], P('dp', None, 'tensor'), may hold values from -9.536743e-07 to 9.536743e-07
- attn_qkv_second: float32 [1536, 3, 1536], P('dp', None, 'tensor'), may hold values from 5.753581e-14 to 9.294246e-13
- heed_exit_matrix: float32 [1536, 1536], P('tensor', 'dp'), may hold values from -0.625 to 0.625
- attn_out_first: float32 [1536, 1536], P('tensor', 'dp'), may hold values from -9.536743e-07 to 9.536743e-07
- attn_out_second: float32 [1536, 1536], P('tensor', 'dp'), may hold values from 5.753581e-14 to 9.294246e-13
- lifting_matrix: float32 [1536, 2, 4096], P('dp', None, 'tensor'), may hold values from -0.15625 to 0.15625
- mlp_gate_up_first: float32 [1536, 2, 4096], P('dp', None, 'tensor'), may hold values from -9.536743e-07 to 9.536743e-07
- mlp_gate_up_second: float32 [1536, 2, 4096], P('dp', None, 'tensor'), may hold values from 5.753581e-14 to 9.294246e-13
- lowering_matrix: float32 [4096, 1536], P('tensor', 'dp'), may hold values from -0.09375 to 0.09375
- mlp_down_first: float32 [4096, 1536], P('tensor', 'dp'), may hold values from -9.536743e-07 to 9.536743e-07
- mlp_down_second: float32 [4096, 1536], P('tensor', 'dp'), may hold values from 5.753581e-14 to 9.294246e-13
Outputs:
- loss_sum: float32 [], replicated
- byte_count: float32 [], replicated
- grad_norm: float32 [], replicated
- tables_first_new: float32 [2, 256, 1024], P(None, ('dp', 'tensor'))
- tables_second_new: float32 [2, 256, 1024], P(None, ('dp', 'tensor'))
- tables_new: float32 [2, 256, 1024], P(None, ('dp', 'tensor'))
- mamba_in_first_new: float32 [2, 1024, 4384], P(None, ('dp', 'tensor'))
- mamba_in_second_new: float32 [2, 1024, 4384], P(None, ('dp', 'tensor'))
- mamba_in_new: float32 [2, 1024, 4384], P(None, ('dp', 'tensor'))
- mamba_out_first_new: float32 [2, 2048, 1024], P(None, ('dp', 'tensor'))
- mamba_out_second_new: float32 [2, 2048, 1024], P(None, ('dp', 'tensor'))
- mamba_out_new: float32 [2, 2048, 1024], P(None, ('dp', 'tensor'))
- route_proj_first_new: float32 [1024, 3072], P(('dp', 'tensor'))
- route_proj_second_new: float32 [1024, 3072], P(('dp', 'tensor'))
- route_proj_new: float32 [1024, 3072], P(('dp', 'tensor'))
- small_params_first_new: float32 [34944], P(('dp', 'tensor'))
- small_params_second_new: float32 [34944], P(('dp', 'tensor'))
- small_params_new: float32 [34944], P(('dp', 'tensor'))
- attn_qkv_first_new: float32 [1536, 3, 1536], P('dp', None, 'tensor')
- attn_qkv_second_new: float32 [1536, 3, 1536], P('dp', None, 'tensor')
- attn_qkv_new: float32 [1536, 3, 1536], P('dp', None, 'tensor')
- attn_out_first_new: float32 [1536, 1536], P('tensor', 'dp')
- attn_out_second_new: float32 [1536, 1536], P('tensor', 'dp')
- attn_out_new: float32 [1536, 1536], P('tensor', 'dp')
- mlp_gate_up_first_new: float32 [1536, 2, 4096], P('dp', None, 'tensor')
- mlp_gate_up_second_new: float32 [1536, 2, 4096], P('dp', None, 'tensor')
- mlp_gate_up_new: float32 [1536, 2, 4096], P('dp', None, 'tensor')
- mlp_down_first_new: float32 [4096, 1536], P('tensor', 'dp')
- mlp_down_second_new: float32 [4096, 1536], P('tensor', 'dp')
- mlp_down_new: float32 [4096, 1536], P('tensor', 'dp')
The draws below stay inside these ranges and needn't reach their ends.
Inputs may be any that keep to these rules, and one draw needn't show every extreme that they name: `boundaries`: in every sequence the first byte opens a span, and between 64 and 128 bytes do; some sequence has exactly 128 spans. `lengths`: the last sequence counts all its 512 bytes.
All inputs are finite; a program needn't handle non-finite values.
Results may differ from the reference program's by a relative error of at most 0.017.
The reference program's roundings to bfloat16 on the way count: a program that leaves them out, or rounds other values in their place, can miss the bound.
Values may be sent and summed in bfloat16 or wider, within the bound.
A program may use at most 384 MiB of HBM per device.

```python
import math
import jax
import jax.numpy as jnp
from jax import lax

BYTE_WIDTH = 1024
CORE_WIDTH = 1536
HEADS = 16
FFN = 4096
VOCAB = 256
STATE = 128
HEADDIM = 64
STEP = 10
LEN = 512
INNER = 2048
MHEADS = 32
PROJ = 4384
HD = 96
MAX_PIECES = 128
SEQS = 32
SMALL = 34944
NPARAM = 45189248


def draw_byte_ids(key, part):
    key = jax.random.fold_in(key, 15)
    flag_key, value_key = jax.random.split(key)
    opens = jax.random.randint(flag_key, (SEQS, LEN), 0, 16) == 0
    opens = opens.at[:, 0].set(True)
    values = jax.random.randint(value_key, (SEQS, LEN), 0, VOCAB)
    starts = jnp.where(opens, jnp.arange(LEN, dtype=jnp.int32)[None, :], 0)
    latest = lax.cummax(starts, axis=1)
    return jnp.take_along_axis(values, latest, axis=1).astype(jnp.int32)


def draw_boundaries(key, part):
    key = jax.random.fold_in(key, 11)
    count_key, pick_key, score_key = jax.random.split(key, 3)
    counts = jax.random.randint(count_key, (SEQS,), MAX_PIECES // 2, MAX_PIECES + 1)
    chosen = jax.random.randint(pick_key, (), 0, SEQS)
    counts = jnp.where(jnp.arange(SEQS) == chosen, MAX_PIECES, counts)
    scores = jax.random.randint(score_key, (SEQS, LEN), 0, 1 << 16) * LEN + jnp.arange(LEN)[None, :]
    scores = scores.at[:, 0].set(-1)
    ranks = jnp.argsort(jnp.argsort(scores, axis=1, stable=True), axis=1, stable=True)
    return (ranks < counts[:, None]).astype(jnp.int32)


def draw_lengths(key, part):
    key = jax.random.fold_in(key, 12)
    base = LEN // 3 + (LEN - LEN // 3) * jnp.arange(SEQS) // max(SEQS - 1, 1)
    jitter = jax.random.randint(key, (SEQS,), -(LEN // 16), LEN // 16 + 1)
    outcome = jnp.clip(base + jitter, 1, LEN)
    return outcome.at[SEQS - 1].set(LEN).astype(jnp.int32)


def draw_tables(key, part):
    key = jax.random.fold_in(key, 13)
    noise = jax.random.normal(key, (2, VOCAB, BYTE_WIDTH), jnp.float32)
    scales = jnp.array([0.2, BYTE_WIDTH ** (-0.5)], jnp.float32)
    return noise * scales[:, None, None]


def draw_route_proj(key, part):
    key = jax.random.fold_in(key, 16)
    query_key, noise_key, rest_key = jax.random.split(key, 3)
    spread = BYTE_WIDTH ** (-0.5)
    query_block = jax.random.normal(query_key, (BYTE_WIDTH, BYTE_WIDTH), jnp.float32)
    key_block = (query_block + 0.1 * jax.random.normal(noise_key, (BYTE_WIDTH, BYTE_WIDTH), jnp.float32)) / 1.005
    rest_block = jax.random.normal(rest_key, (BYTE_WIDTH, BYTE_WIDTH), jnp.float32)
    whole = jnp.concatenate([query_block, key_block, rest_block], axis=1) * spread
    return jnp.clip(whole, -6.0 * spread, 6.0 * spread)


def draw_small_params(key, part):
    key = jax.random.fold_in(key, 14)
    gain_key, pad_key, conv_key, skip_key, decay_key, bias_key = jax.random.split(key, 6)
    extents = [BYTE_WIDTH, BYTE_WIDTH, INNER, INNER, CORE_WIDTH, CORE_WIDTH, CORE_WIDTH, BYTE_WIDTH]
    rising = jnp.concatenate([jnp.linspace(0.5, 1.5, extent, dtype=jnp.float32) for extent in extents])
    gains = rising * jax.random.uniform(gain_key, rising.shape, jnp.float32, 0.85, 1.15)
    blank_row = jax.random.normal(pad_key, (CORE_WIDTH - BYTE_WIDTH,), jnp.float32)
    conv_taps = 0.5 * jax.random.normal(conv_key, (8 * (INNER + 2 * STATE),), jnp.float32)
    skip_gains = jax.random.uniform(skip_key, (2 * INNER,), jnp.float32, 0.5, 1.5)
    a_logs = jax.random.uniform(decay_key, (2 * MHEADS,), jnp.float32, 0.0, 2.77)
    dt_biases = jax.random.uniform(bias_key, (2 * MHEADS,), jnp.float32, -6.9, -2.3)
    return jnp.concatenate([gains, blank_row, conv_taps, skip_gains, a_logs, dt_biases])


def set_ends(drawn, rng, smallest, largest):
    spot = [jax.random.randint(jax.random.fold_in(rng, axis), (), 0, length) for axis, length in enumerate(drawn.shape)]
    widest = drawn.shape.index(max(drawn.shape))
    neighbour = spot[:widest] + [(spot[widest] + 1) % drawn.shape[widest]] + spot[widest + 1:]
    return drawn.at[tuple(spot)].set(smallest).at[tuple(neighbour)].set(largest)


def block_scale(key, shape, shards, smallest, largest):
    loudness, own = 1.0, jax.random.fold_in(key, 6)
    for dim, shards_of in shards:
        draws = jnp.exp(jax.random.uniform(jax.random.fold_in(own, dim), (shards_of,), jnp.float32, smallest / len(shards), largest / len(shards)))
        loudness = loudness * jnp.repeat(draws, shape[dim] // shards_of).reshape([-1 if axis == dim else 1 for axis in range(len(shape))])
    return loudness


def bell_draw(rng, shape, deviation, limit, shards=(), kind=jnp.bfloat16):
    entries = deviation * jax.random.normal(rng, shape, jnp.float32)
    if shards:
        entries = entries * block_scale(rng, shape, shards, -0.22, 0.18)
    return jnp.clip(entries, -limit, limit).astype(kind)


def setup_inputs(seed: int = 0) -> dict:
    seeds = jax.random.split(jax.random.key(seed), 32)
    return {
        "byte_ids": draw_byte_ids(jax.random.fold_in(seeds[31], 71), 0),
        "targets": set_ends(jax.random.randint(seeds[1], (SEQS, LEN), 0, VOCAB), jax.random.fold_in(seeds[1], 1), 0, VOCAB - 1).astype(jnp.int32),
        "boundaries": draw_boundaries(jax.random.fold_in(seeds[31], 71), 0),
        "lengths": draw_lengths(jax.random.fold_in(seeds[31], 71), 0),
        "tables": draw_tables(jax.random.fold_in(seeds[31], 71), 0),
        "tables_first": bell_draw(seeds[5], (2, VOCAB, BYTE_WIDTH), (0.00111 * NPARAM ** -0.5), 9.5367431640625e-07, ((1, 32),), jnp.float32),
        "tables_second": jnp.clip(jnp.exp(math.log(9.29424614527774e-13) - 2.7821582 * jax.random.uniform(seeds[6], (2, VOCAB, BYTE_WIDTH), jnp.float32) ** block_scale(seeds[6], (2, VOCAB, BYTE_WIDTH), ((1, 32),), -0.2, 0.2)), 5.753581069694799e-14, 9.29424614527774e-13),
        "mamba_in": bell_draw(seeds[7], (2, BYTE_WIDTH, PROJ), BYTE_WIDTH ** -0.5, 0.1875, ((1, 32),), jnp.float32),
        "mamba_in_first": bell_draw(seeds[8], (2, BYTE_WIDTH, PROJ), (0.00111 * NPARAM ** -0.5), 9.5367431640625e-07, ((1, 32),), jnp.float32),
        "mamba_in_second": jnp.clip(jnp.exp(math.log(9.29424614527774e-13) - 2.7821582 * jax.random.uniform(seeds[9], (2, BYTE_WIDTH, PROJ), jnp.float32) ** block_scale(seeds[9], (2, BYTE_WIDTH, PROJ), ((1, 32),), -0.2, 0.2)), 5.753581069694799e-14, 9.29424614527774e-13),
        "mamba_out": bell_draw(seeds[10], (2, INNER, BYTE_WIDTH), INNER ** -0.5, 0.125, ((1, 32),), jnp.float32),
        "mamba_out_first": bell_draw(seeds[11], (2, INNER, BYTE_WIDTH), (0.00111 * NPARAM ** -0.5), 9.5367431640625e-07, ((1, 32),), jnp.float32),
        "mamba_out_second": jnp.clip(jnp.exp(math.log(9.29424614527774e-13) - 2.7821582 * jax.random.uniform(seeds[12], (2, INNER, BYTE_WIDTH), jnp.float32) ** block_scale(seeds[12], (2, INNER, BYTE_WIDTH), ((1, 32),), -0.2, 0.2)), 5.753581069694799e-14, 9.29424614527774e-13),
        "route_proj": draw_route_proj(jax.random.fold_in(seeds[31], 71), 0),
        "route_proj_first": bell_draw(seeds[14], (BYTE_WIDTH, 3 * BYTE_WIDTH), (0.00111 * NPARAM ** -0.5), 9.5367431640625e-07, ((0, 32),), jnp.float32),
        "route_proj_second": jnp.clip(jnp.exp(math.log(9.29424614527774e-13) - 2.7821582 * jax.random.uniform(seeds[15], (BYTE_WIDTH, 3 * BYTE_WIDTH), jnp.float32) ** block_scale(seeds[15], (BYTE_WIDTH, 3 * BYTE_WIDTH), ((0, 32),), -0.2, 0.2)), 5.753581069694799e-14, 9.29424614527774e-13),
        "small_params": draw_small_params(jax.random.fold_in(seeds[31], 71), 0),
        "small_params_first": bell_draw(seeds[17], (SMALL,), (0.0044 * NPARAM ** -0.5), 3.814697265625e-06, ((0, 32),), jnp.float32),
        "small_params_second": jnp.clip(jnp.exp(math.log(1.4826535832401788e-11) - 2.769608 * jax.random.uniform(seeds[18], (SMALL,), jnp.float32) ** block_scale(seeds[18], (SMALL,), ((0, 32),), -0.2, 0.2)), 9.29424614527774e-13, 1.4826535832401788e-11),
        "heed_triple_matrix": bell_draw(seeds[19], (CORE_WIDTH, 3, CORE_WIDTH), CORE_WIDTH ** -0.5, 0.15625, ((0, 8), (2, 4)), jnp.float32),
        "attn_qkv_first": bell_draw(seeds[20], (CORE_WIDTH, 3, CORE_WIDTH), (0.00111 * NPARAM ** -0.5), 9.5367431640625e-07, ((0, 8), (2, 4)), jnp.float32),
        "attn_qkv_second": jnp.clip(jnp.exp(math.log(9.29424614527774e-13) - 2.7821582 * jax.random.uniform(seeds[21], (CORE_WIDTH, 3, CORE_WIDTH), jnp.float32) ** block_scale(seeds[21], (CORE_WIDTH, 3, CORE_WIDTH), ((0, 8), (2, 4)), -0.2, 0.2)), 5.753581069694799e-14, 9.29424614527774e-13),
        "heed_exit_matrix": bell_draw(seeds[22], (CORE_WIDTH, CORE_WIDTH), (CORE_WIDTH // 16) ** -0.5, 0.625, ((0, 4), (1, 8)), jnp.float32),
        "attn_out_first": bell_draw(seeds[23], (CORE_WIDTH, CORE_WIDTH), (0.00111 * NPARAM ** -0.5), 9.5367431640625e-07, ((0, 4), (1, 8)), jnp.float32),
        "attn_out_second": jnp.clip(jnp.exp(math.log(9.29424614527774e-13) - 2.7821582 * jax.random.uniform(seeds[24], (CORE_WIDTH, CORE_WIDTH), jnp.float32) ** block_scale(seeds[24], (CORE_WIDTH, CORE_WIDTH), ((0, 4), (1, 8)), -0.2, 0.2)), 5.753581069694799e-14, 9.29424614527774e-13),
        "lifting_matrix": bell_draw(seeds[25], (CORE_WIDTH, 2, FFN), CORE_WIDTH ** -0.5, 0.15625, ((0, 8), (2, 4)), jnp.float32),
        "mlp_gate_up_first": bell_draw(seeds[26], (CORE_WIDTH, 2, FFN), (0.00111 * NPARAM ** -0.5), 9.5367431640625e-07, ((0, 8), (2, 4)), jnp.float32),
        "mlp_gate_up_second": jnp.clip(jnp.exp(math.log(9.29424614527774e-13) - 2.7821582 * jax.random.uniform(seeds[27], (CORE_WIDTH, 2, FFN), jnp.float32) ** block_scale(seeds[27], (CORE_WIDTH, 2, FFN), ((0, 8), (2, 4)), -0.2, 0.2)), 5.753581069694799e-14, 9.29424614527774e-13),
        "lowering_matrix": bell_draw(seeds[28], (FFN, CORE_WIDTH), FFN ** -0.5, 0.09375, ((0, 4), (1, 8)), jnp.float32),
        "mlp_down_first": bell_draw(seeds[29], (FFN, CORE_WIDTH), (0.00111 * NPARAM ** -0.5), 9.5367431640625e-07, ((0, 4), (1, 8)), jnp.float32),
        "mlp_down_second": jnp.clip(jnp.exp(math.log(9.29424614527774e-13) - 2.7821582 * jax.random.uniform(seeds[30], (FFN, CORE_WIDTH), jnp.float32) ** block_scale(seeds[30], (FFN, CORE_WIDTH), ((0, 4), (1, 8)), -0.2, 0.2)), 5.753581069694799e-14, 9.29424614527774e-13),
    }


@jax.custom_vjp
def coarse_rows(v):
    return lax.optimization_barrier(v.astype(jnp.bfloat16)).astype(jnp.float32)

@jax.custom_vjp
def coarse_rows_grad(v):
    return v

def low_keep(v):
    return (coarse_rows(v), None)

def low_pass(kept, grad):
    return (grad,)

def back_keep(v):
    return (v, None)

def back_low(kept, grad):
    return (coarse_rows(grad),)
coarse_rows.defvjp(low_keep, low_pass)
coarse_rows_grad.defvjp(back_keep, back_low)
deepest_tier = lax.Precision.HIGHEST
norm_eps = 1e-05
ssd_block = 128
beta_one = 0.9
beta_two = 0.95
adam_eps = 1e-08
weight_decay = 0.1
max_norm = 0.01
rate_byte = 0.06
rate_main = 0.05
rate_small = 0.5

def root_mean_rescale(value_entries, gain_vec):
    return value_entries * lax.rsqrt(lax.optimization_barrier(jnp.mean(value_entries * value_entries, axis=-1, keepdims=True)) + norm_eps) * gain_vec

def softplus(value_entries):
    return jnp.log1p(jnp.exp(value_entries))

def unpack_small(vector):
    extents = [2 * BYTE_WIDTH, 2 * INNER, 3 * CORE_WIDTH, BYTE_WIDTH, CORE_WIDTH - BYTE_WIDTH, 8 * (INNER + 2 * STATE), 2 * INNER, 2 * MHEADS, 2 * MHEADS]
    pieces = []
    offset = 0
    for extent in extents:
        pieces.append(vector[offset:offset + extent])
        offset += extent
    return (pieces[0].reshape(2, BYTE_WIDTH), pieces[1].reshape(2, INNER), pieces[2].reshape(3, CORE_WIDTH), pieces[3], pieces[4], pieces[5].reshape(2, 4, INNER + 2 * STATE), pieces[6].reshape(2, INNER), pieces[7].reshape(2, MHEADS), pieces[8].reshape(2, MHEADS))

def ssd_scan(inputs, steps, rates, in_map, out_map):
    blocks = inputs.shape[0] // ssd_block
    cumulative = jnp.cumsum((steps * rates).reshape(blocks, ssd_block, MHEADS), axis=1)
    weighted = (inputs * steps[:, :, None]).reshape(blocks, ssd_block, MHEADS, HEADDIM)
    in_blocks = in_map.reshape(blocks, ssd_block, STATE)
    out_blocks = out_map.reshape(blocks, ssd_block, STATE)
    causal = jnp.tril(jnp.ones((ssd_block, ssd_block), dtype=bool))
    log_gaps = jnp.where(causal[None, :, :, None], cumulative[:, :, None, :] - cumulative[:, None, :, :], -jnp.inf)
    affinity = jnp.einsum('bin,bjn->bij', out_blocks, in_blocks, precision=deepest_tier)
    within = jnp.einsum('bij,bijh,bjhp->bihp', affinity, jnp.exp(log_gaps), weighted, precision=deepest_tier)
    to_end = jnp.exp(cumulative[:, -1:, :] - cumulative)
    states = jnp.einsum('bjn,bjh,bjhp->bhpn', in_blocks, to_end, weighted, precision=deepest_tier)

    def advance(running, scanned):
        total_decay, block_state = scanned
        return (jnp.exp(total_decay)[:, None, None] * running + block_state, running)
    _, starts = lax.scan(advance, jnp.zeros((MHEADS, HEADDIM, STATE), jnp.float32), (cumulative[:, -1, :], states))
    across = jnp.einsum('bin,bih,bhpn->bihp', out_blocks, jnp.exp(cumulative), starts, precision=deepest_tier)
    return (within + across).reshape(-1, MHEADS * HEADDIM)

def mixer_middle(projected, conv_taps, skip_gain, a_log, dt_bias, gated_gain):
    span_extent_size = projected.shape[0]
    gate_part = projected[:, :INNER]
    streams = projected[:, INNER:2 * INNER + 2 * STATE]
    raw_steps = projected[:, 2 * INNER + 2 * STATE:]
    padded = jnp.concatenate([jnp.zeros((3, streams.shape[1]), jnp.float32), streams], axis=0)
    convolved = conv_taps[0] * padded[0:span_extent_size]
    for tap_index in range(1, 4):
        convolved = convolved + conv_taps[tap_index] * padded[tap_index:tap_index + span_extent_size]
    active = jax.nn.silu(convolved)
    inputs = active[:, :INNER]
    steps = softplus(raw_steps + dt_bias)
    outcome = ssd_scan(inputs.reshape(span_extent_size, MHEADS, HEADDIM), steps, -jnp.exp(a_log), active[:, INNER:INNER + STATE], active[:, INNER + STATE:])
    outcome = outcome + inputs * skip_gain
    return root_mean_rescale(outcome * jax.nn.silu(gate_part), gated_gain)

def mixer(value_entries, w_in, exit_matrix, block_gain, smalls):
    rescaled_rows = coarse_rows(root_mean_rescale(value_entries, block_gain))
    projected = coarse_rows_grad(jnp.dot(rescaled_rows, w_in, precision=deepest_tier))
    middle = coarse_rows(mixer_middle(projected, *smalls))
    return value_entries + coarse_rows_grad(jnp.dot(middle, exit_matrix, precision=deepest_tier))

def route_prob(queries, key_rows):
    unit_query = queries * lax.rsqrt(lax.optimization_barrier(jnp.sum(queries * queries, axis=-1, keepdims=True)) + 1e-06)
    unit_key = key_rows * lax.rsqrt(lax.optimization_barrier(jnp.sum(key_rows * key_rows, axis=-1, keepdims=True)) + 1e-06)
    cosine = lax.optimization_barrier(jnp.sum(unit_query[1:] * unit_key[:-1], axis=-1))
    return jnp.concatenate([jnp.ones((1,), jnp.float32), 0.5 * (1.0 - cosine)])

def span_maps(cut_marks):
    owner_slot = jnp.cumsum(cut_marks) - 1
    position_labels = jnp.arange(MAX_PIECES, dtype=jnp.int32)
    broadcast_back = (owner_slot[:, None] == position_labels[None, :]).astype(jnp.float32)
    select_items = broadcast_back.T * cut_marks[None, :].astype(jnp.float32)
    return (select_items, broadcast_back)

def merge_into_pieces(select_items, value_entries, blank_row):
    spans = jnp.dot(select_items, value_entries, precision=deepest_tier)
    return jnp.concatenate([spans, jnp.broadcast_to(blank_row, (MAX_PIECES, CORE_WIDTH - BYTE_WIDTH))], axis=1)

def smooth_spans(piece_output, confidence):

    def update(running, scanned):
        span_row, weight = scanned
        updated = weight * span_row + (1.0 - weight) * running
        return (updated, updated)
    _, smoothed = lax.scan(update, jnp.zeros((piece_output.shape[1],), jnp.float32), (piece_output, confidence))
    return smoothed

def link_layers(select_items, broadcast_back, cut_marks, latent_holder, closing_scale, cut_likelihood, shortcut_sum):
    piece_output = root_mean_rescale(latent_holder, closing_scale)[:, :BYTE_WIDTH]
    smoothed = smooth_spans(piece_output, jnp.dot(select_items, cut_likelihood, precision=deepest_tier))
    confidence = jnp.where(cut_marks == 1, cut_likelihood, 1.0 - cut_likelihood)
    return shortcut_sum + confidence[:, None] * jnp.dot(broadcast_back, smoothed, precision=deepest_tier)

def self_heeding(latent_holder, heed_scale, triple_matrix, exit_matrix):
    rescaled_rows = coarse_rows(root_mean_rescale(latent_holder, heed_scale))
    triple = coarse_rows_grad(coarse_rows(jnp.einsum('td,dsh->tsh', rescaled_rows, triple_matrix, precision=deepest_tier)))
    heads_split = triple.reshape(MAX_PIECES, 3, HEADS, HD)
    scores = coarse_rows_grad(jnp.einsum('qhd,khd->hqk', heads_split[:, 0], heads_split[:, 1], precision=deepest_tier) * HD ** (-0.5))
    causal = jnp.tril(jnp.ones((MAX_PIECES, MAX_PIECES), dtype=bool))
    scores = jnp.where(causal[None], scores, -jnp.inf)
    maxima = lax.optimization_barrier(jnp.max(scores, axis=-1, keepdims=True))
    exp_scores = jnp.exp(scores - maxima)
    weights_soft = coarse_rows(exp_scores / lax.optimization_barrier(jnp.sum(exp_scores, axis=-1, keepdims=True)))
    heads_output = coarse_rows_grad(coarse_rows(jnp.einsum('hqk,khd->qhd', weights_soft, heads_split[:, 2], precision=deepest_tier)))
    return latent_holder + coarse_rows_grad(jnp.dot(heads_output.reshape(MAX_PIECES, CORE_WIDTH), exit_matrix, precision=deepest_tier))

def perceptron_apply(latent_holder, perceptron_scale, lift_matrix, lower_matrix):
    rescaled_rows = coarse_rows(root_mean_rescale(latent_holder, perceptron_scale))
    gate_up = coarse_rows_grad(jnp.einsum('td,dsf->tsf', rescaled_rows, lift_matrix, precision=deepest_tier))
    latent_state = coarse_rows(jax.nn.silu(gate_up[:, 0]) * gate_up[:, 1])
    return latent_holder + coarse_rows_grad(jnp.dot(latent_state, lower_matrix, precision=deepest_tier))

def sequence_loss(params, byte_row, target_row, cut_marks, span_extent_size, byte_count):
    tables, mamba_in, mamba_out, route_proj, small_params, heed_triple_matrix, heed_exit_matrix, lifting_matrix, lowering_matrix = [coarse_rows(weight) for weight in params]
    block_gains, gated_gains, core_scales, head_gain, blank_row, conv_taps, skip_gains, a_logs, dt_biases = unpack_small(small_params)
    layer_smalls = [(conv_taps[layer_index], skip_gains[layer_index], a_logs[layer_index], dt_biases[layer_index], gated_gains[layer_index]) for layer_index in range(2)]
    vocab_ids = jnp.arange(VOCAB, dtype=jnp.int32)
    embedded = jnp.dot((byte_row[:, None] == vocab_ids[None, :]).astype(jnp.float32), tables[0], precision=deepest_tier)
    packer_output = mixer(embedded, mamba_in[0], mamba_out[0], block_gains[0], layer_smalls[0])
    directed_rows = coarse_rows_grad(jnp.dot(coarse_rows(packer_output), route_proj, precision=deepest_tier))
    cut_likelihood = route_prob(directed_rows[:, :BYTE_WIDTH], directed_rows[:, BYTE_WIDTH:2 * BYTE_WIDTH])
    select_items, broadcast_back = span_maps(cut_marks)
    latent_holder = merge_into_pieces(select_items, packer_output, blank_row)
    latent_holder = self_heeding(latent_holder, core_scales[0], heed_triple_matrix, heed_exit_matrix)
    latent_holder = perceptron_apply(latent_holder, core_scales[1], lifting_matrix, lowering_matrix)
    unpacked_bytes = link_layers(select_items, broadcast_back, cut_marks, latent_holder, core_scales[2], cut_likelihood, directed_rows[:, 2 * BYTE_WIDTH:])
    final_out = mixer(unpacked_bytes, mamba_in[1], mamba_out[1], block_gains[1], layer_smalls[1])
    logits = coarse_rows_grad(jnp.dot(coarse_rows(root_mean_rescale(final_out, head_gain)), tables[1].T, precision=deepest_tier))
    maxima = lax.optimization_barrier(jnp.max(logits, axis=-1, keepdims=True))
    log_total = maxima[:, 0] + jnp.log(lax.optimization_barrier(jnp.sum(jnp.exp(logits - maxima), axis=-1)))
    picked = lax.optimization_barrier(jnp.sum(logits * (target_row[:, None] == vocab_ids[None, :]).astype(jnp.float32), axis=-1))
    counted = (jnp.arange(LEN, dtype=jnp.int32) < span_extent_size).astype(jnp.float32)
    loss_sum = jnp.sum((log_total - picked) * counted)
    return (loss_sum / byte_count, loss_sum)

def adam_step(weight, grad, first, second, rate, decay):
    first_new = beta_one * first + (1.0 - beta_one) * grad
    second_new = beta_two * second + (1.0 - beta_two) * grad * grad
    ratio = first_new / (1.0 - beta_one ** STEP) / (jnp.sqrt(second_new / (1.0 - beta_two ** STEP)) + adam_eps)
    return (first_new, second_new, weight - rate * (ratio + decay * weight))

def reference(byte_ids, targets, boundaries, lengths, tables, tables_first, tables_second, mamba_in, mamba_in_first, mamba_in_second, mamba_out, mamba_out_first, mamba_out_second, route_proj, route_proj_first, route_proj_second, small_params, small_params_first, small_params_second, heed_triple_matrix, attn_qkv_first, attn_qkv_second, heed_exit_matrix, attn_out_first, attn_out_second, lifting_matrix, mlp_gate_up_first, mlp_gate_up_second, lowering_matrix, mlp_down_first, mlp_down_second):
    params = (tables, mamba_in, mamba_out, route_proj, small_params, heed_triple_matrix, heed_exit_matrix, lifting_matrix, lowering_matrix)
    firsts = (tables_first, mamba_in_first, mamba_out_first, route_proj_first, small_params_first, attn_qkv_first, attn_out_first, mlp_gate_up_first, mlp_down_first)
    seconds = (tables_second, mamba_in_second, mamba_out_second, route_proj_second, small_params_second, attn_qkv_second, attn_out_second, mlp_gate_up_second, mlp_down_second)
    byte_count = jnp.sum(lengths).astype(jnp.float32)

    def one_sequence(running, scanned):
        grad_sums, loss_running = running
        byte_row, target_row, cut_marks, span_extent_size = scanned

        def scaled_loss(*weights):
            return sequence_loss(weights, byte_row, target_row, cut_marks, span_extent_size, byte_count)
        _, pullback, loss_sum = jax.vjp(scaled_loss, *params, has_aux=True)
        gradients = pullback(jnp.ones((), jnp.float32))
        return ((jax.tree.map(jnp.add, grad_sums, tuple(gradients)), loss_running + loss_sum), None)
    zero_grads = tuple((jnp.zeros_like(weight) for weight in params))
    (gradients, loss_total), _ = lax.scan(one_sequence, (zero_grads, jnp.zeros((), jnp.float32)), (byte_ids, targets, boundaries, lengths))
    grad_norm = jnp.sqrt(sum((jnp.sum(grad * grad) for grad in gradients)))
    clip_factor = jnp.minimum(1.0, max_norm / (grad_norm + 1e-06))
    rate_list = (rate_byte, rate_byte, rate_byte, rate_byte, rate_small, rate_main, rate_main, rate_main, rate_main)
    decay_list = (weight_decay, weight_decay, weight_decay, weight_decay, 0.0, weight_decay, weight_decay, weight_decay, weight_decay)
    updated = [adam_step(params[position], clip_factor * gradients[position], firsts[position], seconds[position], rate_list[position], decay_list[position]) for position in range(9)]
    return (loss_total, byte_count, grad_norm, updated[0][0], updated[0][1], updated[0][2], updated[1][0], updated[1][1], updated[1][2], updated[2][0], updated[2][1], updated[2][2], updated[3][0], updated[3][1], updated[3][2], updated[4][0], updated[4][1], updated[4][2], updated[5][0], updated[5][1], updated[5][2], updated[6][0], updated[6][1], updated[6][2], updated[7][0], updated[7][1], updated[7][2], updated[8][0], updated[8][1], updated[8][2])
```

```python
from functools import partial

import jax
import jax.numpy as jnp
from jax import lax
from jax.experimental import pallas as pl
from jax.experimental.pallas import tpu as pltpu
from jax.sharding import PartitionSpec as P

BYTE_WIDTH = 1024
CORE_WIDTH = 1536
VOCAB = 256
STATE = 128
HEADDIM = 64
STEP = 10
INNER = 2048
MHEADS = 32
HD = 96
MAX_PIECES = 128


deepest_tier = lax.Precision.HIGHEST
norm_eps = 1e-05
ssd_block = 128
beta_one = 0.9
beta_two = 0.95
adam_eps = 1e-08
weight_decay = 0.1
max_norm = 0.01
rate_byte = 0.06
rate_main = 0.05
rate_small = 0.5


def root_mean_rescale(value_entries, gain_vec):
    return (
        value_entries
        * lax.rsqrt(jnp.mean(value_entries * value_entries, axis=-1, keepdims=True) + norm_eps)
        * gain_vec
    )


def softplus(value_entries):
    return jnp.log1p(jnp.exp(value_entries))


def unpack_small(vector):
    extents = [
        2 * BYTE_WIDTH,
        2 * INNER,
        3 * CORE_WIDTH,
        BYTE_WIDTH,
        CORE_WIDTH - BYTE_WIDTH,
        8 * (INNER + 2 * STATE),
        2 * INNER,
        2 * MHEADS,
        2 * MHEADS,
    ]
    pieces = []
    offset = 0
    for extent in extents:
        pieces.append(vector[offset : offset + extent])
        offset += extent
    return (
        pieces[0].reshape(2, BYTE_WIDTH),
        pieces[1].reshape(2, INNER),
        pieces[2].reshape(3, CORE_WIDTH),
        pieces[3],
        pieces[4],
        pieces[5].reshape(2, 4, INNER + 2 * STATE),
        pieces[6].reshape(2, INNER),
        pieces[7].reshape(2, MHEADS),
        pieces[8].reshape(2, MHEADS),
    )


def ssd_scan(inputs, steps, rates, in_map, out_map):
    blocks = inputs.shape[0] // ssd_block
    cumulative = jnp.cumsum((steps * rates).reshape(blocks, ssd_block, MHEADS), axis=1)
    weighted = (inputs * steps[:, :, None]).reshape(blocks, ssd_block, MHEADS, HEADDIM)
    in_blocks = in_map.reshape(blocks, ssd_block, STATE)
    out_blocks = out_map.reshape(blocks, ssd_block, STATE)
    causal = jnp.tril(jnp.ones((ssd_block, ssd_block), dtype=bool))
    log_gaps = jnp.where(
        causal[None, :, :, None], cumulative[:, :, None, :] - cumulative[:, None, :, :], -jnp.inf
    )
    affinity = jnp.einsum("bin,bjn->bij", out_blocks, in_blocks, precision=deepest_tier)
    within = jnp.einsum(
        "bij,bijh,bjhp->bihp", affinity, jnp.exp(log_gaps), weighted, precision=deepest_tier
    )
    to_end = jnp.exp(cumulative[:, -1:, :] - cumulative)
    states = jnp.einsum("bjn,bjh,bjhp->bhpn", in_blocks, to_end, weighted, precision=deepest_tier)

    running = jnp.zeros((MHEADS, HEADDIM, STATE), jnp.float32)
    starts = []
    for block in range(blocks):
        starts.append(running)
        if block + 1 < blocks:
            running = jnp.exp(cumulative[block, -1, :])[:, None, None] * running + states[block]
    starts = jnp.stack(starts)
    across = jnp.einsum(
        "bin,bih,bhpn->bihp", out_blocks, jnp.exp(cumulative), starts, precision=deepest_tier
    )
    return (within + across).reshape(-1, MHEADS * HEADDIM)


def mixer_middle(projected, conv_taps, skip_gain, a_log, dt_bias, gated_gain):
    span_extent_size = projected.shape[0]
    gate_part = projected[:, :INNER]
    streams = projected[:, INNER : 2 * INNER + 2 * STATE]
    raw_steps = projected[:, 2 * INNER + 2 * STATE :]
    padded = jnp.concatenate([jnp.zeros((3, streams.shape[1]), jnp.float32), streams], axis=0)
    convolved = conv_taps[0] * padded[0:span_extent_size]
    for tap_index in range(1, 4):
        convolved = (
            convolved + conv_taps[tap_index] * padded[tap_index : tap_index + span_extent_size]
        )
    active = jax.nn.silu(convolved)
    inputs = active[:, :INNER]
    steps = softplus(raw_steps + dt_bias)
    outcome = ssd_scan(
        inputs.reshape(span_extent_size, MHEADS, HEADDIM),
        steps,
        -jnp.exp(a_log),
        active[:, INNER : INNER + STATE],
        active[:, INNER + STATE :],
    )
    outcome = outcome + inputs * skip_gain
    return root_mean_rescale(outcome * jax.nn.silu(gate_part), gated_gain)


def route_prob(queries, key_rows):
    unit_query = queries * lax.rsqrt(jnp.sum(queries * queries, axis=-1, keepdims=True) + 1e-06)
    unit_key = key_rows * lax.rsqrt(jnp.sum(key_rows * key_rows, axis=-1, keepdims=True) + 1e-06)
    cosine = jnp.sum(unit_query[1:] * unit_key[:-1], axis=-1)
    return jnp.concatenate([jnp.ones((1,), jnp.float32), 0.5 * (1.0 - cosine)])


def span_maps(cut_marks):
    owner_slot = jnp.cumsum(cut_marks) - 1
    position_labels = jnp.arange(MAX_PIECES, dtype=jnp.int32)
    broadcast_back = (owner_slot[:, None] == position_labels[None, :]).astype(jnp.float32)
    select_items = broadcast_back.T * cut_marks[None, :].astype(jnp.float32)
    return (select_items, broadcast_back)


def merge_into_pieces(select_items, value_entries, blank_row):
    spans = jnp.dot(select_items, value_entries, precision=deepest_tier)
    return jnp.concatenate(
        [spans, jnp.broadcast_to(blank_row, (MAX_PIECES, CORE_WIDTH - BYTE_WIDTH))], axis=1
    )


def decay_products(confidence):
    rows = lax.broadcasted_iota(jnp.int32, (MAX_PIECES, MAX_PIECES), 0)
    columns = lax.broadcasted_iota(jnp.int32, (MAX_PIECES, MAX_PIECES), 1)
    products = jnp.where(rows > columns, 1.0 - confidence[:, None], 1.0)
    reach = 1
    while reach < MAX_PIECES:
        shifted = jnp.concatenate(
            [jnp.ones((reach, MAX_PIECES), jnp.float32), products[:-reach]], axis=0
        )
        products = products * shifted
        reach *= 2
    return jnp.where(rows >= columns, products, 0.0)


@jax.custom_vjp
def smooth_spans(piece_output, confidence):
    products = decay_products(confidence)
    return jnp.dot(products, confidence[:, None] * piece_output, precision=deepest_tier)


def smooth_keep(piece_output, confidence):
    products = decay_products(confidence)
    smoothed = jnp.dot(products, confidence[:, None] * piece_output, precision=deepest_tier)
    return smoothed, (piece_output, confidence, products, smoothed)


def smooth_pull(kept, slope):
    piece_output, confidence, products, smoothed = kept
    spread = lax.dot_general(
        products, slope, (((0,), (0,)), ((), ())), precision=deepest_tier
    )
    before = jnp.concatenate([jnp.zeros((1, smoothed.shape[1]), jnp.float32), smoothed[:-1]], axis=0)
    return (confidence[:, None] * spread, jnp.sum(spread * (piece_output - before), axis=-1))


smooth_spans.defvjp(smooth_keep, smooth_pull)


def link_layers(
    select_items,
    broadcast_back,
    cut_marks,
    latent_holder,
    closing_scale,
    cut_likelihood,
    shortcut_sum,
):
    piece_output = root_mean_rescale(latent_holder, closing_scale)[:, :BYTE_WIDTH]
    smoothed = smooth_spans(
        piece_output, jnp.dot(select_items, cut_likelihood, precision=deepest_tier)
    )
    confidence = jnp.where(cut_marks == 1, cut_likelihood, 1.0 - cut_likelihood)
    return shortcut_sum + confidence[:, None] * jnp.dot(
        broadcast_back, smoothed, precision=deepest_tier
    )


def adam_step(weight, grad, first, second, rate, decay):
    first_new = beta_one * first + (1.0 - beta_one) * grad
    second_new = beta_two * second + (1.0 - beta_two) * grad * grad
    ratio = (
        first_new
        / (1.0 - beta_one**STEP)
        / (jnp.sqrt(second_new / (1.0 - beta_two**STEP)) + adam_eps)
    )
    return (first_new, second_new, weight - rate * (ratio + decay * weight))


def to_low(value_entries):
    return value_entries.astype(jnp.bfloat16)


def matmul_apply(left, right):
    return jnp.dot(left, right, preferred_element_type=jnp.float32)


def product_tn(left, right):
    return lax.dot_general(
        left, right, (((0,), (0,)), ((), ())), preferred_element_type=jnp.float32
    )


def product_nt(left, right):
    return lax.dot_general(
        left, right, (((1,), (1,)), ((), ())), preferred_element_type=jnp.float32
    )


def swap(value_entries, axis, mask):
    size = lax.axis_size(axis)
    return lax.ppermute(value_entries, axis, [(place, place ^ mask) for place in range(size)])


def bit_masks(size):
    masks = []
    mask = size // 2
    while mask >= 1:
        masks.append(mask)
        mask //= 2
    return masks


def spread_dp(shard):
    size = lax.axis_size("dp")
    pieces = [shard] + [swap(shard, "dp", mask) for mask in range(2, size, 2)]
    group = jnp.stack(pieces)
    return [(0, 0, group), (1, 0, swap(group, "dp", 1))]


def spread_all(shard):
    groups = spread_dp(shard)
    for mask in bit_masks(lax.axis_size("tensor")):
        groups = groups + [
            (dp_mask, tensor_mask | mask, swap(group, "tensor", mask))
            for dp_mask, tensor_mask, group in groups
        ]
    return groups


def place_kernel(marks, over_tensor, *refs):
    groups, whole, sems = refs[: len(marks)], refs[len(marks)], refs[len(marks) + 1]
    dp_place = lax.axis_index("dp")
    tensor_place = lax.axis_index("tensor")
    copies = []
    for (dp_mask, tensor_mask), group in zip(marks, groups):
        for position in range(group.shape[0]):
            source = dp_place ^ (2 * position + dp_mask)
            if over_tensor:
                source = source * lax.axis_size("tensor") + (tensor_place ^ tensor_mask)
            copies.append(
                pltpu.make_async_copy(group.at[position], whole.at[source], sems.at[len(copies)])
            )
    for copy in copies:
        copy.start()
    for copy in copies:
        copy.wait()


def place(groups, over_tensor):
    marks = [(dp_mask, tensor_mask) for dp_mask, tensor_mask, _ in groups]
    arrays = [group for _, _, group in groups]
    count = sum(array.shape[0] for array in arrays)
    return pl.pallas_call(
        partial(place_kernel, marks, over_tensor),
        out_shape=jax.ShapeDtypeStruct((count,) + arrays[0].shape[1:], arrays[0].dtype),
        in_specs=[pl.BlockSpec(memory_space=pl.ANY)] * len(arrays),
        out_specs=pl.BlockSpec(memory_space=pl.ANY),
        scratch_shapes=[pltpu.SemaphoreType.DMA((count,))],
        cost_estimate=pl.CostEstimate(
            flops=0, transcendentals=0, bytes_accessed=4 * count * arrays[0][0].size
        ),
    )(*arrays)


def gather_all(shard):
    return place(spread_all(shard), True)


def gather_dp(shard):
    return place(spread_dp(shard), False)


def take(value_entries, axis, index):
    return lax.dynamic_index_in_dim(value_entries, index, axis, keepdims=False)


def total(addends):
    result = addends[0].astype(jnp.float32)
    for addend in addends[1:]:
        result = result + addend.astype(jnp.float32)
    return result


def reduce_dp(addends):
    size = lax.axis_size("dp")
    place_dp = lax.axis_index("dp")
    split = [a.reshape((size // 2, 2) + a.shape[1:]) for a in addends]
    low = place_dp % 2
    sent = to_low(total([take(a, 1, 1 - low) for a in split]))
    addends = [take(a, 1, low) for a in split] + [swap(sent, "dp", 1)]
    high = place_dp // 2
    received = [
        swap(to_low(total([take(a, 0, high ^ mask) for a in addends])), "dp", 2 * mask)
        for mask in range(1, size // 2)
    ]
    return total([take(a, 0, high) for a in addends] + received)


def reduce_all(grad):
    tensor_size = lax.axis_size("tensor")
    place_tensor = lax.axis_index("tensor")
    grad = grad.reshape((lax.axis_size("dp"), tensor_size) + grad.shape[1:])
    addends = [grad]
    for mask in reversed(bit_masks(tensor_size)):
        split = [
            a.reshape((a.shape[0], a.shape[1] // 2, 2) + a.shape[2:]) for a in addends
        ]
        low = (place_tensor // mask) % 2
        sent = to_low(total([take(a, 2, 1 - low) for a in split]))
        addends = [take(a, 2, low) for a in split] + [swap(sent, "tensor", mask)]
    return reduce_dp([a[:, 0] for a in addends])


def add_everywhere(value_entries):
    for axis in ("tensor", "dp"):
        for mask in bit_masks(lax.axis_size(axis)):
            value_entries = value_entries + swap(value_entries, axis, mask)
    return value_entries


def gather_rows(value_entries):
    pieces = [value_entries]
    for mask in bit_masks(lax.axis_size("tensor")):
        pieces = pieces + [swap(piece, "tensor", mask) for piece in pieces]
    return jnp.concatenate(pieces, axis=0)


def total_lines(value_entries):
    size = lax.axis_size("tensor")
    rows = value_entries.shape[0] // size
    pieces = [to_low(value_entries[i * rows : (i + 1) * rows]) for i in range(size)]
    for mask in reversed(bit_masks(size)):
        half = len(pieces) // 2
        pieces = [
            pieces[i].astype(jnp.float32)
            + swap(to_low(pieces[half + i]), "tensor", mask).astype(jnp.float32)
            for i in range(half)
        ]
    return pieces[0]


gather_grads = gather_rows
sum_grads = total_lines


def mixer_forward(value_entries, w_in, exit_matrix, block_gain, smalls):
    rescaled_rows, rescale_grad = jax.vjp(root_mean_rescale, value_entries, block_gain)
    normed_low = to_low(rescaled_rows)
    projected = matmul_apply(normed_low, w_in)
    middle, middle_pull = jax.vjp(mixer_middle, projected, *smalls)
    middle_low = to_low(middle)
    return (
        value_entries + matmul_apply(middle_low, exit_matrix),
        (rescale_grad, normed_low, middle_pull, middle_low),
    )


def mixer_backward(slope_emitted, kept, w_in, exit_matrix):
    rescale_grad, normed_low, middle_pull, middle_low = kept
    grad_low = to_low(slope_emitted)
    slope_exit_matrix = product_tn(middle_low, grad_low)
    pulled = middle_pull(product_nt(grad_low, exit_matrix))
    grad_proj = to_low(pulled[0])
    grad_w_in = product_tn(normed_low, grad_proj)
    grad_values, slope_scale = rescale_grad(product_nt(grad_proj, w_in))
    return (grad_values + slope_emitted, grad_w_in, slope_exit_matrix, slope_scale, pulled[1:])


def causal_scores(queries, key_rows):
    scores = jnp.einsum(
        "gqhd,gkhd->ghqk", queries, key_rows, preferred_element_type=jnp.float32
    ) * HD ** (-0.5)
    causal = jnp.tril(jnp.ones((MAX_PIECES, MAX_PIECES), dtype=bool))
    return jnp.where(causal[None, None], scores, -jnp.inf)


def apply_heads(latent_holder, heed_scale, triple_matrix, exit_matrix):
    rescaled_rows, rescale_grad = jax.vjp(root_mean_rescale, latent_holder, heed_scale)
    rows_low = gather_rows(to_low(rescaled_rows))
    triple = to_low(
        jnp.einsum("td,dsh->tsh", rows_low, triple_matrix, preferred_element_type=jnp.float32)
    )
    groups = rows_low.shape[0] // MAX_PIECES
    heads_here = triple_matrix.shape[2] // HD
    split_heads = triple.reshape(groups, MAX_PIECES, 3, heads_here, HD)
    queries, key_rows, value_rows = (
        split_heads[:, :, 0],
        split_heads[:, :, 1],
        split_heads[:, :, 2],
    )
    scores = causal_scores(queries, key_rows)
    maxima = jnp.max(scores, axis=-1, keepdims=True)
    log_total = maxima + jnp.log(jnp.sum(jnp.exp(scores - maxima), axis=-1, keepdims=True))
    weights_soft = to_low(jnp.exp(scores - log_total))
    heads_output = to_low(
        jnp.einsum("ghqk,gkhd->gqhd", weights_soft, value_rows, preferred_element_type=jnp.float32)
    )
    heads_output = heads_output.reshape(rows_low.shape[0], heads_here * HD)
    outcome = latent_holder + total_lines(product_nt(heads_output, exit_matrix))
    return (
        outcome,
        (rescale_grad, rows_low, queries, key_rows, value_rows, log_total, heads_output),
    )


def apply_heads_grad(slope_emitted, kept, triple_matrix, exit_matrix):
    rescale_grad, rows_low, queries, key_rows, value_rows, log_total, heads_output = kept
    grad_rows = gather_grads(to_low(slope_emitted))
    slope_exit_matrix = product_tn(grad_rows, heads_output)
    grad_attended = to_low(matmul_apply(grad_rows, exit_matrix)).reshape(queries.shape)
    weights_soft = jnp.exp(causal_scores(queries, key_rows) - log_total)
    grad_values = jnp.einsum(
        "ghqk,gqhd->gkhd", to_low(weights_soft), grad_attended, preferred_element_type=jnp.float32
    )
    grad_weights = jnp.einsum(
        "gqhd,gkhd->ghqk", grad_attended, value_rows, preferred_element_type=jnp.float32
    )
    grad_scores = to_low(
        weights_soft * (grad_weights - jnp.sum(weights_soft * grad_weights, axis=-1, keepdims=True))
    )
    grad_queries = jnp.einsum(
        "ghqk,gkhd->gqhd", grad_scores, key_rows, preferred_element_type=jnp.float32
    ) * HD ** (-0.5)
    grad_keys = jnp.einsum(
        "ghqk,gqhd->gkhd", grad_scores, queries, preferred_element_type=jnp.float32
    ) * HD ** (-0.5)
    grad_triple = to_low(
        jnp.stack([grad_queries, grad_keys, grad_values], axis=2).reshape(rows_low.shape[0], 3, -1)
    )
    slope_triple_matrix = jnp.einsum(
        "td,tsh->dsh", rows_low, grad_triple, preferred_element_type=jnp.float32
    )
    slope_rescaled = sum_grads(
        jnp.einsum("tsh,dsh->td", grad_triple, triple_matrix, preferred_element_type=jnp.float32)
    )
    gradient_holder, slope_scale = rescale_grad(slope_rescaled)
    return (gradient_holder + slope_emitted, slope_triple_matrix, slope_exit_matrix, slope_scale)


def swiglu(both):
    return jax.nn.silu(both[:, 0]) * both[:, 1]


def perceptron_apply(latent_holder, perceptron_scale, lift_matrix, lower_matrix):
    rescaled_rows, rescale_grad = jax.vjp(root_mean_rescale, latent_holder, perceptron_scale)
    rows_low = gather_rows(to_low(rescaled_rows))
    latent_state, act_pull = jax.vjp(
        swiglu, jnp.einsum("td,dsf->tsf", rows_low, lift_matrix, preferred_element_type=jnp.float32)
    )
    latent_merged = to_low(latent_state)
    outcome = latent_holder + total_lines(product_nt(latent_merged, lower_matrix))
    return (outcome, (rescale_grad, rows_low, act_pull, latent_merged))


def perceptron_grad(slope_emitted, kept, lift_matrix, lower_matrix):
    rescale_grad, rows_low, act_pull, latent_merged = kept
    grad_rows = gather_grads(to_low(slope_emitted))
    slope_lower_matrix = product_tn(grad_rows, latent_merged)
    (grad_both,) = act_pull(matmul_apply(grad_rows, lower_matrix))
    grad_both = to_low(grad_both)
    slope_lift_matrix = jnp.einsum(
        "td,tsf->dsf", rows_low, grad_both, preferred_element_type=jnp.float32
    )
    slope_rescaled = sum_grads(
        jnp.einsum("tsf,dsf->td", grad_both, lift_matrix, preferred_element_type=jnp.float32)
    )
    gradient_holder, slope_scale = rescale_grad(slope_rescaled)
    return (gradient_holder + slope_emitted, slope_lift_matrix, slope_lower_matrix, slope_scale)


def body(
    byte_ids,
    targets,
    boundaries,
    lengths,
    tables,
    tables_first,
    tables_second,
    mamba_in,
    mamba_in_first,
    mamba_in_second,
    mamba_out,
    mamba_out_first,
    mamba_out_second,
    route_proj,
    route_proj_first,
    route_proj_second,
    small_params,
    small_params_first,
    small_params_second,
    heed_triple_matrix,
    attn_qkv_first,
    attn_qkv_second,
    heed_exit_matrix,
    attn_out_first,
    attn_out_second,
    lifting_matrix,
    mlp_gate_up_first,
    mlp_gate_up_second,
    lowering_matrix,
    mlp_down_first,
    mlp_down_second,
):
    devices = lax.axis_size("dp") * lax.axis_size("tensor")
    table_rows = tables.shape[1]
    small_here = small_params.shape[0]
    mixed_rows = 2 * table_rows + 16
    length_pair = jnp.stack([lengths[0] // 16, lengths[0] % 16]).astype(jnp.bfloat16)
    tail = jnp.concatenate([to_low(small_params), length_pair])
    mixed = jnp.concatenate(
        [
            to_low(tables).reshape(2 * table_rows, BYTE_WIDTH),
            jnp.pad(tail, (0, 16 * BYTE_WIDTH - tail.shape[0])).reshape(16, BYTE_WIDTH),
        ]
    )
    mixed_whole = gather_all(mixed)
    full_tables = (
        mixed_whole[:, : 2 * table_rows]
        .reshape(devices, 2, table_rows, BYTE_WIDTH)
        .transpose(1, 0, 2, 3)
        .reshape(2, VOCAB, BYTE_WIDTH)
    )
    tails = mixed_whole[:, 2 * table_rows :].reshape(devices, -1)
    full_small = tails[:, :small_here].reshape(-1)
    pairs = tails[:, small_here : small_here + 2].astype(jnp.float32)
    byte_count = jnp.sum(pairs[:, 0] * 16.0 + pairs[:, 1])
    full_in = [None, None]
    full_out = [None, None]
    full_in[0] = gather_all(to_low(mamba_in[0])).reshape(BYTE_WIDTH, -1)
    full_out[0] = gather_all(to_low(mamba_out[0])).reshape(INNER, BYTE_WIDTH)
    full_route = gather_all(to_low(route_proj)).reshape(BYTE_WIDTH, -1)
    triple_whole = gather_dp(to_low(heed_triple_matrix)).reshape(
        (CORE_WIDTH,) + heed_triple_matrix.shape[1:]
    )
    heed_exit_whole = gather_dp(to_low(heed_exit_matrix).T).reshape(CORE_WIDTH, -1)
    lift_matrix_whole = gather_dp(to_low(lifting_matrix)).reshape(
        (CORE_WIDTH,) + lifting_matrix.shape[1:]
    )
    lower_matrix_whole = gather_dp(to_low(lowering_matrix).T).reshape(CORE_WIDTH, -1)
    full_in[1] = gather_all(to_low(mamba_in[1])).reshape(BYTE_WIDTH, -1)
    full_out[1] = gather_all(to_low(mamba_out[1])).reshape(INNER, BYTE_WIDTH)
    (
        block_gains,
        gated_gains,
        core_scales,
        head_gain,
        blank_row,
        conv_taps,
        skip_gains,
        a_logs,
        dt_biases,
    ) = unpack_small(full_small.astype(jnp.float32))
    layer_smalls = [
        (
            conv_taps[layer_index],
            skip_gains[layer_index],
            a_logs[layer_index],
            dt_biases[layer_index],
            gated_gains[layer_index],
        )
        for layer_index in range(2)
    ]
    cut_marks = boundaries[0]
    seq_len = byte_ids.shape[1]
    vocab_ids = jnp.arange(VOCAB, dtype=jnp.int32)
    onehot_in = (byte_ids[0][:, None] == vocab_ids[None, :]).astype(jnp.bfloat16)
    embedded = matmul_apply(onehot_in, full_tables[0])
    packer_output, kept_enc = mixer_forward(
        embedded, full_in[0], full_out[0], block_gains[0], layer_smalls[0]
    )
    encoded_low = to_low(packer_output)
    directed_rows = matmul_apply(encoded_low, full_route)
    cut_likelihood, prob_pull = jax.vjp(
        route_prob, directed_rows[:, :BYTE_WIDTH], directed_rows[:, BYTE_WIDTH : 2 * BYTE_WIDTH]
    )
    select_items, broadcast_back = span_maps(cut_marks)
    latent_holder, merge_transpose = jax.vjp(
        partial(merge_into_pieces, select_items), packer_output, blank_row
    )
    latent_holder, saved_heeding = apply_heads(
        latent_holder, core_scales[0], triple_whole, heed_exit_whole
    )
    latent_holder, saved_perceptron = perceptron_apply(
        latent_holder, core_scales[1], lift_matrix_whole, lower_matrix_whole
    )
    unpacked_bytes, link_layers_grad = jax.vjp(
        partial(link_layers, select_items, broadcast_back, cut_marks),
        latent_holder,
        core_scales[2],
        cut_likelihood,
        directed_rows[:, 2 * BYTE_WIDTH :],
    )
    final_out, kept_dec = mixer_forward(
        unpacked_bytes, full_in[1], full_out[1], block_gains[1], layer_smalls[1]
    )
    head_in, head_pull = jax.vjp(root_mean_rescale, final_out, head_gain)
    head_low = to_low(head_in)
    logits = product_nt(head_low, full_tables[1])
    maxima = jnp.max(logits, axis=-1, keepdims=True)
    log_total = maxima + jnp.log(jnp.sum(jnp.exp(logits - maxima), axis=-1, keepdims=True))
    onehot_out = (targets[0][:, None] == vocab_ids[None, :]).astype(jnp.float32)
    counted = (jnp.arange(seq_len, dtype=jnp.int32) < lengths[0]).astype(jnp.float32)[:, None]
    loss_local = jnp.sum((log_total - logits) * onehot_out * counted)
    grad_logits = to_low((jnp.exp(logits - log_total) - onehot_out) * counted / byte_count)
    grad_table_out = product_tn(grad_logits, head_low)
    grad_final, grad_head_gain = head_pull(matmul_apply(grad_logits, full_tables[1]))
    slope_unpacked, grad_in_dec, grad_out_dec, grad_block_dec, grad_small_dec = mixer_backward(
        grad_final, kept_dec, full_in[1], full_out[1]
    )
    gradient_holder, slope_closing_scale, slope_likelihood, slope_shortcut = link_layers_grad(
        slope_unpacked
    )
    gradient_holder, slope_lifting, slope_lowering, slope_perceptron_scale = perceptron_grad(
        gradient_holder, saved_perceptron, lift_matrix_whole, lower_matrix_whole
    )
    gradient_holder, slope_triple, slope_heed_exit, slope_heed_scale = apply_heads_grad(
        gradient_holder, saved_heeding, triple_whole, heed_exit_whole
    )
    gradient_merged, gradient_blank = merge_transpose(gradient_holder)
    grad_query, grad_key = prob_pull(slope_likelihood)
    grad_routed = to_low(jnp.concatenate([grad_query, grad_key, slope_shortcut], axis=1))
    grad_route = product_tn(encoded_low, grad_routed)
    grad_embedded, grad_in_enc, grad_out_enc, grad_block_enc, grad_small_enc = mixer_backward(
        gradient_merged + product_nt(grad_routed, full_route), kept_enc, full_in[0], full_out[0]
    )
    grad_table_in = jnp.dot(onehot_in.astype(jnp.float32).T, grad_embedded, precision=deepest_tier)
    grad_small = jnp.concatenate(
        [
            piece.reshape(-1)
            for piece in (
                jnp.stack([grad_block_enc, grad_block_dec]),
                jnp.stack([grad_small_enc[4], grad_small_dec[4]]),
                jnp.stack([slope_heed_scale, slope_perceptron_scale, slope_closing_scale]),
                grad_head_gain,
                gradient_blank,
                jnp.stack([grad_small_enc[0], grad_small_dec[0]]),
                jnp.stack([grad_small_enc[1], grad_small_dec[1]]),
                jnp.stack([grad_small_enc[2], grad_small_dec[2]]),
                jnp.stack([grad_small_enc[3], grad_small_dec[3]]),
            )
        ]
    )
    def by_device(grad):
        return to_low(grad).reshape((devices, grad.shape[0] // devices) + grad.shape[1:])

    def by_dp(grad):
        size = lax.axis_size("dp")
        return to_low(grad).reshape((size, grad.shape[0] // size) + grad.shape[1:])

    reduced_in_dec = reduce_all(by_device(grad_in_dec))
    reduced_out_dec = reduce_all(by_device(grad_out_dec))
    reduced_gate_up = reduce_dp([by_dp(slope_lifting)])
    reduced_down = reduce_dp([by_dp(slope_lowering)]).T
    reduced_qkv = reduce_dp([by_dp(slope_triple)])
    reduced_wo = reduce_dp([by_dp(slope_heed_exit)]).T
    reduced_route = reduce_all(by_device(grad_route))
    reduced_in_enc = reduce_all(by_device(grad_in_enc))
    reduced_out_enc = reduce_all(by_device(grad_out_enc))
    grad_mixed = jnp.concatenate(
        [
            to_low(grad_table_in).reshape(devices, table_rows, BYTE_WIDTH),
            to_low(grad_table_out).reshape(devices, table_rows, BYTE_WIDTH),
            jnp.pad(
                to_low(grad_small).reshape(devices, small_here),
                ((0, 0), (0, 16 * BYTE_WIDTH - small_here)),
            ).reshape(devices, 16, BYTE_WIDTH),
        ],
        axis=1,
    )
    reduced_mixed = reduce_all(grad_mixed)
    reduced_tables = reduced_mixed[: 2 * table_rows].reshape(2, table_rows, BYTE_WIDTH)
    reduced_small = reduced_mixed[2 * table_rows :].reshape(-1)[:small_here]
    reduced_in = jnp.stack([reduced_in_enc, reduced_in_dec])
    reduced_out = jnp.stack([reduced_out_enc, reduced_out_dec])
    reduced = (
        reduced_tables,
        reduced_in,
        reduced_out,
        reduced_route,
        reduced_small,
        reduced_qkv,
        reduced_wo,
        reduced_gate_up,
        reduced_down,
    )
    squares = sum((jnp.sum(grad * grad) for grad in reduced))
    totals = add_everywhere(jnp.stack([squares, loss_local]).reshape(1, 2))
    square_total, loss_sum = (totals[0, 0], totals[0, 1])
    grad_norm = jnp.sqrt(square_total)
    clip_factor = jnp.minimum(1.0, max_norm / (grad_norm + 1e-06))
    masters = (
        tables,
        mamba_in,
        mamba_out,
        route_proj,
        small_params,
        heed_triple_matrix,
        heed_exit_matrix,
        lifting_matrix,
        lowering_matrix,
    )
    firsts = (
        tables_first,
        mamba_in_first,
        mamba_out_first,
        route_proj_first,
        small_params_first,
        attn_qkv_first,
        attn_out_first,
        mlp_gate_up_first,
        mlp_down_first,
    )
    seconds = (
        tables_second,
        mamba_in_second,
        mamba_out_second,
        route_proj_second,
        small_params_second,
        attn_qkv_second,
        attn_out_second,
        mlp_gate_up_second,
        mlp_down_second,
    )
    rate_list = (
        rate_byte,
        rate_byte,
        rate_byte,
        rate_byte,
        rate_small,
        rate_main,
        rate_main,
        rate_main,
        rate_main,
    )
    decay_list = (
        weight_decay,
        weight_decay,
        weight_decay,
        weight_decay,
        0.0,
        weight_decay,
        weight_decay,
        weight_decay,
        weight_decay,
    )
    updated = [
        adam_step(
            masters[position],
            clip_factor * reduced[position],
            firsts[position],
            seconds[position],
            rate_list[position],
            decay_list[position],
        )
        for position in range(9)
    ]
    return (loss_sum, byte_count, grad_norm) + tuple(
        (member for triple_out in updated for member in triple_out)
    )


def solution(mesh):
    return jax.shard_map(
        body,
        mesh=mesh,
        in_specs=(
            P(("dp", "tensor"), None),
            P(("dp", "tensor"), None),
            P(("dp", "tensor"), None),
            P(("dp", "tensor")),
            P(None, ("dp", "tensor"), None),
            P(None, ("dp", "tensor"), None),
            P(None, ("dp", "tensor"), None),
            P(None, ("dp", "tensor"), None),
            P(None, ("dp", "tensor"), None),
            P(None, ("dp", "tensor"), None),
            P(None, ("dp", "tensor"), None),
            P(None, ("dp", "tensor"), None),
            P(None, ("dp", "tensor"), None),
            P(("dp", "tensor"), None),
            P(("dp", "tensor"), None),
            P(("dp", "tensor"), None),
            P(("dp", "tensor")),
            P(("dp", "tensor")),
            P(("dp", "tensor")),
            P("dp", None, "tensor"),
            P("dp", None, "tensor"),
            P("dp", None, "tensor"),
            P("tensor", "dp"),
            P("tensor", "dp"),
            P("tensor", "dp"),
            P("dp", None, "tensor"),
            P("dp", None, "tensor"),
            P("dp", None, "tensor"),
            P("tensor", "dp"),
            P("tensor", "dp"),
            P("tensor", "dp"),
        ),
        out_specs=(
            P(),
            P(),
            P(),
            P(None, ("dp", "tensor"), None),
            P(None, ("dp", "tensor"), None),
            P(None, ("dp", "tensor"), None),
            P(None, ("dp", "tensor"), None),
            P(None, ("dp", "tensor"), None),
            P(None, ("dp", "tensor"), None),
            P(None, ("dp", "tensor"), None),
            P(None, ("dp", "tensor"), None),
            P(None, ("dp", "tensor"), None),
            P(("dp", "tensor"), None),
            P(("dp", "tensor"), None),
            P(("dp", "tensor"), None),
            P(("dp", "tensor")),
            P(("dp", "tensor")),
            P(("dp", "tensor")),
            P("dp", None, "tensor"),
            P("dp", None, "tensor"),
            P("dp", None, "tensor"),
            P("tensor", "dp"),
            P("tensor", "dp"),
            P("tensor", "dp"),
            P("dp", None, "tensor"),
            P("dp", None, "tensor"),
            P("dp", None, "tensor"),
            P("tensor", "dp"),
            P("tensor", "dp"),
            P("tensor", "dp"),
        ),
        check_vma=False,
    )
```

```python
from functools import partial

import jax
import jax.numpy as jnp
from jax import lax
from jax.experimental import pallas as pl
from jax.experimental.pallas import tpu as pltpu
from jax.sharding import PartitionSpec as P

BYTE_WIDTH = 1024
CORE_WIDTH = 1536
VOCAB = 256
STATE = 128
HEADDIM = 64
STEP = 10
INNER = 2048
MHEADS = 32
HD = 96
MAX_PIECES = 128


deepest_tier = lax.Precision.HIGHEST
norm_eps = 1e-05
ssd_block = 128
beta_one = 0.9
beta_two = 0.95
adam_eps = 1e-08
weight_decay = 0.1
max_norm = 0.01
rate_byte = 0.06
rate_main = 0.05
rate_small = 0.5


def root_mean_rescale(value_entries, gain_vec):
    return (
        value_entries
        * lax.rsqrt(jnp.mean(value_entries * value_entries, axis=-1, keepdims=True) + norm_eps)
        * gain_vec
    )


def softplus(value_entries):
    return jnp.log1p(jnp.exp(value_entries))


def unpack_small(vector):
    extents = [
        2 * BYTE_WIDTH,
        2 * INNER,
        3 * CORE_WIDTH,
        BYTE_WIDTH,
        CORE_WIDTH - BYTE_WIDTH,
        8 * (INNER + 2 * STATE),
        2 * INNER,
        2 * MHEADS,
        2 * MHEADS,
    ]
    pieces = []
    offset = 0
    for extent in extents:
        pieces.append(vector[offset : offset + extent])
        offset += extent
    return (
        pieces[0].reshape(2, BYTE_WIDTH),
        pieces[1].reshape(2, INNER),
        pieces[2].reshape(3, CORE_WIDTH),
        pieces[3],
        pieces[4],
        pieces[5].reshape(2, 4, INNER + 2 * STATE),
        pieces[6].reshape(2, INNER),
        pieces[7].reshape(2, MHEADS),
        pieces[8].reshape(2, MHEADS),
    )


def route_prob(queries, key_rows):
    unit_query = queries * lax.rsqrt(jnp.sum(queries * queries, axis=-1, keepdims=True) + 1e-06)
    unit_key = key_rows * lax.rsqrt(jnp.sum(key_rows * key_rows, axis=-1, keepdims=True) + 1e-06)
    cosine = jnp.sum(unit_query[1:] * unit_key[:-1], axis=-1)
    return jnp.concatenate([jnp.ones((1,), jnp.float32), 0.5 * (1.0 - cosine)])


def span_maps(cut_marks):
    owner_slot = jnp.cumsum(cut_marks) - 1
    position_labels = jnp.arange(MAX_PIECES, dtype=jnp.int32)
    broadcast_back = (owner_slot[:, None] == position_labels[None, :]).astype(jnp.float32)
    select_items = broadcast_back.T * cut_marks[None, :].astype(jnp.float32)
    return (select_items, broadcast_back)


def merge_into_pieces(select_items, value_entries, blank_row):
    spans = jnp.dot(select_items, value_entries, precision=deepest_tier)
    return jnp.concatenate(
        [spans, jnp.broadcast_to(blank_row, (MAX_PIECES, CORE_WIDTH - BYTE_WIDTH))], axis=1
    )


def decay_products(confidence):
    rows = lax.broadcasted_iota(jnp.int32, (MAX_PIECES, MAX_PIECES), 0)
    columns = lax.broadcasted_iota(jnp.int32, (MAX_PIECES, MAX_PIECES), 1)
    products = jnp.where(rows > columns, 1.0 - confidence[:, None], 1.0)
    reach = 1
    while reach < MAX_PIECES:
        shifted = jnp.concatenate(
            [jnp.ones((reach, MAX_PIECES), jnp.float32), products[:-reach]], axis=0
        )
        products = products * shifted
        reach *= 2
    return jnp.where(rows >= columns, products, 0.0)


@jax.custom_vjp
def smooth_spans(piece_output, confidence):
    products = decay_products(confidence)
    return jnp.dot(products, confidence[:, None] * piece_output, precision=deepest_tier)


def smooth_keep(piece_output, confidence):
    products = decay_products(confidence)
    smoothed = jnp.dot(products, confidence[:, None] * piece_output, precision=deepest_tier)
    return smoothed, (piece_output, confidence, products, smoothed)


def smooth_pull(kept, slope):
    piece_output, confidence, products, smoothed = kept
    spread = lax.dot_general(
        products, slope, (((0,), (0,)), ((), ())), precision=deepest_tier
    )
    before = jnp.concatenate([jnp.zeros((1, smoothed.shape[1]), jnp.float32), smoothed[:-1]], axis=0)
    return (confidence[:, None] * spread, jnp.sum(spread * (piece_output - before), axis=-1))


smooth_spans.defvjp(smooth_keep, smooth_pull)


def link_layers(
    select_items,
    broadcast_back,
    cut_marks,
    latent_holder,
    closing_scale,
    cut_likelihood,
    shortcut_sum,
):
    piece_output = root_mean_rescale(latent_holder, closing_scale)[:, :BYTE_WIDTH]
    smoothed = smooth_spans(
        piece_output, jnp.dot(select_items, cut_likelihood, precision=deepest_tier)
    )
    confidence = jnp.where(cut_marks == 1, cut_likelihood, 1.0 - cut_likelihood)
    return shortcut_sum + confidence[:, None] * jnp.dot(
        broadcast_back, smoothed, precision=deepest_tier
    )


def adam_step(weight, grad, first, second, rate, decay):
    first_new = beta_one * first + (1.0 - beta_one) * grad
    second_new = beta_two * second + (1.0 - beta_two) * grad * grad
    ratio = (
        first_new
        / (1.0 - beta_one**STEP)
        / (jnp.sqrt(second_new / (1.0 - beta_two**STEP)) + adam_eps)
    )
    return (first_new, second_new, weight - rate * (ratio + decay * weight))


def to_low(value_entries):
    return value_entries.astype(jnp.bfloat16)


def matmul_apply(left, right):
    return jnp.dot(left, right, preferred_element_type=jnp.float32)


def product_tn(left, right):
    return lax.dot_general(
        left, right, (((0,), (0,)), ((), ())), preferred_element_type=jnp.float32
    )


def product_nt(left, right):
    return lax.dot_general(
        left, right, (((1,), (1,)), ((), ())), preferred_element_type=jnp.float32
    )


def swap(value_entries, axis, mask):
    size = lax.axis_size(axis)
    return lax.ppermute(value_entries, axis, [(place, place ^ mask) for place in range(size)])


def bit_masks(size):
    masks = []
    mask = 1
    while mask < size:
        masks.append(mask)
        mask *= 2
    return masks


def after(value_entries, earlier):
    if not earlier:
        return value_entries
    return lax.optimization_barrier((value_entries,) + tuple(earlier))[0]


def spread_masks(over_tensor):
    dp_masks = bit_masks(lax.axis_size("dp"))
    masks = [("dp", mask) for mask in dp_masks[1:] + dp_masks[:1]]
    if over_tensor:
        masks += [("tensor", mask) for mask in reversed(bit_masks(lax.axis_size("tensor")))]
    return masks


class Summing:
    def __init__(self, grad, over_tensor):
        self.masks = list(reversed(spread_masks(over_tensor)))
        names = [("dp", mask) for mask in reversed(bit_masks(lax.axis_size("dp")))]
        if over_tensor:
            names += [("tensor", mask) for mask in reversed(bit_masks(lax.axis_size("tensor")))]
        self.names = names
        rows = grad.shape[0] // 2 ** len(names)
        self.addends = [grad.reshape((2,) * len(names) + (rows,) + grad.shape[1:])]
        self.pending = None

    def operand(self):
        axis, mask = self.masks[0]
        position = self.names.index((axis, mask))
        own = (lax.axis_index(axis) // mask) % 2
        return to_low(total([take(addend, position, 1 - own) for addend in self.addends]))

    def accept(self):
        axis, mask = self.masks.pop(0)
        position = self.names.index((axis, mask))
        own = (lax.axis_index(axis) // mask) % 2
        self.addends = [take(addend, position, own) for addend in self.addends] + [self.pending]
        self.pending = None
        self.names.pop(position)

    def begun_last(self):
        left = [mask for axis, mask in self.masks if axis == "dp" and mask > 1]
        return 0 < len(left) == len(self.masks) < len(bit_masks(lax.axis_size("dp"))) - 1

    def rest(self):
        kind = []
        for axis, mask in self.masks:
            name = ("core", "y")[mask - 1] if axis == "tensor" else ("x" if mask == 1 else "z")
            if name not in kind:
                kind.append(name)
        value_entries = to_low(total(self.addends)) if len(self.addends) > 1 else self.addends[0]
        return value_entries.reshape(-1, value_entries.shape[-1]), tuple(kind)

    def result(self):
        return total(self.addends)


def sum_slowly(job):
    while job.masks:
        axis, mask = job.masks[0]
        job.pending = swap(job.operand(), axis, mask)
        job.accept()
    return job.result()


class Conductor:
    def __init__(self):
        self.clock = 0.0
        self.jobs = []
        self.flights = []

    def add(self, job):
        self.jobs.append(job)
        return job

    def lane(self, job):
        axis, mask = job.masks[0]
        return (axis, mask if axis == "tensor" else min(mask, 2))

    def launch(self, limit, banned, value_entries):
        for job in self.jobs:
            if len(self.flights) >= limit:
                return
            if job.pending is not None or not job.masks:
                continue
            lane = self.lane(job)
            depth = 2 if lane in (("dp", 1), ("tensor", 1)) else 1
            if lane in banned or sum(flight[1] == lane for flight in self.flights) >= depth:
                continue
            axis, mask = job.masks[0]
            operand = job.operand()
            rate = 3.4 if (axis, mask) == ("tensor", 1) else 24.0
            if axis == "dp" and mask > 2:
                rate = 48.0
            job.pending = swap(after(operand, [value_entries]), axis, mask)
            start = max([self.clock] + [flight[0] - 8.0 for flight in self.flights if flight[1] == lane])
            self.flights.append((start + 8.0 + 1.2 * rate * operand.size * 2e-6, lane, job))

    def tick(self, value_entries, elapsed, banned=(), limit=5):
        self.clock += elapsed
        ended = [flight for flight in self.flights if flight[0] <= self.clock]
        if ended:
            value_entries = after(value_entries, [flight[2].pending for flight in ended])
            self.flights = [flight for flight in self.flights if flight[0] > self.clock]
            for flight in ended:
                flight[2].accept()
        self.launch(limit, banned, value_entries)
        return value_entries

    def close(self):
        for _, _, job in sorted(self.flights, key=lambda flight: flight[0]):
            job.accept()
        self.flights = []
        for job in self.jobs:
            while job.begun_last():
                axis, mask = job.masks[0]
                job.pending = swap(job.operand(), axis, mask)
                job.accept()


def flip(place, mask):
    result = place
    bit = 1
    while bit <= mask:
        if mask & bit:
            result = result + bit * (1 - 2 * ((place // bit) % 2))
        bit *= 2
    return result


def order_steps(jobs, depth=2):
    free, busy, flights, plan = {}, {}, [], []
    waiting = [0] * len(jobs)
    clock = 0.0
    while True:
        for job, steps in enumerate(jobs):
            step = waiting[job]
            if step < 0 or step >= len(steps):
                continue
            lane, cost = steps[step]
            if busy.get(lane, 0) >= depth:
                continue
            busy[lane] = busy.get(lane, 0) + 1
            free[lane] = max(free.get(lane, 0.0), clock) + cost
            flights.append((free[lane] + 1.5, job, step, lane))
            plan.append(("start", job, step))
            waiting[job] = -1 - step
        if not flights:
            return plan
        flight = min(flights)
        flights.remove(flight)
        clock, job, step, lane = flight
        busy[lane] -= 1
        plan.append(("wait", job, step))
        waiting[job] = step + 1


def link_cost(lane, elements):
    return elements * 2e-6 * {"core": 3.4, "y": 23.0, "x": 23.0, "z": 46.0}[lane]


def here():
    dp_place, tensor_place = lax.axis_index("dp"), lax.axis_index("tensor")
    return dp_place // 2, dp_place % 2, tensor_place // 2, tensor_place % 2


def partner(lane, mask, coordinates):
    z, x, y, core = coordinates
    if lane == "z":
        z = flip(z, mask)
    if lane == "x":
        x = 1 - x
    if lane == "y":
        y = 1 - y
    if lane == "core":
        core = 1 - core
    return (z * 2 + x, y * 2 + core)


def greet(line, depth_z, coordinates):
    z = coordinates[0]
    barrier = pltpu.get_barrier_semaphore()

    def tell(device):
        pl.semaphore_signal(
            barrier, inc=1, device_id=device, device_id_type=pl.DeviceIdType.MESH
        )

    for lane in ("x", "y", "core"):
        tell(partner(lane, 1, coordinates))
    if not line:
        for mask in range(1, depth_z):
            tell(partner("z", mask, coordinates))
        pl.semaphore_wait(barrier, depth_z + 2)
        return

    @pl.when(z > 0)
    def _():
        tell(beside(-1, coordinates))

    @pl.when(z < depth_z - 1)
    def _():
        tell(beside(1, coordinates))

    ends = (z == 0).astype(jnp.int32) + (z == depth_z - 1).astype(jnp.int32)
    pl.semaphore_wait(barrier, 5 - ends)


def beside(way, coordinates):
    z, x, y, core = coordinates
    return ((z + way) * 2 + x, y * 2 + core)


def spread_kernel(plan, jobs, depth_z, *refs):
    count = (len(refs) - 3) // 2
    shards, wholes = refs[:count], refs[count : 2 * count]
    send_sems, receive_sems, own_sems = refs[2 * count :]
    coordinates = here()
    z = coordinates[0]
    greet(True, depth_z, coordinates)

    def spot(job, free, z_place):
        array, kind, first, size = jobs[job]
        index = [
            slice(None) if name in free else (z_place if name == "z" else place)
            for name, place in zip(("z", "x", "y", "core"), coordinates)
            if name in kind
        ]
        return wholes[array].at[tuple(index) + (slice(None), pl.ds(first, size))]

    def shard(job):
        array, _, first, size = jobs[job]
        return shards[array].at[:, pl.ds(first, size)]

    own = []
    for job in range(len(jobs)):
        own.append(pltpu.make_async_copy(shard(job), spot(job, (), z), own_sems.at[job]))
        own[-1].start()

    def copies(job, step, receiving):
        steps = lanes_of(jobs[job][1], depth_z)
        lane, reach = steps[step]
        free = [name for name, _ in steps[:step] if name != lane]
        base = job * (2 * depth_z + 1)
        pairs = []
        if lane == "z":
            for side, way in enumerate((1, -1)):
                number = base + 2 * (reach - 1) + side
                if receiving:
                    block = z - way * reach
                    condition = (block >= 0) & (block < depth_z)
                    target = spot(job, free, z if step == 0 else block)
                    source = target
                else:
                    block = z - way * (reach - 1)
                    condition = (block >= 0) & (block < depth_z)
                    condition &= (z + way >= 0) & (z + way < depth_z)
                    target = spot(job, free, block)
                    source = shard(job) if step == 0 else target
                copy = pltpu.make_async_remote_copy(
                    src_ref=source,
                    dst_ref=target,
                    send_sem=send_sems.at[number],
                    recv_sem=receive_sems.at[number],
                    device_id=beside(way, coordinates),
                    device_id_type=pl.DeviceIdType.MESH,
                )
                pairs.append((condition, copy))
            return pairs
        number = base + 2 * (depth_z - 1) + ("x", "y", "core").index(lane)
        target = spot(job, free, z)
        copy = pltpu.make_async_remote_copy(
            src_ref=shard(job) if step == 0 else target,
            dst_ref=target,
            send_sem=send_sems.at[number],
            recv_sem=receive_sems.at[number],
            device_id=partner(lane, 1, coordinates),
            device_id_type=pl.DeviceIdType.MESH,
        )
        return [(None, copy)]

    def perform(pairs, action):
        for condition, copy in pairs:
            if condition is None:
                getattr(copy, action)()
            else:
                pl.when(condition)(getattr(copy, action))

    copied = set()
    for action, job, step in plan:
        steps = lanes_of(jobs[job][1], depth_z)
        if action == "start":
            if steps[step][0] != steps[0][0] and job not in copied:
                own[job].wait()
                copied.add(job)
            perform(copies(job, step, False), "start")
        else:
            perform(copies(job, step, True), "wait_recv")
    for action, job, step in plan:
        if action == "start":
            perform(copies(job, step, False), "wait_send")


def lanes_of(kind, depth_z):
    steps = []
    for name in kind:
        steps += [(name, reach) for reach in range(1, depth_z if name == "z" else 2)]
    return steps


def spread_whole(shards, jobs, collective_id):
    depth_z = lax.axis_size("dp") // 2
    costs = []
    for array, kind, first, size in jobs:
        held, steps = shards[array].shape[0] * size, []
        for lane in kind:
            cost = 23.0 if lane != "core" else 3.4
            steps += [(lane, held * 2e-6 * cost)] * (depth_z - 1 if lane == "z" else 1)
            held *= depth_z if lane == "z" else 2
        costs.append(steps)
    plan = order_steps(costs)
    sizes = {"z": depth_z, "x": 2, "y": 2, "core": 2}
    kinds = {array: kind for array, kind, _, _ in jobs}
    shapes = [
        tuple(sizes[name] for name in ("z", "x", "y", "core") if name in kinds[array])
        + shard.shape
        for array, shard in enumerate(shards)
    ]
    numbers = len(jobs) * (2 * depth_z + 1)
    wholes = pl.pallas_call(
        partial(spread_kernel, plan, jobs, depth_z),
        out_shape=tuple(jax.ShapeDtypeStruct(shape, jnp.bfloat16) for shape in shapes),
        in_specs=[pl.BlockSpec(memory_space=pltpu.VMEM)] * len(shards),
        out_specs=(pl.BlockSpec(memory_space=pl.ANY),) * len(shards),
        scratch_shapes=[
            pltpu.SemaphoreType.DMA((numbers,)),
            pltpu.SemaphoreType.DMA((numbers,)),
            pltpu.SemaphoreType.DMA((len(jobs),)),
        ],
        compiler_params=pltpu.CompilerParams(
            collective_id=collective_id, has_side_effects=True, vmem_limit_bytes=24 * 2**20
        ),
    )(*shards)
    return [whole.reshape(-1, whole.shape[-1]) for whole in wholes]


BYTE_LANES = ("z", "x", "y", "core")
MAIN_LANES = ("z", "x")


def sum_kernel(plan, kinds, depth_z, *refs):
    count = len(kinds)
    grads, extra = refs[:count], refs[count]
    outputs, totals = refs[count + 1 : 2 * count + 1], refs[2 * count + 1]
    rest = list(refs[2 * count + 2 :])
    coordinates = here()
    places = dict(zip(BYTE_LANES, coordinates))
    z = coordinates[0]
    mirrored = depth_z - 1 - z
    held, received, held_names = [], [], []
    for kind in kinds:
        held.append(rest.pop(0))
        received.append({lane: rest.pop(0) for lane in kind})
        held_names.append(names_held(kind))
    squares, arrivals, send_sems, receive_sems, own_sems, tile_sems = rest
    loads = []
    for job, kind in enumerate(kinds):
        spot = tuple(
            slice(None) if name in held_names[job] else places[name]
            for name in BYTE_LANES
            if name in kind
        )
        loads.append(pltpu.make_async_copy(grads[job].at[spot], held[job], own_sems.at[job]))
        loads[-1].start()
    squares[...] = jnp.zeros_like(squares)
    greet(False, depth_z, coordinates)

    def chosen(job, step, lane_place):
        steps = lanes_of(kinds[job], depth_z)
        lane = steps[step][0]
        done = [name for name, _ in steps[:step] if name != lane]
        return [
            lane_place if name == lane else (places[name] if name in done else slice(None))
            for name in held_names[job]
        ]

    def slot(reach, side):
        shared = (depth_z - 2) // 2
        return reach - 1 if reach <= shared else shared + 2 * (reach - 1 - shared) + side

    def copies(job, step, receiving):
        kind = kinds[job]
        lane, reach = lanes_of(kind, depth_z)[step]
        base = job * (2 * depth_z + 1)
        if lane == "z":
            pairs = []
            for side, depth in enumerate((z, mirrored)):
                way = 1 - 2 * side
                aim = depth_z - reach + depth
                if side:
                    aim = depth_z - 1 - aim
                landing = received[job]["z"].at[slot(reach, side)]
                number = base + 2 * (reach - 1) + side
                source = landing if receiving else held[job].at[tuple(chosen(job, step, aim))]
                copy = pltpu.make_async_remote_copy(
                    src_ref=source,
                    dst_ref=landing,
                    send_sem=send_sems.at[number],
                    recv_sem=receive_sems.at[number],
                    device_id=beside(way, coordinates),
                    device_id_type=pl.DeviceIdType.MESH,
                )
                condition = (depth >= 1) & (depth <= reach) if receiving else depth <= reach - 1
                pairs.append((condition, copy))
            return pairs
        number = base + 2 * (depth_z - 1) + ("x", "y", "core").index(lane)
        if step == 0:
            spot = tuple(
                1 - places[name] if name == lane else slice(None)
                for name in BYTE_LANES
                if name in kind
            )
            source = grads[job].at[spot]
        else:
            source = held[job].at[tuple(chosen(job, step, 1 - places[lane]))]
        copy = pltpu.make_async_remote_copy(
            src_ref=source,
            dst_ref=received[job][lane],
            send_sem=send_sems.at[number],
            recv_sem=receive_sems.at[number],
            device_id=partner(lane, 1, coordinates),
            device_id_type=pl.DeviceIdType.MESH,
        )
        return [(None, copy)]

    def add_pieces(job, step, lane_place, buffers, last):
        steps = lanes_of(kinds[job], depth_z)
        lane = steps[step][0]
        done = [name for name, _ in steps[:step] if name != lane]
        free = [name for name in BYTE_LANES if name in kinds[job] and name not in done + [lane]]
        sizes = [depth_z if name == "z" else 2 for name in free]
        pieces = 1
        for size in sizes:
            pieces *= size

        def piece(index, carry):
            spots, remainder = {}, index
            for name, size in reversed(list(zip(free, sizes))):
                spots[name] = remainder % size
                remainder = remainder // size
            mine = tuple(
                spots[name] if name in spots else (lane_place if name == lane else places[name])
                for name in held_names[job]
            )
            theirs = tuple(spots[name] for name in free)
            target = held[job].at[mine] if mine else held[job]
            arrived = [buffer.at[theirs] if theirs else buffer for buffer in buffers]
            rows, columns = target.shape[-2:]

            def row_step(number, inner):
                part = pl.ds(pl.multiple_of(number * 16, 16), 16)
                value = target[part, :].astype(jnp.float32)
                for other in arrived:
                    value = value + other[part, :].astype(jnp.float32)
                if last:
                    outputs[job][part, :] = value
                    square = jnp.zeros((16, 128), jnp.float32)
                    for first in range(0, columns, 128):
                        square = square + value[:, first : first + 128] * value[:, first : first + 128]
                    squares[...] += square
                else:
                    target[part, :] = to_low(value)
                return inner

            lax.fori_loop(0, rows // 16, row_step, 0)
            return carry

        if pieces == 1:
            piece(0, 0)
        else:
            lax.fori_loop(0, pieces, piece, 0)

    def accumulate(job, step):
        steps = lanes_of(kinds[job], depth_z)
        lane, reach = steps[step]
        last = step == len(steps) - 1
        if lane != "z":
            add_pieces(job, step, places[lane], [received[job][lane]], last)
            return
        buffers = [received[job]["z"].at[slot(reach, side)] for side in range(2)]
        if reach < depth_z - 1:
            for side, depth in enumerate((z, mirrored)):
                aim = depth_z - reach + depth - 1
                if side:
                    aim = depth_z - 1 - aim
                pl.when((depth >= 1) & (depth <= reach))(
                    partial(add_pieces, job, step, aim, [buffers[side]], False)
                )
            return
        ends = (z == 0) | (mirrored == 0)
        pl.when(jnp.logical_not(ends))(partial(add_pieces, job, step, z, buffers, last))
        pl.when(z == 0)(partial(add_pieces, job, step, z, buffers[1:], last))
        pl.when(mirrored == 0)(partial(add_pieces, job, step, z, buffers[:1], last))

    def perform(pairs, action):
        for condition, copy in pairs:
            if condition is None:
                getattr(copy, action)()
            else:
                pl.when(condition)(getattr(copy, action))

    loaded = set()
    for action, job, step in plan:
        lane = lanes_of(kinds[job], depth_z)[step][0]
        if job not in loaded and (action == "wait" or lane == "z"):
            loads[job].wait()
            loaded.add(job)
        if action == "start":
            perform(copies(job, step, False), "start")
        else:
            perform(copies(job, step, True), "wait_recv")
            accumulate(job, step)
    totals[...] = extra[...]
    totals[0:8, :] += squares[0:8, :] + squares[8:16, :]
    exchanges = [("core", 1), ("y", 1), ("x", 1)]
    mask = 1
    while mask < depth_z:
        exchanges.append(("z", mask))
        mask *= 2
    tiles = []
    for number, (lane, mask) in enumerate(exchanges):
        tiles.append(
            pltpu.make_async_remote_copy(
                src_ref=arrivals.at[2 * number],
                dst_ref=arrivals.at[2 * number + 1],
                send_sem=tile_sems.at[2 * number],
                recv_sem=tile_sems.at[2 * number + 1],
                device_id=partner(lane, mask, coordinates),
                device_id_type=pl.DeviceIdType.MESH,
            )
        )
        arrivals[2 * number] = totals[...]
        tiles[-1].start()
        tiles[-1].wait_recv()
        totals[...] += arrivals[2 * number + 1]
    for copy in tiles:
        copy.wait_send()
    for action, job, step in plan:
        if action == "start":
            perform(copies(job, step, False), "wait_send")


def names_held(kind):
    return [name for name in BYTE_LANES if name in kind and (name == "z" or name != kind[0])]


def sum_whole(grads, kinds, extra, collective_id):
    depth_z = lax.axis_size("dp") // 2
    sizes = {"z": depth_z, "x": 2, "y": 2, "core": 2}
    jobs, arrays, shapes, scratch = [], [], [], []
    for grad, kind in zip(grads, kinds):
        names = [name for name in BYTE_LANES if name in kind]
        pieces = 1
        for name in names:
            pieces *= sizes[name]
        piece = (grad.shape[0] // pieces, grad.shape[1])
        arrays.append(grad.reshape(tuple(sizes[name] for name in names) + piece))
        shapes.append(jax.ShapeDtypeStruct(piece, jnp.float32))
        steps, left = [], list(names)
        scratch.append(
            pltpu.VMEM(tuple(sizes[name] for name in names_held(kind)) + piece, jnp.bfloat16)
        )
        for lane in kind:
            left.remove(lane)
            rest = tuple(sizes[name] for name in left)
            extent = piece[0] * piece[1]
            for size in rest:
                extent *= size
            cost = 23.0 if lane != "core" else 3.4
            steps += [(lane, extent * 2e-6 * cost)] * (depth_z - 1 if lane == "z" else 1)
            lead = (2 * (depth_z - 1) - (depth_z - 2) // 2,) if lane == "z" else ()
            scratch.append(pltpu.VMEM(lead + rest + piece, jnp.bfloat16))
        jobs.append(steps)
    plan = order_steps(jobs)
    numbers = len(grads) * (2 * depth_z + 1)
    tile = jax.ShapeDtypeStruct(extra.shape, jnp.float32)
    rounds = 3 + len(bit_masks(depth_z))
    return pl.pallas_call(
        partial(sum_kernel, plan, kinds, depth_z),
        out_shape=tuple(shapes) + (tile,),
        in_specs=[pl.BlockSpec(memory_space=pl.ANY)] * len(grads)
        + [pl.BlockSpec(memory_space=pltpu.VMEM)],
        out_specs=(pl.BlockSpec(memory_space=pltpu.VMEM),) * (len(grads) + 1),
        scratch_shapes=scratch
        + [
            pltpu.VMEM((16, 128), jnp.float32),
            pltpu.VMEM((2 * rounds, 16, 128), jnp.float32),
            pltpu.SemaphoreType.DMA((numbers,)),
            pltpu.SemaphoreType.DMA((numbers,)),
            pltpu.SemaphoreType.DMA((len(grads),)),
            pltpu.SemaphoreType.DMA((2 * rounds,)),
        ],
        compiler_params=pltpu.CompilerParams(
            collective_id=collective_id, has_side_effects=True, vmem_limit_bytes=60 * 2**20
        ),
    )(*arrays, extra)


def take(value_entries, axis, index):
    return lax.dynamic_index_in_dim(value_entries, index, axis, keepdims=False)


def total(addends):
    result = addends[0].astype(jnp.float32)
    for addend in addends[1:]:
        result = result + addend.astype(jnp.float32)
    return result


def add_everywhere(value_entries):
    for axis in ("tensor", "dp"):
        for mask in bit_masks(lax.axis_size(axis)):
            value_entries = value_entries + swap(value_entries, axis, mask)
    return value_entries


def gather_rows(value_entries):
    pieces = [value_entries]
    for mask in reversed(bit_masks(lax.axis_size("tensor"))):
        pieces = pieces + [swap(piece, "tensor", mask) for piece in pieces]
    return jnp.concatenate(pieces, axis=0)


def total_lines(value_entries):
    size = lax.axis_size("tensor")
    rows = value_entries.shape[0] // size
    pieces = [to_low(value_entries[i * rows : (i + 1) * rows]) for i in range(size)]
    for mask in bit_masks(size):
        half = len(pieces) // 2
        pieces = [
            pieces[i].astype(jnp.float32)
            + swap(to_low(pieces[half + i]), "tensor", mask).astype(jnp.float32)
            for i in range(half)
        ]
    return pieces[0]


gather_grads = gather_rows
sum_grads = total_lines


def low_dot(left, right, left_dim, right_dim):
    return lax.dot_general(
        left, right, (((left_dim,), (right_dim,)), ((), ())), preferred_element_type=jnp.float32
    )


def three_parts(value_entries):
    high = to_low(value_entries)
    rest = value_entries - high.astype(jnp.float32)
    middle = to_low(rest)
    tail = to_low(rest - middle.astype(jnp.float32))
    return jnp.concatenate([high, middle, tail, jnp.zeros_like(high)], axis=1)


def sigmoid(value_entries):
    return 0.5 * jnp.tanh(0.5 * value_entries) + 0.5


def fold_rows(value_entries):
    return jnp.sum(value_entries.reshape(-1, 8, value_entries.shape[1]), axis=0)


def lower_ones():
    rows = lax.broadcasted_iota(jnp.int32, (ssd_block, ssd_block), 0)
    columns = lax.broadcasted_iota(jnp.int32, (ssd_block, ssd_block), 1)
    return (rows >= columns).astype(jnp.float32)


PROJ_WIDE = 2 * INNER + 2 * STATE + 128


def step_terms(raw_steps, decay_refs):
    shifted = raw_steps + decay_refs[1:2, :]
    steps = softplus(shifted)
    rates = -jnp.exp(decay_refs[0:1, :])
    cumulative = jnp.dot(
        lower_ones(), steps * rates, precision=deepest_tier, preferred_element_type=jnp.float32
    )
    return shifted, steps, rates, cumulative


def wide(parts, spread_wide, pair):
    columns = pl.ds(pl.multiple_of(pair * 2 * ssd_block, 2 * ssd_block), 2 * ssd_block)
    return low_dot(parts, spread_wide[:, columns], 1, 0)


def narrow(parts, spread_narrow, pair):
    return low_dot(parts, spread_narrow[:, lanes(pair)], 1, 0)


def head_tables():
    part = jnp.arange(ssd_block) % MHEADS
    valid = jnp.arange(ssd_block) < 3 * MHEADS
    heads = jnp.arange(MHEADS)
    hit = (part[:, None] == heads[None, :]) & valid[:, None]
    spread_wide = to_low(jnp.repeat(hit, ssd_block, axis=1))
    spread_narrow = to_low(jnp.repeat(hit, HEADDIM, axis=1))
    chosen = to_low(
        jnp.arange(INNER)[:, None] // HEADDIM == jnp.arange(ssd_block)[None, :]
    )
    later = jnp.where(
        jnp.arange(ssd_block)[:, None] >= jnp.arange(2 * ssd_block)[None, :] % ssd_block, 0.0, -1e30
    )
    return spread_wide, spread_narrow, chosen, later


def first_head():
    return lax.broadcasted_iota(jnp.int32, (ssd_block, ssd_block), 1) < HEADDIM


def both_heads(value_entries):
    mask = first_head()
    zeros = jnp.zeros_like(value_entries)
    return jnp.concatenate(
        [jnp.where(mask, value_entries, zeros), jnp.where(mask, zeros, value_entries)], axis=0
    )


def gap_decay(cumulative_wide, cumulative_rows, later):
    return jnp.exp((cumulative_wide - cumulative_rows) + later[...])


def store_turned(cumulative, turned_ref):
    blank = jnp.zeros((ssd_block, ssd_block - MHEADS), jnp.float32)
    turned_ref[...] = jnp.concatenate([cumulative, blank], axis=1).T


def turned_rows(turned_ref, pair):
    return jnp.concatenate(
        [turned_ref[pl.ds(2 * pair, 1), :], turned_ref[pl.ds(2 * pair + 1, 1), :]], axis=1
    )


def lanes(block):
    return pl.ds(pl.multiple_of(block * ssd_block, ssd_block), ssd_block)


def convolve(padded_ref, taps_ref, block):
    columns = lanes(block)
    result = taps_ref[0:1, columns] * padded_ref[5 : 5 + ssd_block, columns]
    for tap in range(1, 4):
        result = result + taps_ref[tap : tap + 1, columns] * padded_ref[
            5 + tap : 5 + tap + ssd_block, columns
        ]
    return result


def middle_kernel(
    projected,
    taps,
    skip,
    decay,
    gain,
    spread_wide,
    spread_narrow,
    later,
    middle,
    outcome,
    starts,
    padded,
    turned,
    state,
    gated,
):
    chunk = pl.program_id(0)
    streams_extent = INNER + 2 * STATE

    @pl.when(chunk == 0)
    def _():
        padded[0:8, :] = jnp.zeros((8, streams_extent), jnp.float32)
        state[...] = jnp.zeros_like(state)

    @pl.when(chunk > 0)
    def _():
        padded[0:8, :] = padded[ssd_block : ssd_block + 8, :]

    padded[8 : 8 + ssd_block, :] = projected[:, INNER : INNER + streams_extent]
    _, steps, _, cumulative = step_terms(
        projected[:, INNER + streams_extent : INNER + streams_extent + MHEADS], decay
    )
    store_turned(cumulative, turned)
    step_parts = three_parts(steps)
    cumulative_parts = three_parts(cumulative)

    def active(block):
        convolved = convolve(padded, taps, block)
        return convolved * sigmoid(convolved)

    in_low = to_low(active(INNER // ssd_block))
    out_low = to_low(active(INNER // ssd_block + 1))
    affinity = low_dot(out_low, in_low, 1, 1)
    affinity = jnp.concatenate([affinity, affinity], axis=1)
    mask = first_head()

    def pair_step(pair, square_sum):
        columns = lanes(pair)
        inputs = active(pair)
        weighted = inputs * narrow(step_parts, spread_narrow, pair)
        cumulative_wide = wide(cumulative_parts, spread_wide, pair)
        mixing = to_low(affinity * gap_decay(cumulative_wide, turned_rows(turned, pair), later))
        within = low_dot(mixing, both_heads(to_low(weighted)), 1, 0)
        cumulative_here = jnp.where(
            mask, cumulative_wide[:, :ssd_block], cumulative_wide[:, ssd_block:]
        )
        last = cumulative_here[ssd_block - 1 :, :]
        held = state[:, columns]
        starts[0, :, columns] = held
        across = jnp.exp(cumulative_here) * low_dot(out_low, to_low(held), 1, 0)
        to_end = to_low(weighted * jnp.exp(last - cumulative_here))
        state[:, columns] = jnp.exp(last) * held + low_dot(in_low, to_end, 0, 0)
        result = within + across + inputs * skip[:, columns]
        outcome[:, columns] = result
        gate = projected[:, columns]
        product = result * (gate * sigmoid(gate))
        gated[:, columns] = product
        return square_sum + product * product

    square_sum = lax.fori_loop(
        0,
        INNER // ssd_block,
        pair_step,
        jnp.zeros((ssd_block, ssd_block), jnp.float32),
        unroll=4,
    )
    scale = lax.rsqrt(jnp.sum(square_sum, axis=1, keepdims=True) * (1.0 / INNER) + norm_eps)

    def scale_step(pair, carry):
        columns = lanes(pair)
        middle[:, columns] = to_low(gated[:, columns] * scale * gain[:, columns])
        return carry

    lax.fori_loop(0, INNER // ssd_block, scale_step, 0, unroll=4)


def middle_slope_kernel(
    projected,
    earlier,
    outcome,
    starts,
    slope,
    taps,
    skip,
    decay,
    gain,
    spread_wide,
    spread_narrow,
    chosen_heads,
    masked,
    slope_projected,
    slope_taps,
    slope_skip,
    slope_gain,
    slope_decay,
    padded,
    turned,
    slope_state,
    slope_conv,
    slope_affinity,
    slope_maps,
    slope_cumulative,
    slope_steps,
):
    chunk = pl.num_programs(0) - 1 - pl.program_id(0)
    streams_extent = INNER + 2 * STATE
    pairs = INNER // ssd_block

    @pl.when(pl.program_id(0) == 0)
    def _():
        slope_state[...] = jnp.zeros_like(slope_state)
        slope_conv[ssd_block : ssd_block + 8, :] = jnp.zeros((8, streams_extent), jnp.float32)
        slope_taps[...] = jnp.zeros_like(slope_taps)
        slope_skip[...] = jnp.zeros_like(slope_skip)
        slope_gain[...] = jnp.zeros_like(slope_gain)
        slope_decay[...] = jnp.zeros_like(slope_decay)

    @pl.when(pl.program_id(0) > 0)
    def _():
        slope_conv[ssd_block : ssd_block + 8, :] = slope_conv[0:8, :]

    @pl.when(chunk == 0)
    def _():
        padded[0:8, :] = jnp.zeros((8, streams_extent), jnp.float32)

    @pl.when(chunk > 0)
    def _():
        padded[0:8, :] = earlier[:, INNER : INNER + streams_extent]

    padded[8 : 8 + ssd_block, :] = projected[:, INNER : INNER + streams_extent]
    slope_affinity[...] = jnp.zeros_like(slope_affinity)
    slope_maps[...] = jnp.zeros_like(slope_maps)
    slope_cumulative[...] = jnp.zeros_like(slope_cumulative)
    slope_steps[...] = jnp.zeros_like(slope_steps)
    shifted, steps, rates, cumulative = step_terms(
        projected[:, INNER + streams_extent : INNER + streams_extent + MHEADS], decay
    )
    store_turned(cumulative, turned)
    step_parts = three_parts(steps)
    cumulative_parts = three_parts(cumulative)

    def silu_pair(value_entries):
        share = sigmoid(value_entries)
        return value_entries * share, share * (1.0 + value_entries * (1.0 - share))

    def pull_convolved(block, slope_block):
        columns = lanes(block)
        slope_conv[0:ssd_block, columns] = slope_block
        result = taps[3:4, columns] * slope_block
        for tap in range(3):
            reach = 3 - tap
            result = result + taps[tap : tap + 1, columns] * slope_conv[
                reach : reach + ssd_block, columns
            ]
        for tap in range(4):
            slope_taps[tap, :, columns] += fold_rows(
                slope_block * padded[5 + tap : 5 + tap + ssd_block, columns]
            )
        slope_projected[:, lanes(block + pairs)] = to_low(result)

    in_map, in_pull = silu_pair(convolve(padded, taps, pairs))
    out_map, out_pull = silu_pair(convolve(padded, taps, pairs + 1))
    in_low, out_low = to_low(in_map), to_low(out_map)
    affinity = low_dot(out_low, in_low, 1, 1)
    affinity = jnp.concatenate([affinity, affinity], axis=1)
    mask = first_head()

    def sums_step(pair, sums):
        columns = lanes(pair)
        gate = projected[:, columns]
        product = outcome[:, columns] * (gate * sigmoid(gate))
        return (
            sums[0] + product * product,
            sums[1] + product * (slope[:, columns] * gain[:, columns]),
        )

    blank = jnp.zeros((ssd_block, ssd_block), jnp.float32)
    squares, crossed = lax.fori_loop(0, pairs, sums_step, (blank, blank), unroll=2)
    scale = lax.rsqrt(jnp.sum(squares, axis=1, keepdims=True) * (1.0 / INNER) + norm_eps)
    pulled = scale * scale * scale * (jnp.sum(crossed, axis=1, keepdims=True) * (1.0 / INNER))

    def pair_step(pair, carry):
        columns = lanes(pair)
        gate, total_here = projected[:, columns], outcome[:, columns]
        gate_value, gate_pull = silu_pair(gate)
        product = total_here * gate_value
        slope_here = slope[:, columns]
        slope_gain[:, columns] += fold_rows(slope_here * product * scale)
        slope_product = scale * (slope_here * gain[:, columns]) - product * pulled
        slope_out = slope_product * gate_value
        slope_projected[:, columns] = to_low(slope_product * total_here * gate_pull)
        inputs, inputs_pull = silu_pair(convolve(padded, taps, pair))
        slope_skip[:, columns] += fold_rows(slope_out * inputs)
        skip_here = skip[:, columns]
        scanned = total_here - inputs * skip_here
        steps_here = narrow(step_parts, spread_narrow, pair)
        weighted = inputs * steps_here
        weighted_low = to_low(weighted)
        slope_low = to_low(slope_out)
        cumulative_wide = wide(cumulative_parts, spread_wide, pair)
        gaps = gap_decay(cumulative_wide, turned_rows(turned, pair), masked)
        mixing = to_low(affinity * gaps)
        slope_mixing = low_dot(slope_low, both_heads(weighted_low), 1, 1)
        slope_gaps = slope_mixing * gaps
        slope_affinity[...] += slope_gaps[:, :ssd_block] + slope_gaps[:, ssd_block:]
        turned_back = low_dot(mixing, slope_low, 0, 0)
        slope_weighted = jnp.where(mask, turned_back[:ssd_block], turned_back[ssd_block:])
        cumulative_here = jnp.where(
            mask, cumulative_wide[:, :ssd_block], cumulative_wide[:, ssd_block:]
        )
        last = cumulative_here[ssd_block - 1 :, :]
        decayed = jnp.exp(last)
        held = starts[0, :, columns]
        held_low = to_low(held)
        slope_across = to_low(slope_out * jnp.exp(cumulative_here))
        slope_maps[1] += low_dot(slope_across, held_low, 1, 1)
        later = slope_state[:, columns]
        later_low = to_low(later)
        to_end = jnp.exp(last - cumulative_here)
        carried = to_low(weighted * to_end)
        slope_carried = low_dot(in_low, later_low, 1, 0)
        slope_maps[0] += low_dot(carried, later_low, 1, 1)
        slope_state[:, columns] = decayed * later + low_dot(out_low, slope_across, 0, 0)
        slope_within = slope_weighted
        slope_weighted = slope_weighted + slope_carried * to_end
        carried_slope = slope_carried * carried.astype(jnp.float32)
        ends = jnp.sum(carried_slope, axis=0, keepdims=True) + decayed * jnp.sum(
            later * held, axis=0, keepdims=True
        )
        rows = lax.broadcasted_iota(jnp.int32, (ssd_block, ssd_block), 0)
        slope_gathered = (
            slope_low.astype(jnp.float32) * scanned
            - weighted_low.astype(jnp.float32) * slope_within
            - carried_slope
            + jnp.where(rows == ssd_block - 1, ends, 0.0)
        )
        chosen = chosen_heads[lanes(pair), :]

        def head_sums(value_entries):
            high = to_low(value_entries)
            rest = to_low(value_entries - high.astype(jnp.float32))
            return low_dot(high, chosen, 1, 0) + low_dot(rest, chosen, 1, 0)

        slope_cumulative[...] += head_sums(slope_gathered)
        slope_steps[...] += head_sums(slope_weighted * inputs)
        slope_inputs = slope_out * skip_here + slope_weighted * steps_here
        pull_convolved(pair, slope_inputs * inputs_pull)
        return carry

    lax.fori_loop(0, pairs, pair_step, 0, unroll=2)
    affinity_low = to_low(slope_affinity[...])
    slope_in = slope_maps[0] + low_dot(affinity_low, out_low, 0, 0)
    slope_out_map = slope_maps[1] + low_dot(affinity_low, in_low, 1, 0)
    pull_convolved(pairs, slope_in * in_pull)
    pull_convolved(pairs + 1, slope_out_map * out_pull)
    slope_changes = lax.dot_general(
        lower_ones(),
        slope_cumulative[...],
        (((0,), (0,)), ((), ())),
        precision=deepest_tier,
        preferred_element_type=jnp.float32,
    )[:, :MHEADS]
    slope_step = slope_steps[:, :MHEADS] + slope_changes * rates
    slope_raw = slope_step * sigmoid(shifted)
    slope_decay[0] += fold_rows(slope_changes * steps) * rates
    slope_decay[1] += fold_rows(slope_raw)
    slope_projected[:, INNER + streams_extent :] = jnp.concatenate(
        [to_low(slope_raw), jnp.zeros((ssd_block, 128 - MHEADS), jnp.bfloat16)], axis=1
    )


def fixed(shape):
    return pl.BlockSpec(shape, lambda chunk: (0,) * len(shape))


def middle_forward(projected, smalls):
    conv_taps, skip_gain, a_log, dt_bias, gated_gain = smalls
    spread_wide, spread_narrow, chosen, later = head_tables()
    extent, columns = projected.shape
    chunks = extent // ssd_block
    streams_extent = INNER + 2 * STATE
    return pl.pallas_call(
        middle_kernel,
        grid=(chunks,),
        out_shape=(
            jax.ShapeDtypeStruct((extent, INNER), jnp.bfloat16),
            jax.ShapeDtypeStruct((extent, INNER), jnp.float32),
            jax.ShapeDtypeStruct((chunks, STATE, INNER), jnp.float32),
        ),
        in_specs=[
            pl.BlockSpec((ssd_block, columns), lambda chunk: (chunk, 0)),
            fixed((4, streams_extent)),
            fixed((1, INNER)),
            fixed((2, MHEADS)),
            fixed((1, INNER)),
            fixed(spread_wide.shape),
            fixed(spread_narrow.shape),
            fixed(later.shape),
        ],
        out_specs=(
            pl.BlockSpec((ssd_block, INNER), lambda chunk: (chunk, 0)),
            pl.BlockSpec((ssd_block, INNER), lambda chunk: (chunk, 0)),
            pl.BlockSpec((1, STATE, INNER), lambda chunk: (chunk, 0, 0)),
        ),
        scratch_shapes=[
            pltpu.VMEM((ssd_block + 8, streams_extent), jnp.float32),
            pltpu.VMEM((ssd_block, ssd_block), jnp.float32),
            pltpu.VMEM((STATE, INNER), jnp.float32),
            pltpu.VMEM((ssd_block, INNER), jnp.float32),
        ],
        compiler_params=pltpu.CompilerParams(vmem_limit_bytes=48 * 2**20),
        cost_estimate=pl.CostEstimate(
            flops=2 * 10**10, transcendentals=4 * 10**6, bytes_accessed=20 * 10**6
        ),
    )(
        projected,
        conv_taps,
        skip_gain.reshape(1, INNER),
        jnp.stack([a_log, dt_bias]),
        gated_gain.reshape(1, INNER),
        spread_wide,
        spread_narrow,
        later,
    )


def middle_backward(projected, outcome, starts, slope, smalls):
    conv_taps, skip_gain, a_log, dt_bias, gated_gain = smalls
    spread_wide, spread_narrow, chosen, later = head_tables()
    extent, columns = projected.shape
    chunks = extent // ssd_block
    streams_extent = INNER + 2 * STATE

    def back(chunk):
        return (chunks - 1 - chunk, 0)

    slope_projected, slope_taps, slope_skip, slope_gain, slope_decay = pl.pallas_call(
        middle_slope_kernel,
        grid=(chunks,),
        out_shape=(
            jax.ShapeDtypeStruct((extent, columns), jnp.bfloat16),
            jax.ShapeDtypeStruct((4, 8, streams_extent), jnp.float32),
            jax.ShapeDtypeStruct((8, INNER), jnp.float32),
            jax.ShapeDtypeStruct((8, INNER), jnp.float32),
            jax.ShapeDtypeStruct((2, 8, MHEADS), jnp.float32),
        ),
        in_specs=[
            pl.BlockSpec((ssd_block, columns), back),
            pl.BlockSpec(
                (8, columns),
                lambda chunk: (jnp.maximum((chunks - 1 - chunk) * (ssd_block // 8) - 1, 0), 0),
            ),
            pl.BlockSpec((ssd_block, INNER), back),
            pl.BlockSpec((1, STATE, INNER), lambda chunk: (chunks - 1 - chunk, 0, 0)),
            pl.BlockSpec((ssd_block, INNER), back),
            fixed((4, streams_extent)),
            fixed((1, INNER)),
            fixed((2, MHEADS)),
            fixed((1, INNER)),
            fixed(spread_wide.shape),
            fixed(spread_narrow.shape),
            fixed(chosen.shape),
            fixed(later.shape),
        ],
        out_specs=(
            pl.BlockSpec((ssd_block, columns), back),
            fixed((4, 8, streams_extent)),
            fixed((8, INNER)),
            fixed((8, INNER)),
            fixed((2, 8, MHEADS)),
        ),
        scratch_shapes=[
            pltpu.VMEM((ssd_block + 8, streams_extent), jnp.float32),
            pltpu.VMEM((ssd_block, ssd_block), jnp.float32),
            pltpu.VMEM((STATE, INNER), jnp.float32),
            pltpu.VMEM((ssd_block + 8, streams_extent), jnp.float32),
            pltpu.VMEM((ssd_block, ssd_block), jnp.float32),
            pltpu.VMEM((2, ssd_block, STATE), jnp.float32),
            pltpu.VMEM((ssd_block, ssd_block), jnp.float32),
            pltpu.VMEM((ssd_block, ssd_block), jnp.float32),
        ],
        compiler_params=pltpu.CompilerParams(vmem_limit_bytes=48 * 2**20),
        cost_estimate=pl.CostEstimate(
            flops=5 * 10**10, transcendentals=8 * 10**6, bytes_accessed=30 * 10**6
        ),
    )(
        projected,
        projected,
        outcome,
        starts,
        slope,
        conv_taps,
        skip_gain.reshape(1, INNER),
        jnp.stack([a_log, dt_bias]),
        gated_gain.reshape(1, INNER),
        spread_wide,
        spread_narrow,
        chosen,
        later,
    )
    slope_decay = jnp.sum(slope_decay, axis=1)
    return (
        slope_projected,
        (
            jnp.sum(slope_taps, axis=1),
            jnp.sum(slope_skip, axis=0),
            slope_decay[0],
            slope_decay[1],
            jnp.sum(slope_gain, axis=0),
        ),
    )


Y_LANE = (("tensor", 2),)


def mixer_forward(value_entries, w_in, exit_matrix, block_gain, smalls):
    rescaled_rows, rescale_grad = jax.vjp(root_mean_rescale, value_entries, block_gain)
    normed_low = to_low(rescaled_rows)
    projected = matmul_apply(normed_low, w_in)
    middle_low, outcome, starts = middle_forward(projected, smalls)
    return (
        value_entries + matmul_apply(middle_low, exit_matrix),
        (rescale_grad, normed_low, (projected, outcome, starts), middle_low),
    )


def mixer_backward(conductor, last, slope_emitted, kept, w_in, exit_matrix, smalls):
    rescale_grad, normed_low, middle_kept, middle_low = kept
    grad_low = to_low(slope_emitted)
    slope_exit_matrix = to_low(product_tn(middle_low, grad_low))
    job_out = conductor.add(Summing(slope_exit_matrix, True))
    slope_middle = product_nt(grad_low, exit_matrix)
    slope_middle = conductor.tick(after(slope_middle, [slope_exit_matrix]), 7.0)
    grad_proj, slope_smalls = middle_backward(*middle_kept, slope_middle, smalls)
    grad_proj = conductor.tick(grad_proj, 48.0, limit=0 if last else 5)
    grad_w_in = to_low(product_tn(normed_low, grad_proj))
    job_in = conductor.add(Summing(grad_w_in, True))
    grad_proj = conductor.tick(after(grad_proj, [grad_w_in]), 7.0, limit=0 if last else 5)
    grad_values, slope_scale = rescale_grad(product_nt(grad_proj, w_in))
    slope_value = conductor.tick(grad_values + slope_emitted, 10.0, Y_LANE, limit=0 if last else 5)
    return (slope_value, slope_scale, slope_smalls, (job_out, job_in))


def causal_scores(queries, key_rows):
    scores = jnp.einsum(
        "gqhd,gkhd->ghqk", queries, key_rows, preferred_element_type=jnp.float32
    ) * HD ** (-0.5)
    causal = jnp.tril(jnp.ones((MAX_PIECES, MAX_PIECES), dtype=bool))
    return jnp.where(causal[None, None], scores, -jnp.inf)


def apply_heads(latent_holder, heed_scale, triple_matrix, exit_matrix):
    rescaled_rows, rescale_grad = jax.vjp(root_mean_rescale, latent_holder, heed_scale)
    rows_low = gather_rows(to_low(rescaled_rows))
    triple = to_low(matmul_apply(rows_low, triple_matrix))
    groups = rows_low.shape[0] // MAX_PIECES
    heads_here = triple_matrix.shape[1] // (3 * HD)
    split_heads = triple.reshape(groups, MAX_PIECES, 3, heads_here, HD)
    queries, key_rows, value_rows = (
        split_heads[:, :, 0],
        split_heads[:, :, 1],
        split_heads[:, :, 2],
    )
    scores = causal_scores(queries, key_rows)
    maxima = jnp.max(scores, axis=-1, keepdims=True)
    log_total = maxima + jnp.log(jnp.sum(jnp.exp(scores - maxima), axis=-1, keepdims=True))
    weights_soft = to_low(jnp.exp(scores - log_total))
    heads_output = to_low(
        jnp.einsum("ghqk,gkhd->gqhd", weights_soft, value_rows, preferred_element_type=jnp.float32)
    )
    heads_output = heads_output.reshape(rows_low.shape[0], heads_here * HD)
    outcome = latent_holder + total_lines(product_nt(heads_output, exit_matrix))
    return (
        outcome,
        (rescale_grad, rows_low, queries, key_rows, value_rows, log_total, heads_output),
    )


def apply_heads_grad(conductor, slope_emitted, kept, triple_matrix, exit_matrix):
    rescale_grad, rows_low, queries, key_rows, value_rows, log_total, heads_output = kept
    grad_rows = conductor.tick(gather_grads(to_low(slope_emitted)), 12.0, Y_LANE)
    slope_exit_matrix = to_low(product_tn(grad_rows, heads_output))
    grad_attended = to_low(matmul_apply(grad_rows, exit_matrix)).reshape(queries.shape)
    weights_soft = jnp.exp(causal_scores(queries, key_rows) - log_total)
    grad_values = jnp.einsum(
        "ghqk,gqhd->gkhd", to_low(weights_soft), grad_attended, preferred_element_type=jnp.float32
    )
    grad_weights = jnp.einsum(
        "gqhd,gkhd->ghqk", grad_attended, value_rows, preferred_element_type=jnp.float32
    )
    grad_scores = to_low(
        weights_soft * (grad_weights - jnp.sum(weights_soft * grad_weights, axis=-1, keepdims=True))
    )
    grad_queries = jnp.einsum(
        "ghqk,gkhd->gqhd", grad_scores, key_rows, preferred_element_type=jnp.float32
    ) * HD ** (-0.5)
    grad_keys = jnp.einsum(
        "ghqk,gqhd->gkhd", grad_scores, queries, preferred_element_type=jnp.float32
    ) * HD ** (-0.5)
    grad_triple = to_low(
        jnp.stack([grad_queries, grad_keys, grad_values], axis=2).reshape(rows_low.shape[0], -1)
    )
    grad_triple = conductor.tick(after(grad_triple, [slope_exit_matrix]), 10.0, Y_LANE)
    slope_rescaled = sum_grads(product_nt(grad_triple, triple_matrix))
    slope_triple_matrix = to_low(product_tn(rows_low, grad_triple))
    job_exit = conductor.add(Summing(slope_exit_matrix, False))
    job_triple = conductor.add(Summing(slope_triple_matrix, False))
    slope_rescaled = conductor.tick(
        after(slope_rescaled, [slope_triple_matrix]), 10.0, Y_LANE
    )
    gradient_holder, slope_scale = rescale_grad(slope_rescaled)
    return (gradient_holder + slope_emitted, slope_scale, job_triple, job_exit)


def swiglu(both):
    half = both.shape[1] // 2
    return jax.nn.silu(both[:, :half]) * both[:, half:]


def perceptron_apply(latent_holder, perceptron_scale, lift_matrix, lower_matrix):
    rescaled_rows, rescale_grad = jax.vjp(root_mean_rescale, latent_holder, perceptron_scale)
    rows_low = gather_rows(to_low(rescaled_rows))
    latent_state, act_pull = jax.vjp(swiglu, matmul_apply(rows_low, lift_matrix))
    latent_merged = to_low(latent_state)
    outcome = latent_holder + total_lines(product_nt(latent_merged, lower_matrix))
    return (outcome, (rescale_grad, rows_low, act_pull, latent_merged))


def perceptron_grad(conductor, slope_emitted, kept, lift_matrix, lower_matrix):
    rescale_grad, rows_low, act_pull, latent_merged = kept
    grad_rows = conductor.tick(gather_grads(to_low(slope_emitted)), 13.0, Y_LANE)
    slope_lower_matrix = to_low(product_tn(grad_rows, latent_merged))
    job_lower = conductor.add(Summing(slope_lower_matrix, False))
    grad_rows = conductor.tick(after(grad_rows, [slope_lower_matrix]), 2.0, Y_LANE)
    (grad_both,) = act_pull(matmul_apply(grad_rows, lower_matrix))
    grad_both = conductor.tick(to_low(grad_both), 4.0, Y_LANE)
    slope_rescaled = sum_grads(product_nt(grad_both, lift_matrix))
    half = grad_both.shape[1] // 2
    slope_lifts = [
        to_low(product_tn(rows_low, grad_both[:, :half])),
        to_low(product_tn(rows_low, grad_both[:, half:])),
    ]
    slope_lifts = [conductor.add(Summing(slope, False)) for slope in slope_lifts]
    slope_rescaled = conductor.tick(slope_rescaled, 14.0, Y_LANE)
    gradient_holder, slope_scale = rescale_grad(slope_rescaled)
    return (gradient_holder + slope_emitted, slope_scale, job_lower, slope_lifts)


def body(
    byte_ids,
    targets,
    boundaries,
    lengths,
    tables,
    tables_first,
    tables_second,
    mamba_in,
    mamba_in_first,
    mamba_in_second,
    mamba_out,
    mamba_out_first,
    mamba_out_second,
    route_proj,
    route_proj_first,
    route_proj_second,
    small_params,
    small_params_first,
    small_params_second,
    heed_triple_matrix,
    attn_qkv_first,
    attn_qkv_second,
    heed_exit_matrix,
    attn_out_first,
    attn_out_second,
    lifting_matrix,
    mlp_gate_up_first,
    mlp_gate_up_second,
    lowering_matrix,
    mlp_down_first,
    mlp_down_second,
):
    devices = lax.axis_size("dp") * lax.axis_size("tensor")
    table_rows = tables.shape[1]
    small_here = small_params.shape[0]
    mixed_rows = 2 * table_rows + 16
    length_pair = jnp.stack([lengths[0] // 16, lengths[0] % 16]).astype(jnp.bfloat16)
    tail = jnp.concatenate([to_low(small_params), length_pair])
    mixed = jnp.concatenate(
        [
            to_low(tables).reshape(2 * table_rows, BYTE_WIDTH),
            jnp.pad(tail, (0, 16 * BYTE_WIDTH - tail.shape[0])).reshape(16, BYTE_WIDTH),
        ]
    )
    mixed_rows = mixed.shape[0]

    def wide_in(layer):
        low = to_low(mamba_in[layer])
        return jnp.pad(low, ((0, 0), (0, PROJ_WIDE - low.shape[1])))

    conductor = Conductor()
    exact_tiles = mamba_in.shape[1] % 16 == 0
    shards = [
        mixed,
        wide_in(0),
        to_low(mamba_out[0]),
        to_low(route_proj),
        to_low(heed_triple_matrix).reshape(heed_triple_matrix.shape[0], -1),
        to_low(heed_exit_matrix).T,
        to_low(lifting_matrix).reshape(lifting_matrix.shape[0], -1),
        to_low(lowering_matrix).T,
        wide_in(1),
        to_low(mamba_out[1]),
    ]
    kinds = [BYTE_LANES] * 4 + [MAIN_LANES] * 4 + [BYTE_LANES] * 2
    if exact_tiles:
        fan, late = MAIN_LANES, MAIN_LANES[::-1]
        in_first, in_last = 18 * 128, PROJ_WIDE - 18 * 128
        half_route = route_proj.shape[1] // 2
        half_lift = shards[6].shape[1] // 2
        jobs = [
            (3, BYTE_LANES, half_route, half_route),
            (9, BYTE_LANES, 0, BYTE_WIDTH),
            (8, BYTE_LANES, 0, in_first),
            (0, BYTE_LANES, 0, BYTE_WIDTH),
            (1, BYTE_LANES, in_first, in_last),
            (2, BYTE_LANES, 0, BYTE_WIDTH),
            (8, BYTE_LANES, in_first, in_last),
            (4, fan, 0, shards[4].shape[1]),
            (1, BYTE_LANES, 0, in_first),
            (6, fan, half_lift, half_lift),
            (3, BYTE_LANES, 0, half_route),
            (7, fan, 0, shards[7].shape[1]),
            (5, late, 0, shards[5].shape[1]),
            (6, late, 0, half_lift),
        ]
        wholes = spread_whole(shards, jobs, 0)
    else:
        wholes = [
            lax.all_gather(
                shard, ("dp", "tensor") if kind == BYTE_LANES else "dp", axis=0, tiled=True
            )
            for shard, kind in zip(shards, kinds)
        ]
    mixed_whole = wholes[0]
    full_in, full_out, full_route = [wholes[1], wholes[8]], [wholes[2], wholes[9]], wholes[3]
    triple_whole, heed_exit_whole, lift_matrix_whole, lower_matrix_whole = wholes[4:8]
    mixed_whole = mixed_whole.reshape(devices, mixed_rows, BYTE_WIDTH)
    full_tables = (
        mixed_whole[:, : 2 * table_rows]
        .reshape(devices, 2, table_rows, BYTE_WIDTH)
        .transpose(1, 0, 2, 3)
        .reshape(2, VOCAB, BYTE_WIDTH)
    )
    tails = mixed_whole[:, 2 * table_rows :].reshape(devices, -1)
    full_small = tails[:, :small_here].reshape(-1)
    pairs = tails[:, small_here : small_here + 2].astype(jnp.float32)
    byte_count = jnp.sum(pairs[:, 0] * 16.0 + pairs[:, 1])
    (
        block_gains,
        gated_gains,
        core_scales,
        head_gain,
        blank_row,
        conv_taps,
        skip_gains,
        a_logs,
        dt_biases,
    ) = unpack_small(full_small.astype(jnp.float32))
    layer_smalls = [
        (
            conv_taps[layer_index],
            skip_gains[layer_index],
            a_logs[layer_index],
            dt_biases[layer_index],
            gated_gains[layer_index],
        )
        for layer_index in range(2)
    ]
    cut_marks = boundaries[0]
    seq_len = byte_ids.shape[1]
    vocab_ids = jnp.arange(VOCAB, dtype=jnp.int32)
    onehot_in = (byte_ids[0][:, None] == vocab_ids[None, :]).astype(jnp.bfloat16)
    embedded = matmul_apply(onehot_in, full_tables[0])
    packer_output, kept_enc = mixer_forward(
        embedded, full_in[0], full_out[0], block_gains[0], layer_smalls[0]
    )
    encoded_low = to_low(packer_output)
    directed_rows = matmul_apply(encoded_low, full_route)
    cut_likelihood, prob_pull = jax.vjp(
        route_prob, directed_rows[:, :BYTE_WIDTH], directed_rows[:, BYTE_WIDTH : 2 * BYTE_WIDTH]
    )
    select_items, broadcast_back = span_maps(cut_marks)
    latent_holder, merge_transpose = jax.vjp(
        partial(merge_into_pieces, select_items), packer_output, blank_row
    )
    latent_holder, saved_heeding = apply_heads(
        latent_holder, core_scales[0], triple_whole, heed_exit_whole
    )
    latent_holder, saved_perceptron = perceptron_apply(
        latent_holder, core_scales[1], lift_matrix_whole, lower_matrix_whole
    )
    unpacked_bytes, link_layers_grad = jax.vjp(
        partial(link_layers, select_items, broadcast_back, cut_marks),
        latent_holder,
        core_scales[2],
        cut_likelihood,
        directed_rows[:, 2 * BYTE_WIDTH :],
    )
    final_out, kept_dec = mixer_forward(
        unpacked_bytes, full_in[1], full_out[1], block_gains[1], layer_smalls[1]
    )
    head_in, head_pull = jax.vjp(root_mean_rescale, final_out, head_gain)
    head_low = to_low(head_in)
    logits = product_nt(head_low, full_tables[1])
    maxima = jnp.max(logits, axis=-1, keepdims=True)
    log_total = maxima + jnp.log(jnp.sum(jnp.exp(logits - maxima), axis=-1, keepdims=True))
    onehot_out = (targets[0][:, None] == vocab_ids[None, :]).astype(jnp.float32)
    counted = (jnp.arange(seq_len, dtype=jnp.int32) < lengths[0]).astype(jnp.float32)[:, None]
    loss_local = jnp.sum((log_total - logits) * onehot_out * counted)
    grad_logits = to_low((jnp.exp(logits - log_total) - onehot_out) * counted / byte_count)
    grad_table_out = product_tn(grad_logits, head_low)
    grad_final, grad_head_gain = head_pull(matmul_apply(grad_logits, full_tables[1]))
    slope_unpacked, grad_block_dec, grad_small_dec, jobs_dec = mixer_backward(
        conductor, False, grad_final, kept_dec, full_in[1], full_out[1], layer_smalls[1]
    )
    gradient_holder, slope_closing_scale, slope_likelihood, slope_shortcut = link_layers_grad(
        slope_unpacked
    )
    gradient_holder, slope_perceptron_scale, job_lower, slope_lifts = perceptron_grad(
        conductor, conductor.tick(gradient_holder, 14.0, Y_LANE), saved_perceptron, lift_matrix_whole, lower_matrix_whole
    )
    gradient_holder, slope_heed_scale, *jobs_heads = apply_heads_grad(
        conductor, gradient_holder, saved_heeding, triple_whole, heed_exit_whole
    )
    gradient_merged, gradient_blank = merge_transpose(gradient_holder)
    grad_query, grad_key = prob_pull(slope_likelihood)
    grad_routed = to_low(jnp.concatenate([grad_query, grad_key, slope_shortcut], axis=1))
    grad_route = to_low(product_tn(encoded_low, grad_routed))
    job_route = conductor.add(Summing(grad_route, True))
    grad_routed = conductor.tick(after(grad_routed, [grad_route]), 7.0)
    grad_embedded, grad_block_enc, grad_small_enc, jobs_enc = mixer_backward(
        conductor,
        True,
        gradient_merged + product_nt(grad_routed, full_route),
        kept_enc,
        full_in[0],
        full_out[0],
        layer_smalls[0],
    )
    grad_table_in = jnp.dot(onehot_in.astype(jnp.float32).T, grad_embedded, precision=deepest_tier)
    grad_small = jnp.concatenate(
        [
            piece.reshape(-1)
            for piece in (
                jnp.stack([grad_block_enc, grad_block_dec]),
                jnp.stack([grad_small_enc[4], grad_small_dec[4]]),
                jnp.stack([slope_heed_scale, slope_perceptron_scale, slope_closing_scale]),
                grad_head_gain,
                gradient_blank,
                jnp.stack([grad_small_enc[0], grad_small_dec[0]]),
                jnp.stack([grad_small_enc[1], grad_small_dec[1]]),
                jnp.stack([grad_small_enc[2], grad_small_dec[2]]),
                jnp.stack([grad_small_enc[3], grad_small_dec[3]]),
            )
        ]
    )
    width = mamba_in.shape[2]
    grad_mixed = jnp.concatenate(
        [
            to_low(grad_table_in).reshape(devices, table_rows, BYTE_WIDTH),
            to_low(grad_table_out).reshape(devices, table_rows, BYTE_WIDTH),
            jnp.pad(
                to_low(grad_small).reshape(devices, small_here),
                ((0, 0), (0, 16 * BYTE_WIDTH - small_here)),
            ).reshape(devices, 16, BYTE_WIDTH),
        ],
        axis=1,
    )
    conductor.close()
    parts = [
        jobs_heads[1],
        slope_lifts[0],
        slope_lifts[1],
        jobs_heads[0],
        job_lower,
        jobs_dec[1],
        jobs_dec[0],
        jobs_enc[0],
        job_route,
        jobs_enc[1],
        Summing(grad_mixed.reshape(-1, BYTE_WIDTH), True),
    ]
    sums = [None if part.masks else part.result() for part in parts]
    open_parts = [number for number, part in enumerate(parts) if part.masks]
    rests = [parts[number].rest() for number in open_parts]
    grads = [grad for grad, _ in rests]
    sum_kinds = [
        kind[::-1] if number == 0 and len(kind) == 2 else kind
        for number, (_, kind) in enumerate(rests)
    ]
    if exact_tiles:
        early = sum((jnp.sum(part * part) for part in sums if part is not None), jnp.float32(0.0))
        extra = jnp.zeros((16, 128), jnp.float32).at[0, 0].set(early).at[8, 0].set(loss_local)
        *ends, totals = sum_whole(grads, sum_kinds, extra, 1)
        square_total, loss_sum = jnp.sum(totals[:8]), jnp.sum(totals[8:])
    else:
        ends = [sum_slowly(parts[number]) for number in open_parts]
    for number, end in zip(open_parts, ends):
        sums[number] = end
    reduced_wo = sums[0].T
    reduced_gate_up = jnp.stack([sums[1], sums[2]], axis=1)
    reduced_qkv = sums[3].reshape(heed_triple_matrix.shape)
    reduced_down = sums[4].T
    reduced_in_dec = sums[5][:, :width]
    reduced_out_dec, reduced_out_enc, reduced_route = sums[6:9]
    reduced_in_enc = sums[9][:, :width]
    reduced_mixed = sums[10]
    reduced_tables = reduced_mixed[: 2 * table_rows].reshape(2, table_rows, BYTE_WIDTH)
    reduced_small = reduced_mixed[2 * table_rows :].reshape(-1)[:small_here]
    reduced_in = jnp.stack([reduced_in_enc, reduced_in_dec])
    reduced_out = jnp.stack([reduced_out_enc, reduced_out_dec])
    reduced = (
        reduced_tables,
        reduced_in,
        reduced_out,
        reduced_route,
        reduced_small,
        reduced_qkv,
        reduced_wo,
        reduced_gate_up,
        reduced_down,
    )
    if not exact_tiles:
        squares = sum((jnp.sum(grad * grad) for grad in reduced))
        totals = add_everywhere(jnp.stack([squares, loss_local]).reshape(1, 2))
        square_total, loss_sum = (totals[0, 0], totals[0, 1])
    grad_norm = jnp.sqrt(square_total)
    clip_factor = jnp.minimum(1.0, max_norm / (grad_norm + 1e-06))
    masters = (
        tables,
        mamba_in,
        mamba_out,
        route_proj,
        small_params,
        heed_triple_matrix,
        heed_exit_matrix,
        lifting_matrix,
        lowering_matrix,
    )
    firsts = (
        tables_first,
        mamba_in_first,
        mamba_out_first,
        route_proj_first,
        small_params_first,
        attn_qkv_first,
        attn_out_first,
        mlp_gate_up_first,
        mlp_down_first,
    )
    seconds = (
        tables_second,
        mamba_in_second,
        mamba_out_second,
        route_proj_second,
        small_params_second,
        attn_qkv_second,
        attn_out_second,
        mlp_gate_up_second,
        mlp_down_second,
    )
    rate_list = (
        rate_byte,
        rate_byte,
        rate_byte,
        rate_byte,
        rate_small,
        rate_main,
        rate_main,
        rate_main,
        rate_main,
    )
    decay_list = (
        weight_decay,
        weight_decay,
        weight_decay,
        weight_decay,
        0.0,
        weight_decay,
        weight_decay,
        weight_decay,
        weight_decay,
    )
    updated = [
        adam_step(
            masters[position],
            clip_factor * reduced[position],
            firsts[position],
            seconds[position],
            rate_list[position],
            decay_list[position],
        )
        for position in range(9)
    ]
    return (loss_sum, byte_count, grad_norm) + tuple(
        (member for triple_out in updated for member in triple_out)
    )


def solution(mesh):
    return jax.shard_map(
        body,
        mesh=mesh,
        in_specs=(
            P(("dp", "tensor"), None),
            P(("dp", "tensor"), None),
            P(("dp", "tensor"), None),
            P(("dp", "tensor")),
            P(None, ("dp", "tensor"), None),
            P(None, ("dp", "tensor"), None),
            P(None, ("dp", "tensor"), None),
            P(None, ("dp", "tensor"), None),
            P(None, ("dp", "tensor"), None),
            P(None, ("dp", "tensor"), None),
            P(None, ("dp", "tensor"), None),
            P(None, ("dp", "tensor"), None),
            P(None, ("dp", "tensor"), None),
            P(("dp", "tensor"), None),
            P(("dp", "tensor"), None),
            P(("dp", "tensor"), None),
            P(("dp", "tensor")),
            P(("dp", "tensor")),
            P(("dp", "tensor")),
            P("dp", None, "tensor"),
            P("dp", None, "tensor"),
            P("dp", None, "tensor"),
            P("tensor", "dp"),
            P("tensor", "dp"),
            P("tensor", "dp"),
            P("dp", None, "tensor"),
            P("dp", None, "tensor"),
            P("dp", None, "tensor"),
            P("tensor", "dp"),
            P("tensor", "dp"),
            P("tensor", "dp"),
        ),
        out_specs=(
            P(),
            P(),
            P(),
            P(None, ("dp", "tensor"), None),
            P(None, ("dp", "tensor"), None),
            P(None, ("dp", "tensor"), None),
            P(None, ("dp", "tensor"), None),
            P(None, ("dp", "tensor"), None),
            P(None, ("dp", "tensor"), None),
            P(None, ("dp", "tensor"), None),
            P(None, ("dp", "tensor"), None),
            P(None, ("dp", "tensor"), None),
            P(("dp", "tensor"), None),
            P(("dp", "tensor"), None),
            P(("dp", "tensor"), None),
            P(("dp", "tensor")),
            P(("dp", "tensor")),
            P(("dp", "tensor")),
            P("dp", None, "tensor"),
            P("dp", None, "tensor"),
            P("dp", None, "tensor"),
            P("tensor", "dp"),
            P("tensor", "dp"),
            P("tensor", "dp"),
            P("dp", None, "tensor"),
            P("dp", None, "tensor"),
            P("dp", None, "tensor"),
            P("tensor", "dp"),
            P("tensor", "dp"),
            P("tensor", "dp"),
        ),
        check_vma=False,
    )
```

```python
from functools import partial

import jax
import jax.numpy as jnp
from jax import lax
from jax.experimental import pallas as pl
from jax.experimental.pallas import tpu as pltpu
from jax.sharding import PartitionSpec as P

BYTE_WIDTH = 1024
CORE_WIDTH = 1536
VOCAB = 256
STATE = 128
HEADDIM = 64
STEP = 10
INNER = 2048
MHEADS = 32
HD = 96
MAX_PIECES = 128


deepest_tier = lax.Precision.HIGHEST
norm_eps = 1e-05
ssd_block = 128
beta_one = 0.9
beta_two = 0.95
adam_eps = 1e-08
weight_decay = 0.1
max_norm = 0.01
rate_byte = 0.06
rate_main = 0.05
rate_small = 0.5


def root_mean_rescale(value_entries, gain_vec):
    return (
        value_entries
        * lax.rsqrt(jnp.mean(value_entries * value_entries, axis=-1, keepdims=True) + norm_eps)
        * gain_vec
    )


def softplus(value_entries):
    return jnp.log1p(jnp.exp(value_entries))


def unpack_small(vector):
    extents = [
        2 * BYTE_WIDTH,
        2 * INNER,
        3 * CORE_WIDTH,
        BYTE_WIDTH,
        CORE_WIDTH - BYTE_WIDTH,
        8 * (INNER + 2 * STATE),
        2 * INNER,
        2 * MHEADS,
        2 * MHEADS,
    ]
    pieces = []
    offset = 0
    for extent in extents:
        pieces.append(vector[offset : offset + extent])
        offset += extent
    return (
        pieces[0].reshape(2, BYTE_WIDTH),
        pieces[1].reshape(2, INNER),
        pieces[2].reshape(3, CORE_WIDTH),
        pieces[3],
        pieces[4],
        pieces[5].reshape(2, 4, INNER + 2 * STATE),
        pieces[6].reshape(2, INNER),
        pieces[7].reshape(2, MHEADS),
        pieces[8].reshape(2, MHEADS),
    )


def route_prob(queries, key_rows):
    unit_query = queries * lax.rsqrt(jnp.sum(queries * queries, axis=-1, keepdims=True) + 1e-06)
    unit_key = key_rows * lax.rsqrt(jnp.sum(key_rows * key_rows, axis=-1, keepdims=True) + 1e-06)
    cosine = jnp.sum(unit_query[1:] * unit_key[:-1], axis=-1)
    return jnp.concatenate([jnp.ones((1,), jnp.float32), 0.5 * (1.0 - cosine)])


def span_maps(cut_marks):
    owner_slot = jnp.cumsum(cut_marks) - 1
    position_labels = jnp.arange(MAX_PIECES, dtype=jnp.int32)
    broadcast_back = (owner_slot[:, None] == position_labels[None, :]).astype(jnp.float32)
    select_items = broadcast_back.T * cut_marks[None, :].astype(jnp.float32)
    return (select_items, broadcast_back)


def merge_into_pieces(select_items, value_entries, blank_row):
    spans = jnp.dot(select_items, value_entries, precision=deepest_tier)
    return jnp.concatenate(
        [spans, jnp.broadcast_to(blank_row, (MAX_PIECES, CORE_WIDTH - BYTE_WIDTH))], axis=1
    )


def decay_products(confidence):
    rows = lax.broadcasted_iota(jnp.int32, (MAX_PIECES, MAX_PIECES), 0)
    columns = lax.broadcasted_iota(jnp.int32, (MAX_PIECES, MAX_PIECES), 1)
    products = jnp.where(rows > columns, 1.0 - confidence[:, None], 1.0)
    reach = 1
    while reach < MAX_PIECES:
        shifted = jnp.concatenate(
            [jnp.ones((reach, MAX_PIECES), jnp.float32), products[:-reach]], axis=0
        )
        products = products * shifted
        reach *= 2
    return jnp.where(rows >= columns, products, 0.0)


@jax.custom_vjp
def smooth_spans(piece_output, confidence):
    products = decay_products(confidence)
    return jnp.dot(products, confidence[:, None] * piece_output, precision=deepest_tier)


def smooth_keep(piece_output, confidence):
    products = decay_products(confidence)
    smoothed = jnp.dot(products, confidence[:, None] * piece_output, precision=deepest_tier)
    return smoothed, (piece_output, confidence, products, smoothed)


def smooth_pull(kept, slope):
    piece_output, confidence, products, smoothed = kept
    spread = lax.dot_general(
        products, slope, (((0,), (0,)), ((), ())), precision=deepest_tier
    )
    before = jnp.concatenate([jnp.zeros((1, smoothed.shape[1]), jnp.float32), smoothed[:-1]], axis=0)
    return (confidence[:, None] * spread, jnp.sum(spread * (piece_output - before), axis=-1))


smooth_spans.defvjp(smooth_keep, smooth_pull)


def link_layers(
    select_items,
    broadcast_back,
    cut_marks,
    latent_holder,
    closing_scale,
    cut_likelihood,
    shortcut_sum,
):
    piece_output = root_mean_rescale(latent_holder, closing_scale)[:, :BYTE_WIDTH]
    smoothed = smooth_spans(
        piece_output, jnp.dot(select_items, cut_likelihood, precision=deepest_tier)
    )
    confidence = jnp.where(cut_marks == 1, cut_likelihood, 1.0 - cut_likelihood)
    return shortcut_sum + confidence[:, None] * jnp.dot(
        broadcast_back, smoothed, precision=deepest_tier
    )


def adam_step(weight, grad, first, second, rate, decay):
    first_new = beta_one * first + (1.0 - beta_one) * grad
    second_new = beta_two * second + (1.0 - beta_two) * grad * grad
    ratio = (
        first_new
        / (1.0 - beta_one**STEP)
        / (jnp.sqrt(second_new / (1.0 - beta_two**STEP)) + adam_eps)
    )
    return (first_new, second_new, weight - rate * (ratio + decay * weight))


def to_low(value_entries):
    return value_entries.astype(jnp.bfloat16)


def matmul_apply(left, right):
    return jnp.dot(left, right, preferred_element_type=jnp.float32)


def product_tn(left, right):
    return lax.dot_general(
        left, right, (((0,), (0,)), ((), ())), preferred_element_type=jnp.float32
    )


def product_nt(left, right):
    return lax.dot_general(
        left, right, (((1,), (1,)), ((), ())), preferred_element_type=jnp.float32
    )


def swap(value_entries, axis, mask):
    size = lax.axis_size(axis)
    return lax.ppermute(value_entries, axis, [(place, place ^ mask) for place in range(size)])


def bit_masks(size):
    masks = []
    mask = 1
    while mask < size:
        masks.append(mask)
        mask *= 2
    return masks


def after(value_entries, earlier):
    if not earlier:
        return value_entries
    return lax.optimization_barrier((value_entries,) + tuple(earlier))[0]


def spread_masks(over_tensor):
    dp_masks = bit_masks(lax.axis_size("dp"))
    masks = [("dp", mask) for mask in dp_masks[1:] + dp_masks[:1]]
    if over_tensor:
        masks += [("tensor", mask) for mask in reversed(bit_masks(lax.axis_size("tensor")))]
    return masks


class Summing:
    def __init__(self, grad, over_tensor):
        self.masks = list(reversed(spread_masks(over_tensor)))
        names = [("dp", mask) for mask in reversed(bit_masks(lax.axis_size("dp")))]
        if over_tensor:
            names += [("tensor", mask) for mask in reversed(bit_masks(lax.axis_size("tensor")))]
        self.names = names
        rows = grad.shape[0] // 2 ** len(names)
        self.addends = [grad.reshape((2,) * len(names) + (rows,) + grad.shape[1:])]
        self.pending = None

    def operand(self):
        axis, mask = self.masks[0]
        position = self.names.index((axis, mask))
        own = (lax.axis_index(axis) // mask) % 2
        return to_low(total([take(addend, position, 1 - own) for addend in self.addends]))

    def accept(self):
        axis, mask = self.masks.pop(0)
        position = self.names.index((axis, mask))
        own = (lax.axis_index(axis) // mask) % 2
        self.addends = [take(addend, position, own) for addend in self.addends] + [self.pending]
        self.pending = None
        self.names.pop(position)

    def begun_last(self):
        left = [mask for axis, mask in self.masks if axis == "dp" and mask > 1]
        return 0 < len(left) == len(self.masks) < len(bit_masks(lax.axis_size("dp"))) - 1

    def rest(self, token):
        if len(self.addends) > 1:
            self.addends = [after(addend, [token]) for addend in self.addends]
        kind = []
        for axis, mask in self.masks:
            name = ("core", "y")[mask - 1] if axis == "tensor" else ("x" if mask == 1 else "z")
            if name not in kind:
                kind.append(name)
        value_entries = to_low(total(self.addends)) if len(self.addends) > 1 else self.addends[0]
        return value_entries.reshape(-1, value_entries.shape[-1]), tuple(kind)

    def result(self, token=None):
        if token is not None:
            self.addends = [after(addend, [token]) for addend in self.addends]
        return total(self.addends)


def sum_slowly(job):
    while job.masks:
        axis, mask = job.masks[0]
        job.pending = swap(job.operand(), axis, mask)
        job.accept()
    return job.result()


class Conductor:
    def __init__(self):
        self.clock = 0.0
        self.jobs = []
        self.flights = []

    def add(self, job):
        self.jobs.append(job)
        return job

    def lane(self, job):
        axis, mask = job.masks[0]
        return (axis, mask if axis == "tensor" else min(mask, 2))

    def launch(self, limit, banned, value_entries):
        operands = []
        for job in self.jobs:
            if len(self.flights) >= limit:
                break
            if job.pending is not None or not job.masks:
                continue
            lane = self.lane(job)
            depth = {("dp", 1): 3, ("tensor", 1): 2}.get(lane, 1)
            if lane in banned or sum(flight[1] == lane for flight in self.flights) >= depth:
                continue
            axis, mask = job.masks[0]
            operand = job.operand()
            rate = 3.4 if (axis, mask) == ("tensor", 1) else 25.3
            if axis == "dp" and mask > 2:
                rate = 50.0
            operand = after(operand, [value_entries])
            operands.append(operand)
            job.pending = swap(operand, axis, mask)
            start = max([self.clock] + [flight[0] - 6.0 for flight in self.flights if flight[1] == lane])
            self.flights.append((start + 6.0 + rate * operand.size * 2e-6, lane, job))
        return after(value_entries, operands)

    def tick(self, value_entries, elapsed, banned=(), limit=5):
        self.clock += elapsed
        ended = [flight for flight in self.flights if flight[0] <= self.clock]
        if ended:
            value_entries = after(value_entries, [flight[2].pending for flight in ended])
            self.flights = [flight for flight in self.flights if flight[0] > self.clock]
            for flight in ended:
                flight[2].accept()
        return self.launch(limit, banned, value_entries)

    def close(self):
        for _, _, job in sorted(self.flights, key=lambda flight: flight[0]):
            job.accept()
        self.flights = []
        for job in self.jobs:
            while job.begun_last():
                axis, mask = job.masks[0]
                job.pending = swap(job.operand(), axis, mask)
                job.accept()


def flip(place, mask):
    result = place
    bit = 1
    while bit <= mask:
        if mask & bit:
            result = result + bit * (1 - 2 * ((place // bit) % 2))
        bit *= 2
    return result


def order_steps(jobs, depth=2):
    free, busy, flights, plan = {}, {}, [], []
    waiting = [0] * len(jobs)
    clock = 0.0
    while True:
        for job, steps in enumerate(jobs):
            step = waiting[job]
            if step < 0 or step >= len(steps):
                continue
            lane, cost = steps[step]
            if busy.get(lane, 0) >= depth:
                continue
            busy[lane] = busy.get(lane, 0) + 1
            free[lane] = max(free.get(lane, 0.0), clock) + cost
            flights.append((free[lane] + 1.5, job, step, lane))
            plan.append(("start", job, step))
            waiting[job] = -1 - step
        if not flights:
            return plan
        flight = min(flights)
        flights.remove(flight)
        clock, job, step, lane = flight
        busy[lane] -= 1
        plan.append(("wait", job, step))
        waiting[job] = step + 1


def link_cost(lane, elements):
    return elements * 2e-6 * {"core": 3.4, "y": 23.0, "x": 23.0, "z": 46.0}[lane]


def here():
    dp_place, tensor_place = lax.axis_index("dp"), lax.axis_index("tensor")
    return dp_place // 2, dp_place % 2, tensor_place // 2, tensor_place % 2


def partner(lane, mask, coordinates):
    z, x, y, core = coordinates
    if lane == "z":
        z = flip(z, mask)
    if lane == "x":
        x = 1 - x
    if lane == "y":
        y = 1 - y
    if lane == "core":
        core = 1 - core
    return (z * 2 + x, y * 2 + core)


def greet(line, depth_z, coordinates):
    z = coordinates[0]
    barrier = pltpu.get_barrier_semaphore()

    def tell(device):
        pl.semaphore_signal(
            barrier, inc=1, device_id=device, device_id_type=pl.DeviceIdType.MESH
        )

    for lane in ("x", "y", "core"):
        tell(partner(lane, 1, coordinates))
    if not line:
        for mask in range(1, depth_z):
            tell(partner("z", mask, coordinates))
        pl.semaphore_wait(barrier, depth_z + 2)
        return

    @pl.when(z > 0)
    def _():
        tell(beside(-1, coordinates))

    @pl.when(z < depth_z - 1)
    def _():
        tell(beside(1, coordinates))

    ends = (z == 0).astype(jnp.int32) + (z == depth_z - 1).astype(jnp.int32)
    pl.semaphore_wait(barrier, 5 - ends)


def beside(way, coordinates):
    z, x, y, core = coordinates
    return ((z + way) * 2 + x, y * 2 + core)


def spread_kernel(plan, jobs, depth_z, *refs):
    count = (len(refs) - 3) // 2
    shards, wholes = refs[:count], refs[count : 2 * count]
    send_sems, receive_sems, own_sems = refs[2 * count :]
    coordinates = here()
    z = coordinates[0]
    greet(True, depth_z, coordinates)

    def spot(job, free, z_place):
        array, kind, first, size = jobs[job]
        index = [
            slice(None) if name in free else (z_place if name == "z" else place)
            for name, place in zip(("z", "x", "y", "core"), coordinates)
            if name in kind
        ]
        return wholes[array].at[tuple(index) + (slice(None), pl.ds(first, size))]

    def shard(job):
        array, _, first, size = jobs[job]
        return shards[array].at[:, pl.ds(first, size)]

    own = []
    for job in range(len(jobs)):
        own.append(pltpu.make_async_copy(shard(job), spot(job, (), z), own_sems.at[job]))
        own[-1].start()

    def copies(job, step, receiving):
        steps = lanes_of(jobs[job][1], depth_z)
        lane, reach = steps[step]
        free = [name for name, _ in steps[:step] if name != lane]
        base = job * (2 * depth_z + 1)
        pairs = []
        if lane == "z":
            for side, way in enumerate((1, -1)):
                number = base + 2 * (reach - 1) + side
                if receiving:
                    block = z - way * reach
                    condition = (block >= 0) & (block < depth_z)
                    target = spot(job, free, z if step == 0 else block)
                    source = target
                else:
                    block = z - way * (reach - 1)
                    condition = (block >= 0) & (block < depth_z)
                    condition &= (z + way >= 0) & (z + way < depth_z)
                    target = spot(job, free, block)
                    source = shard(job) if step == 0 else target
                copy = pltpu.make_async_remote_copy(
                    src_ref=source,
                    dst_ref=target,
                    send_sem=send_sems.at[number],
                    recv_sem=receive_sems.at[number],
                    device_id=beside(way, coordinates),
                    device_id_type=pl.DeviceIdType.MESH,
                )
                pairs.append((condition, copy))
            return pairs
        number = base + 2 * (depth_z - 1) + ("x", "y", "core").index(lane)
        target = spot(job, free, z)
        copy = pltpu.make_async_remote_copy(
            src_ref=shard(job) if step == 0 else target,
            dst_ref=target,
            send_sem=send_sems.at[number],
            recv_sem=receive_sems.at[number],
            device_id=partner(lane, 1, coordinates),
            device_id_type=pl.DeviceIdType.MESH,
        )
        return [(None, copy)]

    def perform(pairs, action):
        for condition, copy in pairs:
            if condition is None:
                getattr(copy, action)()
            else:
                pl.when(condition)(getattr(copy, action))

    copied = set()
    for action, job, step in plan:
        steps = lanes_of(jobs[job][1], depth_z)
        if action == "start":
            if steps[step][0] != steps[0][0] and job not in copied:
                own[job].wait()
                copied.add(job)
            perform(copies(job, step, False), "start")
        else:
            perform(copies(job, step, True), "wait_recv")
    for action, job, step in plan:
        if action == "start":
            perform(copies(job, step, False), "wait_send")


def lanes_of(kind, depth_z):
    steps = []
    for name in kind:
        steps += [(name, reach) for reach in range(1, depth_z if name == "z" else 2)]
    return steps


def spread_whole(shards, jobs, collective_id):
    depth_z = lax.axis_size("dp") // 2
    costs = []
    for array, kind, first, size in jobs:
        held, steps = shards[array].shape[0] * size, []
        for lane in kind:
            cost = 23.0 if lane != "core" else 3.4
            steps += [(lane, held * 2e-6 * cost)] * (depth_z - 1 if lane == "z" else 1)
            held *= depth_z if lane == "z" else 2
        costs.append(steps)
    plan = order_steps(costs)
    sizes = {"z": depth_z, "x": 2, "y": 2, "core": 2}
    kinds = {array: kind for array, kind, _, _ in jobs}
    shapes = [
        tuple(sizes[name] for name in ("z", "x", "y", "core") if name in kinds[array])
        + shard.shape
        for array, shard in enumerate(shards)
    ]
    numbers = len(jobs) * (2 * depth_z + 1)
    wholes = pl.pallas_call(
        partial(spread_kernel, plan, jobs, depth_z),
        out_shape=tuple(jax.ShapeDtypeStruct(shape, jnp.bfloat16) for shape in shapes),
        in_specs=[pl.BlockSpec(memory_space=pltpu.VMEM)] * len(shards),
        out_specs=(pl.BlockSpec(memory_space=pl.ANY),) * len(shards),
        scratch_shapes=[
            pltpu.SemaphoreType.DMA((numbers,)),
            pltpu.SemaphoreType.DMA((numbers,)),
            pltpu.SemaphoreType.DMA((len(jobs),)),
        ],
        compiler_params=pltpu.CompilerParams(
            collective_id=collective_id, has_side_effects=True, vmem_limit_bytes=60 * 2**20
        ),
    )(*shards)
    return [whole.reshape(-1, whole.shape[-1]) for whole in wholes]


BYTE_LANES = ("z", "x", "y", "core")
MAIN_LANES = ("z", "x")


def sum_kernel(plan, kinds, depth_z, *refs):
    count = len(kinds)
    grads, extra = refs[:count], refs[count]
    outputs, totals = refs[count + 1 : 2 * count + 1], refs[2 * count + 1]
    rest = list(refs[2 * count + 2 :])
    coordinates = here()
    places = dict(zip(BYTE_LANES, coordinates))
    z = coordinates[0]
    mirrored = depth_z - 1 - z
    held, received, held_names = [], [], []
    for kind in kinds:
        held.append(rest.pop(0))
        received.append({lane: rest.pop(0) for lane in kind})
        held_names.append(names_held(kind))
    squares, arrivals, send_sems, receive_sems, own_sems, tile_sems = rest
    loads = []
    for job, kind in enumerate(kinds):
        spot = tuple(
            slice(None) if name in held_names[job] else places[name]
            for name in BYTE_LANES
            if name in kind
        )
        loads.append(pltpu.make_async_copy(grads[job].at[spot], held[job], own_sems.at[job]))
        loads[-1].start()
    squares[...] = jnp.zeros_like(squares)
    greet(False, depth_z, coordinates)

    def chosen(job, step, lane_place):
        steps = lanes_of(kinds[job], depth_z)
        lane = steps[step][0]
        done = [name for name, _ in steps[:step] if name != lane]
        return [
            lane_place if name == lane else (places[name] if name in done else slice(None))
            for name in held_names[job]
        ]

    def slot(reach, side):
        shared = (depth_z - 2) // 2
        return reach - 1 if reach <= shared else shared + 2 * (reach - 1 - shared) + side

    def copies(job, step, receiving):
        kind = kinds[job]
        lane, reach = lanes_of(kind, depth_z)[step]
        base = job * (2 * depth_z + 1)
        if lane == "z":
            pairs = []
            for side, depth in enumerate((z, mirrored)):
                way = 1 - 2 * side
                aim = depth_z - reach + depth
                if side:
                    aim = depth_z - 1 - aim
                landing = received[job]["z"].at[slot(reach, side)]
                number = base + 2 * (reach - 1) + side
                source = landing if receiving else held[job].at[tuple(chosen(job, step, aim))]
                copy = pltpu.make_async_remote_copy(
                    src_ref=source,
                    dst_ref=landing,
                    send_sem=send_sems.at[number],
                    recv_sem=receive_sems.at[number],
                    device_id=beside(way, coordinates),
                    device_id_type=pl.DeviceIdType.MESH,
                )
                condition = (depth >= 1) & (depth <= reach) if receiving else depth <= reach - 1
                pairs.append((condition, copy))
            return pairs
        number = base + 2 * (depth_z - 1) + ("x", "y", "core").index(lane)
        if step == 0:
            spot = tuple(
                1 - places[name] if name == lane else slice(None)
                for name in BYTE_LANES
                if name in kind
            )
            source = grads[job].at[spot]
        else:
            source = held[job].at[tuple(chosen(job, step, 1 - places[lane]))]
        copy = pltpu.make_async_remote_copy(
            src_ref=source,
            dst_ref=received[job][lane],
            send_sem=send_sems.at[number],
            recv_sem=receive_sems.at[number],
            device_id=partner(lane, 1, coordinates),
            device_id_type=pl.DeviceIdType.MESH,
        )
        return [(None, copy)]

    def add_pieces(job, step, lane_place, buffers, last):
        steps = lanes_of(kinds[job], depth_z)
        lane = steps[step][0]
        done = [name for name, _ in steps[:step] if name != lane]
        free = [name for name in BYTE_LANES if name in kinds[job] and name not in done + [lane]]
        sizes = [depth_z if name == "z" else 2 for name in free]
        pieces = 1
        for size in sizes:
            pieces *= size

        def piece(index, carry):
            spots, remainder = {}, index
            for name, size in reversed(list(zip(free, sizes))):
                spots[name] = remainder % size
                remainder = remainder // size
            mine = tuple(
                spots[name] if name in spots else (lane_place if name == lane else places[name])
                for name in held_names[job]
            )
            theirs = tuple(spots[name] for name in free)
            target = held[job].at[mine] if mine else held[job]
            arrived = [buffer.at[theirs] if theirs else buffer for buffer in buffers]
            rows, columns = target.shape[-2:]

            def row_step(number, inner):
                part = pl.ds(pl.multiple_of(number * 16, 16), 16)
                value = target[part, :].astype(jnp.float32)
                for other in arrived:
                    value = value + other[part, :].astype(jnp.float32)
                if last:
                    outputs[job][part, :] = value
                    square = jnp.zeros((16, 128), jnp.float32)
                    for first in range(0, columns, 128):
                        square = square + value[:, first : first + 128] * value[:, first : first + 128]
                    squares[...] += square
                else:
                    target[part, :] = to_low(value)
                return inner

            lax.fori_loop(0, rows // 16, row_step, 0)
            return carry

        if pieces == 1:
            piece(0, 0)
        else:
            lax.fori_loop(0, pieces, piece, 0)

    def accumulate(job, step):
        steps = lanes_of(kinds[job], depth_z)
        lane, reach = steps[step]
        last = step == len(steps) - 1
        if lane != "z":
            add_pieces(job, step, places[lane], [received[job][lane]], last)
            return
        buffers = [received[job]["z"].at[slot(reach, side)] for side in range(2)]
        if reach < depth_z - 1:
            for side, depth in enumerate((z, mirrored)):
                aim = depth_z - reach + depth - 1
                if side:
                    aim = depth_z - 1 - aim
                pl.when((depth >= 1) & (depth <= reach))(
                    partial(add_pieces, job, step, aim, [buffers[side]], False)
                )
            return
        ends = (z == 0) | (mirrored == 0)
        pl.when(jnp.logical_not(ends))(partial(add_pieces, job, step, z, buffers, last))
        pl.when(z == 0)(partial(add_pieces, job, step, z, buffers[1:], last))
        pl.when(mirrored == 0)(partial(add_pieces, job, step, z, buffers[:1], last))

    def perform(pairs, action):
        for condition, copy in pairs:
            if condition is None:
                getattr(copy, action)()
            else:
                pl.when(condition)(getattr(copy, action))

    loaded = set()
    for action, job, step in plan:
        lane = lanes_of(kinds[job], depth_z)[step][0]
        if job not in loaded and (action == "wait" or lane == "z"):
            loads[job].wait()
            loaded.add(job)
        if action == "start":
            perform(copies(job, step, False), "start")
        else:
            perform(copies(job, step, True), "wait_recv")
            accumulate(job, step)
    totals[...] = extra[...]
    totals[0:8, :] += squares[0:8, :] + squares[8:16, :]
    exchanges = [("core", 1), ("y", 1), ("x", 1)]
    mask = 1
    while mask < depth_z:
        exchanges.append(("z", mask))
        mask *= 2
    tiles = []
    for number, (lane, mask) in enumerate(exchanges):
        tiles.append(
            pltpu.make_async_remote_copy(
                src_ref=arrivals.at[2 * number],
                dst_ref=arrivals.at[2 * number + 1],
                send_sem=tile_sems.at[2 * number],
                recv_sem=tile_sems.at[2 * number + 1],
                device_id=partner(lane, mask, coordinates),
                device_id_type=pl.DeviceIdType.MESH,
            )
        )
        arrivals[2 * number] = totals[...]
        tiles[-1].start()
        tiles[-1].wait_recv()
        totals[...] += arrivals[2 * number + 1]
    for copy in tiles:
        copy.wait_send()
    for action, job, step in plan:
        if action == "start":
            perform(copies(job, step, False), "wait_send")


def names_held(kind):
    return [name for name in BYTE_LANES if name in kind and (name == "z" or name != kind[0])]


def sum_whole(grads, kinds, extra, collective_id):
    depth_z = lax.axis_size("dp") // 2
    sizes = {"z": depth_z, "x": 2, "y": 2, "core": 2}
    jobs, arrays, shapes, scratch = [], [], [], []
    for grad, kind in zip(grads, kinds):
        names = [name for name in BYTE_LANES if name in kind]
        pieces = 1
        for name in names:
            pieces *= sizes[name]
        piece = (grad.shape[0] // pieces, grad.shape[1])
        arrays.append(grad.reshape(tuple(sizes[name] for name in names) + piece))
        shapes.append(jax.ShapeDtypeStruct(piece, jnp.float32))
        steps, left = [], list(names)
        scratch.append(
            pltpu.VMEM(tuple(sizes[name] for name in names_held(kind)) + piece, jnp.bfloat16)
        )
        for lane in kind:
            left.remove(lane)
            rest = tuple(sizes[name] for name in left)
            extent = piece[0] * piece[1]
            for size in rest:
                extent *= size
            cost = 23.0 if lane != "core" else 3.4
            steps += [(lane, extent * 2e-6 * cost)] * (depth_z - 1 if lane == "z" else 1)
            lead = (2 * (depth_z - 1) - (depth_z - 2) // 2,) if lane == "z" else ()
            scratch.append(pltpu.VMEM(lead + rest + piece, jnp.bfloat16))
        jobs.append(steps)
    plan = order_steps(jobs)
    numbers = len(grads) * (2 * depth_z + 1)
    tile = jax.ShapeDtypeStruct(extra.shape, jnp.float32)
    rounds = 3 + len(bit_masks(depth_z))
    return pl.pallas_call(
        partial(sum_kernel, plan, kinds, depth_z),
        out_shape=tuple(shapes) + (tile,),
        in_specs=[pl.BlockSpec(memory_space=pl.ANY)] * len(grads)
        + [pl.BlockSpec(memory_space=pltpu.VMEM)],
        out_specs=(pl.BlockSpec(memory_space=pltpu.VMEM),) * (len(grads) + 1),
        scratch_shapes=scratch
        + [
            pltpu.VMEM((16, 128), jnp.float32),
            pltpu.VMEM((2 * rounds, 16, 128), jnp.float32),
            pltpu.SemaphoreType.DMA((numbers,)),
            pltpu.SemaphoreType.DMA((numbers,)),
            pltpu.SemaphoreType.DMA((len(grads),)),
            pltpu.SemaphoreType.DMA((2 * rounds,)),
        ],
        compiler_params=pltpu.CompilerParams(
            collective_id=collective_id, has_side_effects=True, vmem_limit_bytes=60 * 2**20
        ),
    )(*arrays, extra)


def take(value_entries, axis, index):
    return lax.dynamic_index_in_dim(value_entries, index, axis, keepdims=False)


def total(addends):
    result = addends[0].astype(jnp.float32)
    for addend in addends[1:]:
        result = result + addend.astype(jnp.float32)
    return result


def add_everywhere(value_entries):
    for axis in ("tensor", "dp"):
        for mask in bit_masks(lax.axis_size(axis)):
            value_entries = value_entries + swap(value_entries, axis, mask)
    return value_entries


def gather_rows(value_entries):
    pieces = [value_entries]
    for mask in reversed(bit_masks(lax.axis_size("tensor"))):
        pieces = pieces + [swap(piece, "tensor", mask) for piece in pieces]
    return jnp.concatenate(pieces, axis=0)


def total_lines(value_entries):
    size = lax.axis_size("tensor")
    rows = value_entries.shape[0] // size
    pieces = [to_low(value_entries[i * rows : (i + 1) * rows]) for i in range(size)]
    for mask in bit_masks(size):
        half = len(pieces) // 2
        pieces = [
            pieces[i].astype(jnp.float32)
            + swap(to_low(pieces[half + i]), "tensor", mask).astype(jnp.float32)
            for i in range(half)
        ]
    return pieces[0]


gather_grads = gather_rows
sum_grads = total_lines


def low_dot(left, right, left_dim, right_dim):
    return lax.dot_general(
        left, right, (((left_dim,), (right_dim,)), ((), ())), preferred_element_type=jnp.float32
    )


def sigmoid(value_entries):
    return 0.5 * jnp.tanh(0.5 * value_entries) + 0.5


def fold_rows(value_entries):
    return jnp.sum(value_entries.reshape(-1, 8, value_entries.shape[1]), axis=0)


def lower_ones():
    rows = lax.broadcasted_iota(jnp.int32, (ssd_block, ssd_block), 0)
    columns = lax.broadcasted_iota(jnp.int32, (ssd_block, ssd_block), 1)
    return (rows >= columns).astype(jnp.float32)


FORWARD_UNROLL = 4
BACKWARD_UNROLL = 2
PROJ_WIDE = 2 * INNER + 2 * STATE + 128


def step_terms(raw_steps, decay_refs):
    shifted = raw_steps + decay_refs[1:2, :]
    steps = softplus(shifted)
    rates = -jnp.exp(decay_refs[0:1, :])
    cumulative = jnp.dot(
        lower_ones(), steps * rates, precision=deepest_tier, preferred_element_type=jnp.float32
    )
    return shifted, steps, rates, cumulative


def head_tables():
    chosen = to_low(jnp.arange(INNER)[:, None] // HEADDIM == jnp.arange(ssd_block)[None, :])
    later = jnp.where(
        jnp.arange(ssd_block)[:, None] >= jnp.arange(ssd_block)[None, :], 0.0, -1e30
    )
    return chosen, later


def first_head():
    return lax.broadcasted_iota(jnp.int32, (ssd_block, ssd_block), 1) < HEADDIM


def both_heads(value_entries):
    mask = first_head()
    zeros = jnp.zeros_like(value_entries)
    return jnp.concatenate(
        [jnp.where(mask, value_entries, zeros), jnp.where(mask, zeros, value_entries)], axis=0
    )


def spread_heads(steps, cumulative, turned, wide, narrow):
    blank = jnp.zeros((ssd_block, ssd_block - MHEADS), jnp.float32)
    turned[...] = jnp.concatenate([cumulative, blank], axis=1).T
    mask = first_head()

    def over_lanes(value_entries, head):
        return jnp.broadcast_to(value_entries[:, head : head + 1], (ssd_block, ssd_block))

    for head in range(MHEADS):
        wide[head] = over_lanes(cumulative, head)
    for pair in range(MHEADS // 2):
        narrow[:, pair * ssd_block : (pair + 1) * ssd_block] = jnp.where(
            mask, over_lanes(steps, 2 * pair), over_lanes(steps, 2 * pair + 1)
        )


def gaps_of(wide, turned, later, head):
    return jnp.exp((wide[head] - turned[pl.ds(head, 1), :]) + later[...])


def quad_cumulative(wide, quad):
    mask = first_head()
    return jnp.concatenate(
        [
            jnp.where(mask, wide[4 * quad], wide[4 * quad + 1]),
            jnp.where(mask, wide[4 * quad + 2], wide[4 * quad + 3]),
        ],
        axis=1,
    )


def quad_lanes(quad, first=0):
    return pl.ds(pl.multiple_of(quad * 2 * ssd_block + first, ssd_block), 2 * ssd_block)


def lanes(block):
    return pl.ds(pl.multiple_of(block * ssd_block, ssd_block), ssd_block)


def convolve(padded_ref, taps_ref, columns):
    result = taps_ref[0:1, columns] * padded_ref[5 : 5 + ssd_block, columns]
    for tap in range(1, 4):
        result = result + taps_ref[tap : tap + 1, columns] * padded_ref[
            5 + tap : 5 + tap + ssd_block, columns
        ]
    return result


def middle_kernel(
    projected,
    taps,
    skip,
    decay,
    gain,
    later,
    middle,
    outcome,
    starts,
    padded,
    turned,
    wide,
    narrow,
    state,
    gated,
):
    chunk = pl.program_id(0)
    streams_extent = INNER + 2 * STATE

    @pl.when(chunk == 0)
    def _():
        padded[0:8, :] = jnp.zeros((8, streams_extent), jnp.float32)
        state[...] = jnp.zeros_like(state)

    @pl.when(chunk > 0)
    def _():
        padded[0:8, :] = padded[ssd_block : ssd_block + 8, :]

    padded[8 : 8 + ssd_block, :] = projected[:, INNER : INNER + streams_extent]
    _, steps, _, cumulative = step_terms(
        projected[:, INNER + streams_extent : INNER + streams_extent + MHEADS], decay
    )
    spread_heads(steps, cumulative, turned, wide, narrow)

    def active(columns):
        convolved = convolve(padded, taps, columns)
        return convolved * sigmoid(convolved)

    in_map = active(pl.ds(INNER, STATE))
    in_low = to_low(in_map)
    in_turned = to_low(in_map.T)
    out_low = to_low(active(pl.ds(INNER + STATE, STATE)))
    affinity = low_dot(out_low, in_low, 1, 1)

    def quad_step(quad, square_sum):
        columns = quad_lanes(quad)
        inputs = active(columns)
        weighted = inputs * narrow[:, columns]
        weighted_low = to_low(weighted)
        within = []
        for pair in range(2):
            head = 4 * quad + 2 * pair
            mixing = jnp.concatenate(
                [
                    to_low(affinity * gaps_of(wide, turned, later, head)),
                    to_low(affinity * gaps_of(wide, turned, later, head + 1)),
                ],
                axis=1,
            )
            part = weighted_low[:, pair * ssd_block : (pair + 1) * ssd_block]
            within.append(low_dot(mixing, both_heads(part), 1, 0))
        within = jnp.concatenate(within, axis=1)
        cumulative_here = quad_cumulative(wide, quad)
        last = cumulative_here[ssd_block - 1 :, :]
        held = state[:, columns]
        starts[0, :, columns] = held
        across = jnp.exp(cumulative_here) * low_dot(out_low, to_low(held), 1, 0)
        to_end = to_low(weighted * jnp.exp(last - cumulative_here))
        state[:, columns] = jnp.exp(last) * held + low_dot(in_turned, to_end, 1, 0)
        result = within + across + inputs * skip[:, columns]
        outcome[:, columns] = result
        gate = projected[:, columns]
        product = result * (gate * sigmoid(gate))
        gated[:, columns] = product
        return square_sum + product * product

    square_sum = lax.fori_loop(
        0,
        INNER // (2 * ssd_block),
        quad_step,
        jnp.zeros((ssd_block, 2 * ssd_block), jnp.float32),
        unroll=FORWARD_UNROLL,
    )
    scale = lax.rsqrt(jnp.sum(square_sum, axis=1, keepdims=True) * (1.0 / INNER) + norm_eps)

    def scale_step(quad, carry):
        columns = quad_lanes(quad)
        middle[:, columns] = to_low(gated[:, columns] * scale * gain[:, columns])
        return carry

    lax.fori_loop(0, INNER // (2 * ssd_block), scale_step, 0, unroll=2)


def middle_slope_kernel(
    projected,
    earlier,
    outcome,
    starts,
    slope,
    taps,
    skip,
    decay,
    gain,
    chosen,
    later,
    slope_projected,
    slope_taps,
    slope_skip,
    slope_gain,
    slope_decay,
    padded,
    turned,
    wide,
    narrow,
    slope_state,
    slope_conv,
    slope_affinity,
    slope_maps,
    slope_cumulative,
    slope_steps,
):
    chunk = pl.num_programs(0) - 1 - pl.program_id(0)
    streams_extent = INNER + 2 * STATE
    quads = INNER // (2 * ssd_block)

    @pl.when(pl.program_id(0) == 0)
    def _():
        slope_state[...] = jnp.zeros_like(slope_state)
        slope_conv[ssd_block : ssd_block + 8, :] = jnp.zeros((8, streams_extent), jnp.float32)
        slope_taps[...] = jnp.zeros_like(slope_taps)
        slope_skip[...] = jnp.zeros_like(slope_skip)
        slope_gain[...] = jnp.zeros_like(slope_gain)
        slope_decay[...] = jnp.zeros_like(slope_decay)

    @pl.when(pl.program_id(0) > 0)
    def _():
        slope_conv[ssd_block : ssd_block + 8, :] = slope_conv[0:8, :]

    @pl.when(chunk == 0)
    def _():
        padded[0:8, :] = jnp.zeros((8, streams_extent), jnp.float32)

    @pl.when(chunk > 0)
    def _():
        padded[0:8, :] = earlier[:, INNER : INNER + streams_extent]

    padded[8 : 8 + ssd_block, :] = projected[:, INNER : INNER + streams_extent]
    slope_affinity[...] = jnp.zeros_like(slope_affinity)
    slope_maps[...] = jnp.zeros_like(slope_maps)
    slope_cumulative[...] = jnp.zeros_like(slope_cumulative)
    slope_steps[...] = jnp.zeros_like(slope_steps)
    shifted, steps, rates, cumulative = step_terms(
        projected[:, INNER + streams_extent : INNER + streams_extent + MHEADS], decay
    )
    spread_heads(steps, cumulative, turned, wide, narrow)

    def silu_pair(value_entries):
        share = sigmoid(value_entries)
        return value_entries * share, share * (1.0 + value_entries * (1.0 - share))

    def pull_convolved(columns, target_columns, slope_block):
        slope_conv[0:ssd_block, columns] = slope_block
        result = taps[3:4, columns] * slope_block
        for tap in range(3):
            reach = 3 - tap
            result = result + taps[tap : tap + 1, columns] * slope_conv[
                reach : reach + ssd_block, columns
            ]
        for tap in range(4):
            slope_taps[tap, :, columns] += fold_rows(
                slope_block * padded[5 + tap : 5 + tap + ssd_block, columns]
            )
        slope_projected[:, target_columns] = to_low(result)

    maps = (pl.ds(INNER, STATE), pl.ds(INNER + STATE, STATE))
    in_map, in_pull = silu_pair(convolve(padded, taps, maps[0]))
    out_map, out_pull = silu_pair(convolve(padded, taps, maps[1]))
    in_low, out_low, out_turned = to_low(in_map), to_low(out_map), to_low(out_map.T)
    affinity = low_dot(out_low, in_low, 1, 1)
    mask = first_head()

    def sums_step(quad, sums):
        columns = quad_lanes(quad)
        gate = projected[:, columns]
        product = outcome[:, columns] * (gate * sigmoid(gate))
        return (
            sums[0] + product * product,
            sums[1] + product * (slope[:, columns] * gain[:, columns]),
        )

    blank = jnp.zeros((ssd_block, 2 * ssd_block), jnp.float32)
    squares, crossed = lax.fori_loop(0, quads, sums_step, (blank, blank), unroll=2)
    scale = lax.rsqrt(jnp.sum(squares, axis=1, keepdims=True) * (1.0 / INNER) + norm_eps)
    pulled = scale * scale * scale * (jnp.sum(crossed, axis=1, keepdims=True) * (1.0 / INNER))

    def quad_step(quad, carry):
        columns = quad_lanes(quad)
        gate, total_here = projected[:, columns], outcome[:, columns]
        gate_value, gate_pull = silu_pair(gate)
        product = total_here * gate_value
        slope_here = slope[:, columns]
        slope_gain[:, columns] += fold_rows(slope_here * product * scale)
        slope_product = scale * (slope_here * gain[:, columns]) - product * pulled
        slope_out = slope_product * gate_value
        slope_projected[:, columns] = to_low(slope_product * total_here * gate_pull)
        inputs, inputs_pull = silu_pair(convolve(padded, taps, columns))
        slope_skip[:, columns] += fold_rows(slope_out * inputs)
        skip_here = skip[:, columns]
        scanned = total_here - inputs * skip_here
        steps_here = narrow[:, columns]
        weighted = inputs * steps_here
        weighted_low = to_low(weighted)
        slope_low = to_low(slope_out)
        slope_within = []
        for pair in range(2):
            head = 4 * quad + 2 * pair
            here_low = slope_low[:, pair * ssd_block : (pair + 1) * ssd_block]
            part = weighted_low[:, pair * ssd_block : (pair + 1) * ssd_block]
            slope_mixing = low_dot(here_low, both_heads(part), 1, 1)
            mixing = []
            for side in range(2):
                gaps = gaps_of(wide, turned, later, head + side)
                mixing.append(to_low(affinity * gaps))
                slope_affinity[...] += (
                    slope_mixing[:, side * ssd_block : (side + 1) * ssd_block] * gaps
                )
            turned_back = low_dot(jnp.concatenate(mixing, axis=1), here_low, 0, 0)
            slope_within.append(
                jnp.where(mask, turned_back[:ssd_block], turned_back[ssd_block:])
            )
        slope_within = jnp.concatenate(slope_within, axis=1)
        cumulative_here = quad_cumulative(wide, quad)
        last = cumulative_here[ssd_block - 1 :, :]
        decayed = jnp.exp(last)
        held = starts[0, :, columns]
        slope_across = to_low(slope_out * jnp.exp(cumulative_here))
        slope_maps[1] += low_dot(slope_across, to_low(held), 1, 1)
        carried_state = slope_state[:, columns]
        carried_low = to_low(carried_state)
        to_end = jnp.exp(last - cumulative_here)
        ending = to_low(weighted * to_end)
        slope_ending = low_dot(in_low, carried_low, 1, 0)
        slope_maps[0] += low_dot(ending, carried_low, 1, 1)
        slope_state[:, columns] = decayed * carried_state + low_dot(out_turned, slope_across, 1, 0)
        slope_weighted = slope_within + slope_ending * to_end
        ending_slope = slope_ending * ending.astype(jnp.float32)
        ends = jnp.sum(ending_slope, axis=0, keepdims=True) + decayed * jnp.sum(
            carried_state * held, axis=0, keepdims=True
        )
        rows = lax.broadcasted_iota(jnp.int32, (ssd_block, 2 * ssd_block), 0)
        slope_gathered = (
            slope_low.astype(jnp.float32) * scanned
            - weighted_low.astype(jnp.float32) * slope_within
            - ending_slope
            + jnp.where(rows == ssd_block - 1, ends, 0.0)
        )
        parts = []
        for value_entries in (slope_gathered, slope_weighted * inputs):
            high = to_low(value_entries)
            parts += [high, to_low(value_entries - high.astype(jnp.float32))]
        sums = low_dot(jnp.concatenate(parts, axis=0), chosen[columns, :], 1, 0)
        slope_cumulative[...] += sums[:ssd_block] + sums[ssd_block : 2 * ssd_block]
        slope_steps[...] += sums[2 * ssd_block : 3 * ssd_block] + sums[3 * ssd_block :]
        slope_inputs = slope_out * skip_here + slope_weighted * steps_here
        pull_convolved(columns, quad_lanes(quad, INNER), slope_inputs * inputs_pull)
        return carry

    lax.fori_loop(0, quads, quad_step, 0, unroll=BACKWARD_UNROLL)
    affinity_low = to_low(slope_affinity[...])
    slope_in = slope_maps[0] + low_dot(affinity_low, out_low, 0, 0)
    slope_out_map = slope_maps[1] + low_dot(affinity_low, in_low, 1, 0)
    pull_convolved(maps[0], pl.ds(2 * INNER, STATE), slope_in * in_pull)
    pull_convolved(maps[1], pl.ds(2 * INNER + STATE, STATE), slope_out_map * out_pull)
    slope_changes = lax.dot_general(
        lower_ones(),
        slope_cumulative[...],
        (((0,), (0,)), ((), ())),
        precision=deepest_tier,
        preferred_element_type=jnp.float32,
    )[:, :MHEADS]
    slope_step = slope_steps[:, :MHEADS] + slope_changes * rates
    slope_raw = slope_step * sigmoid(shifted)
    slope_decay[0] += fold_rows(slope_changes * steps) * rates
    slope_decay[1] += fold_rows(slope_raw)
    slope_projected[:, INNER + streams_extent :] = jnp.concatenate(
        [to_low(slope_raw), jnp.zeros((ssd_block, 128 - MHEADS), jnp.bfloat16)], axis=1
    )


def fixed(shape):
    return pl.BlockSpec(shape, lambda chunk: (0,) * len(shape))


def middle_forward(projected, smalls):
    conv_taps, skip_gain, a_log, dt_bias, gated_gain = smalls
    chosen, later = head_tables()
    extent, columns = projected.shape
    chunks = extent // ssd_block
    streams_extent = INNER + 2 * STATE
    return pl.pallas_call(
        middle_kernel,
        grid=(chunks,),
        out_shape=(
            jax.ShapeDtypeStruct((extent, INNER), jnp.bfloat16),
            jax.ShapeDtypeStruct((extent, INNER), jnp.float32),
            jax.ShapeDtypeStruct((chunks, STATE, INNER), jnp.float32),
        ),
        in_specs=[
            pl.BlockSpec((ssd_block, columns), lambda chunk: (chunk, 0)),
            fixed((4, streams_extent)),
            fixed((1, INNER)),
            fixed((2, MHEADS)),
            fixed((1, INNER)),
            fixed(later.shape),
        ],
        out_specs=(
            pl.BlockSpec((ssd_block, INNER), lambda chunk: (chunk, 0)),
            pl.BlockSpec((ssd_block, INNER), lambda chunk: (chunk, 0)),
            pl.BlockSpec((1, STATE, INNER), lambda chunk: (chunk, 0, 0)),
        ),
        scratch_shapes=[
            pltpu.VMEM((ssd_block + 8, streams_extent), jnp.float32),
            pltpu.VMEM((ssd_block, ssd_block), jnp.float32),
            pltpu.VMEM((MHEADS, ssd_block, ssd_block), jnp.float32),
            pltpu.VMEM((ssd_block, INNER), jnp.float32),
            pltpu.VMEM((STATE, INNER), jnp.float32),
            pltpu.VMEM((ssd_block, INNER), jnp.float32),
        ],
        compiler_params=pltpu.CompilerParams(vmem_limit_bytes=48 * 2**20),
        cost_estimate=pl.CostEstimate(
            flops=2 * 10**10, transcendentals=4 * 10**6, bytes_accessed=20 * 10**6
        ),
    )(
        projected,
        conv_taps,
        skip_gain.reshape(1, INNER),
        jnp.stack([a_log, dt_bias]),
        gated_gain.reshape(1, INNER),
        later,
    )


def middle_backward(projected, outcome, starts, slope, smalls):
    conv_taps, skip_gain, a_log, dt_bias, gated_gain = smalls
    chosen, later = head_tables()
    extent, columns = projected.shape
    chunks = extent // ssd_block
    streams_extent = INNER + 2 * STATE

    def back(chunk):
        return (chunks - 1 - chunk, 0)

    slope_projected, slope_taps, slope_skip, slope_gain, slope_decay = pl.pallas_call(
        middle_slope_kernel,
        grid=(chunks,),
        out_shape=(
            jax.ShapeDtypeStruct((extent, columns), jnp.bfloat16),
            jax.ShapeDtypeStruct((4, 8, streams_extent), jnp.float32),
            jax.ShapeDtypeStruct((8, INNER), jnp.float32),
            jax.ShapeDtypeStruct((8, INNER), jnp.float32),
            jax.ShapeDtypeStruct((2, 8, MHEADS), jnp.float32),
        ),
        in_specs=[
            pl.BlockSpec((ssd_block, columns), back),
            pl.BlockSpec(
                (8, columns),
                lambda chunk: (jnp.maximum((chunks - 1 - chunk) * (ssd_block // 8) - 1, 0), 0),
            ),
            pl.BlockSpec((ssd_block, INNER), back),
            pl.BlockSpec((1, STATE, INNER), lambda chunk: (chunks - 1 - chunk, 0, 0)),
            pl.BlockSpec((ssd_block, INNER), back),
            fixed((4, streams_extent)),
            fixed((1, INNER)),
            fixed((2, MHEADS)),
            fixed((1, INNER)),
            fixed(chosen.shape),
            fixed(later.shape),
        ],
        out_specs=(
            pl.BlockSpec((ssd_block, columns), back),
            fixed((4, 8, streams_extent)),
            fixed((8, INNER)),
            fixed((8, INNER)),
            fixed((2, 8, MHEADS)),
        ),
        scratch_shapes=[
            pltpu.VMEM((ssd_block + 8, streams_extent), jnp.float32),
            pltpu.VMEM((ssd_block, ssd_block), jnp.float32),
            pltpu.VMEM((MHEADS, ssd_block, ssd_block), jnp.float32),
            pltpu.VMEM((ssd_block, INNER), jnp.float32),
            pltpu.VMEM((STATE, INNER), jnp.float32),
            pltpu.VMEM((ssd_block + 8, streams_extent), jnp.float32),
            pltpu.VMEM((ssd_block, ssd_block), jnp.float32),
            pltpu.VMEM((2, ssd_block, STATE), jnp.float32),
            pltpu.VMEM((ssd_block, ssd_block), jnp.float32),
            pltpu.VMEM((ssd_block, ssd_block), jnp.float32),
        ],
        compiler_params=pltpu.CompilerParams(vmem_limit_bytes=48 * 2**20),
        cost_estimate=pl.CostEstimate(
            flops=5 * 10**10, transcendentals=8 * 10**6, bytes_accessed=30 * 10**6
        ),
    )(
        projected,
        projected,
        outcome,
        starts,
        slope,
        conv_taps,
        skip_gain.reshape(1, INNER),
        jnp.stack([a_log, dt_bias]),
        gated_gain.reshape(1, INNER),
        chosen,
        later,
    )
    slope_decay = jnp.sum(slope_decay, axis=1)
    return (
        slope_projected,
        (
            jnp.sum(slope_taps, axis=1),
            jnp.sum(slope_skip, axis=0),
            slope_decay[0],
            slope_decay[1],
            jnp.sum(slope_gain, axis=0),
        ),
    )


Y_LANE = (("tensor", 2),)


def mixer_forward(value_entries, w_in, exit_matrix, block_gain, smalls):
    rescaled_rows, rescale_grad = jax.vjp(root_mean_rescale, value_entries, block_gain)
    normed_low = to_low(rescaled_rows)
    projected = matmul_apply(normed_low, w_in)
    middle_low, outcome, starts = middle_forward(projected, smalls)
    return (
        value_entries + matmul_apply(middle_low, exit_matrix),
        (rescale_grad, normed_low, (projected, outcome, starts), middle_low),
    )


def mixer_backward(conductor, last, slope_emitted, kept, w_in, exit_matrix, smalls):
    rescale_grad, normed_low, middle_kept, middle_low = kept
    grad_low = to_low(slope_emitted)
    slope_exit_matrix = to_low(product_tn(middle_low, grad_low))
    job_out = conductor.add(Summing(slope_exit_matrix, True))
    slope_middle = product_nt(grad_low, exit_matrix)
    slope_middle = conductor.tick(after(slope_middle, [slope_exit_matrix]), 7.0)
    grad_proj, slope_smalls = middle_backward(*middle_kept, slope_middle, smalls)
    grad_proj = conductor.tick(grad_proj, 60.0 if last else 44.0, limit=0 if last else 5)
    grad_w_in = to_low(product_tn(normed_low, grad_proj))
    job_in = conductor.add(Summing(grad_w_in, True))
    grad_proj = conductor.tick(after(grad_proj, [grad_w_in]), 7.0, limit=0 if last else 5)
    grad_values, slope_scale = rescale_grad(product_nt(grad_proj, w_in))
    slope_value = conductor.tick(grad_values + slope_emitted, 10.0, Y_LANE, limit=0 if last else 5)
    return (slope_value, slope_scale, slope_smalls, (job_out, job_in))


def causal_scores(queries, key_rows):
    scores = jnp.einsum(
        "gqhd,gkhd->ghqk", queries, key_rows, preferred_element_type=jnp.float32
    ) * HD ** (-0.5)
    causal = jnp.tril(jnp.ones((MAX_PIECES, MAX_PIECES), dtype=bool))
    return jnp.where(causal[None, None], scores, -jnp.inf)


def apply_heads(latent_holder, heed_scale, triple_matrix, exit_matrix):
    rescaled_rows, rescale_grad = jax.vjp(root_mean_rescale, latent_holder, heed_scale)
    rows_low = gather_rows(to_low(rescaled_rows))
    triple = to_low(matmul_apply(rows_low, triple_matrix))
    groups = rows_low.shape[0] // MAX_PIECES
    heads_here = triple_matrix.shape[1] // (3 * HD)
    split_heads = triple.reshape(groups, MAX_PIECES, 3, heads_here, HD)
    queries, key_rows, value_rows = (
        split_heads[:, :, 0],
        split_heads[:, :, 1],
        split_heads[:, :, 2],
    )
    scores = causal_scores(queries, key_rows)
    maxima = jnp.max(scores, axis=-1, keepdims=True)
    log_total = maxima + jnp.log(jnp.sum(jnp.exp(scores - maxima), axis=-1, keepdims=True))
    weights_soft = to_low(jnp.exp(scores - log_total))
    heads_output = to_low(
        jnp.einsum("ghqk,gkhd->gqhd", weights_soft, value_rows, preferred_element_type=jnp.float32)
    )
    heads_output = heads_output.reshape(rows_low.shape[0], heads_here * HD)
    outcome = latent_holder + total_lines(product_nt(heads_output, exit_matrix))
    return (
        outcome,
        (rescale_grad, rows_low, queries, key_rows, value_rows, log_total, heads_output),
    )


def apply_heads_grad(conductor, slope_emitted, kept, triple_matrix, exit_matrix):
    rescale_grad, rows_low, queries, key_rows, value_rows, log_total, heads_output = kept
    grad_rows = conductor.tick(gather_grads(to_low(slope_emitted)), 12.0, Y_LANE)
    slope_exit_matrix = to_low(product_tn(grad_rows, heads_output))
    grad_attended = to_low(matmul_apply(grad_rows, exit_matrix)).reshape(queries.shape)
    weights_soft = jnp.exp(causal_scores(queries, key_rows) - log_total)
    grad_values = jnp.einsum(
        "ghqk,gqhd->gkhd", to_low(weights_soft), grad_attended, preferred_element_type=jnp.float32
    )
    grad_weights = jnp.einsum(
        "gqhd,gkhd->ghqk", grad_attended, value_rows, preferred_element_type=jnp.float32
    )
    grad_scores = to_low(
        weights_soft * (grad_weights - jnp.sum(weights_soft * grad_weights, axis=-1, keepdims=True))
    )
    grad_queries = jnp.einsum(
        "ghqk,gkhd->gqhd", grad_scores, key_rows, preferred_element_type=jnp.float32
    ) * HD ** (-0.5)
    grad_keys = jnp.einsum(
        "ghqk,gqhd->gkhd", grad_scores, queries, preferred_element_type=jnp.float32
    ) * HD ** (-0.5)
    grad_triple = to_low(
        jnp.stack([grad_queries, grad_keys, grad_values], axis=2).reshape(rows_low.shape[0], -1)
    )
    grad_triple = conductor.tick(after(grad_triple, [slope_exit_matrix]), 10.0, Y_LANE)
    slope_rescaled = sum_grads(product_nt(grad_triple, triple_matrix))
    slope_triple_matrix = to_low(product_tn(rows_low, grad_triple))
    job_exit = conductor.add(Summing(slope_exit_matrix, False))
    job_triple = conductor.add(Summing(slope_triple_matrix, False))
    slope_rescaled = conductor.tick(
        after(slope_rescaled, [slope_triple_matrix]), 10.0, Y_LANE
    )
    gradient_holder, slope_scale = rescale_grad(slope_rescaled)
    return (gradient_holder + slope_emitted, slope_scale, job_triple, job_exit)


def swiglu(both):
    half = both.shape[1] // 2
    return jax.nn.silu(both[:, :half]) * both[:, half:]


def perceptron_apply(latent_holder, perceptron_scale, lift_matrix, lower_matrix):
    rescaled_rows, rescale_grad = jax.vjp(root_mean_rescale, latent_holder, perceptron_scale)
    rows_low = gather_rows(to_low(rescaled_rows))
    latent_state, act_pull = jax.vjp(swiglu, matmul_apply(rows_low, lift_matrix))
    latent_merged = to_low(latent_state)
    outcome = latent_holder + total_lines(product_nt(latent_merged, lower_matrix))
    return (outcome, (rescale_grad, rows_low, act_pull, latent_merged))


def perceptron_grad(conductor, slope_emitted, kept, lift_matrix, lower_matrix):
    rescale_grad, rows_low, act_pull, latent_merged = kept
    grad_rows = conductor.tick(gather_grads(to_low(slope_emitted)), 13.0, Y_LANE)
    slope_lower_matrix = to_low(product_tn(grad_rows, latent_merged))
    job_lower = conductor.add(Summing(slope_lower_matrix, False))
    grad_rows = conductor.tick(after(grad_rows, [slope_lower_matrix]), 2.0, Y_LANE)
    (grad_both,) = act_pull(matmul_apply(grad_rows, lower_matrix))
    grad_both = conductor.tick(to_low(grad_both), 4.0, Y_LANE)
    slope_rescaled = sum_grads(product_nt(grad_both, lift_matrix))
    half = grad_both.shape[1] // 2
    slope_lifts = [
        to_low(product_tn(rows_low, grad_both[:, :half])),
        to_low(product_tn(rows_low, grad_both[:, half:])),
    ]
    slope_lifts = [conductor.add(Summing(slope, False)) for slope in slope_lifts]
    slope_rescaled = conductor.tick(slope_rescaled, 14.0, Y_LANE)
    gradient_holder, slope_scale = rescale_grad(slope_rescaled)
    return (gradient_holder + slope_emitted, slope_scale, job_lower, slope_lifts)


def body(
    byte_ids,
    targets,
    boundaries,
    lengths,
    tables,
    tables_first,
    tables_second,
    mamba_in,
    mamba_in_first,
    mamba_in_second,
    mamba_out,
    mamba_out_first,
    mamba_out_second,
    route_proj,
    route_proj_first,
    route_proj_second,
    small_params,
    small_params_first,
    small_params_second,
    heed_triple_matrix,
    attn_qkv_first,
    attn_qkv_second,
    heed_exit_matrix,
    attn_out_first,
    attn_out_second,
    lifting_matrix,
    mlp_gate_up_first,
    mlp_gate_up_second,
    lowering_matrix,
    mlp_down_first,
    mlp_down_second,
):
    devices = lax.axis_size("dp") * lax.axis_size("tensor")
    table_rows = tables.shape[1]
    small_here = small_params.shape[0]
    mixed_rows = 2 * table_rows + 16
    length_pair = jnp.stack([lengths[0] // 16, lengths[0] % 16]).astype(jnp.bfloat16)
    tail = jnp.concatenate([to_low(small_params), length_pair])
    mixed = jnp.concatenate(
        [
            to_low(tables).reshape(2 * table_rows, BYTE_WIDTH),
            jnp.pad(tail, (0, 16 * BYTE_WIDTH - tail.shape[0])).reshape(16, BYTE_WIDTH),
        ]
    )
    mixed_rows = mixed.shape[0]

    def wide_in(layer):
        low = to_low(mamba_in[layer])
        return jnp.pad(low, ((0, 0), (0, PROJ_WIDE - low.shape[1])))

    conductor = Conductor()
    exact_tiles = mamba_in.shape[1] % 16 == 0
    shards = [
        mixed,
        wide_in(0),
        to_low(mamba_out[0]),
        to_low(route_proj),
        to_low(heed_triple_matrix).reshape(heed_triple_matrix.shape[0], -1),
        to_low(heed_exit_matrix).T,
        to_low(lifting_matrix).reshape(lifting_matrix.shape[0], -1),
        to_low(lowering_matrix).T,
        wide_in(1),
        to_low(mamba_out[1]),
    ]
    kinds = [BYTE_LANES] * 4 + [MAIN_LANES] * 4 + [BYTE_LANES] * 2
    if exact_tiles:
        fan, late = MAIN_LANES, MAIN_LANES[::-1]
        in_first, in_last = 18 * 128, PROJ_WIDE - 18 * 128
        half_route = route_proj.shape[1] // 2
        half_lift = shards[6].shape[1] // 2
        jobs = [
            (3, BYTE_LANES, half_route, half_route),
            (9, BYTE_LANES, 0, BYTE_WIDTH),
            (8, BYTE_LANES, 0, in_first),
            (0, BYTE_LANES, 0, BYTE_WIDTH),
            (1, BYTE_LANES, in_first, in_last),
            (2, BYTE_LANES, 0, BYTE_WIDTH),
            (8, BYTE_LANES, in_first, in_last),
            (4, fan, 0, shards[4].shape[1]),
            (1, BYTE_LANES, 0, in_first),
            (6, fan, half_lift, half_lift),
            (3, BYTE_LANES, 0, half_route),
            (7, fan, 0, shards[7].shape[1]),
            (5, late, 0, shards[5].shape[1]),
            (6, late, 0, half_lift),
        ]
        wholes = spread_whole(shards, jobs, 0)
    else:
        wholes = [
            lax.all_gather(
                shard, ("dp", "tensor") if kind == BYTE_LANES else "dp", axis=0, tiled=True
            )
            for shard, kind in zip(shards, kinds)
        ]
    mixed_whole = wholes[0]
    full_in, full_out, full_route = [wholes[1], wholes[8]], [wholes[2], wholes[9]], wholes[3]
    triple_whole, heed_exit_whole, lift_matrix_whole, lower_matrix_whole = wholes[4:8]
    mixed_whole = mixed_whole.reshape(devices, mixed_rows, BYTE_WIDTH)
    full_tables = (
        mixed_whole[:, : 2 * table_rows]
        .reshape(devices, 2, table_rows, BYTE_WIDTH)
        .transpose(1, 0, 2, 3)
        .reshape(2, VOCAB, BYTE_WIDTH)
    )
    tails = mixed_whole[:, 2 * table_rows :].reshape(devices, -1)
    full_small = tails[:, :small_here].reshape(-1)
    pairs = tails[:, small_here : small_here + 2].astype(jnp.float32)
    byte_count = jnp.sum(pairs[:, 0] * 16.0 + pairs[:, 1])
    (
        block_gains,
        gated_gains,
        core_scales,
        head_gain,
        blank_row,
        conv_taps,
        skip_gains,
        a_logs,
        dt_biases,
    ) = unpack_small(full_small.astype(jnp.float32))
    layer_smalls = [
        (
            conv_taps[layer_index],
            skip_gains[layer_index],
            a_logs[layer_index],
            dt_biases[layer_index],
            gated_gains[layer_index],
        )
        for layer_index in range(2)
    ]
    cut_marks = boundaries[0]
    seq_len = byte_ids.shape[1]
    vocab_ids = jnp.arange(VOCAB, dtype=jnp.int32)
    onehot_in = (byte_ids[0][:, None] == vocab_ids[None, :]).astype(jnp.bfloat16)
    embedded = matmul_apply(onehot_in, full_tables[0])
    packer_output, kept_enc = mixer_forward(
        embedded, full_in[0], full_out[0], block_gains[0], layer_smalls[0]
    )
    encoded_low = to_low(packer_output)
    directed_rows = matmul_apply(encoded_low, full_route)
    cut_likelihood, prob_pull = jax.vjp(
        route_prob, directed_rows[:, :BYTE_WIDTH], directed_rows[:, BYTE_WIDTH : 2 * BYTE_WIDTH]
    )
    select_items, broadcast_back = span_maps(cut_marks)
    latent_holder, merge_transpose = jax.vjp(
        partial(merge_into_pieces, select_items), packer_output, blank_row
    )
    latent_holder, saved_heeding = apply_heads(
        latent_holder, core_scales[0], triple_whole, heed_exit_whole
    )
    latent_holder, saved_perceptron = perceptron_apply(
        latent_holder, core_scales[1], lift_matrix_whole, lower_matrix_whole
    )
    unpacked_bytes, link_layers_grad = jax.vjp(
        partial(link_layers, select_items, broadcast_back, cut_marks),
        latent_holder,
        core_scales[2],
        cut_likelihood,
        directed_rows[:, 2 * BYTE_WIDTH :],
    )
    final_out, kept_dec = mixer_forward(
        unpacked_bytes, full_in[1], full_out[1], block_gains[1], layer_smalls[1]
    )
    head_in, head_pull = jax.vjp(root_mean_rescale, final_out, head_gain)
    head_low = to_low(head_in)
    logits = product_nt(head_low, full_tables[1])
    maxima = jnp.max(logits, axis=-1, keepdims=True)
    log_total = maxima + jnp.log(jnp.sum(jnp.exp(logits - maxima), axis=-1, keepdims=True))
    onehot_out = (targets[0][:, None] == vocab_ids[None, :]).astype(jnp.float32)
    counted = (jnp.arange(seq_len, dtype=jnp.int32) < lengths[0]).astype(jnp.float32)[:, None]
    loss_local = jnp.sum((log_total - logits) * onehot_out * counted)
    grad_logits = to_low((jnp.exp(logits - log_total) - onehot_out) * counted / byte_count)
    grad_table_out = product_tn(grad_logits, head_low)
    grad_final, grad_head_gain = head_pull(matmul_apply(grad_logits, full_tables[1]))
    slope_unpacked, grad_block_dec, grad_small_dec, jobs_dec = mixer_backward(
        conductor, False, grad_final, kept_dec, full_in[1], full_out[1], layer_smalls[1]
    )
    gradient_holder, slope_closing_scale, slope_likelihood, slope_shortcut = link_layers_grad(
        slope_unpacked
    )
    gradient_holder, slope_perceptron_scale, job_lower, slope_lifts = perceptron_grad(
        conductor, conductor.tick(gradient_holder, 14.0, Y_LANE), saved_perceptron, lift_matrix_whole, lower_matrix_whole
    )
    gradient_holder, slope_heed_scale, *jobs_heads = apply_heads_grad(
        conductor, gradient_holder, saved_heeding, triple_whole, heed_exit_whole
    )
    gradient_merged, gradient_blank = merge_transpose(gradient_holder)
    grad_query, grad_key = prob_pull(slope_likelihood)
    grad_routed = to_low(jnp.concatenate([grad_query, grad_key, slope_shortcut], axis=1))
    grad_routed = after(grad_routed, [gradient_merged])
    grad_route = to_low(product_tn(encoded_low, grad_routed))
    job_route = conductor.add(Summing(grad_route, True))
    grad_routed = conductor.tick(after(grad_routed, [grad_route]), 7.0)
    grad_embedded, grad_block_enc, grad_small_enc, jobs_enc = mixer_backward(
        conductor,
        True,
        gradient_merged + product_nt(grad_routed, full_route),
        kept_enc,
        full_in[0],
        full_out[0],
        layer_smalls[0],
    )
    grad_table_in = jnp.dot(onehot_in.astype(jnp.float32).T, grad_embedded, precision=deepest_tier)
    grad_small = jnp.concatenate(
        [
            piece.reshape(-1)
            for piece in (
                jnp.stack([grad_block_enc, grad_block_dec]),
                jnp.stack([grad_small_enc[4], grad_small_dec[4]]),
                jnp.stack([slope_heed_scale, slope_perceptron_scale, slope_closing_scale]),
                grad_head_gain,
                gradient_blank,
                jnp.stack([grad_small_enc[0], grad_small_dec[0]]),
                jnp.stack([grad_small_enc[1], grad_small_dec[1]]),
                jnp.stack([grad_small_enc[2], grad_small_dec[2]]),
                jnp.stack([grad_small_enc[3], grad_small_dec[3]]),
            )
        ]
    )
    width = mamba_in.shape[2]
    grad_mixed = jnp.concatenate(
        [
            to_low(grad_table_in).reshape(devices, table_rows, BYTE_WIDTH),
            to_low(grad_table_out).reshape(devices, table_rows, BYTE_WIDTH),
            jnp.pad(
                to_low(grad_small).reshape(devices, small_here),
                ((0, 0), (0, 16 * BYTE_WIDTH - small_here)),
            ).reshape(devices, 16, BYTE_WIDTH),
        ],
        axis=1,
    )
    conductor.close()
    parts = [
        jobs_heads[1],
        slope_lifts[0],
        slope_lifts[1],
        jobs_heads[0],
        job_lower,
        jobs_dec[1],
        jobs_dec[0],
        jobs_enc[0],
        job_route,
        jobs_enc[1],
        Summing(grad_mixed.reshape(-1, BYTE_WIDTH), True),
    ]
    sums = [None if part.masks else part.result(jobs_enc[1].addends[0]) for part in parts]
    open_parts = [number for number, part in enumerate(parts) if part.masks]
    rests = [parts[number].rest(jobs_enc[1].addends[0]) for number in open_parts]
    grads = [grad for grad, _ in rests]
    sum_kinds = [kind for _, kind in rests]
    if exact_tiles:
        early = sum((jnp.sum(part * part) for part in sums if part is not None), jnp.float32(0.0))
        extra = jnp.zeros((16, 128), jnp.float32).at[0, 0].set(early).at[8, 0].set(loss_local)
        *ends, totals = sum_whole(grads, sum_kinds, extra, 1)
        square_total, loss_sum = jnp.sum(totals[:8]), jnp.sum(totals[8:])
    else:
        ends = [sum_slowly(parts[number]) for number in open_parts]
    for number, end in zip(open_parts, ends):
        sums[number] = end
    reduced_wo = sums[0].T
    reduced_gate_up = jnp.stack([sums[1], sums[2]], axis=1)
    reduced_qkv = sums[3].reshape(heed_triple_matrix.shape)
    reduced_down = sums[4].T
    reduced_in_dec = sums[5][:, :width]
    reduced_out_dec, reduced_out_enc, reduced_route = sums[6:9]
    reduced_in_enc = sums[9][:, :width]
    reduced_mixed = sums[10]
    reduced_tables = reduced_mixed[: 2 * table_rows].reshape(2, table_rows, BYTE_WIDTH)
    reduced_small = reduced_mixed[2 * table_rows :].reshape(-1)[:small_here]
    reduced_in = jnp.stack([reduced_in_enc, reduced_in_dec])
    reduced_out = jnp.stack([reduced_out_enc, reduced_out_dec])
    reduced = (
        reduced_tables,
        reduced_in,
        reduced_out,
        reduced_route,
        reduced_small,
        reduced_qkv,
        reduced_wo,
        reduced_gate_up,
        reduced_down,
    )
    if not exact_tiles:
        squares = sum((jnp.sum(grad * grad) for grad in reduced))
        totals = add_everywhere(jnp.stack([squares, loss_local]).reshape(1, 2))
        square_total, loss_sum = (totals[0, 0], totals[0, 1])
    grad_norm = jnp.sqrt(square_total)
    clip_factor = jnp.minimum(1.0, max_norm / (grad_norm + 1e-06))
    masters = (
        tables,
        mamba_in,
        mamba_out,
        route_proj,
        small_params,
        heed_triple_matrix,
        heed_exit_matrix,
        lifting_matrix,
        lowering_matrix,
    )
    firsts = (
        tables_first,
        mamba_in_first,
        mamba_out_first,
        route_proj_first,
        small_params_first,
        attn_qkv_first,
        attn_out_first,
        mlp_gate_up_first,
        mlp_down_first,
    )
    seconds = (
        tables_second,
        mamba_in_second,
        mamba_out_second,
        route_proj_second,
        small_params_second,
        attn_qkv_second,
        attn_out_second,
        mlp_gate_up_second,
        mlp_down_second,
    )
    rate_list = (
        rate_byte,
        rate_byte,
        rate_byte,
        rate_byte,
        rate_small,
        rate_main,
        rate_main,
        rate_main,
        rate_main,
    )
    decay_list = (
        weight_decay,
        weight_decay,
        weight_decay,
        weight_decay,
        0.0,
        weight_decay,
        weight_decay,
        weight_decay,
        weight_decay,
    )
    updated = [
        adam_step(
            masters[position],
            clip_factor * reduced[position],
            firsts[position],
            seconds[position],
            rate_list[position],
            decay_list[position],
        )
        for position in range(9)
    ]
    return (loss_sum, byte_count, grad_norm) + tuple(
        (member for triple_out in updated for member in triple_out)
    )


def solution(mesh):
    return jax.shard_map(
        body,
        mesh=mesh,
        in_specs=(
            P(("dp", "tensor"), None),
            P(("dp", "tensor"), None),
            P(("dp", "tensor"), None),
            P(("dp", "tensor")),
            P(None, ("dp", "tensor"), None),
            P(None, ("dp", "tensor"), None),
            P(None, ("dp", "tensor"), None),
            P(None, ("dp", "tensor"), None),
            P(None, ("dp", "tensor"), None),
            P(None, ("dp", "tensor"), None),
            P(None, ("dp", "tensor"), None),
            P(None, ("dp", "tensor"), None),
            P(None, ("dp", "tensor"), None),
            P(("dp", "tensor"), None),
            P(("dp", "tensor"), None),
            P(("dp", "tensor"), None),
            P(("dp", "tensor")),
            P(("dp", "tensor")),
            P(("dp", "tensor")),
            P("dp", None, "tensor"),
            P("dp", None, "tensor"),
            P("dp", None, "tensor"),
            P("tensor", "dp"),
            P("tensor", "dp"),
            P("tensor", "dp"),
            P("dp", None, "tensor"),
            P("dp", None, "tensor"),
            P("dp", None, "tensor"),
            P("tensor", "dp"),
            P("tensor", "dp"),
            P("tensor", "dp"),
        ),
        out_specs=(
            P(),
            P(),
            P(),
            P(None, ("dp", "tensor"), None),
            P(None, ("dp", "tensor"), None),
            P(None, ("dp", "tensor"), None),
            P(None, ("dp", "tensor"), None),
            P(None, ("dp", "tensor"), None),
            P(None, ("dp", "tensor"), None),
            P(None, ("dp", "tensor"), None),
            P(None, ("dp", "tensor"), None),
            P(None, ("dp", "tensor"), None),
            P(("dp", "tensor"), None),
            P(("dp", "tensor"), None),
            P(("dp", "tensor"), None),
            P(("dp", "tensor")),
            P(("dp", "tensor")),
            P(("dp", "tensor")),
            P("dp", None, "tensor"),
            P("dp", None, "tensor"),
            P("dp", None, "tensor"),
            P("tensor", "dp"),
            P("tensor", "dp"),
            P("tensor", "dp"),
            P("dp", None, "tensor"),
            P("dp", None, "tensor"),
            P("dp", None, "tensor"),
            P("tensor", "dp"),
            P("tensor", "dp"),
            P("tensor", "dp"),
        ),
        check_vma=False,
    )
```

```python
from functools import partial

import jax
import jax.numpy as jnp
from jax import lax
from jax.experimental import pallas as pl
from jax.experimental.pallas import tpu as pltpu
from jax.sharding import PartitionSpec as P

BYTE_WIDTH = 1024
CORE_WIDTH = 1536
VOCAB = 256
STATE = 128
HEADDIM = 64
STEP = 10
INNER = 2048
MHEADS = 32
HD = 96
MAX_PIECES = 128


deepest_tier = lax.Precision.HIGHEST
norm_eps = 1e-05
ssd_block = 128
beta_one = 0.9
beta_two = 0.95
adam_eps = 1e-08
weight_decay = 0.1
max_norm = 0.01
rate_byte = 0.06
rate_main = 0.05
rate_small = 0.5


def root_mean_rescale(value_entries, gain_vec):
    return (
        value_entries
        * lax.rsqrt(jnp.mean(value_entries * value_entries, axis=-1, keepdims=True) + norm_eps)
        * gain_vec
    )


def softplus(value_entries):
    return jnp.log1p(jnp.exp(value_entries))


def unpack_small(vector):
    extents = [
        2 * BYTE_WIDTH,
        2 * INNER,
        3 * CORE_WIDTH,
        BYTE_WIDTH,
        CORE_WIDTH - BYTE_WIDTH,
        8 * (INNER + 2 * STATE),
        2 * INNER,
        2 * MHEADS,
        2 * MHEADS,
    ]
    pieces = []
    offset = 0
    for extent in extents:
        pieces.append(vector[offset : offset + extent])
        offset += extent
    return (
        pieces[0].reshape(2, BYTE_WIDTH),
        pieces[1].reshape(2, INNER),
        pieces[2].reshape(3, CORE_WIDTH),
        pieces[3],
        pieces[4],
        pieces[5].reshape(2, 4, INNER + 2 * STATE),
        pieces[6].reshape(2, INNER),
        pieces[7].reshape(2, MHEADS),
        pieces[8].reshape(2, MHEADS),
    )


def route_prob(queries, key_rows):
    unit_query = queries * lax.rsqrt(jnp.sum(queries * queries, axis=-1, keepdims=True) + 1e-06)
    unit_key = key_rows * lax.rsqrt(jnp.sum(key_rows * key_rows, axis=-1, keepdims=True) + 1e-06)
    cosine = jnp.sum(unit_query[1:] * unit_key[:-1], axis=-1)
    return jnp.concatenate([jnp.ones((1,), jnp.float32), 0.5 * (1.0 - cosine)])


def span_maps(cut_marks):
    owner_slot = jnp.cumsum(cut_marks) - 1
    position_labels = jnp.arange(MAX_PIECES, dtype=jnp.int32)
    broadcast_back = (owner_slot[:, None] == position_labels[None, :]).astype(jnp.float32)
    select_items = broadcast_back.T * cut_marks[None, :].astype(jnp.float32)
    return (select_items, broadcast_back)


def merge_into_pieces(select_items, value_entries, blank_row):
    spans = jnp.dot(select_items, value_entries, precision=deepest_tier)
    return jnp.concatenate(
        [spans, jnp.broadcast_to(blank_row, (MAX_PIECES, CORE_WIDTH - BYTE_WIDTH))], axis=1
    )


def decay_products(confidence):
    rows = lax.broadcasted_iota(jnp.int32, (MAX_PIECES, MAX_PIECES), 0)
    columns = lax.broadcasted_iota(jnp.int32, (MAX_PIECES, MAX_PIECES), 1)
    products = jnp.where(rows > columns, 1.0 - confidence[:, None], 1.0)
    reach = 1
    while reach < MAX_PIECES:
        shifted = jnp.concatenate(
            [jnp.ones((reach, MAX_PIECES), jnp.float32), products[:-reach]], axis=0
        )
        products = products * shifted
        reach *= 2
    return jnp.where(rows >= columns, products, 0.0)


@jax.custom_vjp
def smooth_spans(piece_output, confidence):
    products = decay_products(confidence)
    return jnp.dot(products, confidence[:, None] * piece_output, precision=deepest_tier)


def smooth_keep(piece_output, confidence):
    products = decay_products(confidence)
    smoothed = jnp.dot(products, confidence[:, None] * piece_output, precision=deepest_tier)
    return smoothed, (piece_output, confidence, products, smoothed)


def smooth_pull(kept, slope):
    piece_output, confidence, products, smoothed = kept
    spread = lax.dot_general(
        products, slope, (((0,), (0,)), ((), ())), precision=deepest_tier
    )
    before = jnp.concatenate([jnp.zeros((1, smoothed.shape[1]), jnp.float32), smoothed[:-1]], axis=0)
    return (confidence[:, None] * spread, jnp.sum(spread * (piece_output - before), axis=-1))


smooth_spans.defvjp(smooth_keep, smooth_pull)


def link_layers(
    select_items,
    broadcast_back,
    cut_marks,
    latent_holder,
    closing_scale,
    cut_likelihood,
    shortcut_sum,
):
    piece_output = root_mean_rescale(latent_holder, closing_scale)[:, :BYTE_WIDTH]
    smoothed = smooth_spans(
        piece_output, jnp.dot(select_items, cut_likelihood, precision=deepest_tier)
    )
    confidence = jnp.where(cut_marks == 1, cut_likelihood, 1.0 - cut_likelihood)
    return shortcut_sum + confidence[:, None] * jnp.dot(
        broadcast_back, smoothed, precision=deepest_tier
    )


def adam_step(weight, grad, first, second, rate, decay):
    first_new = beta_one * first + (1.0 - beta_one) * grad
    second_new = beta_two * second + (1.0 - beta_two) * grad * grad
    ratio = (
        first_new
        / (1.0 - beta_one**STEP)
        / (jnp.sqrt(second_new / (1.0 - beta_two**STEP)) + adam_eps)
    )
    return (first_new, second_new, weight - rate * (ratio + decay * weight))


def to_low(value_entries):
    return value_entries.astype(jnp.bfloat16)


def matmul_apply(left, right):
    return jnp.dot(left, right, preferred_element_type=jnp.float32)


def product_tn(left, right):
    return lax.dot_general(
        left, right, (((0,), (0,)), ((), ())), preferred_element_type=jnp.float32
    )


def product_nt(left, right):
    return lax.dot_general(
        left, right, (((1,), (1,)), ((), ())), preferred_element_type=jnp.float32
    )


def swap(value_entries, axis, mask):
    size = lax.axis_size(axis)
    return lax.ppermute(value_entries, axis, [(place, place ^ mask) for place in range(size)])


def bit_masks(size):
    masks = []
    mask = 1
    while mask < size:
        masks.append(mask)
        mask *= 2
    return masks


def after(value_entries, earlier):
    if not earlier:
        return value_entries
    return lax.optimization_barrier((value_entries,) + tuple(earlier))[0]


def spread_masks(over_tensor):
    dp_masks = bit_masks(lax.axis_size("dp"))
    masks = [("dp", mask) for mask in dp_masks[1:] + dp_masks[:1]]
    if over_tensor:
        masks += [("tensor", mask) for mask in reversed(bit_masks(lax.axis_size("tensor")))]
    return masks


class Summing:
    def __init__(self, grad, over_tensor):
        self.masks = list(reversed(spread_masks(over_tensor)))
        names = [("dp", mask) for mask in reversed(bit_masks(lax.axis_size("dp")))]
        if over_tensor:
            names += [("tensor", mask) for mask in reversed(bit_masks(lax.axis_size("tensor")))]
        self.names = names
        rows = grad.shape[0] // 2 ** len(names)
        self.addends = [(grad.reshape((2,) * len(names) + (rows,) + grad.shape[1:]), names)]
        self.pending = None

    def picked(self, other=None, token=None):
        result = []
        for array, names in self.addends:
            if token is not None:
                array = after(array, [token])
            for position in reversed(range(len(names))):
                axis, mask = names[position]
                own = (lax.axis_index(axis) // mask) % 2
                if names[position] == other:
                    array = take(array, position, 1 - own)
                elif names[position] not in self.names:
                    array = take(array, position, own)
            result.append(array)
        return result

    def operand(self):
        return to_low(total(self.picked(self.masks[0])))

    def accept(self):
        self.names = [name for name in self.names if name != self.masks[0]]
        self.masks = self.masks[1:]
        self.addends.append((self.pending, self.names))
        self.pending = None

    def begun_last(self):
        left = [mask for axis, mask in self.masks if axis == "dp" and mask > 1]
        return 0 < len(left) == len(self.masks) < len(bit_masks(lax.axis_size("dp"))) - 1

    def rest(self, token):
        kind = []
        for axis, mask in self.masks:
            if lane_name(axis, mask) not in kind:
                kind.append(lane_name(axis, mask))
        if len(self.addends) == 1 or kind[0] in ("core", "y"):
            array = self.addends[0][0]
            if len(self.addends) > 1:
                array = to_low(total(self.picked(token=token)))
            return [(array, tuple(name for name in BYTE_LANES if name in kind))], tuple(kind)
        arrays = []
        for array, names in self.addends:
            lanes_here = {lane_name(axis, mask) for axis, mask in names}
            arrays.append((array, tuple(name for name in BYTE_LANES if name in lanes_here)))
        return arrays, tuple(kind)

    def result(self, token=None):
        return total(self.picked(token=token))


def lane_name(axis, mask):
    if axis == "tensor":
        return ("core", "y")[mask - 1]
    return "x" if mask == 1 else "z"


def sum_slowly(job):
    while job.masks:
        axis, mask = job.masks[0]
        job.pending = swap(job.operand(), axis, mask)
        job.accept()
    return job.result()


class Conductor:
    def __init__(self):
        self.clock = 0.0
        self.jobs = []
        self.flights = []

    def add(self, job):
        self.jobs.append(job)
        return job

    def lane(self, job):
        axis, mask = job.masks[0]
        return (axis, mask if axis == "tensor" else min(mask, 2))

    def launch(self, limit, banned, value_entries):
        operands = []
        for job in self.jobs:
            if len(self.flights) >= limit:
                break
            if job.pending is not None or not job.masks:
                continue
            lane = self.lane(job)
            depth = {("dp", 1): 3, ("tensor", 1): 2}.get(lane, 1)
            if lane in banned or sum(flight[1] == lane for flight in self.flights) >= depth:
                continue
            axis, mask = job.masks[0]
            operand = job.operand()
            rate = 3.4 if (axis, mask) == ("tensor", 1) else 25.3
            if axis == "dp" and mask > 2:
                rate = 50.0
            operand = after(operand, [value_entries])
            operands.append(operand)
            job.pending = swap(operand, axis, mask)
            start = max([self.clock] + [flight[0] - 6.0 for flight in self.flights if flight[1] == lane])
            self.flights.append((start + 6.0 + rate * operand.size * 2e-6, lane, job))
        return after(value_entries, operands)

    def tick(self, value_entries, elapsed, banned=(), limit=5):
        self.clock += elapsed
        ended = [flight for flight in self.flights if flight[0] <= self.clock]
        if ended:
            value_entries = after(value_entries, [flight[2].pending for flight in ended])
            self.flights = [flight for flight in self.flights if flight[0] > self.clock]
            for flight in ended:
                flight[2].accept()
        return self.launch(limit, banned, value_entries)

    def close(self):
        for _, _, job in sorted(self.flights, key=lambda flight: flight[0]):
            job.accept()
        self.flights = []
        for job in self.jobs:
            while job.begun_last():
                axis, mask = job.masks[0]
                job.pending = swap(job.operand(), axis, mask)
                job.accept()


def flip(place, mask):
    result = place
    bit = 1
    while bit <= mask:
        if mask & bit:
            result = result + bit * (1 - 2 * ((place // bit) % 2))
        bit *= 2
    return result


def order_steps(jobs, depth=2):
    free, busy, flights, plan = {}, {}, [], []
    waiting = [0] * len(jobs)
    clock = 0.0
    while True:
        for job, steps in enumerate(jobs):
            step = waiting[job]
            if step < 0 or step >= len(steps):
                continue
            lane, cost = steps[step]
            if busy.get(lane, 0) >= depth:
                continue
            busy[lane] = busy.get(lane, 0) + 1
            free[lane] = max(free.get(lane, 0.0), clock) + cost
            flights.append((free[lane] + 1.5, job, step, lane))
            plan.append(("start", job, step))
            waiting[job] = -1 - step
        if not flights:
            return plan
        flight = min(flights)
        flights.remove(flight)
        clock, job, step, lane = flight
        busy[lane] -= 1
        plan.append(("wait", job, step))
        waiting[job] = step + 1


def link_cost(lane, elements):
    return elements * 2e-6 * {"core": 3.4, "y": 23.0, "x": 23.0, "z": 46.0}[lane]


def here():
    dp_place, tensor_place = lax.axis_index("dp"), lax.axis_index("tensor")
    return dp_place // 2, dp_place % 2, tensor_place // 2, tensor_place % 2


def partner(lane, mask, coordinates):
    z, x, y, core = coordinates
    if lane == "z":
        z = flip(z, mask)
    if lane == "x":
        x = 1 - x
    if lane == "y":
        y = 1 - y
    if lane == "core":
        core = 1 - core
    return (z * 2 + x, y * 2 + core)


def greet(line, depth_z, coordinates):
    z = coordinates[0]
    barrier = pltpu.get_barrier_semaphore()

    def tell(device):
        pl.semaphore_signal(
            barrier, inc=1, device_id=device, device_id_type=pl.DeviceIdType.MESH
        )

    for lane in ("x", "y", "core"):
        tell(partner(lane, 1, coordinates))
    if not line:
        for mask in range(1, depth_z):
            tell(partner("z", mask, coordinates))
        pl.semaphore_wait(barrier, depth_z + 2)
        return

    @pl.when(z > 0)
    def _():
        tell(beside(-1, coordinates))

    @pl.when(z < depth_z - 1)
    def _():
        tell(beside(1, coordinates))

    ends = (z == 0).astype(jnp.int32) + (z == depth_z - 1).astype(jnp.int32)
    pl.semaphore_wait(barrier, 5 - ends)


def beside(way, coordinates):
    z, x, y, core = coordinates
    return ((z + way) * 2 + x, y * 2 + core)


def spread_kernel(plan, jobs, depth_z, *refs):
    count = (len(refs) - 3) // 2
    shards, wholes = refs[:count], refs[count : 2 * count]
    send_sems, receive_sems, own_sems = refs[2 * count :]
    coordinates = here()
    z = coordinates[0]
    greet(True, depth_z, coordinates)

    def spot(job, free, z_place):
        array, kind, first, size = jobs[job]
        index = [
            slice(None) if name in free else (z_place if name == "z" else place)
            for name, place in zip(("z", "x", "y", "core"), coordinates)
            if name in kind
        ]
        return wholes[array].at[tuple(index) + (slice(None), pl.ds(first, size))]

    def shard(job):
        array, _, first, size = jobs[job]
        return shards[array].at[:, pl.ds(first, size)]

    own = []
    for job in range(len(jobs)):
        own.append(pltpu.make_async_copy(shard(job), spot(job, (), z), own_sems.at[job]))
        own[-1].start()

    def copies(job, step, receiving):
        steps = lanes_of(jobs[job][1], depth_z)
        lane, reach = steps[step]
        free = [name for name, _ in steps[:step] if name != lane]
        base = job * (2 * depth_z + 1)
        pairs = []
        if lane == "z":
            for side, way in enumerate((1, -1)):
                number = base + 2 * (reach - 1) + side
                if receiving:
                    block = z - way * reach
                    condition = (block >= 0) & (block < depth_z)
                    target = spot(job, free, z if step == 0 else block)
                    source = target
                else:
                    block = z - way * (reach - 1)
                    condition = (block >= 0) & (block < depth_z)
                    condition &= (z + way >= 0) & (z + way < depth_z)
                    target = spot(job, free, block)
                    source = shard(job) if step == 0 else target
                copy = pltpu.make_async_remote_copy(
                    src_ref=source,
                    dst_ref=target,
                    send_sem=send_sems.at[number],
                    recv_sem=receive_sems.at[number],
                    device_id=beside(way, coordinates),
                    device_id_type=pl.DeviceIdType.MESH,
                )
                pairs.append((condition, copy))
            return pairs
        number = base + 2 * (depth_z - 1) + ("x", "y", "core").index(lane)
        target = spot(job, free, z)
        copy = pltpu.make_async_remote_copy(
            src_ref=shard(job) if step == 0 else target,
            dst_ref=target,
            send_sem=send_sems.at[number],
            recv_sem=receive_sems.at[number],
            device_id=partner(lane, 1, coordinates),
            device_id_type=pl.DeviceIdType.MESH,
        )
        return [(None, copy)]

    def perform(pairs, action):
        for condition, copy in pairs:
            if condition is None:
                getattr(copy, action)()
            else:
                pl.when(condition)(getattr(copy, action))

    copied = set()
    for action, job, step in plan:
        steps = lanes_of(jobs[job][1], depth_z)
        if action == "start":
            if steps[step][0] != steps[0][0] and job not in copied:
                own[job].wait()
                copied.add(job)
            perform(copies(job, step, False), "start")
        else:
            perform(copies(job, step, True), "wait_recv")
    for action, job, step in plan:
        if action == "start":
            perform(copies(job, step, False), "wait_send")


def lanes_of(kind, depth_z):
    steps = []
    for name in kind:
        steps += [(name, reach) for reach in range(1, depth_z if name == "z" else 2)]
    return steps


def spread_whole(shards, jobs, collective_id):
    depth_z = lax.axis_size("dp") // 2
    costs = []
    for array, kind, first, size in jobs:
        held, steps = shards[array].shape[0] * size, []
        for lane in kind:
            cost = 23.0 if lane != "core" else 3.4
            steps += [(lane, held * 2e-6 * cost)] * (depth_z - 1 if lane == "z" else 1)
            held *= depth_z if lane == "z" else 2
        costs.append(steps)
    plan = order_steps(costs)
    sizes = {"z": depth_z, "x": 2, "y": 2, "core": 2}
    kinds = {array: kind for array, kind, _, _ in jobs}
    shapes = [
        tuple(sizes[name] for name in ("z", "x", "y", "core") if name in kinds[array])
        + shard.shape
        for array, shard in enumerate(shards)
    ]
    numbers = len(jobs) * (2 * depth_z + 1)
    wholes = pl.pallas_call(
        partial(spread_kernel, plan, jobs, depth_z),
        out_shape=tuple(jax.ShapeDtypeStruct(shape, jnp.bfloat16) for shape in shapes),
        in_specs=[pl.BlockSpec(memory_space=pltpu.VMEM)] * len(shards),
        out_specs=(pl.BlockSpec(memory_space=pl.ANY),) * len(shards),
        scratch_shapes=[
            pltpu.SemaphoreType.DMA((numbers,)),
            pltpu.SemaphoreType.DMA((numbers,)),
            pltpu.SemaphoreType.DMA((len(jobs),)),
        ],
        compiler_params=pltpu.CompilerParams(
            collective_id=collective_id, has_side_effects=True, vmem_limit_bytes=60 * 2**20
        ),
    )(*shards)
    return [whole.reshape(-1, whole.shape[-1]) for whole in wholes]


BYTE_LANES = ("z", "x", "y", "core")
MAIN_LANES = ("z", "x")


def sum_kernel(plan, kinds, sources, depth_z, *refs):
    count = len(kinds)
    pieces_in = [[refs[number] for number, _ in parts] for parts in sources]
    total_in = sum(len(parts) for parts in sources)
    grads, extra = [parts[0] for parts in pieces_in], refs[total_in]
    outputs = refs[total_in + 1 : total_in + 1 + count]
    totals = refs[total_in + 1 + count]
    rest = list(refs[total_in + 2 + count :])
    coordinates = here()
    places = dict(zip(BYTE_LANES, coordinates))
    z = coordinates[0]
    mirrored = depth_z - 1 - z
    held, received, held_names, temporary = [], [], [], {}
    for job, kind in enumerate(kinds):
        held.append(rest.pop(0))
        received.append({lane: rest.pop(0) for lane in kind})
        held_names.append(names_held(kind, len(sources[job])))
    for key in temporary_shapes(kinds, sources, [ref.shape for ref in held]):
        temporary[key] = rest.pop(0)
    squares, arrivals, send_sems, receive_sems, own_sems, tile_sems = rest

    def slice_of(job, part):
        names = sources[job][part][1]
        spot = tuple(slice(None) if name in held_names[job] else places[name] for name in names)
        return pieces_in[job][part].at[spot]

    loads = []
    for job in range(count):
        loads.append(pltpu.make_async_copy(slice_of(job, 0), held[job], own_sems.at[job]))
        loads[-1].start()
    squares[...] = jnp.zeros_like(squares)
    greet(False, depth_z, coordinates)

    def prepare(job):
        loads[job].wait()
        for part in range(1, len(sources[job])):
            buffer = temporary[held[job].shape]
            copy = pltpu.make_async_copy(slice_of(job, part), buffer, own_sems.at[job])
            copy.start()
            copy.wait()
            lead, rows = held[job].shape[:-2], held[job].shape[-2]
            pieces = 1
            for size in lead:
                pieces *= size

            def piece(index, carry, buffer=buffer, lead=lead, rows=rows):
                spot, remainder = [], index
                for size in reversed(lead):
                    spot.insert(0, remainder % size)
                    remainder = remainder // size
                target, other = held[job].at[tuple(spot)], buffer.at[tuple(spot)]

                def row_step(number, inner):
                    part_rows = pl.ds(pl.multiple_of(number * 16, 16), 16)
                    target[part_rows, :] = to_low(
                        target[part_rows, :].astype(jnp.float32)
                        + other[part_rows, :].astype(jnp.float32)
                    )
                    return inner

                lax.fori_loop(0, rows // 16, row_step, 0)
                return carry

            lax.fori_loop(0, pieces, piece, 0)

    def chosen(job, step, lane_place):
        steps = lanes_of(kinds[job], depth_z)
        lane = steps[step][0]
        done = [name for name, _ in steps[:step] if name != lane]
        return [
            lane_place if name == lane else (places[name] if name in done else slice(None))
            for name in held_names[job]
        ]

    def slot(reach, side):
        shared = (depth_z - 2) // 2
        return reach - 1 if reach <= shared else shared + 2 * (reach - 1 - shared) + side

    def copies(job, step, receiving):
        kind = kinds[job]
        lane, reach = lanes_of(kind, depth_z)[step]
        base = job * (2 * depth_z + 1)
        if lane == "z":
            pairs = []
            for side, depth in enumerate((z, mirrored)):
                way = 1 - 2 * side
                aim = depth_z - reach + depth
                if side:
                    aim = depth_z - 1 - aim
                landing = received[job]["z"].at[slot(reach, side)]
                number = base + 2 * (reach - 1) + side
                source = landing if receiving else held[job].at[tuple(chosen(job, step, aim))]
                copy = pltpu.make_async_remote_copy(
                    src_ref=source,
                    dst_ref=landing,
                    send_sem=send_sems.at[number],
                    recv_sem=receive_sems.at[number],
                    device_id=beside(way, coordinates),
                    device_id_type=pl.DeviceIdType.MESH,
                )
                condition = (depth >= 1) & (depth <= reach) if receiving else depth <= reach - 1
                pairs.append((condition, copy))
            return pairs
        number = base + 2 * (depth_z - 1) + ("x", "y", "core").index(lane)
        if step == 0 and len(sources[job]) == 1:
            spot = tuple(
                1 - places[name] if name == lane else slice(None)
                for name in BYTE_LANES
                if name in kind
            )
            source = grads[job].at[spot]
        else:
            source = held[job].at[tuple(chosen(job, step, 1 - places[lane]))]
        copy = pltpu.make_async_remote_copy(
            src_ref=source,
            dst_ref=received[job][lane],
            send_sem=send_sems.at[number],
            recv_sem=receive_sems.at[number],
            device_id=partner(lane, 1, coordinates),
            device_id_type=pl.DeviceIdType.MESH,
        )
        return [(None, copy)]

    def add_pieces(job, step, lane_place, buffers, last):
        steps = lanes_of(kinds[job], depth_z)
        lane = steps[step][0]
        done = [name for name, _ in steps[:step] if name != lane]
        free = [name for name in BYTE_LANES if name in kinds[job] and name not in done + [lane]]
        sizes = [depth_z if name == "z" else 2 for name in free]
        pieces = 1
        for size in sizes:
            pieces *= size

        def piece(index, carry):
            spots, remainder = {}, index
            for name, size in reversed(list(zip(free, sizes))):
                spots[name] = remainder % size
                remainder = remainder // size
            mine = tuple(
                spots[name] if name in spots else (lane_place if name == lane else places[name])
                for name in held_names[job]
            )
            theirs = tuple(spots[name] for name in free)
            target = held[job].at[mine] if mine else held[job]
            arrived = [buffer.at[theirs] if theirs else buffer for buffer in buffers]
            rows, columns = target.shape[-2:]

            def row_step(number, inner):
                part = pl.ds(pl.multiple_of(number * 16, 16), 16)
                value = target[part, :].astype(jnp.float32)
                for other in arrived:
                    value = value + other[part, :].astype(jnp.float32)
                if last:
                    outputs[job][part, :] = value
                    square = jnp.zeros((16, 128), jnp.float32)
                    for first in range(0, columns, 128):
                        square = square + value[:, first : first + 128] * value[:, first : first + 128]
                    squares[...] += square
                else:
                    target[part, :] = to_low(value)
                return inner

            lax.fori_loop(0, rows // 16, row_step, 0)
            return carry

        if pieces == 1:
            piece(0, 0)
        else:
            lax.fori_loop(0, pieces, piece, 0)

    def accumulate(job, step):
        steps = lanes_of(kinds[job], depth_z)
        lane, reach = steps[step]
        last = step == len(steps) - 1
        if lane != "z":
            add_pieces(job, step, places[lane], [received[job][lane]], last)
            return
        buffers = [received[job]["z"].at[slot(reach, side)] for side in range(2)]
        if reach < depth_z - 1:
            for side, depth in enumerate((z, mirrored)):
                aim = depth_z - reach + depth - 1
                if side:
                    aim = depth_z - 1 - aim
                pl.when((depth >= 1) & (depth <= reach))(
                    partial(add_pieces, job, step, aim, [buffers[side]], False)
                )
            return
        ends = (z == 0) | (mirrored == 0)
        pl.when(jnp.logical_not(ends))(partial(add_pieces, job, step, z, buffers, last))
        pl.when(z == 0)(partial(add_pieces, job, step, z, buffers[1:], last))
        pl.when(mirrored == 0)(partial(add_pieces, job, step, z, buffers[:1], last))

    def perform(pairs, action):
        for condition, copy in pairs:
            if condition is None:
                getattr(copy, action)()
            else:
                pl.when(condition)(getattr(copy, action))

    loaded = set()
    for action, job, step in plan:
        lane = lanes_of(kinds[job], depth_z)[step][0]
        if job not in loaded and (action == "wait" or lane == "z" or len(sources[job]) > 1):
            prepare(job)
            loaded.add(job)
        if action == "start":
            perform(copies(job, step, False), "start")
        else:
            perform(copies(job, step, True), "wait_recv")
            accumulate(job, step)
    totals[...] = extra[...]
    totals[0:8, :] += squares[0:8, :] + squares[8:16, :]
    exchanges = [("core", 1), ("y", 1), ("x", 1)]
    mask = 1
    while mask < depth_z:
        exchanges.append(("z", mask))
        mask *= 2
    tiles = []
    for number, (lane, mask) in enumerate(exchanges):
        tiles.append(
            pltpu.make_async_remote_copy(
                src_ref=arrivals.at[2 * number],
                dst_ref=arrivals.at[2 * number + 1],
                send_sem=tile_sems.at[2 * number],
                recv_sem=tile_sems.at[2 * number + 1],
                device_id=partner(lane, mask, coordinates),
                device_id_type=pl.DeviceIdType.MESH,
            )
        )
        arrivals[2 * number] = totals[...]
        tiles[-1].start()
        tiles[-1].wait_recv()
        totals[...] += arrivals[2 * number + 1]
    for copy in tiles:
        copy.wait_send()
    for action, job, step in plan:
        if action == "start":
            perform(copies(job, step, False), "wait_send")


def names_held(kind, addends):
    return [
        name
        for name in BYTE_LANES
        if name in kind and (name == "z" or addends > 1 or name != kind[0])
    ]


def temporary_shapes(kinds, sources, shapes):
    return list(
        dict.fromkeys(
            tuple(shape) for shape, parts in zip(shapes, sources) if len(parts) > 1
        )
    )


def sum_whole(grads, kinds, extra, collective_id):
    depth_z = lax.axis_size("dp") // 2
    sizes = {"z": depth_z, "x": 2, "y": 2, "core": 2}
    jobs, arrays, shapes, scratch, sources, held_shapes = [], [], [], [], [], []
    for parts, kind in zip(grads, kinds):
        sources.append([])
        for array, names in parts:
            piece = array.shape[-2:]
            lead = tuple(sizes[name] for name in names)
            if array.ndim == 2:
                pieces = 1
                for size in lead:
                    pieces *= size
                piece = (array.shape[0] // pieces, array.shape[1])
            sources[-1].append((len(arrays), names))
            arrays.append(array.reshape(lead + piece))
        shapes.append(jax.ShapeDtypeStruct(piece, jnp.float32))
        steps, left = [], [name for name in BYTE_LANES if name in kind]
        held_shapes.append(tuple(sizes[name] for name in names_held(kind, len(parts))) + piece)
        scratch.append(pltpu.VMEM(held_shapes[-1], jnp.bfloat16))
        for lane in kind:
            left.remove(lane)
            rest = tuple(sizes[name] for name in left)
            extent = piece[0] * piece[1]
            for size in rest:
                extent *= size
            cost = 23.0 if lane != "core" else 3.4
            steps += [(lane, extent * 2e-6 * cost)] * (depth_z - 1 if lane == "z" else 1)
            lead = (2 * (depth_z - 1) - (depth_z - 2) // 2,) if lane == "z" else ()
            scratch.append(pltpu.VMEM(lead + rest + piece, jnp.bfloat16))
        jobs.append(steps)
    scratch += [
        pltpu.VMEM(shape, jnp.bfloat16)
        for shape in temporary_shapes(kinds, sources, held_shapes)
    ]
    plan = order_steps(jobs)
    numbers = len(grads) * (2 * depth_z + 1)
    tile = jax.ShapeDtypeStruct(extra.shape, jnp.float32)
    rounds = 3 + len(bit_masks(depth_z))
    return pl.pallas_call(
        partial(sum_kernel, plan, kinds, sources, depth_z),
        out_shape=tuple(shapes) + (tile,),
        in_specs=[pl.BlockSpec(memory_space=pl.ANY)] * len(arrays)
        + [pl.BlockSpec(memory_space=pltpu.VMEM)],
        out_specs=(pl.BlockSpec(memory_space=pltpu.VMEM),) * (len(grads) + 1),
        scratch_shapes=scratch
        + [
            pltpu.VMEM((16, 128), jnp.float32),
            pltpu.VMEM((2 * rounds, 16, 128), jnp.float32),
            pltpu.SemaphoreType.DMA((numbers,)),
            pltpu.SemaphoreType.DMA((numbers,)),
            pltpu.SemaphoreType.DMA((len(grads),)),
            pltpu.SemaphoreType.DMA((2 * rounds,)),
        ],
        compiler_params=pltpu.CompilerParams(
            collective_id=collective_id, has_side_effects=True, vmem_limit_bytes=60 * 2**20
        ),
    )(*arrays, extra)


def take(value_entries, axis, index):
    return lax.dynamic_index_in_dim(value_entries, index, axis, keepdims=False)


def total(addends):
    result = addends[0].astype(jnp.float32)
    for addend in addends[1:]:
        result = result + addend.astype(jnp.float32)
    return result


def add_everywhere(value_entries):
    for axis in ("tensor", "dp"):
        for mask in bit_masks(lax.axis_size(axis)):
            value_entries = value_entries + swap(value_entries, axis, mask)
    return value_entries


def gather_rows(value_entries):
    pieces = [value_entries]
    for mask in reversed(bit_masks(lax.axis_size("tensor"))):
        pieces = pieces + [swap(piece, "tensor", mask) for piece in pieces]
    return jnp.concatenate(pieces, axis=0)


def total_lines(value_entries):
    size = lax.axis_size("tensor")
    rows = value_entries.shape[0] // size
    pieces = [to_low(value_entries[i * rows : (i + 1) * rows]) for i in range(size)]
    for mask in bit_masks(size):
        half = len(pieces) // 2
        pieces = [
            pieces[i].astype(jnp.float32)
            + swap(to_low(pieces[half + i]), "tensor", mask).astype(jnp.float32)
            for i in range(half)
        ]
    return pieces[0]


gather_grads = gather_rows
sum_grads = total_lines


def low_dot(left, right, left_dim, right_dim):
    return lax.dot_general(
        left, right, (((left_dim,), (right_dim,)), ((), ())), preferred_element_type=jnp.float32
    )


def sigmoid(value_entries):
    return 0.5 * jnp.tanh(0.5 * value_entries) + 0.5


def fold_rows(value_entries):
    return jnp.sum(value_entries.reshape(-1, 8, value_entries.shape[1]), axis=0)


def lower_ones():
    rows = lax.broadcasted_iota(jnp.int32, (ssd_block, ssd_block), 0)
    columns = lax.broadcasted_iota(jnp.int32, (ssd_block, ssd_block), 1)
    return (rows >= columns).astype(jnp.float32)


FORWARD_UNROLL = 4
BACKWARD_UNROLL = 2
PROJ_WIDE = 2 * INNER + 2 * STATE + 128


def step_terms(raw_steps, decay_refs):
    shifted = raw_steps + decay_refs[1:2, :]
    steps = softplus(shifted)
    rates = -jnp.exp(decay_refs[0:1, :])
    cumulative = jnp.dot(
        lower_ones(), steps * rates, precision=deepest_tier, preferred_element_type=jnp.float32
    )
    return shifted, steps, rates, cumulative


def head_tables():
    chosen = to_low(jnp.arange(INNER)[:, None] // HEADDIM == jnp.arange(ssd_block)[None, :])
    later = jnp.where(
        jnp.arange(ssd_block)[:, None] >= jnp.arange(ssd_block)[None, :], 0.0, -1e30
    )
    return chosen, later


def first_head():
    return lax.broadcasted_iota(jnp.int32, (ssd_block, ssd_block), 1) < HEADDIM


def both_heads(value_entries):
    mask = first_head()
    zeros = jnp.zeros_like(value_entries)
    return jnp.concatenate(
        [jnp.where(mask, value_entries, zeros), jnp.where(mask, zeros, value_entries)], axis=0
    )


def spread_heads(steps, cumulative, turned, wide, narrow):
    blank = jnp.zeros((ssd_block, ssd_block - MHEADS), jnp.float32)
    turned[...] = jnp.concatenate([cumulative, blank], axis=1).T
    mask = first_head()

    def over_lanes(value_entries, head):
        return jnp.broadcast_to(value_entries[:, head : head + 1], (ssd_block, ssd_block))

    for head in range(MHEADS):
        wide[head] = over_lanes(cumulative, head)
    for pair in range(MHEADS // 2):
        narrow[:, pair * ssd_block : (pair + 1) * ssd_block] = jnp.where(
            mask, over_lanes(steps, 2 * pair), over_lanes(steps, 2 * pair + 1)
        )


def gaps_of(wide, turned, later, head):
    return jnp.exp((wide[head] - turned[pl.ds(head, 1), :]) + later[...])


def quad_cumulative(wide, quad):
    mask = first_head()
    return jnp.concatenate(
        [
            jnp.where(mask, wide[4 * quad], wide[4 * quad + 1]),
            jnp.where(mask, wide[4 * quad + 2], wide[4 * quad + 3]),
        ],
        axis=1,
    )


def quad_lanes(quad, first=0):
    return pl.ds(pl.multiple_of(quad * 2 * ssd_block + first, ssd_block), 2 * ssd_block)


def lanes(block):
    return pl.ds(pl.multiple_of(block * ssd_block, ssd_block), ssd_block)


def convolve(padded_ref, taps_ref, columns):
    result = taps_ref[0:1, columns] * padded_ref[5 : 5 + ssd_block, columns]
    for tap in range(1, 4):
        result = result + taps_ref[tap : tap + 1, columns] * padded_ref[
            5 + tap : 5 + tap + ssd_block, columns
        ]
    return result


def middle_kernel(
    projected,
    taps,
    skip,
    decay,
    gain,
    later,
    middle,
    outcome,
    starts,
    padded,
    turned,
    wide,
    narrow,
    state,
    gated,
):
    chunk = pl.program_id(0)
    streams_extent = INNER + 2 * STATE

    @pl.when(chunk == 0)
    def _():
        padded[0:8, :] = jnp.zeros((8, streams_extent), jnp.float32)
        state[...] = jnp.zeros_like(state)

    @pl.when(chunk > 0)
    def _():
        padded[0:8, :] = padded[ssd_block : ssd_block + 8, :]

    padded[8 : 8 + ssd_block, :] = projected[:, INNER : INNER + streams_extent]
    _, steps, _, cumulative = step_terms(
        projected[:, INNER + streams_extent : INNER + streams_extent + MHEADS], decay
    )
    spread_heads(steps, cumulative, turned, wide, narrow)

    def active(columns):
        convolved = convolve(padded, taps, columns)
        return convolved * sigmoid(convolved)

    in_map = active(pl.ds(INNER, STATE))
    in_low = to_low(in_map)
    in_turned = to_low(in_map.T)
    out_low = to_low(active(pl.ds(INNER + STATE, STATE)))
    affinity = low_dot(out_low, in_low, 1, 1)

    def quad_step(quad, square_sum):
        columns = quad_lanes(quad)
        inputs = active(columns)
        weighted = inputs * narrow[:, columns]
        weighted_low = to_low(weighted)
        within = []
        for pair in range(2):
            head = 4 * quad + 2 * pair
            mixing = jnp.concatenate(
                [
                    to_low(affinity * gaps_of(wide, turned, later, head)),
                    to_low(affinity * gaps_of(wide, turned, later, head + 1)),
                ],
                axis=1,
            )
            part = weighted_low[:, pair * ssd_block : (pair + 1) * ssd_block]
            within.append(low_dot(mixing, both_heads(part), 1, 0))
        within = jnp.concatenate(within, axis=1)
        cumulative_here = quad_cumulative(wide, quad)
        last = cumulative_here[ssd_block - 1 :, :]
        held = state[:, columns]
        starts[0, :, columns] = held
        across = jnp.exp(cumulative_here) * low_dot(out_low, to_low(held), 1, 0)
        to_end = to_low(weighted * jnp.exp(last - cumulative_here))
        state[:, columns] = jnp.exp(last) * held + low_dot(in_turned, to_end, 1, 0)
        result = within + across + inputs * skip[:, columns]
        outcome[:, columns] = result
        gate = projected[:, columns]
        product = result * (gate * sigmoid(gate))
        gated[:, columns] = product
        return square_sum + product * product

    square_sum = lax.fori_loop(
        0,
        INNER // (2 * ssd_block),
        quad_step,
        jnp.zeros((ssd_block, 2 * ssd_block), jnp.float32),
        unroll=FORWARD_UNROLL,
    )
    scale = lax.rsqrt(jnp.sum(square_sum, axis=1, keepdims=True) * (1.0 / INNER) + norm_eps)

    def scale_step(quad, carry):
        columns = quad_lanes(quad)
        middle[:, columns] = to_low(gated[:, columns] * scale * gain[:, columns])
        return carry

    lax.fori_loop(0, INNER // (2 * ssd_block), scale_step, 0, unroll=2)


def middle_slope_kernel(
    projected,
    earlier,
    outcome,
    starts,
    slope,
    taps,
    skip,
    decay,
    gain,
    chosen,
    later,
    slope_projected,
    slope_taps,
    slope_skip,
    slope_gain,
    slope_decay,
    padded,
    turned,
    wide,
    narrow,
    slope_state,
    slope_conv,
    slope_affinity,
    slope_maps,
    slope_cumulative,
    slope_steps,
):
    chunk = pl.num_programs(0) - 1 - pl.program_id(0)
    streams_extent = INNER + 2 * STATE
    quads = INNER // (2 * ssd_block)

    @pl.when(pl.program_id(0) == 0)
    def _():
        slope_state[...] = jnp.zeros_like(slope_state)
        slope_conv[ssd_block : ssd_block + 8, :] = jnp.zeros((8, streams_extent), jnp.float32)
        slope_taps[...] = jnp.zeros_like(slope_taps)
        slope_skip[...] = jnp.zeros_like(slope_skip)
        slope_gain[...] = jnp.zeros_like(slope_gain)
        slope_decay[...] = jnp.zeros_like(slope_decay)

    @pl.when(pl.program_id(0) > 0)
    def _():
        slope_conv[ssd_block : ssd_block + 8, :] = slope_conv[0:8, :]

    @pl.when(chunk == 0)
    def _():
        padded[0:8, :] = jnp.zeros((8, streams_extent), jnp.float32)

    @pl.when(chunk > 0)
    def _():
        padded[0:8, :] = earlier[:, INNER : INNER + streams_extent]

    padded[8 : 8 + ssd_block, :] = projected[:, INNER : INNER + streams_extent]
    slope_affinity[...] = jnp.zeros_like(slope_affinity)
    slope_maps[...] = jnp.zeros_like(slope_maps)
    slope_cumulative[...] = jnp.zeros_like(slope_cumulative)
    slope_steps[...] = jnp.zeros_like(slope_steps)
    shifted, steps, rates, cumulative = step_terms(
        projected[:, INNER + streams_extent : INNER + streams_extent + MHEADS], decay
    )
    spread_heads(steps, cumulative, turned, wide, narrow)

    def silu_pair(value_entries):
        share = sigmoid(value_entries)
        return value_entries * share, share * (1.0 + value_entries * (1.0 - share))

    def pull_convolved(columns, target_columns, slope_block):
        slope_conv[0:ssd_block, columns] = slope_block
        result = taps[3:4, columns] * slope_block
        for tap in range(3):
            reach = 3 - tap
            result = result + taps[tap : tap + 1, columns] * slope_conv[
                reach : reach + ssd_block, columns
            ]
        for tap in range(4):
            slope_taps[tap, :, columns] += fold_rows(
                slope_block * padded[5 + tap : 5 + tap + ssd_block, columns]
            )
        slope_projected[:, target_columns] = to_low(result)

    maps = (pl.ds(INNER, STATE), pl.ds(INNER + STATE, STATE))
    in_map, in_pull = silu_pair(convolve(padded, taps, maps[0]))
    out_map, out_pull = silu_pair(convolve(padded, taps, maps[1]))
    in_low, out_low, out_turned = to_low(in_map), to_low(out_map), to_low(out_map.T)
    affinity = low_dot(out_low, in_low, 1, 1)
    mask = first_head()

    def sums_step(quad, sums):
        columns = quad_lanes(quad)
        gate = projected[:, columns]
        product = outcome[:, columns] * (gate * sigmoid(gate))
        return (
            sums[0] + product * product,
            sums[1] + product * (slope[:, columns] * gain[:, columns]),
        )

    blank = jnp.zeros((ssd_block, 2 * ssd_block), jnp.float32)
    squares, crossed = lax.fori_loop(0, quads, sums_step, (blank, blank), unroll=2)
    scale = lax.rsqrt(jnp.sum(squares, axis=1, keepdims=True) * (1.0 / INNER) + norm_eps)
    pulled = scale * scale * scale * (jnp.sum(crossed, axis=1, keepdims=True) * (1.0 / INNER))

    def quad_step(quad, carry):
        columns = quad_lanes(quad)
        gate, total_here = projected[:, columns], outcome[:, columns]
        gate_value, gate_pull = silu_pair(gate)
        product = total_here * gate_value
        slope_here = slope[:, columns]
        slope_gain[:, columns] += fold_rows(slope_here * product * scale)
        slope_product = scale * (slope_here * gain[:, columns]) - product * pulled
        slope_out = slope_product * gate_value
        slope_projected[:, columns] = to_low(slope_product * total_here * gate_pull)
        inputs, inputs_pull = silu_pair(convolve(padded, taps, columns))
        slope_skip[:, columns] += fold_rows(slope_out * inputs)
        skip_here = skip[:, columns]
        scanned = total_here - inputs * skip_here
        steps_here = narrow[:, columns]
        weighted = inputs * steps_here
        weighted_low = to_low(weighted)
        slope_low = to_low(slope_out)
        slope_within = []
        for pair in range(2):
            head = 4 * quad + 2 * pair
            here_low = slope_low[:, pair * ssd_block : (pair + 1) * ssd_block]
            part = weighted_low[:, pair * ssd_block : (pair + 1) * ssd_block]
            slope_mixing = low_dot(here_low, both_heads(part), 1, 1)
            mixing = []
            for side in range(2):
                gaps = gaps_of(wide, turned, later, head + side)
                mixing.append(to_low(affinity * gaps))
                slope_affinity[...] += (
                    slope_mixing[:, side * ssd_block : (side + 1) * ssd_block] * gaps
                )
            turned_back = low_dot(jnp.concatenate(mixing, axis=1), here_low, 0, 0)
            slope_within.append(
                jnp.where(mask, turned_back[:ssd_block], turned_back[ssd_block:])
            )
        slope_within = jnp.concatenate(slope_within, axis=1)
        cumulative_here = quad_cumulative(wide, quad)
        last = cumulative_here[ssd_block - 1 :, :]
        decayed = jnp.exp(last)
        held = starts[0, :, columns]
        slope_across = to_low(slope_out * jnp.exp(cumulative_here))
        slope_maps[1] += low_dot(slope_across, to_low(held), 1, 1)
        carried_state = slope_state[:, columns]
        carried_low = to_low(carried_state)
        to_end = jnp.exp(last - cumulative_here)
        ending = to_low(weighted * to_end)
        slope_ending = low_dot(in_low, carried_low, 1, 0)
        slope_maps[0] += low_dot(ending, carried_low, 1, 1)
        slope_state[:, columns] = decayed * carried_state + low_dot(out_turned, slope_across, 1, 0)
        slope_weighted = slope_within + slope_ending * to_end
        ending_slope = slope_ending * ending.astype(jnp.float32)
        ends = jnp.sum(ending_slope, axis=0, keepdims=True) + decayed * jnp.sum(
            carried_state * held, axis=0, keepdims=True
        )
        rows = lax.broadcasted_iota(jnp.int32, (ssd_block, 2 * ssd_block), 0)
        slope_gathered = (
            slope_low.astype(jnp.float32) * scanned
            - weighted_low.astype(jnp.float32) * slope_within
            - ending_slope
            + jnp.where(rows == ssd_block - 1, ends, 0.0)
        )
        parts = []
        for value_entries in (slope_gathered, slope_weighted * inputs):
            high = to_low(value_entries)
            parts += [high, to_low(value_entries - high.astype(jnp.float32))]
        sums = low_dot(jnp.concatenate(parts, axis=0), chosen[columns, :], 1, 0)
        slope_cumulative[...] += sums[:ssd_block] + sums[ssd_block : 2 * ssd_block]
        slope_steps[...] += sums[2 * ssd_block : 3 * ssd_block] + sums[3 * ssd_block :]
        slope_inputs = slope_out * skip_here + slope_weighted * steps_here
        pull_convolved(columns, quad_lanes(quad, INNER), slope_inputs * inputs_pull)
        return carry

    lax.fori_loop(0, quads, quad_step, 0, unroll=BACKWARD_UNROLL)
    affinity_low = to_low(slope_affinity[...])
    slope_in = slope_maps[0] + low_dot(affinity_low, out_low, 0, 0)
    slope_out_map = slope_maps[1] + low_dot(affinity_low, in_low, 1, 0)
    pull_convolved(maps[0], pl.ds(2 * INNER, STATE), slope_in * in_pull)
    pull_convolved(maps[1], pl.ds(2 * INNER + STATE, STATE), slope_out_map * out_pull)
    slope_changes = lax.dot_general(
        lower_ones(),
        slope_cumulative[...],
        (((0,), (0,)), ((), ())),
        precision=deepest_tier,
        preferred_element_type=jnp.float32,
    )[:, :MHEADS]
    slope_step = slope_steps[:, :MHEADS] + slope_changes * rates
    slope_raw = slope_step * sigmoid(shifted)
    slope_decay[0] += fold_rows(slope_changes * steps) * rates
    slope_decay[1] += fold_rows(slope_raw)
    slope_projected[:, INNER + streams_extent :] = jnp.concatenate(
        [to_low(slope_raw), jnp.zeros((ssd_block, 128 - MHEADS), jnp.bfloat16)], axis=1
    )


def fixed(shape):
    return pl.BlockSpec(shape, lambda chunk: (0,) * len(shape))


def middle_forward(projected, smalls):
    conv_taps, skip_gain, a_log, dt_bias, gated_gain = smalls
    chosen, later = head_tables()
    extent, columns = projected.shape
    chunks = extent // ssd_block
    streams_extent = INNER + 2 * STATE
    return pl.pallas_call(
        middle_kernel,
        grid=(chunks,),
        out_shape=(
            jax.ShapeDtypeStruct((extent, INNER), jnp.bfloat16),
            jax.ShapeDtypeStruct((extent, INNER), jnp.float32),
            jax.ShapeDtypeStruct((chunks, STATE, INNER), jnp.float32),
        ),
        in_specs=[
            pl.BlockSpec((ssd_block, columns), lambda chunk: (chunk, 0)),
            fixed((4, streams_extent)),
            fixed((1, INNER)),
            fixed((2, MHEADS)),
            fixed((1, INNER)),
            fixed(later.shape),
        ],
        out_specs=(
            pl.BlockSpec((ssd_block, INNER), lambda chunk: (chunk, 0)),
            pl.BlockSpec((ssd_block, INNER), lambda chunk: (chunk, 0)),
            pl.BlockSpec((1, STATE, INNER), lambda chunk: (chunk, 0, 0)),
        ),
        scratch_shapes=[
            pltpu.VMEM((ssd_block + 8, streams_extent), jnp.float32),
            pltpu.VMEM((ssd_block, ssd_block), jnp.float32),
            pltpu.VMEM((MHEADS, ssd_block, ssd_block), jnp.float32),
            pltpu.VMEM((ssd_block, INNER), jnp.float32),
            pltpu.VMEM((STATE, INNER), jnp.float32),
            pltpu.VMEM((ssd_block, INNER), jnp.float32),
        ],
        compiler_params=pltpu.CompilerParams(vmem_limit_bytes=48 * 2**20),
        cost_estimate=pl.CostEstimate(
            flops=2 * 10**10, transcendentals=4 * 10**6, bytes_accessed=20 * 10**6
        ),
    )(
        projected,
        conv_taps,
        skip_gain.reshape(1, INNER),
        jnp.stack([a_log, dt_bias]),
        gated_gain.reshape(1, INNER),
        later,
    )


def middle_backward(projected, outcome, starts, slope, smalls):
    conv_taps, skip_gain, a_log, dt_bias, gated_gain = smalls
    chosen, later = head_tables()
    extent, columns = projected.shape
    chunks = extent // ssd_block
    streams_extent = INNER + 2 * STATE

    def back(chunk):
        return (chunks - 1 - chunk, 0)

    slope_projected, slope_taps, slope_skip, slope_gain, slope_decay = pl.pallas_call(
        middle_slope_kernel,
        grid=(chunks,),
        out_shape=(
            jax.ShapeDtypeStruct((extent, columns), jnp.bfloat16),
            jax.ShapeDtypeStruct((4, 8, streams_extent), jnp.float32),
            jax.ShapeDtypeStruct((8, INNER), jnp.float32),
            jax.ShapeDtypeStruct((8, INNER), jnp.float32),
            jax.ShapeDtypeStruct((2, 8, MHEADS), jnp.float32),
        ),
        in_specs=[
            pl.BlockSpec((ssd_block, columns), back),
            pl.BlockSpec(
                (8, columns),
                lambda chunk: (jnp.maximum((chunks - 1 - chunk) * (ssd_block // 8) - 1, 0), 0),
            ),
            pl.BlockSpec((ssd_block, INNER), back),
            pl.BlockSpec((1, STATE, INNER), lambda chunk: (chunks - 1 - chunk, 0, 0)),
            pl.BlockSpec((ssd_block, INNER), back),
            fixed((4, streams_extent)),
            fixed((1, INNER)),
            fixed((2, MHEADS)),
            fixed((1, INNER)),
            fixed(chosen.shape),
            fixed(later.shape),
        ],
        out_specs=(
            pl.BlockSpec((ssd_block, columns), back),
            fixed((4, 8, streams_extent)),
            fixed((8, INNER)),
            fixed((8, INNER)),
            fixed((2, 8, MHEADS)),
        ),
        scratch_shapes=[
            pltpu.VMEM((ssd_block + 8, streams_extent), jnp.float32),
            pltpu.VMEM((ssd_block, ssd_block), jnp.float32),
            pltpu.VMEM((MHEADS, ssd_block, ssd_block), jnp.float32),
            pltpu.VMEM((ssd_block, INNER), jnp.float32),
            pltpu.VMEM((STATE, INNER), jnp.float32),
            pltpu.VMEM((ssd_block + 8, streams_extent), jnp.float32),
            pltpu.VMEM((ssd_block, ssd_block), jnp.float32),
            pltpu.VMEM((2, ssd_block, STATE), jnp.float32),
            pltpu.VMEM((ssd_block, ssd_block), jnp.float32),
            pltpu.VMEM((ssd_block, ssd_block), jnp.float32),
        ],
        compiler_params=pltpu.CompilerParams(vmem_limit_bytes=48 * 2**20),
        cost_estimate=pl.CostEstimate(
            flops=5 * 10**10, transcendentals=8 * 10**6, bytes_accessed=30 * 10**6
        ),
    )(
        projected,
        projected,
        outcome,
        starts,
        slope,
        conv_taps,
        skip_gain.reshape(1, INNER),
        jnp.stack([a_log, dt_bias]),
        gated_gain.reshape(1, INNER),
        chosen,
        later,
    )
    slope_decay = jnp.sum(slope_decay, axis=1)
    return (
        slope_projected,
        (
            jnp.sum(slope_taps, axis=1),
            jnp.sum(slope_skip, axis=0),
            slope_decay[0],
            slope_decay[1],
            jnp.sum(slope_gain, axis=0),
        ),
    )


Y_LANE = (("tensor", 2),)


def mixer_forward(value_entries, w_in, exit_matrix, block_gain, smalls):
    rescaled_rows, rescale_grad = jax.vjp(root_mean_rescale, value_entries, block_gain)
    normed_low = to_low(rescaled_rows)
    projected = matmul_apply(normed_low, w_in)
    middle_low, outcome, starts = middle_forward(projected, smalls)
    return (
        value_entries + matmul_apply(middle_low, exit_matrix),
        (rescale_grad, normed_low, (projected, outcome, starts), middle_low),
    )


def mixer_backward(conductor, last, slope_emitted, kept, w_in, exit_matrix, smalls):
    rescale_grad, normed_low, middle_kept, middle_low = kept
    grad_low = to_low(slope_emitted)
    slope_exit_matrix = to_low(product_tn(middle_low, grad_low))
    job_out = conductor.add(Summing(slope_exit_matrix, True))
    slope_middle = product_nt(grad_low, exit_matrix)
    slope_middle = conductor.tick(after(slope_middle, [slope_exit_matrix]), 7.0)
    grad_proj, slope_smalls = middle_backward(*middle_kept, slope_middle, smalls)
    grad_proj = conductor.tick(grad_proj, 60.0 if last else 44.0, limit=0 if last else 5)
    grad_w_in = to_low(product_tn(normed_low, grad_proj))
    job_in = conductor.add(Summing(grad_w_in, True))
    grad_proj = conductor.tick(after(grad_proj, [grad_w_in]), 7.0, limit=0 if last else 5)
    grad_values, slope_scale = rescale_grad(product_nt(grad_proj, w_in))
    slope_value = conductor.tick(grad_values + slope_emitted, 10.0, Y_LANE, limit=0 if last else 5)
    return (slope_value, slope_scale, slope_smalls, (job_out, job_in))


def head_mask(head, extent):
    columns = lax.broadcasted_iota(jnp.int32, (1, extent), 1)
    inside = (columns >= head * HD) & (columns < (head + 1) * HD)
    return jnp.where(inside, 1.0, 0.0).astype(jnp.bfloat16)


def head_weights(queries, key_rows):
    scores = low_dot(queries, key_rows, 1, 1) * HD ** (-0.5)
    rows = lax.broadcasted_iota(jnp.int32, (MAX_PIECES, MAX_PIECES), 0)
    columns = lax.broadcasted_iota(jnp.int32, (MAX_PIECES, MAX_PIECES), 1)
    scores = jnp.where(rows >= columns, scores, -jnp.inf)
    exponents = jnp.exp(scores - jnp.max(scores, axis=-1, keepdims=True))
    return exponents / jnp.sum(exponents, axis=-1, keepdims=True)


def attend_kernel(triple, output):
    extent = output.shape[1]
    queries, key_rows = triple[:, :extent], triple[:, extent : 2 * extent]
    value_rows = triple[:, 2 * extent :]
    attended = jnp.zeros(output.shape, jnp.float32)
    for head in range(extent // HD):
        mask = head_mask(head, extent)
        weights = to_low(head_weights(queries * mask, key_rows))
        attended = attended + low_dot(weights, value_rows * mask, 1, 0)
    output[...] = to_low(attended)


def attend_slope_kernel(triple, slope, output):
    extent = slope.shape[1]
    queries, key_rows = triple[:, :extent], triple[:, extent : 2 * extent]
    value_rows = triple[:, 2 * extent :]
    slope_here = slope[...]
    slopes = [jnp.zeros(slope.shape, jnp.float32)] * 3
    for head in range(extent // HD):
        mask = head_mask(head, extent)
        weights = head_weights(queries * mask, key_rows)
        slope_masked = slope_here * mask
        slope_weights = low_dot(slope_masked, value_rows, 1, 1)
        slope_scores = to_low(
            weights
            * (slope_weights - jnp.sum(weights * slope_weights, axis=-1, keepdims=True))
        )
        slopes[0] = slopes[0] + low_dot(slope_scores, key_rows * mask, 1, 0)
        slopes[1] = slopes[1] + low_dot(slope_scores, queries * mask, 0, 0)
        slopes[2] = slopes[2] + low_dot(to_low(weights), slope_masked, 0, 0)
    output[:, :extent] = to_low(slopes[0] * HD ** (-0.5))
    output[:, extent : 2 * extent] = to_low(slopes[1] * HD ** (-0.5))
    output[:, 2 * extent :] = to_low(slopes[2])


def by_sequence(kernel, columns, *arrays):
    rows = arrays[0].shape[0]
    return pl.pallas_call(
        kernel,
        grid=(rows // MAX_PIECES,),
        out_shape=jax.ShapeDtypeStruct((rows, columns), jnp.bfloat16),
        in_specs=[
            pl.BlockSpec((MAX_PIECES, array.shape[1]), lambda group: (group, 0)) for array in arrays
        ],
        out_specs=pl.BlockSpec((MAX_PIECES, columns), lambda group: (group, 0)),
        compiler_params=pltpu.CompilerParams(vmem_limit_bytes=24 * 2**20),
        cost_estimate=pl.CostEstimate(
            flops=3 * 10**9, transcendentals=3 * 10**5, bytes_accessed=4 * 10**6
        ),
    )(*arrays)


def apply_heads(latent_holder, heed_scale, triple_matrix, exit_matrix):
    rescaled_rows, rescale_grad = jax.vjp(root_mean_rescale, latent_holder, heed_scale)
    rows_low = gather_rows(to_low(rescaled_rows))
    triple = to_low(matmul_apply(rows_low, triple_matrix))
    heads_output = by_sequence(attend_kernel, triple.shape[1] // 3, triple)
    outcome = latent_holder + total_lines(product_nt(heads_output, exit_matrix))
    return outcome, (rescale_grad, rows_low, triple, heads_output)


def apply_heads_grad(conductor, slope_emitted, kept, triple_matrix, exit_matrix):
    rescale_grad, rows_low, triple, heads_output = kept
    grad_rows = conductor.tick(gather_grads(to_low(slope_emitted)), 12.0, Y_LANE)
    slope_exit_matrix = to_low(product_tn(grad_rows, heads_output))
    grad_attended = to_low(matmul_apply(grad_rows, exit_matrix))
    grad_triple = by_sequence(attend_slope_kernel, triple.shape[1], triple, grad_attended)
    grad_triple = conductor.tick(after(grad_triple, [slope_exit_matrix]), 10.0, Y_LANE)
    slope_rescaled = sum_grads(product_nt(grad_triple, triple_matrix))
    slope_triple_matrix = to_low(product_tn(rows_low, grad_triple))
    job_exit = conductor.add(Summing(slope_exit_matrix, False))
    job_triple = conductor.add(Summing(slope_triple_matrix, False))
    slope_rescaled = conductor.tick(
        after(slope_rescaled, [slope_triple_matrix]), 10.0, Y_LANE
    )
    gradient_holder, slope_scale = rescale_grad(slope_rescaled)
    return (gradient_holder + slope_emitted, slope_scale, job_triple, job_exit)


def swiglu(both):
    half = both.shape[1] // 2
    return jax.nn.silu(both[:, :half]) * both[:, half:]


def perceptron_apply(latent_holder, perceptron_scale, lift_matrix, lower_matrix):
    rescaled_rows, rescale_grad = jax.vjp(root_mean_rescale, latent_holder, perceptron_scale)
    rows_low = gather_rows(to_low(rescaled_rows))
    latent_state, act_pull = jax.vjp(swiglu, matmul_apply(rows_low, lift_matrix))
    latent_merged = to_low(latent_state)
    outcome = latent_holder + total_lines(product_nt(latent_merged, lower_matrix))
    return (outcome, (rescale_grad, rows_low, act_pull, latent_merged))


def perceptron_grad(conductor, slope_emitted, kept, lift_matrix, lower_matrix):
    rescale_grad, rows_low, act_pull, latent_merged = kept
    grad_rows = conductor.tick(gather_grads(to_low(slope_emitted)), 13.0, Y_LANE)
    slope_lower_matrix = to_low(product_tn(grad_rows, latent_merged))
    job_lower = conductor.add(Summing(slope_lower_matrix, False))
    grad_rows = conductor.tick(after(grad_rows, [slope_lower_matrix]), 2.0, Y_LANE)
    (grad_both,) = act_pull(matmul_apply(grad_rows, lower_matrix))
    grad_both = conductor.tick(to_low(grad_both), 4.0, Y_LANE)
    slope_rescaled = sum_grads(product_nt(grad_both, lift_matrix))
    half = grad_both.shape[1] // 2
    slope_lifts = [
        to_low(product_tn(rows_low, grad_both[:, :half])),
        to_low(product_tn(rows_low, grad_both[:, half:])),
    ]
    slope_lifts = [conductor.add(Summing(slope, False)) for slope in slope_lifts]
    slope_rescaled = conductor.tick(slope_rescaled, 14.0, Y_LANE)
    gradient_holder, slope_scale = rescale_grad(slope_rescaled)
    return (gradient_holder + slope_emitted, slope_scale, job_lower, slope_lifts)


def body(
    byte_ids,
    targets,
    boundaries,
    lengths,
    tables,
    tables_first,
    tables_second,
    mamba_in,
    mamba_in_first,
    mamba_in_second,
    mamba_out,
    mamba_out_first,
    mamba_out_second,
    route_proj,
    route_proj_first,
    route_proj_second,
    small_params,
    small_params_first,
    small_params_second,
    heed_triple_matrix,
    attn_qkv_first,
    attn_qkv_second,
    heed_exit_matrix,
    attn_out_first,
    attn_out_second,
    lifting_matrix,
    mlp_gate_up_first,
    mlp_gate_up_second,
    lowering_matrix,
    mlp_down_first,
    mlp_down_second,
):
    devices = lax.axis_size("dp") * lax.axis_size("tensor")
    table_rows = tables.shape[1]
    small_here = small_params.shape[0]
    mixed_rows = 2 * table_rows + 16
    length_pair = jnp.stack([lengths[0] // 16, lengths[0] % 16]).astype(jnp.bfloat16)
    tail = jnp.concatenate([to_low(small_params), length_pair])
    mixed = jnp.concatenate(
        [
            to_low(tables).reshape(2 * table_rows, BYTE_WIDTH),
            jnp.pad(tail, (0, 16 * BYTE_WIDTH - tail.shape[0])).reshape(16, BYTE_WIDTH),
        ]
    )
    mixed_rows = mixed.shape[0]

    def wide_in(layer):
        low = to_low(mamba_in[layer])
        return jnp.pad(low, ((0, 0), (0, PROJ_WIDE - low.shape[1])))

    conductor = Conductor()
    exact_tiles = mamba_in.shape[1] % 16 == 0
    shards = [
        mixed,
        wide_in(0),
        to_low(mamba_out[0]),
        to_low(route_proj),
        to_low(heed_triple_matrix).reshape(heed_triple_matrix.shape[0], -1),
        to_low(heed_exit_matrix).T,
        to_low(lifting_matrix).reshape(lifting_matrix.shape[0], -1),
        to_low(lowering_matrix).T,
        wide_in(1),
        to_low(mamba_out[1]),
    ]
    kinds = [BYTE_LANES] * 4 + [MAIN_LANES] * 4 + [BYTE_LANES] * 2
    if exact_tiles:
        fan, late = MAIN_LANES, MAIN_LANES[::-1]
        in_first, in_last = 18 * 128, PROJ_WIDE - 18 * 128
        half_route = route_proj.shape[1] // 2
        half_lift = shards[6].shape[1] // 2
        jobs = [
            (3, BYTE_LANES, half_route, half_route),
            (9, BYTE_LANES, 0, BYTE_WIDTH),
            (8, BYTE_LANES, 0, in_first),
            (0, BYTE_LANES, 0, BYTE_WIDTH),
            (1, BYTE_LANES, in_first, in_last),
            (2, BYTE_LANES, 0, BYTE_WIDTH),
            (8, BYTE_LANES, in_first, in_last),
            (4, fan, 0, shards[4].shape[1]),
            (1, BYTE_LANES, 0, in_first),
            (6, fan, half_lift, half_lift),
            (3, BYTE_LANES, 0, half_route),
            (7, fan, 0, shards[7].shape[1]),
            (5, late, 0, shards[5].shape[1]),
            (6, late, 0, half_lift),
        ]
        wholes = spread_whole(shards, jobs, 0)
    else:
        wholes = [
            lax.all_gather(
                shard, ("dp", "tensor") if kind == BYTE_LANES else "dp", axis=0, tiled=True
            )
            for shard, kind in zip(shards, kinds)
        ]
    mixed_whole = wholes[0]
    full_in, full_out, full_route = [wholes[1], wholes[8]], [wholes[2], wholes[9]], wholes[3]
    triple_whole, heed_exit_whole, lift_matrix_whole, lower_matrix_whole = wholes[4:8]
    mixed_whole = mixed_whole.reshape(devices, mixed_rows, BYTE_WIDTH)
    full_tables = (
        mixed_whole[:, : 2 * table_rows]
        .reshape(devices, 2, table_rows, BYTE_WIDTH)
        .transpose(1, 0, 2, 3)
        .reshape(2, VOCAB, BYTE_WIDTH)
    )
    tails = mixed_whole[:, 2 * table_rows :].reshape(devices, -1)
    full_small = tails[:, :small_here].reshape(-1)
    pairs = tails[:, small_here : small_here + 2].astype(jnp.float32)
    byte_count = jnp.sum(pairs[:, 0] * 16.0 + pairs[:, 1])
    (
        block_gains,
        gated_gains,
        core_scales,
        head_gain,
        blank_row,
        conv_taps,
        skip_gains,
        a_logs,
        dt_biases,
    ) = unpack_small(full_small.astype(jnp.float32))
    layer_smalls = [
        (
            conv_taps[layer_index],
            skip_gains[layer_index],
            a_logs[layer_index],
            dt_biases[layer_index],
            gated_gains[layer_index],
        )
        for layer_index in range(2)
    ]
    cut_marks = boundaries[0]
    seq_len = byte_ids.shape[1]
    vocab_ids = jnp.arange(VOCAB, dtype=jnp.int32)
    onehot_in = (byte_ids[0][:, None] == vocab_ids[None, :]).astype(jnp.bfloat16)
    embedded = matmul_apply(onehot_in, full_tables[0])
    packer_output, kept_enc = mixer_forward(
        embedded, full_in[0], full_out[0], block_gains[0], layer_smalls[0]
    )
    encoded_low = to_low(packer_output)
    directed_rows = matmul_apply(encoded_low, full_route)
    cut_likelihood, prob_pull = jax.vjp(
        route_prob, directed_rows[:, :BYTE_WIDTH], directed_rows[:, BYTE_WIDTH : 2 * BYTE_WIDTH]
    )
    select_items, broadcast_back = span_maps(cut_marks)
    latent_holder, merge_transpose = jax.vjp(
        partial(merge_into_pieces, select_items), packer_output, blank_row
    )
    latent_holder, saved_heeding = apply_heads(
        latent_holder, core_scales[0], triple_whole, heed_exit_whole
    )
    latent_holder, saved_perceptron = perceptron_apply(
        latent_holder, core_scales[1], lift_matrix_whole, lower_matrix_whole
    )
    unpacked_bytes, link_layers_grad = jax.vjp(
        partial(link_layers, select_items, broadcast_back, cut_marks),
        latent_holder,
        core_scales[2],
        cut_likelihood,
        directed_rows[:, 2 * BYTE_WIDTH :],
    )
    final_out, kept_dec = mixer_forward(
        unpacked_bytes, full_in[1], full_out[1], block_gains[1], layer_smalls[1]
    )
    head_in, head_pull = jax.vjp(root_mean_rescale, final_out, head_gain)
    head_low = to_low(head_in)
    logits = product_nt(head_low, full_tables[1])
    maxima = jnp.max(logits, axis=-1, keepdims=True)
    log_total = maxima + jnp.log(jnp.sum(jnp.exp(logits - maxima), axis=-1, keepdims=True))
    onehot_out = (targets[0][:, None] == vocab_ids[None, :]).astype(jnp.float32)
    counted = (jnp.arange(seq_len, dtype=jnp.int32) < lengths[0]).astype(jnp.float32)[:, None]
    loss_local = jnp.sum((log_total - logits) * onehot_out * counted)
    grad_logits = to_low((jnp.exp(logits - log_total) - onehot_out) * counted / byte_count)
    grad_table_out = product_tn(grad_logits, head_low)
    grad_final, grad_head_gain = head_pull(matmul_apply(grad_logits, full_tables[1]))
    slope_unpacked, grad_block_dec, grad_small_dec, jobs_dec = mixer_backward(
        conductor, False, grad_final, kept_dec, full_in[1], full_out[1], layer_smalls[1]
    )
    gradient_holder, slope_closing_scale, slope_likelihood, slope_shortcut = link_layers_grad(
        slope_unpacked
    )
    gradient_holder, slope_perceptron_scale, job_lower, slope_lifts = perceptron_grad(
        conductor, conductor.tick(gradient_holder, 14.0, Y_LANE), saved_perceptron, lift_matrix_whole, lower_matrix_whole
    )
    gradient_holder, slope_heed_scale, *jobs_heads = apply_heads_grad(
        conductor, gradient_holder, saved_heeding, triple_whole, heed_exit_whole
    )
    gradient_merged, gradient_blank = merge_transpose(gradient_holder)
    grad_query, grad_key = prob_pull(slope_likelihood)
    grad_routed = to_low(jnp.concatenate([grad_query, grad_key, slope_shortcut], axis=1))
    grad_routed = after(grad_routed, [gradient_merged])
    grad_route = to_low(product_tn(encoded_low, grad_routed))
    job_route = conductor.add(Summing(grad_route, True))
    grad_routed = conductor.tick(after(grad_routed, [grad_route]), 7.0)
    grad_embedded, grad_block_enc, grad_small_enc, jobs_enc = mixer_backward(
        conductor,
        True,
        gradient_merged + product_nt(grad_routed, full_route),
        kept_enc,
        full_in[0],
        full_out[0],
        layer_smalls[0],
    )
    grad_table_in = jnp.dot(onehot_in.astype(jnp.float32).T, grad_embedded, precision=deepest_tier)
    grad_small = jnp.concatenate(
        [
            piece.reshape(-1)
            for piece in (
                jnp.stack([grad_block_enc, grad_block_dec]),
                jnp.stack([grad_small_enc[4], grad_small_dec[4]]),
                jnp.stack([slope_heed_scale, slope_perceptron_scale, slope_closing_scale]),
                grad_head_gain,
                gradient_blank,
                jnp.stack([grad_small_enc[0], grad_small_dec[0]]),
                jnp.stack([grad_small_enc[1], grad_small_dec[1]]),
                jnp.stack([grad_small_enc[2], grad_small_dec[2]]),
                jnp.stack([grad_small_enc[3], grad_small_dec[3]]),
            )
        ]
    )
    width = mamba_in.shape[2]
    grad_mixed = jnp.concatenate(
        [
            to_low(grad_table_in).reshape(devices, table_rows, BYTE_WIDTH),
            to_low(grad_table_out).reshape(devices, table_rows, BYTE_WIDTH),
            jnp.pad(
                to_low(grad_small).reshape(devices, small_here),
                ((0, 0), (0, 16 * BYTE_WIDTH - small_here)),
            ).reshape(devices, 16, BYTE_WIDTH),
        ],
        axis=1,
    )
    conductor.close()
    parts = [
        jobs_heads[1],
        slope_lifts[0],
        slope_lifts[1],
        jobs_heads[0],
        job_lower,
        jobs_dec[1],
        jobs_dec[0],
        jobs_enc[0],
        job_route,
        jobs_enc[1],
        Summing(grad_mixed.reshape(-1, BYTE_WIDTH), True),
    ]
    sums = [None if part.masks else part.result(jobs_enc[1].addends[0][0]) for part in parts]
    open_parts = [number for number in (8, 9, 7, 10, 3, 0, 1, 2, 4, 5, 6) if parts[number].masks]
    rests = [parts[number].rest(jobs_enc[1].addends[0][0]) for number in open_parts]
    grads = [grad for grad, _ in rests]
    sum_kinds = [kind for _, kind in rests]
    if exact_tiles:
        early = sum((jnp.sum(part * part) for part in sums if part is not None), jnp.float32(0.0))
        extra = jnp.zeros((16, 128), jnp.float32).at[0, 0].set(early).at[8, 0].set(loss_local)
        *ends, totals = sum_whole(grads, sum_kinds, extra, 1)
        square_total, loss_sum = jnp.sum(totals[:8]), jnp.sum(totals[8:])
    else:
        ends = [sum_slowly(parts[number]) for number in open_parts]
    for number, end in zip(open_parts, ends):
        sums[number] = end
    reduced_wo = sums[0].T
    reduced_gate_up = jnp.stack([sums[1], sums[2]], axis=1)
    reduced_qkv = sums[3].reshape(heed_triple_matrix.shape)
    reduced_down = sums[4].T
    reduced_in_dec = sums[5][:, :width]
    reduced_out_dec, reduced_out_enc, reduced_route = sums[6:9]
    reduced_in_enc = sums[9][:, :width]
    reduced_mixed = sums[10]
    reduced_tables = reduced_mixed[: 2 * table_rows].reshape(2, table_rows, BYTE_WIDTH)
    reduced_small = reduced_mixed[2 * table_rows :].reshape(-1)[:small_here]
    reduced_in = jnp.stack([reduced_in_enc, reduced_in_dec])
    reduced_out = jnp.stack([reduced_out_enc, reduced_out_dec])
    reduced = (
        reduced_tables,
        reduced_in,
        reduced_out,
        reduced_route,
        reduced_small,
        reduced_qkv,
        reduced_wo,
        reduced_gate_up,
        reduced_down,
    )
    if not exact_tiles:
        squares = sum((jnp.sum(grad * grad) for grad in reduced))
        totals = add_everywhere(jnp.stack([squares, loss_local]).reshape(1, 2))
        square_total, loss_sum = (totals[0, 0], totals[0, 1])
    grad_norm = jnp.sqrt(square_total)
    clip_factor = jnp.minimum(1.0, max_norm / (grad_norm + 1e-06))
    masters = (
        tables,
        mamba_in,
        mamba_out,
        route_proj,
        small_params,
        heed_triple_matrix,
        heed_exit_matrix,
        lifting_matrix,
        lowering_matrix,
    )
    firsts = (
        tables_first,
        mamba_in_first,
        mamba_out_first,
        route_proj_first,
        small_params_first,
        attn_qkv_first,
        attn_out_first,
        mlp_gate_up_first,
        mlp_down_first,
    )
    seconds = (
        tables_second,
        mamba_in_second,
        mamba_out_second,
        route_proj_second,
        small_params_second,
        attn_qkv_second,
        attn_out_second,
        mlp_gate_up_second,
        mlp_down_second,
    )
    rate_list = (
        rate_byte,
        rate_byte,
        rate_byte,
        rate_byte,
        rate_small,
        rate_main,
        rate_main,
        rate_main,
        rate_main,
    )
    decay_list = (
        weight_decay,
        weight_decay,
        weight_decay,
        weight_decay,
        0.0,
        weight_decay,
        weight_decay,
        weight_decay,
        weight_decay,
    )
    updated = [
        adam_step(
            masters[position],
            clip_factor * reduced[position],
            firsts[position],
            seconds[position],
            rate_list[position],
            decay_list[position],
        )
        for position in range(9)
    ]
    return (loss_sum, byte_count, grad_norm) + tuple(
        (member for triple_out in updated for member in triple_out)
    )


def solution(mesh):
    return jax.shard_map(
        body,
        mesh=mesh,
        in_specs=(
            P(("dp", "tensor"), None),
            P(("dp", "tensor"), None),
            P(("dp", "tensor"), None),
            P(("dp", "tensor")),
            P(None, ("dp", "tensor"), None),
            P(None, ("dp", "tensor"), None),
            P(None, ("dp", "tensor"), None),
            P(None, ("dp", "tensor"), None),
            P(None, ("dp", "tensor"), None),
            P(None, ("dp", "tensor"), None),
            P(None, ("dp", "tensor"), None),
            P(None, ("dp", "tensor"), None),
            P(None, ("dp", "tensor"), None),
            P(("dp", "tensor"), None),
            P(("dp", "tensor"), None),
            P(("dp", "tensor"), None),
            P(("dp", "tensor")),
            P(("dp", "tensor")),
            P(("dp", "tensor")),
            P("dp", None, "tensor"),
            P("dp", None, "tensor"),
            P("dp", None, "tensor"),
            P("tensor", "dp"),
            P("tensor", "dp"),
            P("tensor", "dp"),
            P("dp", None, "tensor"),
            P("dp", None, "tensor"),
            P("dp", None, "tensor"),
            P("tensor", "dp"),
            P("tensor", "dp"),
            P("tensor", "dp"),
        ),
        out_specs=(
            P(),
            P(),
            P(),
            P(None, ("dp", "tensor"), None),
            P(None, ("dp", "tensor"), None),
            P(None, ("dp", "tensor"), None),
            P(None, ("dp", "tensor"), None),
            P(None, ("dp", "tensor"), None),
            P(None, ("dp", "tensor"), None),
            P(None, ("dp", "tensor"), None),
            P(None, ("dp", "tensor"), None),
            P(None, ("dp", "tensor"), None),
            P(("dp", "tensor"), None),
            P(("dp", "tensor"), None),
            P(("dp", "tensor"), None),
            P(("dp", "tensor")),
            P(("dp", "tensor")),
            P(("dp", "tensor")),
            P("dp", None, "tensor"),
            P("dp", None, "tensor"),
            P("dp", None, "tensor"),
            P("tensor", "dp"),
            P("tensor", "dp"),
            P("tensor", "dp"),
            P("dp", None, "tensor"),
            P("dp", None, "tensor"),
            P("dp", None, "tensor"),
            P("tensor", "dp"),
            P("tensor", "dp"),
            P("tensor", "dp"),
        ),
        check_vma=False,
    )
```

```python
from functools import partial

import jax
import jax.numpy as jnp
from jax import lax
from jax.experimental import pallas as pl
from jax.experimental.pallas import tpu as pltpu
from jax.sharding import PartitionSpec as P

BYTE_WIDTH = 1024
CORE_WIDTH = 1536
VOCAB = 256
STATE = 128
HEADDIM = 64
STEP = 10
INNER = 2048
MHEADS = 32
HD = 96
MAX_PIECES = 128


deepest_tier = lax.Precision.HIGHEST
norm_eps = 1e-05
ssd_block = 128
beta_one = 0.9
beta_two = 0.95
adam_eps = 1e-08
weight_decay = 0.1
max_norm = 0.01
rate_byte = 0.06
rate_main = 0.05
rate_small = 0.5


def root_mean_rescale(value_entries, gain_vec):
    return (
        value_entries
        * lax.rsqrt(jnp.mean(value_entries * value_entries, axis=-1, keepdims=True) + norm_eps)
        * gain_vec
    )


def softplus(value_entries):
    return jnp.log1p(jnp.exp(value_entries))


def unpack_small(vector):
    extents = [
        2 * BYTE_WIDTH,
        2 * INNER,
        3 * CORE_WIDTH,
        BYTE_WIDTH,
        CORE_WIDTH - BYTE_WIDTH,
        8 * (INNER + 2 * STATE),
        2 * INNER,
        2 * MHEADS,
        2 * MHEADS,
    ]
    pieces = []
    offset = 0
    for extent in extents:
        pieces.append(vector[offset : offset + extent])
        offset += extent
    return (
        pieces[0].reshape(2, BYTE_WIDTH),
        pieces[1].reshape(2, INNER),
        pieces[2].reshape(3, CORE_WIDTH),
        pieces[3],
        pieces[4],
        pieces[5].reshape(2, 4, INNER + 2 * STATE),
        pieces[6].reshape(2, INNER),
        pieces[7].reshape(2, MHEADS),
        pieces[8].reshape(2, MHEADS),
    )


def route_prob(queries, key_rows):
    unit_query = queries * lax.rsqrt(jnp.sum(queries * queries, axis=-1, keepdims=True) + 1e-06)
    unit_key = key_rows * lax.rsqrt(jnp.sum(key_rows * key_rows, axis=-1, keepdims=True) + 1e-06)
    cosine = jnp.sum(unit_query[1:] * unit_key[:-1], axis=-1)
    return jnp.concatenate([jnp.ones((1,), jnp.float32), 0.5 * (1.0 - cosine)])


def span_maps(cut_marks):
    owner_slot = jnp.cumsum(cut_marks) - 1
    position_labels = jnp.arange(MAX_PIECES, dtype=jnp.int32)
    broadcast_back = (owner_slot[:, None] == position_labels[None, :]).astype(jnp.float32)
    select_items = broadcast_back.T * cut_marks[None, :].astype(jnp.float32)
    return (select_items, broadcast_back)


def merge_into_pieces(select_items, value_entries, blank_row):
    spans = jnp.dot(select_items, value_entries, precision=deepest_tier)
    return jnp.concatenate(
        [spans, jnp.broadcast_to(blank_row, (MAX_PIECES, CORE_WIDTH - BYTE_WIDTH))], axis=1
    )


def decay_products(confidence):
    rows = lax.broadcasted_iota(jnp.int32, (MAX_PIECES, MAX_PIECES), 0)
    columns = lax.broadcasted_iota(jnp.int32, (MAX_PIECES, MAX_PIECES), 1)
    products = jnp.where(rows > columns, 1.0 - confidence[:, None], 1.0)
    reach = 1
    while reach < MAX_PIECES:
        shifted = jnp.concatenate(
            [jnp.ones((reach, MAX_PIECES), jnp.float32), products[:-reach]], axis=0
        )
        products = products * shifted
        reach *= 2
    return jnp.where(rows >= columns, products, 0.0)


@jax.custom_vjp
def smooth_spans(piece_output, confidence):
    products = decay_products(confidence)
    return jnp.dot(products, confidence[:, None] * piece_output, precision=deepest_tier)


def smooth_keep(piece_output, confidence):
    products = decay_products(confidence)
    smoothed = jnp.dot(products, confidence[:, None] * piece_output, precision=deepest_tier)
    return smoothed, (piece_output, confidence, products, smoothed)


def smooth_pull(kept, slope):
    piece_output, confidence, products, smoothed = kept
    spread = lax.dot_general(
        products, slope, (((0,), (0,)), ((), ())), precision=deepest_tier
    )
    before = jnp.concatenate([jnp.zeros((1, smoothed.shape[1]), jnp.float32), smoothed[:-1]], axis=0)
    return (confidence[:, None] * spread, jnp.sum(spread * (piece_output - before), axis=-1))


smooth_spans.defvjp(smooth_keep, smooth_pull)


def link_layers(
    select_items,
    broadcast_back,
    cut_marks,
    latent_holder,
    closing_scale,
    cut_likelihood,
    shortcut_sum,
):
    piece_output = root_mean_rescale(latent_holder, closing_scale)[:, :BYTE_WIDTH]
    smoothed = smooth_spans(
        piece_output, jnp.dot(select_items, cut_likelihood, precision=deepest_tier)
    )
    confidence = jnp.where(cut_marks == 1, cut_likelihood, 1.0 - cut_likelihood)
    return shortcut_sum + confidence[:, None] * jnp.dot(
        broadcast_back, smoothed, precision=deepest_tier
    )


def adam_step(weight, grad, first, second, rate, decay):
    first_new = beta_one * first + (1.0 - beta_one) * grad
    second_new = beta_two * second + (1.0 - beta_two) * grad * grad
    ratio = (
        first_new
        / (1.0 - beta_one**STEP)
        / (jnp.sqrt(second_new / (1.0 - beta_two**STEP)) + adam_eps)
    )
    return (first_new, second_new, weight - rate * (ratio + decay * weight))


def lift_kernel(clip, gate, up, weight, first, second, *outputs):
    for side, grad in enumerate((gate, up)):
        updated = adam_step(
            weight[:, side, :],
            clip[0, 0] * grad[...],
            first[:, side, :],
            second[:, side, :],
            rate_main,
            weight_decay,
        )
        for output, value_entries in zip(outputs, updated):
            output[:, side, :] = value_entries


def lift_step(clip_factor, gate, up, weight, first, second):
    rows, columns = gate.shape
    block = 48 if rows % 48 == 0 else rows
    flat = pl.BlockSpec((block, columns), lambda part: (part, 0))
    paired = pl.BlockSpec((block, 2, columns), lambda part: (part, 0, 0))
    return pl.pallas_call(
        lift_kernel,
        grid=(rows // block,),
        out_shape=(jax.ShapeDtypeStruct(weight.shape, jnp.float32),) * 3,
        in_specs=[pl.BlockSpec(memory_space=pltpu.SMEM), flat, flat, paired, paired, paired],
        out_specs=(paired,) * 3,
        compiler_params=pltpu.CompilerParams(vmem_limit_bytes=32 * 2**20),
    )(clip_factor.reshape(1, 1), gate, up, weight, first, second)


def to_low(value_entries):
    return value_entries.astype(jnp.bfloat16)


def matmul_apply(left, right):
    return jnp.dot(left, right, preferred_element_type=jnp.float32)


def product_tn(left, right):
    return lax.dot_general(
        left, right, (((0,), (0,)), ((), ())), preferred_element_type=jnp.float32
    )


def product_nt(left, right):
    return lax.dot_general(
        left, right, (((1,), (1,)), ((), ())), preferred_element_type=jnp.float32
    )


def swap(value_entries, axis, mask):
    size = lax.axis_size(axis)
    return lax.ppermute(value_entries, axis, [(place, place ^ mask) for place in range(size)])


def bit_masks(size):
    masks = []
    mask = 1
    while mask < size:
        masks.append(mask)
        mask *= 2
    return masks


def after(value_entries, earlier):
    if not earlier:
        return value_entries
    return lax.optimization_barrier((value_entries,) + tuple(earlier))[0]


def spread_masks(over_tensor):
    dp_masks = bit_masks(lax.axis_size("dp"))
    masks = [("dp", mask) for mask in dp_masks[1:] + dp_masks[:1]]
    if over_tensor:
        masks += [("tensor", mask) for mask in reversed(bit_masks(lax.axis_size("tensor")))]
    return masks


class Summing:
    def __init__(self, grad, over_tensor):
        self.masks = list(reversed(spread_masks(over_tensor)))
        names = [("dp", mask) for mask in reversed(bit_masks(lax.axis_size("dp")))]
        if over_tensor:
            names += [("tensor", mask) for mask in reversed(bit_masks(lax.axis_size("tensor")))]
        self.names = names
        rows = grad.shape[0] // 2 ** len(names)
        self.addends = [(grad.reshape((2,) * len(names) + (rows,) + grad.shape[1:]), names)]
        self.pending = None

    def picked(self, other=None, token=None):
        result = []
        for array, names in self.addends:
            if token is not None:
                array = after(array, [token])
            for position in reversed(range(len(names))):
                axis, mask = names[position]
                own = (lax.axis_index(axis) // mask) % 2
                if names[position] == other:
                    array = take(array, position, 1 - own)
                elif names[position] not in self.names:
                    array = take(array, position, own)
            result.append(array)
        return result

    def operand(self):
        return to_low(total(self.picked(self.masks[0])))

    def accept(self):
        self.names = [name for name in self.names if name != self.masks[0]]
        self.masks = self.masks[1:]
        self.addends.append((self.pending, self.names))
        self.pending = None

    def begun_last(self):
        left = [mask for axis, mask in self.masks if axis == "dp" and mask > 1]
        return 0 < len(left) == len(self.masks) < len(bit_masks(lax.axis_size("dp"))) - 1

    def rest(self, token):
        kind = []
        for axis, mask in self.masks:
            if lane_name(axis, mask) not in kind:
                kind.append(lane_name(axis, mask))
        if len(self.addends) == 1 or kind[0] in ("core", "y"):
            array = self.addends[0][0]
            if len(self.addends) > 1:
                array = to_low(total(self.picked(token=token)))
            return [(array, tuple(name for name in BYTE_LANES if name in kind))], tuple(kind)
        arrays = []
        for array, names in self.addends:
            lanes_here = {lane_name(axis, mask) for axis, mask in names}
            arrays.append((array, tuple(name for name in BYTE_LANES if name in lanes_here)))
        return arrays, tuple(kind)

    def result(self, token=None):
        return total(self.picked(token=token))


def lane_name(axis, mask):
    if axis == "tensor":
        return ("core", "y")[mask - 1]
    return "x" if mask == 1 else "z"


def sum_slowly(job):
    while job.masks:
        axis, mask = job.masks[0]
        job.pending = swap(job.operand(), axis, mask)
        job.accept()
    return job.result()


class Conductor:
    def __init__(self):
        self.clock = 0.0
        self.jobs = []
        self.flights = []

    def add(self, job):
        self.jobs.append(job)
        return job

    def lane(self, job):
        axis, mask = job.masks[0]
        return (axis, mask if axis == "tensor" else min(mask, 2))

    def launch(self, limit, banned, value_entries):
        operands = []
        for job in self.jobs:
            if len(self.flights) >= limit:
                break
            if job.pending is not None or not job.masks:
                continue
            lane = self.lane(job)
            depth = {("dp", 1): 3, ("tensor", 1): 2}.get(lane, 1)
            if lane in banned or sum(flight[1] == lane for flight in self.flights) >= depth:
                continue
            axis, mask = job.masks[0]
            operand = job.operand()
            rate = 3.4 if (axis, mask) == ("tensor", 1) else 25.3
            if axis == "dp" and mask > 2:
                rate = 50.0
            operand = after(operand, [value_entries])
            operands.append(operand)
            job.pending = swap(operand, axis, mask)
            start = max([self.clock] + [flight[0] - 6.0 for flight in self.flights if flight[1] == lane])
            self.flights.append((start + 6.0 + rate * operand.size * 2e-6, lane, job))
        return after(value_entries, operands)

    def tick(self, value_entries, elapsed, banned=(), limit=5):
        self.clock += elapsed
        ended = [flight for flight in self.flights if flight[0] <= self.clock]
        if ended:
            value_entries = after(value_entries, [flight[2].pending for flight in ended])
            self.flights = [flight for flight in self.flights if flight[0] > self.clock]
            for flight in ended:
                flight[2].accept()
        return self.launch(limit, banned, value_entries)

    def close(self):
        for _, _, job in sorted(self.flights, key=lambda flight: flight[0]):
            job.accept()
        self.flights = []
        for job in self.jobs:
            while job.begun_last():
                axis, mask = job.masks[0]
                job.pending = swap(job.operand(), axis, mask)
                job.accept()


def flip(place, mask):
    result = place
    bit = 1
    while bit <= mask:
        if mask & bit:
            result = result + bit * (1 - 2 * ((place // bit) % 2))
        bit *= 2
    return result


def order_steps(jobs, depth=2):
    free, busy, flights, plan = {}, {}, [], []
    waiting = [0] * len(jobs)
    clock = 0.0
    while True:
        for job, steps in enumerate(jobs):
            step = waiting[job]
            if step < 0 or step >= len(steps):
                continue
            lane, cost = steps[step]
            if busy.get(lane, 0) >= depth:
                continue
            busy[lane] = busy.get(lane, 0) + 1
            free[lane] = max(free.get(lane, 0.0), clock) + cost
            flights.append((free[lane] + 1.5, job, step, lane))
            plan.append(("start", job, step))
            waiting[job] = -1 - step
        if not flights:
            return plan
        flight = min(flights)
        flights.remove(flight)
        clock, job, step, lane = flight
        busy[lane] -= 1
        plan.append(("wait", job, step))
        waiting[job] = step + 1


def link_cost(lane, elements):
    return elements * 2e-6 * {"core": 3.4, "y": 23.0, "x": 23.0, "z": 46.0}[lane]


def here():
    dp_place, tensor_place = lax.axis_index("dp"), lax.axis_index("tensor")
    return dp_place // 2, dp_place % 2, tensor_place // 2, tensor_place % 2


def partner(lane, mask, coordinates):
    z, x, y, core = coordinates
    if lane == "z":
        z = flip(z, mask)
    if lane == "x":
        x = 1 - x
    if lane == "y":
        y = 1 - y
    if lane == "core":
        core = 1 - core
    return (z * 2 + x, y * 2 + core)


def greet(line, depth_z, coordinates):
    z = coordinates[0]
    barrier = pltpu.get_barrier_semaphore()

    def tell(device):
        pl.semaphore_signal(
            barrier, inc=1, device_id=device, device_id_type=pl.DeviceIdType.MESH
        )

    if not line:
        others = peers("tensor", 4) + peers("dp", 2 * depth_z)
        for device in others:
            tell(device)
        pl.semaphore_wait(barrier, len(others))
        return

    for lane in ("x", "y", "core"):
        tell(partner(lane, 1, coordinates))

    @pl.when(z > 0)
    def _():
        tell(beside(-1, coordinates))

    @pl.when(z < depth_z - 1)
    def _():
        tell(beside(1, coordinates))

    ends = (z == 0).astype(jnp.int32) + (z == depth_z - 1).astype(jnp.int32)
    pl.semaphore_wait(barrier, 5 - ends)


def peers(axis, size):
    dp_place, tensor_place = lax.axis_index("dp"), lax.axis_index("tensor")
    if axis == "dp":
        return [(flip(dp_place, mask), tensor_place) for mask in range(1, size)]
    return [(dp_place, flip(tensor_place, mask)) for mask in range(1, size)]


def beside(way, coordinates):
    z, x, y, core = coordinates
    return ((z + way) * 2 + x, y * 2 + core)


def spread_kernel(plan, jobs, depth_z, *refs):
    count = (len(refs) - 3) // 2
    shards, wholes = refs[:count], refs[count : 2 * count]
    send_sems, receive_sems, own_sems = refs[2 * count :]
    coordinates = here()
    z = coordinates[0]
    greet(True, depth_z, coordinates)

    def spot(job, free, z_place):
        array, kind, first, size = jobs[job]
        index = [
            slice(None) if name in free else (z_place if name == "z" else place)
            for name, place in zip(("z", "x", "y", "core"), coordinates)
            if name in kind
        ]
        return wholes[array].at[tuple(index) + (slice(None), pl.ds(first, size))]

    def shard(job):
        array, _, first, size = jobs[job]
        return shards[array].at[:, pl.ds(first, size)]

    own = []
    for job in range(len(jobs)):
        own.append(pltpu.make_async_copy(shard(job), spot(job, (), z), own_sems.at[job]))
        own[-1].start()

    def copies(job, step, receiving):
        steps = lanes_of(jobs[job][1], depth_z)
        lane, reach = steps[step]
        free = [name for name, _ in steps[:step] if name != lane]
        base = job * (2 * depth_z + 1)
        pairs = []
        if lane == "z":
            for side, way in enumerate((1, -1)):
                number = base + 2 * (reach - 1) + side
                if receiving:
                    block = z - way * reach
                    condition = (block >= 0) & (block < depth_z)
                    target = spot(job, free, z if step == 0 else block)
                    source = target
                else:
                    block = z - way * (reach - 1)
                    condition = (block >= 0) & (block < depth_z)
                    condition &= (z + way >= 0) & (z + way < depth_z)
                    target = spot(job, free, block)
                    source = shard(job) if step == 0 else target
                copy = pltpu.make_async_remote_copy(
                    src_ref=source,
                    dst_ref=target,
                    send_sem=send_sems.at[number],
                    recv_sem=receive_sems.at[number],
                    device_id=beside(way, coordinates),
                    device_id_type=pl.DeviceIdType.MESH,
                )
                pairs.append((condition, copy))
            return pairs
        number = base + 2 * (depth_z - 1) + ("x", "y", "core").index(lane)
        target = spot(job, free, z)
        copy = pltpu.make_async_remote_copy(
            src_ref=shard(job) if step == 0 else target,
            dst_ref=target,
            send_sem=send_sems.at[number],
            recv_sem=receive_sems.at[number],
            device_id=partner(lane, 1, coordinates),
            device_id_type=pl.DeviceIdType.MESH,
        )
        return [(None, copy)]

    def perform(pairs, action):
        for condition, copy in pairs:
            if condition is None:
                getattr(copy, action)()
            else:
                pl.when(condition)(getattr(copy, action))

    copied = set()
    for action, job, step in plan:
        steps = lanes_of(jobs[job][1], depth_z)
        if action == "start":
            if steps[step][0] != steps[0][0] and job not in copied:
                own[job].wait()
                copied.add(job)
            perform(copies(job, step, False), "start")
        else:
            perform(copies(job, step, True), "wait_recv")
    for action, job, step in plan:
        if action == "start":
            perform(copies(job, step, False), "wait_send")


def lanes_of(kind, depth_z):
    steps = []
    for name in kind:
        steps += [(name, reach) for reach in range(1, depth_z if name == "z" else 2)]
    return steps


def spread_whole(shards, jobs, collective_id):
    depth_z = lax.axis_size("dp") // 2
    costs = []
    for array, kind, first, size in jobs:
        held, steps = shards[array].shape[0] * size, []
        for lane in kind:
            cost = 23.0 if lane != "core" else 3.4
            steps += [(lane, held * 2e-6 * cost)] * (depth_z - 1 if lane == "z" else 1)
            held *= depth_z if lane == "z" else 2
        costs.append(steps)
    plan = order_steps(costs)
    sizes = {"z": depth_z, "x": 2, "y": 2, "core": 2}
    kinds = {array: kind for array, kind, _, _ in jobs}
    shapes = [
        tuple(sizes[name] for name in ("z", "x", "y", "core") if name in kinds[array])
        + shard.shape
        for array, shard in enumerate(shards)
    ]
    numbers = len(jobs) * (2 * depth_z + 1)
    wholes = pl.pallas_call(
        partial(spread_kernel, plan, jobs, depth_z),
        out_shape=tuple(jax.ShapeDtypeStruct(shape, jnp.bfloat16) for shape in shapes),
        in_specs=[pl.BlockSpec(memory_space=pltpu.VMEM)] * len(shards),
        out_specs=(pl.BlockSpec(memory_space=pl.ANY),) * len(shards),
        scratch_shapes=[
            pltpu.SemaphoreType.DMA((numbers,)),
            pltpu.SemaphoreType.DMA((numbers,)),
            pltpu.SemaphoreType.DMA((len(jobs),)),
        ],
        compiler_params=pltpu.CompilerParams(
            collective_id=collective_id, has_side_effects=True, vmem_limit_bytes=60 * 2**20
        ),
    )(*shards)
    return [whole.reshape(-1, whole.shape[-1]) for whole in wholes]


BYTE_LANES = ("z", "x", "y", "core")
MAIN_LANES = ("z", "x")


def sum_kernel(plan, kinds, sources, depth_z, *refs):
    count = len(kinds)
    pieces_in = [[refs[number] for number, _ in parts] for parts in sources]
    total_in = sum(len(parts) for parts in sources)
    grads, extra = [parts[0] for parts in pieces_in], refs[total_in]
    outputs = refs[total_in + 1 : total_in + 1 + count]
    totals = refs[total_in + 1 + count]
    rest = list(refs[total_in + 2 + count :])
    coordinates = here()
    places = dict(zip(BYTE_LANES, coordinates))
    z = coordinates[0]
    mirrored = depth_z - 1 - z
    held, received, held_names, temporary = [], [], [], {}
    for job, kind in enumerate(kinds):
        held.append(rest.pop(0))
        received.append({lane: rest.pop(0) for lane in kind})
        held_names.append(names_held(kind, len(sources[job])))
    for key in temporary_shapes(kinds, sources, [ref.shape for ref in held]):
        temporary[key] = rest.pop(0)
    squares, arrivals, send_sems, receive_sems, own_sems, tile_sems = rest

    def slice_of(job, part):
        names = sources[job][part][1]
        spot = tuple(slice(None) if name in held_names[job] else places[name] for name in names)
        return pieces_in[job][part].at[spot]

    loads = []
    for job in range(count):
        loads.append(pltpu.make_async_copy(slice_of(job, 0), held[job], own_sems.at[job]))
        loads[-1].start()
    squares[...] = jnp.zeros_like(squares)
    greet(False, depth_z, coordinates)

    def prepare(job):
        loads[job].wait()
        for part in range(1, len(sources[job])):
            buffer = temporary[held[job].shape]
            copy = pltpu.make_async_copy(slice_of(job, part), buffer, own_sems.at[job])
            copy.start()
            copy.wait()
            lead, rows = held[job].shape[:-2], held[job].shape[-2]
            pieces = 1
            for size in lead:
                pieces *= size

            def piece(index, carry, buffer=buffer, lead=lead, rows=rows):
                spot, remainder = [], index
                for size in reversed(lead):
                    spot.insert(0, remainder % size)
                    remainder = remainder // size
                target, other = held[job].at[tuple(spot)], buffer.at[tuple(spot)]

                def row_step(number, inner):
                    part_rows = pl.ds(pl.multiple_of(number * 16, 16), 16)
                    target[part_rows, :] = to_low(
                        target[part_rows, :].astype(jnp.float32)
                        + other[part_rows, :].astype(jnp.float32)
                    )
                    return inner

                lax.fori_loop(0, rows // 16, row_step, 0)
                return carry

            lax.fori_loop(0, pieces, piece, 0)

    def chosen(job, step, lane_place):
        steps = lanes_of(kinds[job], depth_z)
        lane = steps[step][0]
        done = [name for name, _ in steps[:step] if name != lane]
        return [
            lane_place if name == lane else (places[name] if name in done else slice(None))
            for name in held_names[job]
        ]

    def slot(reach, side):
        shared = (depth_z - 2) // 2
        return reach - 1 if reach <= shared else shared + 2 * (reach - 1 - shared) + side

    def copies(job, step, receiving):
        kind = kinds[job]
        lane, reach = lanes_of(kind, depth_z)[step]
        base = job * (2 * depth_z + 1)
        if lane == "z":
            pairs = []
            for side, depth in enumerate((z, mirrored)):
                way = 1 - 2 * side
                aim = depth_z - reach + depth
                if side:
                    aim = depth_z - 1 - aim
                landing = received[job]["z"].at[slot(reach, side)]
                number = base + 2 * (reach - 1) + side
                source = landing if receiving else held[job].at[tuple(chosen(job, step, aim))]
                copy = pltpu.make_async_remote_copy(
                    src_ref=source,
                    dst_ref=landing,
                    send_sem=send_sems.at[number],
                    recv_sem=receive_sems.at[number],
                    device_id=beside(way, coordinates),
                    device_id_type=pl.DeviceIdType.MESH,
                )
                condition = (depth >= 1) & (depth <= reach) if receiving else depth <= reach - 1
                pairs.append((condition, copy))
            return pairs
        number = base + 2 * (depth_z - 1) + ("x", "y", "core").index(lane)
        if step == 0 and len(sources[job]) == 1:
            spot = tuple(
                1 - places[name] if name == lane else slice(None)
                for name in BYTE_LANES
                if name in kind
            )
            source = grads[job].at[spot]
        else:
            source = held[job].at[tuple(chosen(job, step, 1 - places[lane]))]
        copy = pltpu.make_async_remote_copy(
            src_ref=source,
            dst_ref=received[job][lane],
            send_sem=send_sems.at[number],
            recv_sem=receive_sems.at[number],
            device_id=partner(lane, 1, coordinates),
            device_id_type=pl.DeviceIdType.MESH,
        )
        return [(None, copy)]

    def add_pieces(job, step, lane_place, buffers, last):
        steps = lanes_of(kinds[job], depth_z)
        lane = steps[step][0]
        done = [name for name, _ in steps[:step] if name != lane]
        free = [name for name in BYTE_LANES if name in kinds[job] and name not in done + [lane]]
        sizes = [depth_z if name == "z" else 2 for name in free]
        pieces = 1
        for size in sizes:
            pieces *= size

        def piece(index, carry):
            spots, remainder = {}, index
            for name, size in reversed(list(zip(free, sizes))):
                spots[name] = remainder % size
                remainder = remainder // size
            mine = tuple(
                spots[name] if name in spots else (lane_place if name == lane else places[name])
                for name in held_names[job]
            )
            theirs = tuple(spots[name] for name in free)
            target = held[job].at[mine] if mine else held[job]
            arrived = [buffer.at[theirs] if theirs else buffer for buffer in buffers]
            rows, columns = target.shape[-2:]

            def row_step(number, inner):
                part = pl.ds(pl.multiple_of(number * 16, 16), 16)
                value = target[part, :].astype(jnp.float32)
                for other in arrived:
                    value = value + other[part, :].astype(jnp.float32)
                if last:
                    outputs[job][part, :] = value
                    square = jnp.zeros((16, 128), jnp.float32)
                    for first in range(0, columns, 128):
                        square = square + value[:, first : first + 128] * value[:, first : first + 128]
                    squares[...] += square
                else:
                    target[part, :] = to_low(value)
                return inner

            lax.fori_loop(0, rows // 16, row_step, 0)
            return carry

        if pieces == 1:
            piece(0, 0)
        else:
            lax.fori_loop(0, pieces, piece, 0)

    def accumulate(job, step):
        steps = lanes_of(kinds[job], depth_z)
        lane, reach = steps[step]
        last = step == len(steps) - 1
        if lane != "z":
            add_pieces(job, step, places[lane], [received[job][lane]], last)
            return
        buffers = [received[job]["z"].at[slot(reach, side)] for side in range(2)]
        if reach < depth_z - 1:
            for side, depth in enumerate((z, mirrored)):
                aim = depth_z - reach + depth - 1
                if side:
                    aim = depth_z - 1 - aim
                pl.when((depth >= 1) & (depth <= reach))(
                    partial(add_pieces, job, step, aim, [buffers[side]], False)
                )
            return
        ends = (z == 0) | (mirrored == 0)
        pl.when(jnp.logical_not(ends))(partial(add_pieces, job, step, z, buffers, last))
        pl.when(z == 0)(partial(add_pieces, job, step, z, buffers[1:], last))
        pl.when(mirrored == 0)(partial(add_pieces, job, step, z, buffers[:1], last))

    def perform(pairs, action):
        for condition, copy in pairs:
            if condition is None:
                getattr(copy, action)()
            else:
                pl.when(condition)(getattr(copy, action))

    loaded = set()
    for action, job, step in plan:
        lane = lanes_of(kinds[job], depth_z)[step][0]
        if job not in loaded and (action == "wait" or lane == "z" or len(sources[job]) > 1):
            prepare(job)
            loaded.add(job)
        if action == "start":
            perform(copies(job, step, False), "start")
        else:
            perform(copies(job, step, True), "wait_recv")
            accumulate(job, step)
    totals[...] = extra[...]
    totals[0:8, :] += squares[0:8, :] + squares[8:16, :]
    tiles = []
    for axis, size, first in (("tensor", 4, 0), ("dp", 2 * depth_z, 4)):
        spot = first + lax.axis_index(axis)
        arrivals[spot] = totals[...]
        for mask, device in enumerate(peers(axis, size), 1):
            tiles.append(
                pltpu.make_async_remote_copy(
                    src_ref=arrivals.at[spot],
                    dst_ref=arrivals.at[spot],
                    send_sem=tile_sems.at[2 * (first + mask)],
                    recv_sem=tile_sems.at[2 * (first + mask) + 1],
                    device_id=device,
                    device_id_type=pl.DeviceIdType.MESH,
                )
            )
            tiles[-1].start()
        for copy in tiles[1 - size :]:
            copy.wait_recv()
        result = arrivals[first]
        for place in range(1, size):
            result = result + arrivals[first + place]
        totals[...] = result
    for copy in tiles:
        copy.wait_send()
    for action, job, step in plan:
        if action == "start":
            perform(copies(job, step, False), "wait_send")


def names_held(kind, addends):
    return [
        name
        for name in BYTE_LANES
        if name in kind and (name == "z" or addends > 1 or name != kind[0])
    ]


def temporary_shapes(kinds, sources, shapes):
    return list(
        dict.fromkeys(
            tuple(shape) for shape, parts in zip(shapes, sources) if len(parts) > 1
        )
    )


def sum_whole(grads, kinds, extra, collective_id):
    depth_z = lax.axis_size("dp") // 2
    sizes = {"z": depth_z, "x": 2, "y": 2, "core": 2}
    jobs, arrays, shapes, scratch, sources, held_shapes = [], [], [], [], [], []
    for parts, kind in zip(grads, kinds):
        sources.append([])
        for array, names in parts:
            piece = array.shape[-2:]
            lead = tuple(sizes[name] for name in names)
            if array.ndim == 2:
                pieces = 1
                for size in lead:
                    pieces *= size
                piece = (array.shape[0] // pieces, array.shape[1])
            sources[-1].append((len(arrays), names))
            arrays.append(array.reshape(lead + piece))
        shapes.append(jax.ShapeDtypeStruct(piece, jnp.float32))
        steps, left = [], [name for name in BYTE_LANES if name in kind]
        held_shapes.append(tuple(sizes[name] for name in names_held(kind, len(parts))) + piece)
        scratch.append(pltpu.VMEM(held_shapes[-1], jnp.bfloat16))
        for lane in kind:
            left.remove(lane)
            rest = tuple(sizes[name] for name in left)
            extent = piece[0] * piece[1]
            for size in rest:
                extent *= size
            cost = 23.0 if lane != "core" else 3.4
            steps += [(lane, extent * 2e-6 * cost)] * (depth_z - 1 if lane == "z" else 1)
            lead = (2 * (depth_z - 1) - (depth_z - 2) // 2,) if lane == "z" else ()
            scratch.append(pltpu.VMEM(lead + rest + piece, jnp.bfloat16))
        jobs.append(steps)
    scratch += [
        pltpu.VMEM(shape, jnp.bfloat16)
        for shape in temporary_shapes(kinds, sources, held_shapes)
    ]
    plan = order_steps(jobs)
    numbers = len(grads) * (2 * depth_z + 1)
    tile = jax.ShapeDtypeStruct(extra.shape, jnp.float32)
    places = 4 + 2 * depth_z
    return pl.pallas_call(
        partial(sum_kernel, plan, kinds, sources, depth_z),
        out_shape=tuple(shapes) + (tile,),
        in_specs=[pl.BlockSpec(memory_space=pl.ANY)] * len(arrays)
        + [pl.BlockSpec(memory_space=pltpu.VMEM)],
        out_specs=(pl.BlockSpec(memory_space=pltpu.VMEM),) * (len(grads) + 1),
        scratch_shapes=scratch
        + [
            pltpu.VMEM((16, 128), jnp.float32),
            pltpu.VMEM((places, 16, 128), jnp.float32),
            pltpu.SemaphoreType.DMA((numbers,)),
            pltpu.SemaphoreType.DMA((numbers,)),
            pltpu.SemaphoreType.DMA((len(grads),)),
            pltpu.SemaphoreType.DMA((2 * places,)),
        ],
        compiler_params=pltpu.CompilerParams(
            collective_id=collective_id, has_side_effects=True, vmem_limit_bytes=60 * 2**20
        ),
    )(*arrays, extra)


def take(value_entries, axis, index):
    return lax.dynamic_index_in_dim(value_entries, index, axis, keepdims=False)


def total(addends):
    result = addends[0].astype(jnp.float32)
    for addend in addends[1:]:
        result = result + addend.astype(jnp.float32)
    return result


def add_everywhere(value_entries):
    for axis in ("tensor", "dp"):
        for mask in bit_masks(lax.axis_size(axis)):
            value_entries = value_entries + swap(value_entries, axis, mask)
    return value_entries


def gather_rows(value_entries):
    pieces = [value_entries]
    for mask in reversed(bit_masks(lax.axis_size("tensor"))):
        pieces = pieces + [swap(piece, "tensor", mask) for piece in pieces]
    return jnp.concatenate(pieces, axis=0)


def total_lines(value_entries):
    size = lax.axis_size("tensor")
    rows = value_entries.shape[0] // size
    pieces = [to_low(value_entries[i * rows : (i + 1) * rows]) for i in range(size)]
    for mask in bit_masks(size):
        half = len(pieces) // 2
        pieces = [
            pieces[i].astype(jnp.float32)
            + swap(to_low(pieces[half + i]), "tensor", mask).astype(jnp.float32)
            for i in range(half)
        ]
    return pieces[0]


gather_grads = gather_rows
sum_grads = total_lines


def low_dot(left, right, left_dim, right_dim):
    return lax.dot_general(
        left, right, (((left_dim,), (right_dim,)), ((), ())), preferred_element_type=jnp.float32
    )


def sigmoid(value_entries):
    return 0.5 * jnp.tanh(0.5 * value_entries) + 0.5


def fold_rows(value_entries):
    return jnp.sum(value_entries.reshape(-1, 8, value_entries.shape[1]), axis=0)


def lower_ones():
    rows = lax.broadcasted_iota(jnp.int32, (ssd_block, ssd_block), 0)
    columns = lax.broadcasted_iota(jnp.int32, (ssd_block, ssd_block), 1)
    return (rows >= columns).astype(jnp.float32)


FORWARD_UNROLL = 4
BACKWARD_UNROLL = 2
PROJ_WIDE = 2 * INNER + 2 * STATE + 128


def step_terms(raw_steps, decay_refs):
    shifted = raw_steps + decay_refs[1:2, :]
    steps = softplus(shifted)
    rates = -jnp.exp(decay_refs[0:1, :])
    cumulative = jnp.dot(
        lower_ones(), steps * rates, precision=deepest_tier, preferred_element_type=jnp.float32
    )
    return shifted, steps, rates, cumulative


def head_tables():
    chosen = to_low(jnp.arange(INNER)[:, None] // HEADDIM == jnp.arange(ssd_block)[None, :])
    later = jnp.where(
        jnp.arange(ssd_block)[:, None] >= jnp.arange(ssd_block)[None, :], 0.0, -1e30
    )
    return chosen, later


def first_head():
    return lax.broadcasted_iota(jnp.int32, (ssd_block, ssd_block), 1) < HEADDIM


def both_heads(value_entries):
    mask = first_head()
    zeros = jnp.zeros_like(value_entries)
    return jnp.concatenate(
        [jnp.where(mask, value_entries, zeros), jnp.where(mask, zeros, value_entries)], axis=0
    )


def spread_heads(steps, cumulative, turned, wide, narrow):
    blank = jnp.zeros((ssd_block, ssd_block - MHEADS), jnp.float32)
    turned[...] = jnp.concatenate([cumulative, blank], axis=1).T
    mask = first_head()

    def over_lanes(value_entries, head):
        return jnp.broadcast_to(value_entries[:, head : head + 1], (ssd_block, ssd_block))

    for head in range(MHEADS):
        wide[head] = over_lanes(cumulative, head)
    for pair in range(MHEADS // 2):
        narrow[:, pair * ssd_block : (pair + 1) * ssd_block] = jnp.where(
            mask, over_lanes(steps, 2 * pair), over_lanes(steps, 2 * pair + 1)
        )


def gaps_of(wide, turned, later, head):
    return jnp.exp((wide[head] - turned[pl.ds(head, 1), :]) + later[...])


def quad_cumulative(wide, quad):
    mask = first_head()
    return jnp.concatenate(
        [
            jnp.where(mask, wide[4 * quad], wide[4 * quad + 1]),
            jnp.where(mask, wide[4 * quad + 2], wide[4 * quad + 3]),
        ],
        axis=1,
    )


def quad_lanes(quad, first=0):
    return pl.ds(pl.multiple_of(quad * 2 * ssd_block + first, ssd_block), 2 * ssd_block)


def lanes(block):
    return pl.ds(pl.multiple_of(block * ssd_block, ssd_block), ssd_block)


def convolve(padded_ref, taps_ref, columns):
    result = taps_ref[0:1, columns] * padded_ref[5 : 5 + ssd_block, columns]
    for tap in range(1, 4):
        result = result + taps_ref[tap : tap + 1, columns] * padded_ref[
            5 + tap : 5 + tap + ssd_block, columns
        ]
    return result


def middle_kernel(
    projected,
    taps,
    skip,
    decay,
    gain,
    later,
    middle,
    outcome,
    starts,
    padded,
    turned,
    wide,
    narrow,
    state,
    gated,
):
    chunk = pl.program_id(0)
    streams_extent = INNER + 2 * STATE

    @pl.when(chunk == 0)
    def _():
        padded[0:8, :] = jnp.zeros((8, streams_extent), jnp.float32)
        state[...] = jnp.zeros_like(state)

    @pl.when(chunk > 0)
    def _():
        padded[0:8, :] = padded[ssd_block : ssd_block + 8, :]

    padded[8 : 8 + ssd_block, :] = projected[:, INNER : INNER + streams_extent]
    _, steps, _, cumulative = step_terms(
        projected[:, INNER + streams_extent : INNER + streams_extent + MHEADS], decay
    )
    spread_heads(steps, cumulative, turned, wide, narrow)

    def active(columns):
        convolved = convolve(padded, taps, columns)
        return convolved * sigmoid(convolved)

    in_map = active(pl.ds(INNER, STATE))
    in_low = to_low(in_map)
    in_turned = to_low(in_map.T)
    out_low = to_low(active(pl.ds(INNER + STATE, STATE)))
    affinity = low_dot(out_low, in_low, 1, 1)

    def quad_step(quad, square_sum):
        columns = quad_lanes(quad)
        inputs = active(columns)
        weighted = inputs * narrow[:, columns]
        weighted_low = to_low(weighted)
        within = []
        for pair in range(2):
            head = 4 * quad + 2 * pair
            mixing = jnp.concatenate(
                [
                    to_low(affinity * gaps_of(wide, turned, later, head)),
                    to_low(affinity * gaps_of(wide, turned, later, head + 1)),
                ],
                axis=1,
            )
            part = weighted_low[:, pair * ssd_block : (pair + 1) * ssd_block]
            within.append(low_dot(mixing, both_heads(part), 1, 0))
        within = jnp.concatenate(within, axis=1)
        cumulative_here = quad_cumulative(wide, quad)
        last = cumulative_here[ssd_block - 1 :, :]
        held = state[:, columns]
        starts[0, :, columns] = held
        across = jnp.exp(cumulative_here) * low_dot(out_low, to_low(held), 1, 0)
        to_end = to_low(weighted * jnp.exp(last - cumulative_here))
        state[:, columns] = jnp.exp(last) * held + low_dot(in_turned, to_end, 1, 0)
        result = within + across + inputs * skip[:, columns]
        outcome[:, columns] = result
        gate = projected[:, columns]
        product = result * (gate * sigmoid(gate))
        gated[:, columns] = product
        return square_sum + product * product

    square_sum = lax.fori_loop(
        0,
        INNER // (2 * ssd_block),
        quad_step,
        jnp.zeros((ssd_block, 2 * ssd_block), jnp.float32),
        unroll=FORWARD_UNROLL,
    )
    scale = lax.rsqrt(jnp.sum(square_sum, axis=1, keepdims=True) * (1.0 / INNER) + norm_eps)

    def scale_step(quad, carry):
        columns = quad_lanes(quad)
        middle[:, columns] = to_low(gated[:, columns] * scale * gain[:, columns])
        return carry

    lax.fori_loop(0, INNER // (2 * ssd_block), scale_step, 0, unroll=2)


def middle_slope_kernel(
    projected,
    earlier,
    outcome,
    starts,
    slope,
    taps,
    skip,
    decay,
    gain,
    chosen,
    later,
    slope_projected,
    slope_taps,
    slope_skip,
    slope_gain,
    slope_decay,
    padded,
    turned,
    wide,
    narrow,
    slope_state,
    slope_conv,
    slope_affinity,
    slope_maps,
    slope_cumulative,
    slope_steps,
):
    chunk = pl.num_programs(0) - 1 - pl.program_id(0)
    streams_extent = INNER + 2 * STATE
    quads = INNER // (2 * ssd_block)

    @pl.when(pl.program_id(0) == 0)
    def _():
        slope_state[...] = jnp.zeros_like(slope_state)
        slope_conv[ssd_block : ssd_block + 8, :] = jnp.zeros((8, streams_extent), jnp.float32)
        slope_taps[...] = jnp.zeros_like(slope_taps)
        slope_skip[...] = jnp.zeros_like(slope_skip)
        slope_gain[...] = jnp.zeros_like(slope_gain)
        slope_decay[...] = jnp.zeros_like(slope_decay)

    @pl.when(pl.program_id(0) > 0)
    def _():
        slope_conv[ssd_block : ssd_block + 8, :] = slope_conv[0:8, :]

    @pl.when(chunk == 0)
    def _():
        padded[0:8, :] = jnp.zeros((8, streams_extent), jnp.float32)

    @pl.when(chunk > 0)
    def _():
        padded[0:8, :] = earlier[:, INNER : INNER + streams_extent]

    padded[8 : 8 + ssd_block, :] = projected[:, INNER : INNER + streams_extent]
    slope_affinity[...] = jnp.zeros_like(slope_affinity)
    slope_maps[...] = jnp.zeros_like(slope_maps)
    slope_cumulative[...] = jnp.zeros_like(slope_cumulative)
    slope_steps[...] = jnp.zeros_like(slope_steps)
    shifted, steps, rates, cumulative = step_terms(
        projected[:, INNER + streams_extent : INNER + streams_extent + MHEADS], decay
    )
    spread_heads(steps, cumulative, turned, wide, narrow)

    def silu_pair(value_entries):
        share = sigmoid(value_entries)
        return value_entries * share, share * (1.0 + value_entries * (1.0 - share))

    def pull_convolved(columns, target_columns, slope_block):
        slope_conv[0:ssd_block, columns] = slope_block
        result = taps[3:4, columns] * slope_block
        for tap in range(3):
            reach = 3 - tap
            result = result + taps[tap : tap + 1, columns] * slope_conv[
                reach : reach + ssd_block, columns
            ]
        for tap in range(4):
            slope_taps[tap, :, columns] += fold_rows(
                slope_block * padded[5 + tap : 5 + tap + ssd_block, columns]
            )
        slope_projected[:, target_columns] = to_low(result)

    maps = (pl.ds(INNER, STATE), pl.ds(INNER + STATE, STATE))
    in_map, in_pull = silu_pair(convolve(padded, taps, maps[0]))
    out_map, out_pull = silu_pair(convolve(padded, taps, maps[1]))
    in_low, out_low, out_turned = to_low(in_map), to_low(out_map), to_low(out_map.T)
    affinity = low_dot(out_low, in_low, 1, 1)
    mask = first_head()

    def sums_step(quad, sums):
        columns = quad_lanes(quad)
        gate = projected[:, columns]
        product = outcome[:, columns] * (gate * sigmoid(gate))
        return (
            sums[0] + product * product,
            sums[1] + product * (slope[:, columns] * gain[:, columns]),
        )

    blank = jnp.zeros((ssd_block, 2 * ssd_block), jnp.float32)
    squares, crossed = lax.fori_loop(0, quads, sums_step, (blank, blank), unroll=2)
    scale = lax.rsqrt(jnp.sum(squares, axis=1, keepdims=True) * (1.0 / INNER) + norm_eps)
    pulled = scale * scale * scale * (jnp.sum(crossed, axis=1, keepdims=True) * (1.0 / INNER))

    def quad_step(quad, carry):
        columns = quad_lanes(quad)
        gate, total_here = projected[:, columns], outcome[:, columns]
        gate_value, gate_pull = silu_pair(gate)
        product = total_here * gate_value
        slope_here = slope[:, columns]
        slope_gain[:, columns] += fold_rows(slope_here * product * scale)
        slope_product = scale * (slope_here * gain[:, columns]) - product * pulled
        slope_out = slope_product * gate_value
        slope_projected[:, columns] = to_low(slope_product * total_here * gate_pull)
        inputs, inputs_pull = silu_pair(convolve(padded, taps, columns))
        slope_skip[:, columns] += fold_rows(slope_out * inputs)
        skip_here = skip[:, columns]
        scanned = total_here - inputs * skip_here
        steps_here = narrow[:, columns]
        weighted = inputs * steps_here
        weighted_low = to_low(weighted)
        slope_low = to_low(slope_out)
        slope_within = []
        for pair in range(2):
            head = 4 * quad + 2 * pair
            here_low = slope_low[:, pair * ssd_block : (pair + 1) * ssd_block]
            part = weighted_low[:, pair * ssd_block : (pair + 1) * ssd_block]
            slope_mixing = low_dot(here_low, both_heads(part), 1, 1)
            mixing = []
            for side in range(2):
                gaps = gaps_of(wide, turned, later, head + side)
                mixing.append(to_low(affinity * gaps))
                slope_affinity[...] += (
                    slope_mixing[:, side * ssd_block : (side + 1) * ssd_block] * gaps
                )
            turned_back = low_dot(jnp.concatenate(mixing, axis=1), here_low, 0, 0)
            slope_within.append(
                jnp.where(mask, turned_back[:ssd_block], turned_back[ssd_block:])
            )
        slope_within = jnp.concatenate(slope_within, axis=1)
        cumulative_here = quad_cumulative(wide, quad)
        last = cumulative_here[ssd_block - 1 :, :]
        decayed = jnp.exp(last)
        held = starts[0, :, columns]
        slope_across = to_low(slope_out * jnp.exp(cumulative_here))
        slope_maps[1] += low_dot(slope_across, to_low(held), 1, 1)
        carried_state = slope_state[:, columns]
        carried_low = to_low(carried_state)
        to_end = jnp.exp(last - cumulative_here)
        ending = to_low(weighted * to_end)
        slope_ending = low_dot(in_low, carried_low, 1, 0)
        slope_maps[0] += low_dot(ending, carried_low, 1, 1)
        slope_state[:, columns] = decayed * carried_state + low_dot(out_turned, slope_across, 1, 0)
        slope_weighted = slope_within + slope_ending * to_end
        ending_slope = slope_ending * ending.astype(jnp.float32)
        ends = jnp.sum(ending_slope, axis=0, keepdims=True) + decayed * jnp.sum(
            carried_state * held, axis=0, keepdims=True
        )
        rows = lax.broadcasted_iota(jnp.int32, (ssd_block, 2 * ssd_block), 0)
        slope_gathered = (
            slope_low.astype(jnp.float32) * scanned
            - weighted_low.astype(jnp.float32) * slope_within
            - ending_slope
            + jnp.where(rows == ssd_block - 1, ends, 0.0)
        )
        high = to_low(slope_gathered)
        rest = to_low(slope_gathered - high.astype(jnp.float32))
        parts = [high, rest, to_low(slope_weighted * inputs)]
        sums = low_dot(jnp.concatenate(parts, axis=0), chosen[columns, :], 1, 0)
        slope_cumulative[...] += sums[:ssd_block] + sums[ssd_block : 2 * ssd_block]
        slope_steps[...] += sums[2 * ssd_block :]
        slope_inputs = slope_out * skip_here + slope_weighted * steps_here
        pull_convolved(columns, quad_lanes(quad, INNER), slope_inputs * inputs_pull)
        return carry

    lax.fori_loop(0, quads, quad_step, 0, unroll=BACKWARD_UNROLL)
    affinity_low = to_low(slope_affinity[...])
    slope_in = slope_maps[0] + low_dot(affinity_low, out_low, 0, 0)
    slope_out_map = slope_maps[1] + low_dot(affinity_low, in_low, 1, 0)
    pull_convolved(maps[0], pl.ds(2 * INNER, STATE), slope_in * in_pull)
    pull_convolved(maps[1], pl.ds(2 * INNER + STATE, STATE), slope_out_map * out_pull)
    slope_changes = lax.dot_general(
        lower_ones(),
        slope_cumulative[...],
        (((0,), (0,)), ((), ())),
        precision=deepest_tier,
        preferred_element_type=jnp.float32,
    )[:, :MHEADS]
    slope_step = slope_steps[:, :MHEADS] + slope_changes * rates
    slope_raw = slope_step * sigmoid(shifted)
    slope_decay[0] += fold_rows(slope_changes * steps) * rates
    slope_decay[1] += fold_rows(slope_raw)
    slope_projected[:, INNER + streams_extent :] = jnp.concatenate(
        [to_low(slope_raw), jnp.zeros((ssd_block, 128 - MHEADS), jnp.bfloat16)], axis=1
    )


def fixed(shape):
    return pl.BlockSpec(shape, lambda chunk: (0,) * len(shape))


def middle_forward(projected, smalls):
    conv_taps, skip_gain, a_log, dt_bias, gated_gain = smalls
    chosen, later = head_tables()
    extent, columns = projected.shape
    chunks = extent // ssd_block
    streams_extent = INNER + 2 * STATE
    return pl.pallas_call(
        middle_kernel,
        grid=(chunks,),
        out_shape=(
            jax.ShapeDtypeStruct((extent, INNER), jnp.bfloat16),
            jax.ShapeDtypeStruct((extent, INNER), jnp.float32),
            jax.ShapeDtypeStruct((chunks, STATE, INNER), jnp.float32),
        ),
        in_specs=[
            pl.BlockSpec((ssd_block, columns), lambda chunk: (chunk, 0)),
            fixed((4, streams_extent)),
            fixed((1, INNER)),
            fixed((2, MHEADS)),
            fixed((1, INNER)),
            fixed(later.shape),
        ],
        out_specs=(
            pl.BlockSpec((ssd_block, INNER), lambda chunk: (chunk, 0)),
            pl.BlockSpec((ssd_block, INNER), lambda chunk: (chunk, 0)),
            pl.BlockSpec((1, STATE, INNER), lambda chunk: (chunk, 0, 0)),
        ),
        scratch_shapes=[
            pltpu.VMEM((ssd_block + 8, streams_extent), jnp.float32),
            pltpu.VMEM((ssd_block, ssd_block), jnp.float32),
            pltpu.VMEM((MHEADS, ssd_block, ssd_block), jnp.float32),
            pltpu.VMEM((ssd_block, INNER), jnp.float32),
            pltpu.VMEM((STATE, INNER), jnp.float32),
            pltpu.VMEM((ssd_block, INNER), jnp.float32),
        ],
        compiler_params=pltpu.CompilerParams(vmem_limit_bytes=48 * 2**20),
        cost_estimate=pl.CostEstimate(
            flops=2 * 10**10, transcendentals=4 * 10**6, bytes_accessed=20 * 10**6
        ),
    )(
        projected,
        conv_taps,
        skip_gain.reshape(1, INNER),
        jnp.stack([a_log, dt_bias]),
        gated_gain.reshape(1, INNER),
        later,
    )


def middle_backward(projected, outcome, starts, slope, smalls):
    conv_taps, skip_gain, a_log, dt_bias, gated_gain = smalls
    chosen, later = head_tables()
    extent, columns = projected.shape
    chunks = extent // ssd_block
    streams_extent = INNER + 2 * STATE

    def back(chunk):
        return (chunks - 1 - chunk, 0)

    slope_projected, slope_taps, slope_skip, slope_gain, slope_decay = pl.pallas_call(
        middle_slope_kernel,
        grid=(chunks,),
        out_shape=(
            jax.ShapeDtypeStruct((extent, columns), jnp.bfloat16),
            jax.ShapeDtypeStruct((4, 8, streams_extent), jnp.float32),
            jax.ShapeDtypeStruct((8, INNER), jnp.float32),
            jax.ShapeDtypeStruct((8, INNER), jnp.float32),
            jax.ShapeDtypeStruct((2, 8, MHEADS), jnp.float32),
        ),
        in_specs=[
            pl.BlockSpec((ssd_block, columns), back),
            pl.BlockSpec(
                (8, columns),
                lambda chunk: (jnp.maximum((chunks - 1 - chunk) * (ssd_block // 8) - 1, 0), 0),
            ),
            pl.BlockSpec((ssd_block, INNER), back),
            pl.BlockSpec((1, STATE, INNER), lambda chunk: (chunks - 1 - chunk, 0, 0)),
            pl.BlockSpec((ssd_block, INNER), back),
            fixed((4, streams_extent)),
            fixed((1, INNER)),
            fixed((2, MHEADS)),
            fixed((1, INNER)),
            fixed(chosen.shape),
            fixed(later.shape),
        ],
        out_specs=(
            pl.BlockSpec((ssd_block, columns), back),
            fixed((4, 8, streams_extent)),
            fixed((8, INNER)),
            fixed((8, INNER)),
            fixed((2, 8, MHEADS)),
        ),
        scratch_shapes=[
            pltpu.VMEM((ssd_block + 8, streams_extent), jnp.float32),
            pltpu.VMEM((ssd_block, ssd_block), jnp.float32),
            pltpu.VMEM((MHEADS, ssd_block, ssd_block), jnp.float32),
            pltpu.VMEM((ssd_block, INNER), jnp.float32),
            pltpu.VMEM((STATE, INNER), jnp.float32),
            pltpu.VMEM((ssd_block + 8, streams_extent), jnp.float32),
            pltpu.VMEM((ssd_block, ssd_block), jnp.float32),
            pltpu.VMEM((2, ssd_block, STATE), jnp.float32),
            pltpu.VMEM((ssd_block, ssd_block), jnp.float32),
            pltpu.VMEM((ssd_block, ssd_block), jnp.float32),
        ],
        compiler_params=pltpu.CompilerParams(vmem_limit_bytes=48 * 2**20),
        cost_estimate=pl.CostEstimate(
            flops=5 * 10**10, transcendentals=8 * 10**6, bytes_accessed=30 * 10**6
        ),
    )(
        projected,
        projected,
        outcome,
        starts,
        slope,
        conv_taps,
        skip_gain.reshape(1, INNER),
        jnp.stack([a_log, dt_bias]),
        gated_gain.reshape(1, INNER),
        chosen,
        later,
    )
    slope_decay = jnp.sum(slope_decay, axis=1)
    return (
        slope_projected,
        (
            jnp.sum(slope_taps, axis=1),
            jnp.sum(slope_skip, axis=0),
            slope_decay[0],
            slope_decay[1],
            jnp.sum(slope_gain, axis=0),
        ),
    )


Y_LANE = (("tensor", 2),)


def mixer_forward(value_entries, w_in, exit_matrix, block_gain, smalls):
    rescaled_rows, rescale_grad = jax.vjp(root_mean_rescale, value_entries, block_gain)
    normed_low = to_low(rescaled_rows)
    projected = matmul_apply(normed_low, w_in)
    middle_low, outcome, starts = middle_forward(projected, smalls)
    return (
        value_entries + matmul_apply(middle_low, exit_matrix),
        (rescale_grad, normed_low, (projected, outcome, starts), middle_low),
    )


def mixer_backward(conductor, last, slope_emitted, kept, w_in, exit_matrix, smalls):
    rescale_grad, normed_low, middle_kept, middle_low = kept
    grad_low = to_low(slope_emitted)
    slope_exit_matrix = to_low(product_tn(middle_low, grad_low))
    job_out = conductor.add(Summing(slope_exit_matrix, True))
    slope_middle = product_nt(grad_low, exit_matrix)
    slope_middle = conductor.tick(after(slope_middle, [slope_exit_matrix]), 7.0)
    grad_proj, slope_smalls = middle_backward(*middle_kept, slope_middle, smalls)
    grad_proj = conductor.tick(grad_proj, 60.0 if last else 44.0, limit=0 if last else 5)
    grad_w_in = to_low(product_tn(normed_low, grad_proj))
    job_in = conductor.add(Summing(grad_w_in, True))
    grad_proj = conductor.tick(after(grad_proj, [grad_w_in]), 7.0, limit=0 if last else 5)
    grad_values, slope_scale = rescale_grad(product_nt(grad_proj, w_in))
    slope_value = conductor.tick(grad_values + slope_emitted, 10.0, Y_LANE, limit=0 if last else 5)
    return (slope_value, slope_scale, slope_smalls, (job_out, job_in))


def head_mask(head, extent):
    columns = lax.broadcasted_iota(jnp.int32, (1, extent), 1)
    inside = (columns >= head * HD) & (columns < (head + 1) * HD)
    return jnp.where(inside, 1.0, 0.0).astype(jnp.bfloat16)


def head_weights(queries, key_rows):
    scores = low_dot(queries, key_rows, 1, 1) * HD ** (-0.5)
    rows = lax.broadcasted_iota(jnp.int32, (MAX_PIECES, MAX_PIECES), 0)
    columns = lax.broadcasted_iota(jnp.int32, (MAX_PIECES, MAX_PIECES), 1)
    scores = jnp.where(rows >= columns, scores, -jnp.inf)
    exponents = jnp.exp(scores - jnp.max(scores, axis=-1, keepdims=True))
    return exponents / jnp.sum(exponents, axis=-1, keepdims=True)


def attend_kernel(triple, output):
    extent = output.shape[1]
    queries, key_rows = triple[:, :extent], triple[:, extent : 2 * extent]
    value_rows = triple[:, 2 * extent :]
    attended = jnp.zeros(output.shape, jnp.float32)
    for head in range(extent // HD):
        mask = head_mask(head, extent)
        weights = to_low(head_weights(queries * mask, key_rows))
        attended = attended + low_dot(weights, value_rows * mask, 1, 0)
    output[...] = to_low(attended)


def attend_slope_kernel(triple, slope, output):
    extent = slope.shape[1]
    queries, key_rows = triple[:, :extent], triple[:, extent : 2 * extent]
    value_rows = triple[:, 2 * extent :]
    slope_here = slope[...]
    slopes = [jnp.zeros(slope.shape, jnp.float32)] * 3
    for head in range(extent // HD):
        mask = head_mask(head, extent)
        weights = head_weights(queries * mask, key_rows)
        slope_masked = slope_here * mask
        slope_weights = low_dot(slope_masked, value_rows, 1, 1)
        slope_scores = to_low(
            weights
            * (slope_weights - jnp.sum(weights * slope_weights, axis=-1, keepdims=True))
        )
        slopes[0] = slopes[0] + low_dot(slope_scores, key_rows * mask, 1, 0)
        slopes[1] = slopes[1] + low_dot(slope_scores, queries * mask, 0, 0)
        slopes[2] = slopes[2] + low_dot(to_low(weights), slope_masked, 0, 0)
    output[:, :extent] = to_low(slopes[0] * HD ** (-0.5))
    output[:, extent : 2 * extent] = to_low(slopes[1] * HD ** (-0.5))
    output[:, 2 * extent :] = to_low(slopes[2])


def by_sequence(kernel, columns, *arrays):
    rows = arrays[0].shape[0]
    return pl.pallas_call(
        kernel,
        grid=(rows // MAX_PIECES,),
        out_shape=jax.ShapeDtypeStruct((rows, columns), jnp.bfloat16),
        in_specs=[
            pl.BlockSpec((MAX_PIECES, array.shape[1]), lambda group: (group, 0)) for array in arrays
        ],
        out_specs=pl.BlockSpec((MAX_PIECES, columns), lambda group: (group, 0)),
        compiler_params=pltpu.CompilerParams(vmem_limit_bytes=24 * 2**20),
        cost_estimate=pl.CostEstimate(
            flops=3 * 10**9, transcendentals=3 * 10**5, bytes_accessed=4 * 10**6
        ),
    )(*arrays)


def apply_heads(latent_holder, heed_scale, triple_matrix, exit_matrix):
    rescaled_rows, rescale_grad = jax.vjp(root_mean_rescale, latent_holder, heed_scale)
    rows_low = gather_rows(to_low(rescaled_rows))
    triple = to_low(matmul_apply(rows_low, triple_matrix))
    heads_output = by_sequence(attend_kernel, triple.shape[1] // 3, triple)
    outcome = latent_holder + total_lines(product_nt(heads_output, exit_matrix))
    return outcome, (rescale_grad, rows_low, triple, heads_output)


def apply_heads_grad(conductor, slope_emitted, kept, triple_matrix, exit_matrix):
    rescale_grad, rows_low, triple, heads_output = kept
    grad_rows = conductor.tick(gather_grads(to_low(slope_emitted)), 12.0, Y_LANE)
    slope_exit_matrix = to_low(product_tn(grad_rows, heads_output))
    grad_attended = to_low(matmul_apply(grad_rows, exit_matrix))
    grad_triple = by_sequence(attend_slope_kernel, triple.shape[1], triple, grad_attended)
    grad_triple = conductor.tick(after(grad_triple, [slope_exit_matrix]), 10.0, Y_LANE)
    slope_rescaled = sum_grads(product_nt(grad_triple, triple_matrix))
    slope_triple_matrix = to_low(product_tn(rows_low, grad_triple))
    job_exit = conductor.add(Summing(slope_exit_matrix, False))
    job_triple = conductor.add(Summing(slope_triple_matrix, False))
    slope_rescaled = conductor.tick(
        after(slope_rescaled, [slope_triple_matrix]), 10.0, Y_LANE
    )
    gradient_holder, slope_scale = rescale_grad(slope_rescaled)
    return (gradient_holder + slope_emitted, slope_scale, job_triple, job_exit)


def swiglu(both):
    half = both.shape[1] // 2
    return jax.nn.silu(both[:, :half]) * both[:, half:]


def perceptron_apply(latent_holder, perceptron_scale, lift_matrix, lower_matrix):
    rescaled_rows, rescale_grad = jax.vjp(root_mean_rescale, latent_holder, perceptron_scale)
    rows_low = gather_rows(to_low(rescaled_rows))
    latent_state, act_pull = jax.vjp(swiglu, matmul_apply(rows_low, lift_matrix))
    latent_merged = to_low(latent_state)
    outcome = latent_holder + total_lines(product_nt(latent_merged, lower_matrix))
    return (outcome, (rescale_grad, rows_low, act_pull, latent_merged))


def perceptron_grad(conductor, slope_emitted, kept, lift_matrix, lower_matrix):
    rescale_grad, rows_low, act_pull, latent_merged = kept
    grad_rows = conductor.tick(gather_grads(to_low(slope_emitted)), 13.0, Y_LANE)
    slope_lower_matrix = to_low(product_tn(grad_rows, latent_merged))
    job_lower = conductor.add(Summing(slope_lower_matrix, False))
    grad_rows = conductor.tick(after(grad_rows, [slope_lower_matrix]), 2.0, Y_LANE)
    (grad_both,) = act_pull(matmul_apply(grad_rows, lower_matrix))
    grad_both = conductor.tick(to_low(grad_both), 4.0, Y_LANE)
    slope_rescaled = sum_grads(product_nt(grad_both, lift_matrix))
    half = grad_both.shape[1] // 2
    slope_lifts = [
        to_low(product_tn(rows_low, grad_both[:, :half])),
        to_low(product_tn(rows_low, grad_both[:, half:])),
    ]
    slope_lifts = [conductor.add(Summing(slope, False)) for slope in slope_lifts]
    slope_rescaled = conductor.tick(slope_rescaled, 14.0, Y_LANE)
    gradient_holder, slope_scale = rescale_grad(slope_rescaled)
    return (gradient_holder + slope_emitted, slope_scale, job_lower, slope_lifts)


def body(
    byte_ids,
    targets,
    boundaries,
    lengths,
    tables,
    tables_first,
    tables_second,
    mamba_in,
    mamba_in_first,
    mamba_in_second,
    mamba_out,
    mamba_out_first,
    mamba_out_second,
    route_proj,
    route_proj_first,
    route_proj_second,
    small_params,
    small_params_first,
    small_params_second,
    heed_triple_matrix,
    attn_qkv_first,
    attn_qkv_second,
    heed_exit_matrix,
    attn_out_first,
    attn_out_second,
    lifting_matrix,
    mlp_gate_up_first,
    mlp_gate_up_second,
    lowering_matrix,
    mlp_down_first,
    mlp_down_second,
):
    devices = lax.axis_size("dp") * lax.axis_size("tensor")
    table_rows = tables.shape[1]
    small_here = small_params.shape[0]
    mixed_rows = 2 * table_rows
    length_pair = jnp.stack([lengths[0] // 16, lengths[0] % 16]).astype(jnp.bfloat16)
    tail = jnp.concatenate([to_low(small_params), length_pair])
    mixed = jnp.concatenate(
        [
            to_low(tables).reshape(mixed_rows, BYTE_WIDTH),
            jnp.pad(tail, (0, mixed_rows * 128 - tail.shape[0])).reshape(mixed_rows, 128),
        ],
        axis=1,
    )

    def wide_in(layer):
        low = to_low(mamba_in[layer])
        return jnp.pad(low, ((0, 0), (0, PROJ_WIDE - low.shape[1])))

    conductor = Conductor()
    exact_tiles = mamba_in.shape[1] % 16 == 0
    shards = [
        mixed,
        wide_in(0),
        to_low(mamba_out[0]),
        to_low(route_proj),
        to_low(heed_triple_matrix).reshape(heed_triple_matrix.shape[0], -1),
        to_low(heed_exit_matrix).T,
        to_low(lifting_matrix).reshape(lifting_matrix.shape[0], -1),
        to_low(lowering_matrix).T,
        wide_in(1),
        to_low(mamba_out[1]),
    ]
    kinds = [BYTE_LANES] * 4 + [MAIN_LANES] * 4 + [BYTE_LANES] * 2
    if exact_tiles:
        fan, late = MAIN_LANES, MAIN_LANES[::-1]
        in_first, in_last = 18 * 128, PROJ_WIDE - 18 * 128
        half_route = route_proj.shape[1] // 2
        half_lift = shards[6].shape[1] // 2
        jobs = [
            (3, BYTE_LANES, half_route, half_route),
            (9, BYTE_LANES, 0, BYTE_WIDTH),
            (8, BYTE_LANES, 0, in_first),
            (0, BYTE_LANES, 0, BYTE_WIDTH + 128),
            (1, BYTE_LANES, in_first, in_last),
            (2, BYTE_LANES, 0, BYTE_WIDTH),
            (8, BYTE_LANES, in_first, in_last),
            (4, fan, 0, shards[4].shape[1]),
            (1, BYTE_LANES, 0, in_first),
            (6, fan, half_lift, half_lift),
            (3, BYTE_LANES, 0, half_route),
            (7, fan, 0, shards[7].shape[1]),
            (5, late, 0, shards[5].shape[1]),
            (6, late, 0, half_lift),
        ]
        wholes = spread_whole(shards, jobs, 0)
    else:
        wholes = [
            lax.all_gather(
                shard, ("dp", "tensor") if kind == BYTE_LANES else "dp", axis=0, tiled=True
            )
            for shard, kind in zip(shards, kinds)
        ]
    mixed_whole = wholes[0]
    full_in, full_out, full_route = [wholes[1], wholes[8]], [wholes[2], wholes[9]], wholes[3]
    triple_whole, heed_exit_whole, lift_matrix_whole, lower_matrix_whole = wholes[4:8]
    mixed_whole = mixed_whole.reshape(devices, mixed_rows, BYTE_WIDTH + 128)
    full_tables = (
        mixed_whole[:, :, :BYTE_WIDTH]
        .reshape(devices, 2, table_rows, BYTE_WIDTH)
        .transpose(1, 0, 2, 3)
        .reshape(2, VOCAB, BYTE_WIDTH)
    )
    tails = mixed_whole[:, :, BYTE_WIDTH:].reshape(devices, -1)
    full_small = tails[:, :small_here].reshape(-1)
    pairs = tails[:, small_here : small_here + 2].astype(jnp.float32)
    byte_count = jnp.sum(pairs[:, 0] * 16.0 + pairs[:, 1])
    (
        block_gains,
        gated_gains,
        core_scales,
        head_gain,
        blank_row,
        conv_taps,
        skip_gains,
        a_logs,
        dt_biases,
    ) = unpack_small(full_small.astype(jnp.float32))
    layer_smalls = [
        (
            conv_taps[layer_index],
            skip_gains[layer_index],
            a_logs[layer_index],
            dt_biases[layer_index],
            gated_gains[layer_index],
        )
        for layer_index in range(2)
    ]
    cut_marks = boundaries[0]
    seq_len = byte_ids.shape[1]
    vocab_ids = jnp.arange(VOCAB, dtype=jnp.int32)
    onehot_in = (byte_ids[0][:, None] == vocab_ids[None, :]).astype(jnp.bfloat16)
    embedded = matmul_apply(onehot_in, full_tables[0])
    packer_output, kept_enc = mixer_forward(
        embedded, full_in[0], full_out[0], block_gains[0], layer_smalls[0]
    )
    encoded_low = to_low(packer_output)
    directed_rows = matmul_apply(encoded_low, full_route)
    cut_likelihood, prob_pull = jax.vjp(
        route_prob, directed_rows[:, :BYTE_WIDTH], directed_rows[:, BYTE_WIDTH : 2 * BYTE_WIDTH]
    )
    select_items, broadcast_back = span_maps(cut_marks)
    latent_holder, merge_transpose = jax.vjp(
        partial(merge_into_pieces, select_items), packer_output, blank_row
    )
    latent_holder, saved_heeding = apply_heads(
        latent_holder, core_scales[0], triple_whole, heed_exit_whole
    )
    latent_holder, saved_perceptron = perceptron_apply(
        latent_holder, core_scales[1], lift_matrix_whole, lower_matrix_whole
    )
    unpacked_bytes, link_layers_grad = jax.vjp(
        partial(link_layers, select_items, broadcast_back, cut_marks),
        latent_holder,
        core_scales[2],
        cut_likelihood,
        directed_rows[:, 2 * BYTE_WIDTH :],
    )
    final_out, kept_dec = mixer_forward(
        unpacked_bytes, full_in[1], full_out[1], block_gains[1], layer_smalls[1]
    )
    head_in, head_pull = jax.vjp(root_mean_rescale, final_out, head_gain)
    head_low = to_low(head_in)
    logits = product_nt(head_low, full_tables[1])
    maxima = jnp.max(logits, axis=-1, keepdims=True)
    log_total = maxima + jnp.log(jnp.sum(jnp.exp(logits - maxima), axis=-1, keepdims=True))
    onehot_out = (targets[0][:, None] == vocab_ids[None, :]).astype(jnp.float32)
    counted = (jnp.arange(seq_len, dtype=jnp.int32) < lengths[0]).astype(jnp.float32)[:, None]
    loss_local = jnp.sum((log_total - logits) * onehot_out * counted)
    grad_logits = to_low((jnp.exp(logits - log_total) - onehot_out) * counted / byte_count)
    grad_table_out = product_tn(grad_logits, head_low)
    grad_final, grad_head_gain = head_pull(matmul_apply(grad_logits, full_tables[1]))
    slope_unpacked, grad_block_dec, grad_small_dec, jobs_dec = mixer_backward(
        conductor, False, grad_final, kept_dec, full_in[1], full_out[1], layer_smalls[1]
    )
    gradient_holder, slope_closing_scale, slope_likelihood, slope_shortcut = link_layers_grad(
        slope_unpacked
    )
    gradient_holder, slope_perceptron_scale, job_lower, slope_lifts = perceptron_grad(
        conductor, conductor.tick(gradient_holder, 14.0, Y_LANE), saved_perceptron, lift_matrix_whole, lower_matrix_whole
    )
    gradient_holder, slope_heed_scale, *jobs_heads = apply_heads_grad(
        conductor, gradient_holder, saved_heeding, triple_whole, heed_exit_whole
    )
    gradient_merged, gradient_blank = merge_transpose(gradient_holder)
    grad_query, grad_key = prob_pull(slope_likelihood)
    grad_routed = to_low(jnp.concatenate([grad_query, grad_key, slope_shortcut], axis=1))
    grad_routed = after(grad_routed, [gradient_merged])
    grad_route = to_low(product_tn(encoded_low, grad_routed))
    job_route = conductor.add(Summing(grad_route, True))
    grad_routed = conductor.tick(after(grad_routed, [grad_route]), 7.0)
    grad_embedded, grad_block_enc, grad_small_enc, jobs_enc = mixer_backward(
        conductor,
        True,
        gradient_merged + product_nt(grad_routed, full_route),
        kept_enc,
        full_in[0],
        full_out[0],
        layer_smalls[0],
    )
    grad_table_in = jnp.dot(onehot_in.astype(jnp.float32).T, grad_embedded, precision=deepest_tier)
    grad_small = jnp.concatenate(
        [
            piece.reshape(-1)
            for piece in (
                jnp.stack([grad_block_enc, grad_block_dec]),
                jnp.stack([grad_small_enc[4], grad_small_dec[4]]),
                jnp.stack([slope_heed_scale, slope_perceptron_scale, slope_closing_scale]),
                grad_head_gain,
                gradient_blank,
                jnp.stack([grad_small_enc[0], grad_small_dec[0]]),
                jnp.stack([grad_small_enc[1], grad_small_dec[1]]),
                jnp.stack([grad_small_enc[2], grad_small_dec[2]]),
                jnp.stack([grad_small_enc[3], grad_small_dec[3]]),
            )
        ]
    )
    width = mamba_in.shape[2]
    grad_mixed = jnp.concatenate(
        [
            jnp.concatenate(
                [
                    to_low(grad_table_in).reshape(devices, table_rows, BYTE_WIDTH),
                    to_low(grad_table_out).reshape(devices, table_rows, BYTE_WIDTH),
                ],
                axis=1,
            ),
            jnp.pad(
                to_low(grad_small).reshape(devices, small_here),
                ((0, 0), (0, mixed_rows * 128 - small_here)),
            ).reshape(devices, mixed_rows, 128),
        ],
        axis=2,
    )
    conductor.close()
    parts = [
        jobs_heads[1],
        slope_lifts[0],
        slope_lifts[1],
        jobs_heads[0],
        job_lower,
        jobs_dec[1],
        jobs_dec[0],
        jobs_enc[0],
        job_route,
        jobs_enc[1],
        Summing(grad_mixed.reshape(-1, BYTE_WIDTH + 128), True),
    ]
    sums = [None if part.masks else part.result(jobs_enc[1].addends[0][0]) for part in parts]
    open_parts = [number for number in (8, 9, 7, 10, 3, 0, 1, 2, 4, 5, 6) if parts[number].masks]
    rests = [parts[number].rest(jobs_enc[1].addends[0][0]) for number in open_parts]
    grads = [grad for grad, _ in rests]
    sum_kinds = [kind for _, kind in rests]
    if exact_tiles:
        early = sum((jnp.sum(part * part) for part in sums if part is not None), jnp.float32(0.0))
        extra = jnp.zeros((16, 128), jnp.float32).at[0, 0].set(early).at[8, 0].set(loss_local)
        *ends, totals = sum_whole(grads, sum_kinds, extra, 1)
        square_total, loss_sum = jnp.sum(totals[:8]), jnp.sum(totals[8:])
    else:
        ends = [sum_slowly(parts[number]) for number in open_parts]
    for number, end in zip(open_parts, ends):
        sums[number] = end
    reduced_wo = sums[0].T
    reduced_gate_up = jnp.stack([sums[1], sums[2]], axis=1)
    reduced_qkv = sums[3].reshape(heed_triple_matrix.shape)
    reduced_down = sums[4].T
    reduced_in_dec = sums[5][:, :width]
    reduced_out_dec, reduced_out_enc, reduced_route = sums[6:9]
    reduced_in_enc = sums[9][:, :width]
    reduced_mixed = sums[10]
    reduced_tables = reduced_mixed[:, :BYTE_WIDTH].reshape(2, table_rows, BYTE_WIDTH)
    reduced_small = reduced_mixed[:, BYTE_WIDTH:].reshape(-1)[:small_here]
    reduced_in = jnp.stack([reduced_in_enc, reduced_in_dec])
    reduced_out = jnp.stack([reduced_out_enc, reduced_out_dec])
    reduced = (
        reduced_tables,
        reduced_in,
        reduced_out,
        reduced_route,
        reduced_small,
        reduced_qkv,
        reduced_wo,
        reduced_gate_up,
        reduced_down,
    )
    if not exact_tiles:
        squares = sum((jnp.sum(grad * grad) for grad in reduced))
        totals = add_everywhere(jnp.stack([squares, loss_local]).reshape(1, 2))
        square_total, loss_sum = (totals[0, 0], totals[0, 1])
    grad_norm = jnp.sqrt(square_total)
    clip_factor = jnp.minimum(1.0, max_norm / (grad_norm + 1e-06))
    masters = (
        tables,
        mamba_in,
        mamba_out,
        route_proj,
        small_params,
        heed_triple_matrix,
        heed_exit_matrix,
        lifting_matrix,
        lowering_matrix,
    )
    firsts = (
        tables_first,
        mamba_in_first,
        mamba_out_first,
        route_proj_first,
        small_params_first,
        attn_qkv_first,
        attn_out_first,
        mlp_gate_up_first,
        mlp_down_first,
    )
    seconds = (
        tables_second,
        mamba_in_second,
        mamba_out_second,
        route_proj_second,
        small_params_second,
        attn_qkv_second,
        attn_out_second,
        mlp_gate_up_second,
        mlp_down_second,
    )
    rate_list = (
        rate_byte,
        rate_byte,
        rate_byte,
        rate_byte,
        rate_small,
        rate_main,
        rate_main,
        rate_main,
        rate_main,
    )
    decay_list = (
        weight_decay,
        weight_decay,
        weight_decay,
        weight_decay,
        0.0,
        weight_decay,
        weight_decay,
        weight_decay,
        weight_decay,
    )
    updated = [
        adam_step(
            masters[position],
            clip_factor * reduced[position],
            firsts[position],
            seconds[position],
            rate_list[position],
            decay_list[position],
        )
        for position in range(9)
    ]
    updated[7] = lift_step(
        clip_factor, sums[1], sums[2], lifting_matrix, mlp_gate_up_first, mlp_gate_up_second
    )
    return (loss_sum, byte_count, grad_norm) + tuple(
        (member for triple_out in updated for member in triple_out)
    )


def solution(mesh):
    return jax.shard_map(
        body,
        mesh=mesh,
        in_specs=(
            P(("dp", "tensor"), None),
            P(("dp", "tensor"), None),
            P(("dp", "tensor"), None),
            P(("dp", "tensor")),
            P(None, ("dp", "tensor"), None),
            P(None, ("dp", "tensor"), None),
            P(None, ("dp", "tensor"), None),
            P(None, ("dp", "tensor"), None),
            P(None, ("dp", "tensor"), None),
            P(None, ("dp", "tensor"), None),
            P(None, ("dp", "tensor"), None),
            P(None, ("dp", "tensor"), None),
            P(None, ("dp", "tensor"), None),
            P(("dp", "tensor"), None),
            P(("dp", "tensor"), None),
            P(("dp", "tensor"), None),
            P(("dp", "tensor")),
            P(("dp", "tensor")),
            P(("dp", "tensor")),
            P("dp", None, "tensor"),
            P("dp", None, "tensor"),
            P("dp", None, "tensor"),
            P("tensor", "dp"),
            P("tensor", "dp"),
            P("tensor", "dp"),
            P("dp", None, "tensor"),
            P("dp", None, "tensor"),
            P("dp", None, "tensor"),
            P("tensor", "dp"),
            P("tensor", "dp"),
            P("tensor", "dp"),
        ),
        out_specs=(
            P(),
            P(),
            P(),
            P(None, ("dp", "tensor"), None),
            P(None, ("dp", "tensor"), None),
            P(None, ("dp", "tensor"), None),
            P(None, ("dp", "tensor"), None),
            P(None, ("dp", "tensor"), None),
            P(None, ("dp", "tensor"), None),
            P(None, ("dp", "tensor"), None),
            P(None, ("dp", "tensor"), None),
            P(None, ("dp", "tensor"), None),
            P(("dp", "tensor"), None),
            P(("dp", "tensor"), None),
            P(("dp", "tensor"), None),
            P(("dp", "tensor")),
            P(("dp", "tensor")),
            P(("dp", "tensor")),
            P("dp", None, "tensor"),
            P("dp", None, "tensor"),
            P("dp", None, "tensor"),
            P("tensor", "dp"),
            P("tensor", "dp"),
            P("tensor", "dp"),
            P("dp", None, "tensor"),
            P("dp", None, "tensor"),
            P("dp", None, "tensor"),
            P("tensor", "dp"),
            P("tensor", "dp"),
            P("tensor", "dp"),
        ),
        check_vma=False,
    )
```

```python
from functools import partial

import jax
import jax.numpy as jnp
from jax import lax
from jax.experimental import pallas as pl
from jax.experimental.pallas import tpu as pltpu
from jax.sharding import PartitionSpec as P

BYTE_WIDTH = 1024
CORE_WIDTH = 1536
VOCAB = 256
STATE = 128
HEADDIM = 64
STEP = 10
INNER = 2048
MHEADS = 32
HD = 96
MAX_PIECES = 128


deepest_tier = lax.Precision.HIGHEST
norm_eps = 1e-05
ssd_block = 128
beta_one = 0.9
beta_two = 0.95
adam_eps = 1e-08
weight_decay = 0.1
max_norm = 0.01
rate_byte = 0.06
rate_main = 0.05
rate_small = 0.5


def root_mean_rescale(value_entries, gain_vec):
    return (
        value_entries
        * lax.rsqrt(jnp.mean(value_entries * value_entries, axis=-1, keepdims=True) + norm_eps)
        * gain_vec
    )


def softplus(value_entries):
    return jnp.log1p(jnp.exp(value_entries))


def unpack_small(vector):
    extents = [
        2 * BYTE_WIDTH,
        2 * INNER,
        3 * CORE_WIDTH,
        BYTE_WIDTH,
        CORE_WIDTH - BYTE_WIDTH,
        8 * (INNER + 2 * STATE),
        2 * INNER,
        2 * MHEADS,
        2 * MHEADS,
    ]
    pieces = []
    offset = 0
    for extent in extents:
        pieces.append(vector[offset : offset + extent])
        offset += extent
    return (
        pieces[0].reshape(2, BYTE_WIDTH),
        pieces[1].reshape(2, INNER),
        pieces[2].reshape(3, CORE_WIDTH),
        pieces[3],
        pieces[4],
        pieces[5].reshape(2, 4, INNER + 2 * STATE),
        pieces[6].reshape(2, INNER),
        pieces[7].reshape(2, MHEADS),
        pieces[8].reshape(2, MHEADS),
    )


def route_prob(queries, key_rows):
    unit_query = queries * lax.rsqrt(jnp.sum(queries * queries, axis=-1, keepdims=True) + 1e-06)
    unit_key = key_rows * lax.rsqrt(jnp.sum(key_rows * key_rows, axis=-1, keepdims=True) + 1e-06)
    cosine = jnp.sum(unit_query[1:] * unit_key[:-1], axis=-1)
    return jnp.concatenate([jnp.ones((1,), jnp.float32), 0.5 * (1.0 - cosine)])


def span_maps(cut_marks):
    owner_slot = jnp.cumsum(cut_marks) - 1
    position_labels = jnp.arange(MAX_PIECES, dtype=jnp.int32)
    broadcast_back = (owner_slot[:, None] == position_labels[None, :]).astype(jnp.float32)
    select_items = broadcast_back.T * cut_marks[None, :].astype(jnp.float32)
    return (select_items, broadcast_back)


def merge_into_pieces(select_items, value_entries, blank_row):
    spans = jnp.dot(select_items, value_entries, precision=deepest_tier)
    return jnp.concatenate(
        [spans, jnp.broadcast_to(blank_row, (MAX_PIECES, CORE_WIDTH - BYTE_WIDTH))], axis=1
    )


def decay_products(confidence):
    rows = lax.broadcasted_iota(jnp.int32, (MAX_PIECES, MAX_PIECES), 0)
    columns = lax.broadcasted_iota(jnp.int32, (MAX_PIECES, MAX_PIECES), 1)
    products = jnp.where(rows > columns, 1.0 - confidence[:, None], 1.0)
    reach = 1
    while reach < MAX_PIECES:
        shifted = jnp.concatenate(
            [jnp.ones((reach, MAX_PIECES), jnp.float32), products[:-reach]], axis=0
        )
        products = products * shifted
        reach *= 2
    return jnp.where(rows >= columns, products, 0.0)


@jax.custom_vjp
def smooth_spans(piece_output, confidence):
    products = decay_products(confidence)
    return jnp.dot(products, confidence[:, None] * piece_output, precision=deepest_tier)


def smooth_keep(piece_output, confidence):
    products = decay_products(confidence)
    smoothed = jnp.dot(products, confidence[:, None] * piece_output, precision=deepest_tier)
    return smoothed, (piece_output, confidence, products, smoothed)


def smooth_pull(kept, slope):
    piece_output, confidence, products, smoothed = kept
    spread = lax.dot_general(
        products, slope, (((0,), (0,)), ((), ())), precision=deepest_tier
    )
    before = jnp.concatenate([jnp.zeros((1, smoothed.shape[1]), jnp.float32), smoothed[:-1]], axis=0)
    return (confidence[:, None] * spread, jnp.sum(spread * (piece_output - before), axis=-1))


smooth_spans.defvjp(smooth_keep, smooth_pull)


def link_layers(
    select_items,
    broadcast_back,
    cut_marks,
    latent_holder,
    closing_scale,
    cut_likelihood,
    shortcut_sum,
):
    piece_output = root_mean_rescale(latent_holder, closing_scale)[:, :BYTE_WIDTH]
    smoothed = smooth_spans(
        piece_output, jnp.dot(select_items, cut_likelihood, precision=deepest_tier)
    )
    confidence = jnp.where(cut_marks == 1, cut_likelihood, 1.0 - cut_likelihood)
    return shortcut_sum + confidence[:, None] * jnp.dot(
        broadcast_back, smoothed, precision=deepest_tier
    )


def adam_step(weight, grad, first, second, rate, decay):
    first_new = beta_one * first + (1.0 - beta_one) * grad
    second_new = beta_two * second + (1.0 - beta_two) * grad * grad
    ratio = (
        first_new
        / (1.0 - beta_one**STEP)
        / (jnp.sqrt(second_new / (1.0 - beta_two**STEP)) + adam_eps)
    )
    return (first_new, second_new, weight - rate * (ratio + decay * weight))


def lift_kernel(clip, gate, up, weight, first, second, *outputs):
    for side, grad in enumerate((gate, up)):
        updated = adam_step(
            weight[:, side, :],
            clip[0, 0] * grad[...],
            first[:, side, :],
            second[:, side, :],
            rate_main,
            weight_decay,
        )
        for output, value_entries in zip(outputs, updated):
            output[:, side, :] = value_entries


def lift_step(clip_factor, gate, up, weight, first, second):
    rows, columns = gate.shape
    block = 48 if rows % 48 == 0 else rows
    flat = pl.BlockSpec((block, columns), lambda part: (part, 0))
    paired = pl.BlockSpec((block, 2, columns), lambda part: (part, 0, 0))
    return pl.pallas_call(
        lift_kernel,
        grid=(rows // block,),
        out_shape=(jax.ShapeDtypeStruct(weight.shape, jnp.float32),) * 3,
        in_specs=[pl.BlockSpec(memory_space=pltpu.SMEM), flat, flat, paired, paired, paired],
        out_specs=(paired,) * 3,
        compiler_params=pltpu.CompilerParams(vmem_limit_bytes=32 * 2**20),
    )(clip_factor.reshape(1, 1), gate, up, weight, first, second)


def to_low(value_entries):
    return value_entries.astype(jnp.bfloat16)


def matmul_apply(left, right):
    return jnp.dot(left, right, preferred_element_type=jnp.float32)


def product_tn(left, right):
    return lax.dot_general(
        left, right, (((0,), (0,)), ((), ())), preferred_element_type=jnp.float32
    )


def product_nt(left, right):
    return lax.dot_general(
        left, right, (((1,), (1,)), ((), ())), preferred_element_type=jnp.float32
    )


def swap(value_entries, axis, mask):
    size = lax.axis_size(axis)
    return lax.ppermute(value_entries, axis, [(place, place ^ mask) for place in range(size)])


def bit_masks(size):
    masks = []
    mask = 1
    while mask < size:
        masks.append(mask)
        mask *= 2
    return masks


def after(value_entries, earlier):
    if not earlier:
        return value_entries
    return lax.optimization_barrier((value_entries,) + tuple(earlier))[0]


def spread_masks(over_tensor):
    dp_masks = bit_masks(lax.axis_size("dp"))
    masks = [("dp", mask) for mask in dp_masks[1:] + dp_masks[:1]]
    if over_tensor:
        masks += [("tensor", mask) for mask in reversed(bit_masks(lax.axis_size("tensor")))]
    return masks


class Summing:
    def __init__(self, grad, over_tensor):
        self.masks = list(reversed(spread_masks(over_tensor)))
        names = [("dp", mask) for mask in reversed(bit_masks(lax.axis_size("dp")))]
        if over_tensor:
            names += [("tensor", mask) for mask in reversed(bit_masks(lax.axis_size("tensor")))]
        self.names = names
        rows = grad.shape[0] // 2 ** len(names)
        self.addends = [(grad.reshape((2,) * len(names) + (rows,) + grad.shape[1:]), names)]
        self.pending = None

    def picked(self, other=None, token=None):
        result = []
        for array, names in self.addends:
            if token is not None:
                array = after(array, [token])
            for position in reversed(range(len(names))):
                axis, mask = names[position]
                own = (lax.axis_index(axis) // mask) % 2
                if names[position] == other:
                    array = take(array, position, 1 - own)
                elif names[position] not in self.names:
                    array = take(array, position, own)
            result.append(array)
        return result

    def operand(self):
        return to_low(total(self.picked(self.masks[0])))

    def accept(self):
        self.names = [name for name in self.names if name != self.masks[0]]
        self.masks = self.masks[1:]
        self.addends.append((self.pending, self.names))
        self.pending = None

    def begun_last(self):
        left = [mask for axis, mask in self.masks if axis == "dp" and mask > 1]
        return 0 < len(left) == len(self.masks) < len(bit_masks(lax.axis_size("dp"))) - 1

    def rest(self, token):
        kind = []
        for axis, mask in self.masks:
            if lane_name(axis, mask) not in kind:
                kind.append(lane_name(axis, mask))
        if len(self.addends) == 1 or kind[0] in ("core", "y"):
            array = self.addends[0][0]
            if len(self.addends) > 1:
                array = to_low(total(self.picked(token=token)))
            return [(array, tuple(name for name in BYTE_LANES if name in kind))], tuple(kind)
        arrays = []
        for array, names in self.addends:
            lanes_here = {lane_name(axis, mask) for axis, mask in names}
            arrays.append((array, tuple(name for name in BYTE_LANES if name in lanes_here)))
        return arrays, tuple(kind)

    def result(self, token=None):
        return total(self.picked(token=token))


def lane_name(axis, mask):
    if axis == "tensor":
        return ("core", "y")[mask - 1]
    return "x" if mask == 1 else "z"


def sum_slowly(job):
    while job.masks:
        axis, mask = job.masks[0]
        job.pending = swap(job.operand(), axis, mask)
        job.accept()
    return job.result()


class Conductor:
    def __init__(self):
        self.clock = 0.0
        self.jobs = []
        self.flights = []

    def add(self, job):
        self.jobs.append(job)
        return job

    def lane(self, job):
        axis, mask = job.masks[0]
        return (axis, mask if axis == "tensor" else min(mask, 2))

    def launch(self, limit, banned, value_entries):
        operands = []
        for job in self.jobs:
            if len(self.flights) >= limit:
                break
            if job.pending is not None or not job.masks:
                continue
            lane = self.lane(job)
            depth = {("dp", 1): 3, ("tensor", 1): 2}.get(lane, 1)
            if lane in banned or sum(flight[1] == lane for flight in self.flights) >= depth:
                continue
            axis, mask = job.masks[0]
            operand = job.operand()
            rate = 3.4 if (axis, mask) == ("tensor", 1) else 25.3
            if axis == "dp" and mask > 2:
                rate = 50.0
            operand = after(operand, [value_entries])
            operands.append(operand)
            job.pending = swap(operand, axis, mask)
            start = max([self.clock] + [flight[0] - 6.0 for flight in self.flights if flight[1] == lane])
            self.flights.append((start + 6.0 + rate * operand.size * 2e-6, lane, job))
        return after(value_entries, operands)

    def tick(self, value_entries, elapsed, banned=(), limit=5):
        self.clock += elapsed
        ended = [flight for flight in self.flights if flight[0] <= self.clock]
        if ended:
            value_entries = after(value_entries, [flight[2].pending for flight in ended])
            self.flights = [flight for flight in self.flights if flight[0] > self.clock]
            for flight in ended:
                flight[2].accept()
        return self.launch(limit, banned, value_entries)

    def close(self):
        for _, _, job in sorted(self.flights, key=lambda flight: flight[0]):
            job.accept()
        self.flights = []
        for job in self.jobs:
            while job.begun_last():
                axis, mask = job.masks[0]
                job.pending = swap(job.operand(), axis, mask)
                job.accept()


def flip(place, mask):
    result = place
    bit = 1
    while bit <= mask:
        if mask & bit:
            result = result + bit * (1 - 2 * ((place // bit) % 2))
        bit *= 2
    return result


def order_steps(jobs, depth=2):
    free, busy, flights, plan = {}, {}, [], []
    waiting = [0] * len(jobs)
    clock = 0.0
    while True:
        for job, steps in enumerate(jobs):
            step = waiting[job]
            if step < 0 or step >= len(steps):
                continue
            lane, cost = steps[step]
            if busy.get(lane, 0) >= depth:
                continue
            busy[lane] = busy.get(lane, 0) + 1
            free[lane] = max(free.get(lane, 0.0), clock) + cost
            flights.append((free[lane] + 1.5, job, step, lane))
            plan.append(("start", job, step))
            waiting[job] = -1 - step
        if not flights:
            return plan
        flight = min(flights)
        flights.remove(flight)
        clock, job, step, lane = flight
        busy[lane] -= 1
        plan.append(("wait", job, step))
        waiting[job] = step + 1


def link_cost(lane, elements):
    return elements * 2e-6 * {"core": 3.4, "y": 23.0, "x": 23.0, "z": 46.0}[lane]


def here():
    dp_place, tensor_place = lax.axis_index("dp"), lax.axis_index("tensor")
    return dp_place // 2, dp_place % 2, tensor_place // 2, tensor_place % 2


def partner(lane, mask, coordinates):
    z, x, y, core = coordinates
    if lane == "z":
        z = flip(z, mask)
    if lane == "x":
        x = 1 - x
    if lane == "y":
        y = 1 - y
    if lane == "core":
        core = 1 - core
    return (z * 2 + x, y * 2 + core)


def greet(line, depth_z, coordinates):
    z = coordinates[0]
    barrier = pltpu.get_barrier_semaphore()

    def tell(device):
        pl.semaphore_signal(
            barrier, inc=1, device_id=device, device_id_type=pl.DeviceIdType.MESH
        )

    if not line:
        others = peers("tensor", 4) + peers("dp", 2 * depth_z)
        for device in others:
            tell(device)
        pl.semaphore_wait(barrier, len(others))
        return

    for lane in ("x", "y", "core"):
        tell(partner(lane, 1, coordinates))

    @pl.when(z > 0)
    def _():
        tell(beside(-1, coordinates))

    @pl.when(z < depth_z - 1)
    def _():
        tell(beside(1, coordinates))

    ends = (z == 0).astype(jnp.int32) + (z == depth_z - 1).astype(jnp.int32)
    pl.semaphore_wait(barrier, 5 - ends)


def peers(axis, size):
    dp_place, tensor_place = lax.axis_index("dp"), lax.axis_index("tensor")
    if axis == "dp":
        return [(flip(dp_place, mask), tensor_place) for mask in range(1, size)]
    return [(dp_place, flip(tensor_place, mask)) for mask in range(1, size)]


def beside(way, coordinates):
    z, x, y, core = coordinates
    return ((z + way) * 2 + x, y * 2 + core)


def spread_kernel(plan, jobs, depth_z, *refs):
    count = (len(refs) - 3) // 2
    shards, wholes = refs[:count], refs[count : 2 * count]
    send_sems, receive_sems, own_sems = refs[2 * count :]
    coordinates = here()
    z = coordinates[0]
    greet(True, depth_z, coordinates)

    def spot(job, free, z_place):
        array, kind, first, size = jobs[job]
        index = [
            slice(None) if name in free else (z_place if name == "z" else place)
            for name, place in zip(("z", "x", "y", "core"), coordinates)
            if name in kind
        ]
        return wholes[array].at[tuple(index) + (slice(None), pl.ds(first, size))]

    def shard(job):
        array, _, first, size = jobs[job]
        return shards[array].at[:, pl.ds(first, size)]

    own = []
    for job in range(len(jobs)):
        own.append(pltpu.make_async_copy(shard(job), spot(job, (), z), own_sems.at[job]))
        own[-1].start()

    def copies(job, step, receiving):
        steps = lanes_of(jobs[job][1], depth_z)
        lane, reach = steps[step]
        free = [name for name, _ in steps[:step] if name != lane]
        base = job * (2 * depth_z + 1)
        pairs = []
        if lane == "z":
            for side, way in enumerate((1, -1)):
                number = base + 2 * (reach - 1) + side
                if receiving:
                    block = z - way * reach
                    condition = (block >= 0) & (block < depth_z)
                    target = spot(job, free, z if step == 0 else block)
                    source = target
                else:
                    block = z - way * (reach - 1)
                    condition = (block >= 0) & (block < depth_z)
                    condition &= (z + way >= 0) & (z + way < depth_z)
                    target = spot(job, free, block)
                    source = shard(job) if step == 0 else target
                copy = pltpu.make_async_remote_copy(
                    src_ref=source,
                    dst_ref=target,
                    send_sem=send_sems.at[number],
                    recv_sem=receive_sems.at[number],
                    device_id=beside(way, coordinates),
                    device_id_type=pl.DeviceIdType.MESH,
                )
                pairs.append((condition, copy))
            return pairs
        number = base + 2 * (depth_z - 1) + ("x", "y", "core").index(lane)
        target = spot(job, free, z)
        copy = pltpu.make_async_remote_copy(
            src_ref=shard(job) if step == 0 else target,
            dst_ref=target,
            send_sem=send_sems.at[number],
            recv_sem=receive_sems.at[number],
            device_id=partner(lane, 1, coordinates),
            device_id_type=pl.DeviceIdType.MESH,
        )
        return [(None, copy)]

    def perform(pairs, action):
        for condition, copy in pairs:
            if condition is None:
                getattr(copy, action)()
            else:
                pl.when(condition)(getattr(copy, action))

    copied = set()
    for action, job, step in plan:
        steps = lanes_of(jobs[job][1], depth_z)
        if action == "start":
            if steps[step][0] != steps[0][0] and job not in copied:
                own[job].wait()
                copied.add(job)
            perform(copies(job, step, False), "start")
        else:
            perform(copies(job, step, True), "wait_recv")
    for action, job, step in plan:
        if action == "start":
            perform(copies(job, step, False), "wait_send")


def lanes_of(kind, depth_z):
    steps = []
    for name in kind:
        steps += [(name, reach) for reach in range(1, depth_z if name == "z" else 2)]
    return steps


def spread_whole(shards, jobs, collective_id):
    depth_z = lax.axis_size("dp") // 2
    costs = []
    for array, kind, first, size in jobs:
        held, steps = shards[array].shape[0] * size, []
        for lane in kind:
            cost = 23.0 if lane != "core" else 3.4
            steps += [(lane, held * 2e-6 * cost)] * (depth_z - 1 if lane == "z" else 1)
            held *= depth_z if lane == "z" else 2
        costs.append(steps)
    plan = order_steps(costs)
    sizes = {"z": depth_z, "x": 2, "y": 2, "core": 2}
    kinds = {array: kind for array, kind, _, _ in jobs}
    shapes = [
        tuple(sizes[name] for name in ("z", "x", "y", "core") if name in kinds[array])
        + shard.shape
        for array, shard in enumerate(shards)
    ]
    numbers = len(jobs) * (2 * depth_z + 1)
    wholes = pl.pallas_call(
        partial(spread_kernel, plan, jobs, depth_z),
        out_shape=tuple(jax.ShapeDtypeStruct(shape, jnp.bfloat16) for shape in shapes),
        in_specs=[pl.BlockSpec(memory_space=pltpu.VMEM)] * len(shards),
        out_specs=(pl.BlockSpec(memory_space=pl.ANY),) * len(shards),
        scratch_shapes=[
            pltpu.SemaphoreType.DMA((numbers,)),
            pltpu.SemaphoreType.DMA((numbers,)),
            pltpu.SemaphoreType.DMA((len(jobs),)),
        ],
        compiler_params=pltpu.CompilerParams(
            collective_id=collective_id, has_side_effects=True, vmem_limit_bytes=60 * 2**20
        ),
    )(*shards)
    return [whole.reshape(-1, whole.shape[-1]) for whole in wholes]


BYTE_LANES = ("z", "x", "y", "core")
MAIN_LANES = ("z", "x")


def sum_kernel(plan, kinds, sources, depth_z, *refs):
    count = len(kinds)
    pieces_in = [[refs[number] for number, _ in parts] for parts in sources]
    total_in = sum(len(parts) for parts in sources)
    grads, extra = [parts[0] for parts in pieces_in], refs[total_in]
    outputs = refs[total_in + 1 : total_in + 1 + count]
    totals = refs[total_in + 1 + count]
    rest = list(refs[total_in + 2 + count :])
    coordinates = here()
    places = dict(zip(BYTE_LANES, coordinates))
    z = coordinates[0]
    mirrored = depth_z - 1 - z
    held, received, held_names, temporary = [], [], [], {}
    for job, kind in enumerate(kinds):
        held.append(rest.pop(0))
        received.append({lane: rest.pop(0) for lane in kind})
        held_names.append(names_held(kind, len(sources[job])))
    for key in temporary_shapes(kinds, sources, [ref.shape for ref in held]):
        temporary[key] = rest.pop(0)
    squares, arrivals, send_sems, receive_sems, own_sems, tile_sems = rest

    def slice_of(job, part):
        names = sources[job][part][1]
        spot = tuple(slice(None) if name in held_names[job] else places[name] for name in names)
        return pieces_in[job][part].at[spot]

    loads = []
    for job in range(count):
        loads.append(pltpu.make_async_copy(slice_of(job, 0), held[job], own_sems.at[job]))
        loads[-1].start()
    squares[...] = jnp.zeros_like(squares)
    greet(False, depth_z, coordinates)

    def prepare(job):
        loads[job].wait()
        for part in range(1, len(sources[job])):
            buffer = temporary[held[job].shape]
            copy = pltpu.make_async_copy(slice_of(job, part), buffer, own_sems.at[job])
            copy.start()
            copy.wait()
            lead, rows = held[job].shape[:-2], held[job].shape[-2]
            pieces = 1
            for size in lead:
                pieces *= size

            def piece(index, carry, buffer=buffer, lead=lead, rows=rows):
                spot, remainder = [], index
                for size in reversed(lead):
                    spot.insert(0, remainder % size)
                    remainder = remainder // size
                target, other = held[job].at[tuple(spot)], buffer.at[tuple(spot)]

                def row_step(number, inner):
                    part_rows = pl.ds(pl.multiple_of(number * 16, 16), 16)
                    target[part_rows, :] = to_low(
                        target[part_rows, :].astype(jnp.float32)
                        + other[part_rows, :].astype(jnp.float32)
                    )
                    return inner

                lax.fori_loop(0, rows // 16, row_step, 0)
                return carry

            lax.fori_loop(0, pieces, piece, 0)

    def chosen(job, step, lane_place):
        steps = lanes_of(kinds[job], depth_z)
        lane = steps[step][0]
        done = [name for name, _ in steps[:step] if name != lane]
        return [
            lane_place if name == lane else (places[name] if name in done else slice(None))
            for name in held_names[job]
        ]

    def slot(reach, side):
        shared = (depth_z - 2) // 2
        return reach - 1 if reach <= shared else shared + 2 * (reach - 1 - shared) + side

    def copies(job, step, receiving):
        kind = kinds[job]
        lane, reach = lanes_of(kind, depth_z)[step]
        base = job * (2 * depth_z + 1)
        if lane == "z":
            pairs = []
            for side, depth in enumerate((z, mirrored)):
                way = 1 - 2 * side
                aim = depth_z - reach + depth
                if side:
                    aim = depth_z - 1 - aim
                landing = received[job]["z"].at[slot(reach, side)]
                number = base + 2 * (reach - 1) + side
                source = landing if receiving else held[job].at[tuple(chosen(job, step, aim))]
                copy = pltpu.make_async_remote_copy(
                    src_ref=source,
                    dst_ref=landing,
                    send_sem=send_sems.at[number],
                    recv_sem=receive_sems.at[number],
                    device_id=beside(way, coordinates),
                    device_id_type=pl.DeviceIdType.MESH,
                )
                condition = (depth >= 1) & (depth <= reach) if receiving else depth <= reach - 1
                pairs.append((condition, copy))
            return pairs
        number = base + 2 * (depth_z - 1) + ("x", "y", "core").index(lane)
        if step == 0 and len(sources[job]) == 1:
            spot = tuple(
                1 - places[name] if name == lane else slice(None)
                for name in BYTE_LANES
                if name in kind
            )
            source = grads[job].at[spot]
        else:
            source = held[job].at[tuple(chosen(job, step, 1 - places[lane]))]
        copy = pltpu.make_async_remote_copy(
            src_ref=source,
            dst_ref=received[job][lane],
            send_sem=send_sems.at[number],
            recv_sem=receive_sems.at[number],
            device_id=partner(lane, 1, coordinates),
            device_id_type=pl.DeviceIdType.MESH,
        )
        return [(None, copy)]

    def add_pieces(job, step, lane_place, buffers, last):
        steps = lanes_of(kinds[job], depth_z)
        lane = steps[step][0]
        done = [name for name, _ in steps[:step] if name != lane]
        free = [name for name in BYTE_LANES if name in kinds[job] and name not in done + [lane]]
        sizes = [depth_z if name == "z" else 2 for name in free]
        pieces = 1
        for size in sizes:
            pieces *= size

        def piece(index, carry):
            spots, remainder = {}, index
            for name, size in reversed(list(zip(free, sizes))):
                spots[name] = remainder % size
                remainder = remainder // size
            mine = tuple(
                spots[name] if name in spots else (lane_place if name == lane else places[name])
                for name in held_names[job]
            )
            theirs = tuple(spots[name] for name in free)
            target = held[job].at[mine] if mine else held[job]
            arrived = [buffer.at[theirs] if theirs else buffer for buffer in buffers]
            rows, columns = target.shape[-2:]

            def row_step(number, inner):
                part = pl.ds(pl.multiple_of(number * 16, 16), 16)
                value = target[part, :].astype(jnp.float32)
                for other in arrived:
                    value = value + other[part, :].astype(jnp.float32)
                if last:
                    outputs[job][part, :] = value
                    square = jnp.zeros((16, 128), jnp.float32)
                    for first in range(0, columns, 128):
                        square = square + value[:, first : first + 128] * value[:, first : first + 128]
                    squares[...] += square
                else:
                    target[part, :] = to_low(value)
                return inner

            lax.fori_loop(0, rows // 16, row_step, 0)
            return carry

        if pieces == 1:
            piece(0, 0)
        else:
            lax.fori_loop(0, pieces, piece, 0)

    def accumulate(job, step):
        steps = lanes_of(kinds[job], depth_z)
        lane, reach = steps[step]
        last = step == len(steps) - 1
        if lane != "z":
            add_pieces(job, step, places[lane], [received[job][lane]], last)
            return
        buffers = [received[job]["z"].at[slot(reach, side)] for side in range(2)]
        if reach < depth_z - 1:
            for side, depth in enumerate((z, mirrored)):
                aim = depth_z - reach + depth - 1
                if side:
                    aim = depth_z - 1 - aim
                pl.when((depth >= 1) & (depth <= reach))(
                    partial(add_pieces, job, step, aim, [buffers[side]], False)
                )
            return
        ends = (z == 0) | (mirrored == 0)
        pl.when(jnp.logical_not(ends))(partial(add_pieces, job, step, z, buffers, last))
        pl.when(z == 0)(partial(add_pieces, job, step, z, buffers[1:], last))
        pl.when(mirrored == 0)(partial(add_pieces, job, step, z, buffers[:1], last))

    def perform(pairs, action):
        for condition, copy in pairs:
            if condition is None:
                getattr(copy, action)()
            else:
                pl.when(condition)(getattr(copy, action))

    loaded = set()
    for action, job, step in plan:
        lane = lanes_of(kinds[job], depth_z)[step][0]
        if job not in loaded and (action == "wait" or lane == "z" or len(sources[job]) > 1):
            prepare(job)
            loaded.add(job)
        if action == "start":
            perform(copies(job, step, False), "start")
        else:
            perform(copies(job, step, True), "wait_recv")
            accumulate(job, step)
    totals[...] = extra[...]
    totals[0:8, :] += squares[0:8, :] + squares[8:16, :]
    tiles = []
    for axis, size, first in (("tensor", 4, 0), ("dp", 2 * depth_z, 4)):
        spot = first + lax.axis_index(axis)
        arrivals[spot] = totals[...]
        for mask, device in enumerate(peers(axis, size), 1):
            tiles.append(
                pltpu.make_async_remote_copy(
                    src_ref=arrivals.at[spot],
                    dst_ref=arrivals.at[spot],
                    send_sem=tile_sems.at[2 * (first + mask)],
                    recv_sem=tile_sems.at[2 * (first + mask) + 1],
                    device_id=device,
                    device_id_type=pl.DeviceIdType.MESH,
                )
            )
            tiles[-1].start()
        for copy in tiles[1 - size :]:
            copy.wait_recv()
        result = arrivals[first]
        for place in range(1, size):
            result = result + arrivals[first + place]
        totals[...] = result
    for copy in tiles:
        copy.wait_send()
    for action, job, step in plan:
        if action == "start":
            perform(copies(job, step, False), "wait_send")


def names_held(kind, addends):
    return [
        name
        for name in BYTE_LANES
        if name in kind and (name == "z" or addends > 1 or name != kind[0])
    ]


def temporary_shapes(kinds, sources, shapes):
    return list(
        dict.fromkeys(
            tuple(shape) for shape, parts in zip(shapes, sources) if len(parts) > 1
        )
    )


def sum_whole(grads, kinds, extra, collective_id):
    depth_z = lax.axis_size("dp") // 2
    sizes = {"z": depth_z, "x": 2, "y": 2, "core": 2}
    jobs, arrays, shapes, scratch, sources, held_shapes = [], [], [], [], [], []
    for parts, kind in zip(grads, kinds):
        sources.append([])
        for array, names in parts:
            piece = array.shape[-2:]
            lead = tuple(sizes[name] for name in names)
            if array.ndim == 2:
                pieces = 1
                for size in lead:
                    pieces *= size
                piece = (array.shape[0] // pieces, array.shape[1])
            sources[-1].append((len(arrays), names))
            arrays.append(array.reshape(lead + piece))
        shapes.append(jax.ShapeDtypeStruct(piece, jnp.float32))
        steps, left = [], [name for name in BYTE_LANES if name in kind]
        held_shapes.append(tuple(sizes[name] for name in names_held(kind, len(parts))) + piece)
        scratch.append(pltpu.VMEM(held_shapes[-1], jnp.bfloat16))
        for lane in kind:
            left.remove(lane)
            rest = tuple(sizes[name] for name in left)
            extent = piece[0] * piece[1]
            for size in rest:
                extent *= size
            cost = 23.0 if lane != "core" else 3.4
            steps += [(lane, extent * 2e-6 * cost)] * (depth_z - 1 if lane == "z" else 1)
            lead = (2 * (depth_z - 1) - (depth_z - 2) // 2,) if lane == "z" else ()
            scratch.append(pltpu.VMEM(lead + rest + piece, jnp.bfloat16))
        jobs.append(steps)
    scratch += [
        pltpu.VMEM(shape, jnp.bfloat16)
        for shape in temporary_shapes(kinds, sources, held_shapes)
    ]
    plan = order_steps(jobs)
    numbers = len(grads) * (2 * depth_z + 1)
    tile = jax.ShapeDtypeStruct(extra.shape, jnp.float32)
    places = 4 + 2 * depth_z
    return pl.pallas_call(
        partial(sum_kernel, plan, kinds, sources, depth_z),
        out_shape=tuple(shapes) + (tile,),
        in_specs=[pl.BlockSpec(memory_space=pl.ANY)] * len(arrays)
        + [pl.BlockSpec(memory_space=pltpu.VMEM)],
        out_specs=(pl.BlockSpec(memory_space=pltpu.VMEM),) * (len(grads) + 1),
        scratch_shapes=scratch
        + [
            pltpu.VMEM((16, 128), jnp.float32),
            pltpu.VMEM((places, 16, 128), jnp.float32),
            pltpu.SemaphoreType.DMA((numbers,)),
            pltpu.SemaphoreType.DMA((numbers,)),
            pltpu.SemaphoreType.DMA((len(grads),)),
            pltpu.SemaphoreType.DMA((2 * places,)),
        ],
        compiler_params=pltpu.CompilerParams(
            collective_id=collective_id, has_side_effects=True, vmem_limit_bytes=60 * 2**20
        ),
    )(*arrays, extra)


def take(value_entries, axis, index):
    return lax.dynamic_index_in_dim(value_entries, index, axis, keepdims=False)


def total(addends):
    result = addends[0].astype(jnp.float32)
    for addend in addends[1:]:
        result = result + addend.astype(jnp.float32)
    return result


def add_everywhere(value_entries):
    for axis in ("tensor", "dp"):
        for mask in bit_masks(lax.axis_size(axis)):
            value_entries = value_entries + swap(value_entries, axis, mask)
    return value_entries


def gather_rows(value_entries):
    pieces = [value_entries]
    for mask in reversed(bit_masks(lax.axis_size("tensor"))):
        pieces = pieces + [swap(piece, "tensor", mask) for piece in pieces]
    return jnp.concatenate(pieces, axis=0)


def total_lines(value_entries):
    size = lax.axis_size("tensor")
    rows = value_entries.shape[0] // size
    pieces = [to_low(value_entries[i * rows : (i + 1) * rows]) for i in range(size)]
    for mask in bit_masks(size):
        half = len(pieces) // 2
        pieces = [
            pieces[i].astype(jnp.float32)
            + swap(to_low(pieces[half + i]), "tensor", mask).astype(jnp.float32)
            for i in range(half)
        ]
    return pieces[0]


gather_grads = gather_rows
sum_grads = total_lines


def low_dot(left, right, left_dim, right_dim):
    return lax.dot_general(
        left, right, (((left_dim,), (right_dim,)), ((), ())), preferred_element_type=jnp.float32
    )


def sigmoid(value_entries):
    return 0.5 * jnp.tanh(0.5 * value_entries) + 0.5


def fold_rows(value_entries):
    return jnp.sum(value_entries.reshape(-1, 8, value_entries.shape[1]), axis=0)


def lower_ones():
    rows = lax.broadcasted_iota(jnp.int32, (ssd_block, ssd_block), 0)
    columns = lax.broadcasted_iota(jnp.int32, (ssd_block, ssd_block), 1)
    return (rows >= columns).astype(jnp.float32)


FORWARD_UNROLL = 4
BACKWARD_UNROLL = 4
PROJ_WIDE = 2 * INNER + 2 * STATE + 128


def step_terms(raw_steps, decay_refs):
    shifted = raw_steps + decay_refs[1:2, :]
    steps = softplus(shifted)
    rates = -jnp.exp(decay_refs[0:1, :])
    cumulative = jnp.dot(
        lower_ones(), steps * rates, precision=deepest_tier, preferred_element_type=jnp.float32
    )
    return shifted, steps, rates, cumulative


def head_tables():
    chosen = to_low(jnp.arange(INNER)[:, None] // HEADDIM == jnp.arange(ssd_block)[None, :])
    later = jnp.where(
        jnp.arange(ssd_block)[:, None] >= jnp.arange(ssd_block)[None, :], 0.0, -1e30
    )
    return chosen, later


def first_head():
    return lax.broadcasted_iota(jnp.int32, (ssd_block, ssd_block), 1) < HEADDIM


def both_heads(value_entries):
    mask = first_head()
    zeros = jnp.zeros_like(value_entries)
    return jnp.concatenate(
        [jnp.where(mask, value_entries, zeros), jnp.where(mask, zeros, value_entries)], axis=0
    )


def spread_heads(steps, cumulative, turned, wide, narrow):
    blank = jnp.zeros((ssd_block, ssd_block - MHEADS), jnp.float32)
    turned[...] = jnp.concatenate([cumulative, blank], axis=1).T
    mask = first_head()

    def over_lanes(value_entries, head):
        return jnp.broadcast_to(value_entries[:, head : head + 1], (ssd_block, ssd_block))

    for head in range(MHEADS):
        wide[head] = over_lanes(cumulative, head)
    for pair in range(MHEADS // 2):
        narrow[:, pair * ssd_block : (pair + 1) * ssd_block] = jnp.where(
            mask, over_lanes(steps, 2 * pair), over_lanes(steps, 2 * pair + 1)
        )


def gaps_of(wide, turned, later, head):
    return jnp.exp((wide[head] - turned[pl.ds(head, 1), :]) + later[...])


def quad_cumulative(wide, quad):
    mask = first_head()
    return jnp.concatenate(
        [
            jnp.where(mask, wide[4 * quad], wide[4 * quad + 1]),
            jnp.where(mask, wide[4 * quad + 2], wide[4 * quad + 3]),
        ],
        axis=1,
    )


def quad_lanes(quad, first=0):
    return pl.ds(pl.multiple_of(quad * 2 * ssd_block + first, ssd_block), 2 * ssd_block)


def lanes(block):
    return pl.ds(pl.multiple_of(block * ssd_block, ssd_block), ssd_block)


def convolve(padded_ref, taps_ref, columns):
    result = taps_ref[0:1, columns] * padded_ref[5 : 5 + ssd_block, columns]
    for tap in range(1, 4):
        result = result + taps_ref[tap : tap + 1, columns] * padded_ref[
            5 + tap : 5 + tap + ssd_block, columns
        ]
    return result


def middle_kernel(
    projected,
    taps,
    skip,
    decay,
    gain,
    later,
    middle,
    outcome,
    starts,
    padded,
    turned,
    wide,
    narrow,
    state,
    gated,
):
    chunk = pl.program_id(0)
    streams_extent = INNER + 2 * STATE

    @pl.when(chunk == 0)
    def _():
        padded[0:8, :] = jnp.zeros((8, streams_extent), jnp.float32)
        state[...] = jnp.zeros_like(state)

    @pl.when(chunk > 0)
    def _():
        padded[0:8, :] = padded[ssd_block : ssd_block + 8, :]

    padded[8 : 8 + ssd_block, :] = projected[:, INNER : INNER + streams_extent]
    _, steps, _, cumulative = step_terms(
        projected[:, INNER + streams_extent : INNER + streams_extent + MHEADS], decay
    )
    spread_heads(steps, cumulative, turned, wide, narrow)

    def active(columns):
        convolved = convolve(padded, taps, columns)
        return convolved * sigmoid(convolved)

    in_map = active(pl.ds(INNER, STATE))
    in_low = to_low(in_map)
    in_turned = to_low(in_map.T)
    out_low = to_low(active(pl.ds(INNER + STATE, STATE)))
    affinity = low_dot(out_low, in_low, 1, 1)

    def quad_step(quad, square_sum):
        columns = quad_lanes(quad)
        inputs = active(columns)
        weighted = inputs * narrow[:, columns]
        weighted_low = to_low(weighted)
        within = []
        for pair in range(2):
            head = 4 * quad + 2 * pair
            mixing = jnp.concatenate(
                [
                    to_low(affinity * gaps_of(wide, turned, later, head)),
                    to_low(affinity * gaps_of(wide, turned, later, head + 1)),
                ],
                axis=1,
            )
            part = weighted_low[:, pair * ssd_block : (pair + 1) * ssd_block]
            within.append(low_dot(mixing, both_heads(part), 1, 0))
        within = jnp.concatenate(within, axis=1)
        cumulative_here = quad_cumulative(wide, quad)
        last = cumulative_here[ssd_block - 1 :, :]
        held = state[:, columns]
        starts[0, :, columns] = held
        across = jnp.exp(cumulative_here) * low_dot(out_low, to_low(held), 1, 0)
        to_end = to_low(weighted * jnp.exp(last - cumulative_here))
        state[:, columns] = jnp.exp(last) * held + low_dot(in_turned, to_end, 1, 0)
        result = within + across + inputs * skip[:, columns]
        outcome[:, columns] = result
        gate = projected[:, columns]
        product = result * (gate * sigmoid(gate))
        gated[:, columns] = product
        return square_sum + product * product

    square_sum = lax.fori_loop(
        0,
        INNER // (2 * ssd_block),
        quad_step,
        jnp.zeros((ssd_block, 2 * ssd_block), jnp.float32),
        unroll=FORWARD_UNROLL,
    )
    scale = lax.rsqrt(jnp.sum(square_sum, axis=1, keepdims=True) * (1.0 / INNER) + norm_eps)

    def scale_step(quad, carry):
        columns = quad_lanes(quad)
        middle[:, columns] = to_low(gated[:, columns] * scale * gain[:, columns])
        return carry

    lax.fori_loop(0, INNER // (2 * ssd_block), scale_step, 0, unroll=2)


def middle_slope_kernel(
    projected,
    earlier,
    outcome,
    starts,
    slope,
    taps,
    skip,
    decay,
    gain,
    chosen,
    later,
    slope_projected,
    slope_taps,
    slope_skip,
    slope_gain,
    slope_decay,
    padded,
    turned,
    wide,
    narrow,
    slope_state,
    slope_conv,
    slope_affinity,
    slope_maps,
    slope_cumulative,
    slope_steps,
):
    chunk = pl.num_programs(0) - 1 - pl.program_id(0)
    streams_extent = INNER + 2 * STATE
    quads = INNER // (2 * ssd_block)

    @pl.when(pl.program_id(0) == 0)
    def _():
        slope_state[...] = jnp.zeros_like(slope_state)
        slope_conv[ssd_block : ssd_block + 8, :] = jnp.zeros((8, streams_extent), jnp.float32)
        slope_taps[...] = jnp.zeros_like(slope_taps)
        slope_skip[...] = jnp.zeros_like(slope_skip)
        slope_gain[...] = jnp.zeros_like(slope_gain)
        slope_decay[...] = jnp.zeros_like(slope_decay)

    @pl.when(pl.program_id(0) > 0)
    def _():
        slope_conv[ssd_block : ssd_block + 8, :] = slope_conv[0:8, :]

    @pl.when(chunk == 0)
    def _():
        padded[0:8, :] = jnp.zeros((8, streams_extent), jnp.float32)

    @pl.when(chunk > 0)
    def _():
        padded[0:8, :] = earlier[:, INNER : INNER + streams_extent]

    padded[8 : 8 + ssd_block, :] = projected[:, INNER : INNER + streams_extent]
    slope_affinity[...] = jnp.zeros_like(slope_affinity)
    slope_maps[...] = jnp.zeros_like(slope_maps)
    slope_cumulative[...] = jnp.zeros_like(slope_cumulative)
    slope_steps[...] = jnp.zeros_like(slope_steps)
    shifted, steps, rates, cumulative = step_terms(
        projected[:, INNER + streams_extent : INNER + streams_extent + MHEADS], decay
    )
    spread_heads(steps, cumulative, turned, wide, narrow)

    def silu_pair(value_entries):
        share = sigmoid(value_entries)
        return value_entries * share, share * (1.0 + value_entries * (1.0 - share))

    def pull_convolved(columns, target_columns, slope_block):
        slope_conv[0:ssd_block, columns] = slope_block
        result = taps[3:4, columns] * slope_block
        for tap in range(3):
            reach = 3 - tap
            result = result + taps[tap : tap + 1, columns] * slope_conv[
                reach : reach + ssd_block, columns
            ]
        for tap in range(4):
            slope_taps[tap, :, columns] += fold_rows(
                slope_block * padded[5 + tap : 5 + tap + ssd_block, columns]
            )
        slope_projected[:, target_columns] = to_low(result)

    maps = (pl.ds(INNER, STATE), pl.ds(INNER + STATE, STATE))
    in_map, in_pull = silu_pair(convolve(padded, taps, maps[0]))
    out_map, out_pull = silu_pair(convolve(padded, taps, maps[1]))
    in_low, out_low, out_turned = to_low(in_map), to_low(out_map), to_low(out_map.T)
    affinity = low_dot(out_low, in_low, 1, 1)
    mask = first_head()

    def sums_step(quad, sums):
        columns = quad_lanes(quad)
        gate = projected[:, columns]
        product = outcome[:, columns] * (gate * sigmoid(gate))
        return (
            sums[0] + product * product,
            sums[1] + product * (slope[:, columns] * gain[:, columns]),
        )

    blank = jnp.zeros((ssd_block, 2 * ssd_block), jnp.float32)
    squares, crossed = lax.fori_loop(0, quads, sums_step, (blank, blank), unroll=2)
    scale = lax.rsqrt(jnp.sum(squares, axis=1, keepdims=True) * (1.0 / INNER) + norm_eps)
    pulled = scale * scale * scale * (jnp.sum(crossed, axis=1, keepdims=True) * (1.0 / INNER))

    def quad_step(quad, carry):
        columns = quad_lanes(quad)
        gate, total_here = projected[:, columns], outcome[:, columns]
        gate_value, gate_pull = silu_pair(gate)
        product = total_here * gate_value
        slope_here = slope[:, columns]
        slope_gain[:, columns] += fold_rows(slope_here * product * scale)
        slope_product = scale * (slope_here * gain[:, columns]) - product * pulled
        slope_out = slope_product * gate_value
        slope_projected[:, columns] = to_low(slope_product * total_here * gate_pull)
        inputs, inputs_pull = silu_pair(convolve(padded, taps, columns))
        slope_skip[:, columns] += fold_rows(slope_out * inputs)
        skip_here = skip[:, columns]
        scanned = total_here - inputs * skip_here
        steps_here = narrow[:, columns]
        weighted = inputs * steps_here
        weighted_low = to_low(weighted)
        slope_low = to_low(slope_out)
        slope_within = []
        for pair in range(2):
            head = 4 * quad + 2 * pair
            here_low = slope_low[:, pair * ssd_block : (pair + 1) * ssd_block]
            part = weighted_low[:, pair * ssd_block : (pair + 1) * ssd_block]
            slope_mixing = low_dot(here_low, both_heads(part), 1, 1)
            mixing = []
            for side in range(2):
                gaps = gaps_of(wide, turned, later, head + side)
                mixing.append(to_low(affinity * gaps))
                slope_affinity[...] += (
                    slope_mixing[:, side * ssd_block : (side + 1) * ssd_block] * gaps
                )
            turned_back = low_dot(jnp.concatenate(mixing, axis=1), here_low, 0, 0)
            slope_within.append(
                jnp.where(mask, turned_back[:ssd_block], turned_back[ssd_block:])
            )
        slope_within = jnp.concatenate(slope_within, axis=1)
        cumulative_here = quad_cumulative(wide, quad)
        last = cumulative_here[ssd_block - 1 :, :]
        decayed = jnp.exp(last)
        held = starts[0, :, columns]
        slope_across = to_low(slope_out * jnp.exp(cumulative_here))
        slope_maps[1] += low_dot(slope_across, to_low(held), 1, 1)
        carried_state = slope_state[:, columns]
        carried_low = to_low(carried_state)
        to_end = jnp.exp(last - cumulative_here)
        ending = to_low(weighted * to_end)
        slope_ending = low_dot(in_low, carried_low, 1, 0)
        slope_maps[0] += low_dot(ending, carried_low, 1, 1)
        slope_state[:, columns] = decayed * carried_state + low_dot(out_turned, slope_across, 1, 0)
        slope_weighted = slope_within + slope_ending * to_end
        ending_slope = slope_ending * ending.astype(jnp.float32)
        ends = jnp.sum(ending_slope, axis=0, keepdims=True) + decayed * jnp.sum(
            carried_state * held, axis=0, keepdims=True
        )
        rows = lax.broadcasted_iota(jnp.int32, (ssd_block, 2 * ssd_block), 0)
        slope_gathered = (
            slope_low.astype(jnp.float32) * scanned
            - weighted_low.astype(jnp.float32) * slope_within
            - ending_slope
            + jnp.where(rows == ssd_block - 1, ends, 0.0)
        )
        high = to_low(slope_gathered)
        rest = to_low(slope_gathered - high.astype(jnp.float32))
        parts = [high, rest, to_low(slope_weighted * inputs)]
        sums = low_dot(jnp.concatenate(parts, axis=0), chosen[columns, :], 1, 0)
        slope_cumulative[...] += sums[:ssd_block] + sums[ssd_block : 2 * ssd_block]
        slope_steps[...] += sums[2 * ssd_block :]
        slope_inputs = slope_out * skip_here + slope_weighted * steps_here
        pull_convolved(columns, quad_lanes(quad, INNER), slope_inputs * inputs_pull)
        return carry

    lax.fori_loop(0, quads, quad_step, 0, unroll=BACKWARD_UNROLL)
    affinity_low = to_low(slope_affinity[...])
    slope_in = slope_maps[0] + low_dot(affinity_low, out_low, 0, 0)
    slope_out_map = slope_maps[1] + low_dot(affinity_low, in_low, 1, 0)
    pull_convolved(maps[0], pl.ds(2 * INNER, STATE), slope_in * in_pull)
    pull_convolved(maps[1], pl.ds(2 * INNER + STATE, STATE), slope_out_map * out_pull)
    slope_changes = lax.dot_general(
        lower_ones(),
        slope_cumulative[...],
        (((0,), (0,)), ((), ())),
        precision=deepest_tier,
        preferred_element_type=jnp.float32,
    )[:, :MHEADS]
    slope_step = slope_steps[:, :MHEADS] + slope_changes * rates
    slope_raw = slope_step * sigmoid(shifted)
    slope_decay[0] += fold_rows(slope_changes * steps) * rates
    slope_decay[1] += fold_rows(slope_raw)
    slope_projected[:, INNER + streams_extent :] = jnp.concatenate(
        [to_low(slope_raw), jnp.zeros((ssd_block, 128 - MHEADS), jnp.bfloat16)], axis=1
    )


def fixed(shape):
    return pl.BlockSpec(shape, lambda chunk: (0,) * len(shape))


def middle_forward(projected, smalls):
    conv_taps, skip_gain, a_log, dt_bias, gated_gain = smalls
    chosen, later = head_tables()
    extent, columns = projected.shape
    chunks = extent // ssd_block
    streams_extent = INNER + 2 * STATE
    return pl.pallas_call(
        middle_kernel,
        grid=(chunks,),
        out_shape=(
            jax.ShapeDtypeStruct((extent, INNER), jnp.bfloat16),
            jax.ShapeDtypeStruct((extent, INNER), jnp.float32),
            jax.ShapeDtypeStruct((chunks, STATE, INNER), jnp.float32),
        ),
        in_specs=[
            pl.BlockSpec((ssd_block, columns), lambda chunk: (chunk, 0)),
            fixed((4, streams_extent)),
            fixed((1, INNER)),
            fixed((2, MHEADS)),
            fixed((1, INNER)),
            fixed(later.shape),
        ],
        out_specs=(
            pl.BlockSpec((ssd_block, INNER), lambda chunk: (chunk, 0)),
            pl.BlockSpec((ssd_block, INNER), lambda chunk: (chunk, 0)),
            pl.BlockSpec((1, STATE, INNER), lambda chunk: (chunk, 0, 0)),
        ),
        scratch_shapes=[
            pltpu.VMEM((ssd_block + 8, streams_extent), jnp.float32),
            pltpu.VMEM((ssd_block, ssd_block), jnp.float32),
            pltpu.VMEM((MHEADS, ssd_block, ssd_block), jnp.float32),
            pltpu.VMEM((ssd_block, INNER), jnp.float32),
            pltpu.VMEM((STATE, INNER), jnp.float32),
            pltpu.VMEM((ssd_block, INNER), jnp.float32),
        ],
        compiler_params=pltpu.CompilerParams(vmem_limit_bytes=48 * 2**20),
        cost_estimate=pl.CostEstimate(
            flops=2 * 10**10, transcendentals=4 * 10**6, bytes_accessed=20 * 10**6
        ),
    )(
        projected,
        conv_taps,
        skip_gain.reshape(1, INNER),
        jnp.stack([a_log, dt_bias]),
        gated_gain.reshape(1, INNER),
        later,
    )


def middle_backward(projected, outcome, starts, slope, smalls):
    conv_taps, skip_gain, a_log, dt_bias, gated_gain = smalls
    chosen, later = head_tables()
    extent, columns = projected.shape
    chunks = extent // ssd_block
    streams_extent = INNER + 2 * STATE

    def back(chunk):
        return (chunks - 1 - chunk, 0)

    slope_projected, slope_taps, slope_skip, slope_gain, slope_decay = pl.pallas_call(
        middle_slope_kernel,
        grid=(chunks,),
        out_shape=(
            jax.ShapeDtypeStruct((extent, columns), jnp.bfloat16),
            jax.ShapeDtypeStruct((4, 8, streams_extent), jnp.float32),
            jax.ShapeDtypeStruct((8, INNER), jnp.float32),
            jax.ShapeDtypeStruct((8, INNER), jnp.float32),
            jax.ShapeDtypeStruct((2, 8, MHEADS), jnp.float32),
        ),
        in_specs=[
            pl.BlockSpec((ssd_block, columns), back),
            pl.BlockSpec(
                (8, columns),
                lambda chunk: (jnp.maximum((chunks - 1 - chunk) * (ssd_block // 8) - 1, 0), 0),
            ),
            pl.BlockSpec((ssd_block, INNER), back),
            pl.BlockSpec((1, STATE, INNER), lambda chunk: (chunks - 1 - chunk, 0, 0)),
            pl.BlockSpec((ssd_block, INNER), back),
            fixed((4, streams_extent)),
            fixed((1, INNER)),
            fixed((2, MHEADS)),
            fixed((1, INNER)),
            fixed(chosen.shape),
            fixed(later.shape),
        ],
        out_specs=(
            pl.BlockSpec((ssd_block, columns), back),
            fixed((4, 8, streams_extent)),
            fixed((8, INNER)),
            fixed((8, INNER)),
            fixed((2, 8, MHEADS)),
        ),
        scratch_shapes=[
            pltpu.VMEM((ssd_block + 8, streams_extent), jnp.float32),
            pltpu.VMEM((ssd_block, ssd_block), jnp.float32),
            pltpu.VMEM((MHEADS, ssd_block, ssd_block), jnp.float32),
            pltpu.VMEM((ssd_block, INNER), jnp.float32),
            pltpu.VMEM((STATE, INNER), jnp.float32),
            pltpu.VMEM((ssd_block + 8, streams_extent), jnp.float32),
            pltpu.VMEM((ssd_block, ssd_block), jnp.float32),
            pltpu.VMEM((2, ssd_block, STATE), jnp.float32),
            pltpu.VMEM((ssd_block, ssd_block), jnp.float32),
            pltpu.VMEM((ssd_block, ssd_block), jnp.float32),
        ],
        compiler_params=pltpu.CompilerParams(vmem_limit_bytes=48 * 2**20),
        cost_estimate=pl.CostEstimate(
            flops=5 * 10**10, transcendentals=8 * 10**6, bytes_accessed=30 * 10**6
        ),
    )(
        projected,
        projected,
        outcome,
        starts,
        slope,
        conv_taps,
        skip_gain.reshape(1, INNER),
        jnp.stack([a_log, dt_bias]),
        gated_gain.reshape(1, INNER),
        chosen,
        later,
    )
    slope_decay = jnp.sum(slope_decay, axis=1)
    return (
        slope_projected,
        (
            jnp.sum(slope_taps, axis=1),
            jnp.sum(slope_skip, axis=0),
            slope_decay[0],
            slope_decay[1],
            jnp.sum(slope_gain, axis=0),
        ),
    )


Y_LANE = (("tensor", 2),)


def mixer_forward(value_entries, w_in, exit_matrix, block_gain, smalls):
    rescaled_rows, rescale_grad = jax.vjp(root_mean_rescale, value_entries, block_gain)
    normed_low = to_low(rescaled_rows)
    projected = matmul_apply(normed_low, w_in)
    middle_low, outcome, starts = middle_forward(projected, smalls)
    return (
        value_entries + matmul_apply(middle_low, exit_matrix),
        (rescale_grad, normed_low, (projected, outcome, starts), middle_low),
    )


def mixer_backward(conductor, last, slope_emitted, kept, w_in, exit_matrix, smalls):
    rescale_grad, normed_low, middle_kept, middle_low = kept
    grad_low = to_low(slope_emitted)
    slope_exit_matrix = to_low(product_tn(middle_low, grad_low))
    job_out = conductor.add(Summing(slope_exit_matrix, True))
    slope_middle = product_nt(grad_low, exit_matrix)
    slope_middle = conductor.tick(after(slope_middle, [slope_exit_matrix]), 7.0)
    grad_proj, slope_smalls = middle_backward(*middle_kept, slope_middle, smalls)
    grad_proj = conductor.tick(grad_proj, 60.0 if last else 44.0, limit=0 if last else 5)
    grad_w_in = to_low(product_tn(normed_low, grad_proj))
    job_in = conductor.add(Summing(grad_w_in, True))
    grad_proj = conductor.tick(after(grad_proj, [grad_w_in]), 7.0, limit=0 if last else 5)
    grad_values, slope_scale = rescale_grad(product_nt(grad_proj, w_in))
    slope_value = conductor.tick(grad_values + slope_emitted, 10.0, Y_LANE, limit=0 if last else 5)
    return (slope_value, slope_scale, slope_smalls, (job_out, job_in))


def head_mask(head, extent):
    columns = lax.broadcasted_iota(jnp.int32, (1, extent), 1)
    inside = (columns >= head * HD) & (columns < (head + 1) * HD)
    return jnp.where(inside, 1.0, 0.0).astype(jnp.bfloat16)


def head_weights(queries, key_rows):
    scores = low_dot(queries, key_rows, 1, 1) * HD ** (-0.5)
    rows = lax.broadcasted_iota(jnp.int32, (MAX_PIECES, MAX_PIECES), 0)
    columns = lax.broadcasted_iota(jnp.int32, (MAX_PIECES, MAX_PIECES), 1)
    scores = jnp.where(rows >= columns, scores, -jnp.inf)
    exponents = jnp.exp(scores - jnp.max(scores, axis=-1, keepdims=True))
    return exponents / jnp.sum(exponents, axis=-1, keepdims=True)


def attend_kernel(triple, output):
    extent = output.shape[1]
    queries, key_rows = triple[:, :extent], triple[:, extent : 2 * extent]
    value_rows = triple[:, 2 * extent :]
    attended = jnp.zeros(output.shape, jnp.float32)
    for head in range(extent // HD):
        mask = head_mask(head, extent)
        weights = to_low(head_weights(queries * mask, key_rows))
        attended = attended + low_dot(weights, value_rows * mask, 1, 0)
    output[...] = to_low(attended)


def attend_slope_kernel(triple, slope, output):
    extent = slope.shape[1]
    queries, key_rows = triple[:, :extent], triple[:, extent : 2 * extent]
    value_rows = triple[:, 2 * extent :]
    slope_here = slope[...]
    slopes = [jnp.zeros(slope.shape, jnp.float32)] * 3
    for head in range(extent // HD):
        mask = head_mask(head, extent)
        weights = head_weights(queries * mask, key_rows)
        slope_masked = slope_here * mask
        slope_weights = low_dot(slope_masked, value_rows, 1, 1)
        slope_scores = to_low(
            weights
            * (slope_weights - jnp.sum(weights * slope_weights, axis=-1, keepdims=True))
        )
        slopes[0] = slopes[0] + low_dot(slope_scores, key_rows * mask, 1, 0)
        slopes[1] = slopes[1] + low_dot(slope_scores, queries * mask, 0, 0)
        slopes[2] = slopes[2] + low_dot(to_low(weights), slope_masked, 0, 0)
    output[:, :extent] = to_low(slopes[0] * HD ** (-0.5))
    output[:, extent : 2 * extent] = to_low(slopes[1] * HD ** (-0.5))
    output[:, 2 * extent :] = to_low(slopes[2])


def by_sequence(kernel, columns, *arrays):
    rows = arrays[0].shape[0]
    return pl.pallas_call(
        kernel,
        grid=(rows // MAX_PIECES,),
        out_shape=jax.ShapeDtypeStruct((rows, columns), jnp.bfloat16),
        in_specs=[
            pl.BlockSpec((MAX_PIECES, array.shape[1]), lambda group: (group, 0)) for array in arrays
        ],
        out_specs=pl.BlockSpec((MAX_PIECES, columns), lambda group: (group, 0)),
        compiler_params=pltpu.CompilerParams(vmem_limit_bytes=24 * 2**20),
        cost_estimate=pl.CostEstimate(
            flops=3 * 10**9, transcendentals=3 * 10**5, bytes_accessed=4 * 10**6
        ),
    )(*arrays)


def apply_heads(latent_holder, heed_scale, triple_matrix, exit_matrix):
    rescaled_rows, rescale_grad = jax.vjp(root_mean_rescale, latent_holder, heed_scale)
    rows_low = gather_rows(to_low(rescaled_rows))
    triple = to_low(matmul_apply(rows_low, triple_matrix))
    heads_output = by_sequence(attend_kernel, triple.shape[1] // 3, triple)
    outcome = latent_holder + total_lines(product_nt(heads_output, exit_matrix))
    return outcome, (rescale_grad, rows_low, triple, heads_output)


def apply_heads_grad(conductor, slope_emitted, kept, triple_matrix, exit_matrix):
    rescale_grad, rows_low, triple, heads_output = kept
    grad_rows = conductor.tick(gather_grads(to_low(slope_emitted)), 12.0, Y_LANE)
    slope_exit_matrix = to_low(product_tn(grad_rows, heads_output))
    grad_attended = to_low(matmul_apply(grad_rows, exit_matrix))
    grad_triple = by_sequence(attend_slope_kernel, triple.shape[1], triple, grad_attended)
    grad_triple = conductor.tick(after(grad_triple, [slope_exit_matrix]), 10.0, Y_LANE)
    slope_rescaled = sum_grads(product_nt(grad_triple, triple_matrix))
    slope_triple_matrix = to_low(product_tn(rows_low, grad_triple))
    job_exit = conductor.add(Summing(slope_exit_matrix, False))
    job_triple = conductor.add(Summing(slope_triple_matrix, False))
    slope_rescaled = conductor.tick(
        after(slope_rescaled, [slope_triple_matrix]), 10.0, Y_LANE
    )
    gradient_holder, slope_scale = rescale_grad(slope_rescaled)
    return (gradient_holder + slope_emitted, slope_scale, job_triple, job_exit)


def swiglu(both):
    half = both.shape[1] // 2
    return jax.nn.silu(both[:, :half]) * both[:, half:]


def perceptron_apply(latent_holder, perceptron_scale, lift_matrix, lower_matrix):
    rescaled_rows, rescale_grad = jax.vjp(root_mean_rescale, latent_holder, perceptron_scale)
    rows_low = gather_rows(to_low(rescaled_rows))
    latent_state, act_pull = jax.vjp(swiglu, matmul_apply(rows_low, lift_matrix))
    latent_merged = to_low(latent_state)
    outcome = latent_holder + total_lines(product_nt(latent_merged, lower_matrix))
    return (outcome, (rescale_grad, rows_low, act_pull, latent_merged))


def perceptron_grad(conductor, slope_emitted, kept, lift_matrix, lower_matrix):
    rescale_grad, rows_low, act_pull, latent_merged = kept
    grad_rows = conductor.tick(gather_grads(to_low(slope_emitted)), 13.0, Y_LANE)
    slope_lower_matrix = to_low(product_tn(grad_rows, latent_merged))
    job_lower = conductor.add(Summing(slope_lower_matrix, False))
    grad_rows = conductor.tick(after(grad_rows, [slope_lower_matrix]), 2.0, Y_LANE)
    (grad_both,) = act_pull(matmul_apply(grad_rows, lower_matrix))
    grad_both = conductor.tick(to_low(grad_both), 4.0, Y_LANE)
    slope_rescaled = sum_grads(product_nt(grad_both, lift_matrix))
    half = grad_both.shape[1] // 2
    slope_lifts = [
        to_low(product_tn(rows_low, grad_both[:, :half])),
        to_low(product_tn(rows_low, grad_both[:, half:])),
    ]
    slope_lifts = [conductor.add(Summing(slope, False)) for slope in slope_lifts]
    slope_rescaled = conductor.tick(slope_rescaled, 14.0, Y_LANE)
    gradient_holder, slope_scale = rescale_grad(slope_rescaled)
    return (gradient_holder + slope_emitted, slope_scale, job_lower, slope_lifts)


def body(
    byte_ids,
    targets,
    boundaries,
    lengths,
    tables,
    tables_first,
    tables_second,
    mamba_in,
    mamba_in_first,
    mamba_in_second,
    mamba_out,
    mamba_out_first,
    mamba_out_second,
    route_proj,
    route_proj_first,
    route_proj_second,
    small_params,
    small_params_first,
    small_params_second,
    heed_triple_matrix,
    attn_qkv_first,
    attn_qkv_second,
    heed_exit_matrix,
    attn_out_first,
    attn_out_second,
    lifting_matrix,
    mlp_gate_up_first,
    mlp_gate_up_second,
    lowering_matrix,
    mlp_down_first,
    mlp_down_second,
):
    devices = lax.axis_size("dp") * lax.axis_size("tensor")
    table_rows = tables.shape[1]
    small_here = small_params.shape[0]
    mixed_rows = 2 * table_rows
    length_pair = jnp.stack([lengths[0] // 16, lengths[0] % 16]).astype(jnp.bfloat16)
    tail = jnp.concatenate([to_low(small_params), length_pair])
    mixed = jnp.concatenate(
        [
            to_low(tables).reshape(mixed_rows, BYTE_WIDTH),
            jnp.pad(tail, (0, mixed_rows * 128 - tail.shape[0])).reshape(mixed_rows, 128),
        ],
        axis=1,
    )

    def wide_in(layer):
        low = to_low(mamba_in[layer])
        return jnp.pad(low, ((0, 0), (0, PROJ_WIDE - low.shape[1])))

    conductor = Conductor()
    exact_tiles = mamba_in.shape[1] % 16 == 0
    shards = [
        mixed,
        wide_in(0),
        to_low(mamba_out[0]),
        to_low(route_proj),
        to_low(heed_triple_matrix).reshape(heed_triple_matrix.shape[0], -1),
        to_low(heed_exit_matrix).T,
        to_low(lifting_matrix).reshape(lifting_matrix.shape[0], -1),
        to_low(lowering_matrix).T,
        wide_in(1),
        to_low(mamba_out[1]),
    ]
    kinds = [BYTE_LANES] * 4 + [MAIN_LANES] * 4 + [BYTE_LANES] * 2
    if exact_tiles:
        fan, late = MAIN_LANES, MAIN_LANES[::-1]
        in_first, in_last = 18 * 128, PROJ_WIDE - 18 * 128
        half_route = route_proj.shape[1] // 2
        half_lift = shards[6].shape[1] // 2
        jobs = [
            (3, BYTE_LANES, half_route, half_route),
            (9, BYTE_LANES, 0, BYTE_WIDTH),
            (8, BYTE_LANES, 0, in_first),
            (0, BYTE_LANES, 0, BYTE_WIDTH + 128),
            (1, BYTE_LANES, in_first, in_last),
            (2, BYTE_LANES, 0, BYTE_WIDTH),
            (8, BYTE_LANES, in_first, in_last),
            (4, fan, 0, shards[4].shape[1]),
            (1, BYTE_LANES, 0, in_first),
            (6, fan, half_lift, half_lift),
            (3, BYTE_LANES, 0, half_route),
            (7, fan, 0, shards[7].shape[1]),
            (5, late, 0, shards[5].shape[1]),
            (6, late, 0, half_lift),
        ]
        wholes = spread_whole(shards, jobs, 0)
    else:
        wholes = [
            lax.all_gather(
                shard, ("dp", "tensor") if kind == BYTE_LANES else "dp", axis=0, tiled=True
            )
            for shard, kind in zip(shards, kinds)
        ]
    mixed_whole = wholes[0]
    full_in, full_out, full_route = [wholes[1], wholes[8]], [wholes[2], wholes[9]], wholes[3]
    triple_whole, heed_exit_whole, lift_matrix_whole, lower_matrix_whole = wholes[4:8]
    mixed_whole = mixed_whole.reshape(devices, mixed_rows, BYTE_WIDTH + 128)
    full_tables = (
        mixed_whole[:, :, :BYTE_WIDTH]
        .reshape(devices, 2, table_rows, BYTE_WIDTH)
        .transpose(1, 0, 2, 3)
        .reshape(2, VOCAB, BYTE_WIDTH)
    )
    tails = mixed_whole[:, :, BYTE_WIDTH:].reshape(devices, -1)
    full_small = tails[:, :small_here].reshape(-1)
    pairs = tails[:, small_here : small_here + 2].astype(jnp.float32)
    byte_count = jnp.sum(pairs[:, 0] * 16.0 + pairs[:, 1])
    (
        block_gains,
        gated_gains,
        core_scales,
        head_gain,
        blank_row,
        conv_taps,
        skip_gains,
        a_logs,
        dt_biases,
    ) = unpack_small(full_small.astype(jnp.float32))
    layer_smalls = [
        (
            conv_taps[layer_index],
            skip_gains[layer_index],
            a_logs[layer_index],
            dt_biases[layer_index],
            gated_gains[layer_index],
        )
        for layer_index in range(2)
    ]
    cut_marks = boundaries[0]
    seq_len = byte_ids.shape[1]
    vocab_ids = jnp.arange(VOCAB, dtype=jnp.int32)
    onehot_in = (byte_ids[0][:, None] == vocab_ids[None, :]).astype(jnp.bfloat16)
    embedded = matmul_apply(onehot_in, full_tables[0])
    packer_output, kept_enc = mixer_forward(
        embedded, full_in[0], full_out[0], block_gains[0], layer_smalls[0]
    )
    encoded_low = to_low(packer_output)
    directed_rows = matmul_apply(encoded_low, full_route)
    cut_likelihood, prob_pull = jax.vjp(
        route_prob, directed_rows[:, :BYTE_WIDTH], directed_rows[:, BYTE_WIDTH : 2 * BYTE_WIDTH]
    )
    select_items, broadcast_back = span_maps(cut_marks)
    latent_holder, merge_transpose = jax.vjp(
        partial(merge_into_pieces, select_items), packer_output, blank_row
    )
    latent_holder, saved_heeding = apply_heads(
        latent_holder, core_scales[0], triple_whole, heed_exit_whole
    )
    latent_holder, saved_perceptron = perceptron_apply(
        latent_holder, core_scales[1], lift_matrix_whole, lower_matrix_whole
    )
    unpacked_bytes, link_layers_grad = jax.vjp(
        partial(link_layers, select_items, broadcast_back, cut_marks),
        latent_holder,
        core_scales[2],
        cut_likelihood,
        directed_rows[:, 2 * BYTE_WIDTH :],
    )
    final_out, kept_dec = mixer_forward(
        unpacked_bytes, full_in[1], full_out[1], block_gains[1], layer_smalls[1]
    )
    head_in, head_pull = jax.vjp(root_mean_rescale, final_out, head_gain)
    head_low = to_low(head_in)
    logits = product_nt(head_low, full_tables[1])
    maxima = jnp.max(logits, axis=-1, keepdims=True)
    log_total = maxima + jnp.log(jnp.sum(jnp.exp(logits - maxima), axis=-1, keepdims=True))
    onehot_out = (targets[0][:, None] == vocab_ids[None, :]).astype(jnp.float32)
    counted = (jnp.arange(seq_len, dtype=jnp.int32) < lengths[0]).astype(jnp.float32)[:, None]
    loss_local = jnp.sum((log_total - logits) * onehot_out * counted)
    grad_logits = to_low((jnp.exp(logits - log_total) - onehot_out) * counted / byte_count)
    grad_table_out = product_tn(grad_logits, head_low)
    grad_final, grad_head_gain = head_pull(matmul_apply(grad_logits, full_tables[1]))
    slope_unpacked, grad_block_dec, grad_small_dec, jobs_dec = mixer_backward(
        conductor, False, grad_final, kept_dec, full_in[1], full_out[1], layer_smalls[1]
    )
    gradient_holder, slope_closing_scale, slope_likelihood, slope_shortcut = link_layers_grad(
        slope_unpacked
    )
    gradient_holder, slope_perceptron_scale, job_lower, slope_lifts = perceptron_grad(
        conductor, conductor.tick(gradient_holder, 14.0, Y_LANE), saved_perceptron, lift_matrix_whole, lower_matrix_whole
    )
    gradient_holder, slope_heed_scale, *jobs_heads = apply_heads_grad(
        conductor, gradient_holder, saved_heeding, triple_whole, heed_exit_whole
    )
    gradient_merged, gradient_blank = merge_transpose(gradient_holder)
    grad_query, grad_key = prob_pull(slope_likelihood)
    grad_routed = to_low(jnp.concatenate([grad_query, grad_key, slope_shortcut], axis=1))
    grad_routed = after(grad_routed, [gradient_merged])
    grad_route = to_low(product_tn(encoded_low, grad_routed))
    job_route = Summing(grad_route, True)
    grad_routed = conductor.tick(after(grad_routed, [grad_route]), 7.0)
    grad_embedded, grad_block_enc, grad_small_enc, jobs_enc = mixer_backward(
        conductor,
        True,
        gradient_merged + product_nt(grad_routed, full_route),
        kept_enc,
        full_in[0],
        full_out[0],
        layer_smalls[0],
    )
    embedded_high = to_low(grad_embedded)
    embedded_rest = to_low(grad_embedded - embedded_high.astype(jnp.float32))
    grad_table_in = product_tn(onehot_in, embedded_high) + product_tn(onehot_in, embedded_rest)
    grad_small = jnp.concatenate(
        [
            piece.reshape(-1)
            for piece in (
                jnp.stack([grad_block_enc, grad_block_dec]),
                jnp.stack([grad_small_enc[4], grad_small_dec[4]]),
                jnp.stack([slope_heed_scale, slope_perceptron_scale, slope_closing_scale]),
                grad_head_gain,
                gradient_blank,
                jnp.stack([grad_small_enc[0], grad_small_dec[0]]),
                jnp.stack([grad_small_enc[1], grad_small_dec[1]]),
                jnp.stack([grad_small_enc[2], grad_small_dec[2]]),
                jnp.stack([grad_small_enc[3], grad_small_dec[3]]),
            )
        ]
    )
    width = mamba_in.shape[2]
    grad_mixed = jnp.concatenate(
        [
            jnp.concatenate(
                [
                    to_low(grad_table_in).reshape(devices, table_rows, BYTE_WIDTH),
                    to_low(grad_table_out).reshape(devices, table_rows, BYTE_WIDTH),
                ],
                axis=1,
            ),
            jnp.pad(
                to_low(grad_small).reshape(devices, small_here),
                ((0, 0), (0, mixed_rows * 128 - small_here)),
            ).reshape(devices, mixed_rows, 128),
        ],
        axis=2,
    )
    conductor.close()
    parts = [
        jobs_heads[1],
        slope_lifts[0],
        slope_lifts[1],
        jobs_heads[0],
        job_lower,
        jobs_dec[1],
        jobs_dec[0],
        jobs_enc[0],
        job_route,
        jobs_enc[1],
        Summing(grad_mixed.reshape(-1, BYTE_WIDTH + 128), True),
    ]
    sums = [None if part.masks else part.result(jobs_enc[1].addends[0][0]) for part in parts]
    open_parts = [number for number in (8, 9, 7, 10, 3, 0, 1, 2, 4, 5, 6) if parts[number].masks]
    rests = [parts[number].rest(jobs_enc[1].addends[0][0]) for number in open_parts]
    grads = [grad for grad, _ in rests]
    sum_kinds = [kind for _, kind in rests]
    if exact_tiles:
        early = sum((jnp.sum(part * part) for part in sums if part is not None), jnp.float32(0.0))
        extra = jnp.zeros((16, 128), jnp.float32).at[0, 0].set(early).at[8, 0].set(loss_local)
        *ends, totals = sum_whole(grads, sum_kinds, extra, 1)
        square_total, loss_sum = jnp.sum(totals[:8]), jnp.sum(totals[8:])
    else:
        ends = [sum_slowly(parts[number]) for number in open_parts]
    for number, end in zip(open_parts, ends):
        sums[number] = end
    reduced_wo = sums[0].T
    reduced_gate_up = jnp.stack([sums[1], sums[2]], axis=1)
    reduced_qkv = sums[3].reshape(heed_triple_matrix.shape)
    reduced_down = sums[4].T
    reduced_in_dec = sums[5][:, :width]
    reduced_out_dec, reduced_out_enc, reduced_route = sums[6:9]
    reduced_in_enc = sums[9][:, :width]
    reduced_mixed = sums[10]
    reduced_tables = reduced_mixed[:, :BYTE_WIDTH].reshape(2, table_rows, BYTE_WIDTH)
    reduced_small = reduced_mixed[:, BYTE_WIDTH:].reshape(-1)[:small_here]
    reduced_in = jnp.stack([reduced_in_enc, reduced_in_dec])
    reduced_out = jnp.stack([reduced_out_enc, reduced_out_dec])
    reduced = (
        reduced_tables,
        reduced_in,
        reduced_out,
        reduced_route,
        reduced_small,
        reduced_qkv,
        reduced_wo,
        reduced_gate_up,
        reduced_down,
    )
    if not exact_tiles:
        squares = sum((jnp.sum(grad * grad) for grad in reduced))
        totals = add_everywhere(jnp.stack([squares, loss_local]).reshape(1, 2))
        square_total, loss_sum = (totals[0, 0], totals[0, 1])
    grad_norm = jnp.sqrt(square_total)
    clip_factor = jnp.minimum(1.0, max_norm / (grad_norm + 1e-06))
    masters = (
        tables,
        mamba_in,
        mamba_out,
        route_proj,
        small_params,
        heed_triple_matrix,
        heed_exit_matrix,
        lifting_matrix,
        lowering_matrix,
    )
    firsts = (
        tables_first,
        mamba_in_first,
        mamba_out_first,
        route_proj_first,
        small_params_first,
        attn_qkv_first,
        attn_out_first,
        mlp_gate_up_first,
        mlp_down_first,
    )
    seconds = (
        tables_second,
        mamba_in_second,
        mamba_out_second,
        route_proj_second,
        small_params_second,
        attn_qkv_second,
        attn_out_second,
        mlp_gate_up_second,
        mlp_down_second,
    )
    rate_list = (
        rate_byte,
        rate_byte,
        rate_byte,
        rate_byte,
        rate_small,
        rate_main,
        rate_main,
        rate_main,
        rate_main,
    )
    decay_list = (
        weight_decay,
        weight_decay,
        weight_decay,
        weight_decay,
        0.0,
        weight_decay,
        weight_decay,
        weight_decay,
        weight_decay,
    )
    updated = [
        adam_step(
            masters[position],
            clip_factor * reduced[position],
            firsts[position],
            seconds[position],
            rate_list[position],
            decay_list[position],
        )
        for position in range(9)
    ]
    updated[7] = lift_step(
        clip_factor, sums[1], sums[2], lifting_matrix, mlp_gate_up_first, mlp_gate_up_second
    )
    return (loss_sum, byte_count, grad_norm) + tuple(
        (member for triple_out in updated for member in triple_out)
    )


def solution(mesh):
    return jax.shard_map(
        body,
        mesh=mesh,
        in_specs=(
            P(("dp", "tensor"), None),
            P(("dp", "tensor"), None),
            P(("dp", "tensor"), None),
            P(("dp", "tensor")),
            P(None, ("dp", "tensor"), None),
            P(None, ("dp", "tensor"), None),
            P(None, ("dp", "tensor"), None),
            P(None, ("dp", "tensor"), None),
            P(None, ("dp", "tensor"), None),
            P(None, ("dp", "tensor"), None),
            P(None, ("dp", "tensor"), None),
            P(None, ("dp", "tensor"), None),
            P(None, ("dp", "tensor"), None),
            P(("dp", "tensor"), None),
            P(("dp", "tensor"), None),
            P(("dp", "tensor"), None),
            P(("dp", "tensor")),
            P(("dp", "tensor")),
            P(("dp", "tensor")),
            P("dp", None, "tensor"),
            P("dp", None, "tensor"),
            P("dp", None, "tensor"),
            P("tensor", "dp"),
            P("tensor", "dp"),
            P("tensor", "dp"),
            P("dp", None, "tensor"),
            P("dp", None, "tensor"),
            P("dp", None, "tensor"),
            P("tensor", "dp"),
            P("tensor", "dp"),
            P("tensor", "dp"),
        ),
        out_specs=(
            P(),
            P(),
            P(),
            P(None, ("dp", "tensor"), None),
            P(None, ("dp", "tensor"), None),
            P(None, ("dp", "tensor"), None),
            P(None, ("dp", "tensor"), None),
            P(None, ("dp", "tensor"), None),
            P(None, ("dp", "tensor"), None),
            P(None, ("dp", "tensor"), None),
            P(None, ("dp", "tensor"), None),
            P(None, ("dp", "tensor"), None),
            P(("dp", "tensor"), None),
            P(("dp", "tensor"), None),
            P(("dp", "tensor"), None),
            P(("dp", "tensor")),
            P(("dp", "tensor")),
            P(("dp", "tensor")),
            P("dp", None, "tensor"),
            P("dp", None, "tensor"),
            P("dp", None, "tensor"),
            P("tensor", "dp"),
            P("tensor", "dp"),
            P("tensor", "dp"),
            P("dp", None, "tensor"),
            P("dp", None, "tensor"),
            P("dp", None, "tensor"),
            P("tensor", "dp"),
            P("tensor", "dp"),
            P("tensor", "dp"),
        ),
        check_vma=False,
    )
```

```python
from functools import partial

import jax
import jax.numpy as jnp
from jax import lax
from jax.experimental import pallas as pl
from jax.experimental.pallas import tpu as pltpu
from jax.sharding import PartitionSpec as P

BYTE_WIDTH = 1024
CORE_WIDTH = 1536
VOCAB = 256
STATE = 128
HEADDIM = 64
STEP = 10
INNER = 2048
MHEADS = 32
HD = 96
MAX_PIECES = 128


deepest_tier = lax.Precision.HIGHEST
norm_eps = 1e-05
ssd_block = 128
beta_one = 0.9
beta_two = 0.95
adam_eps = 1e-08
weight_decay = 0.1
max_norm = 0.01
rate_byte = 0.06
rate_main = 0.05
rate_small = 0.5


def root_mean_rescale(value_entries, gain_vec):
    return (
        value_entries
        * lax.rsqrt(jnp.mean(value_entries * value_entries, axis=-1, keepdims=True) + norm_eps)
        * gain_vec
    )


def softplus(value_entries):
    return jnp.log1p(jnp.exp(value_entries))


def unpack_small(vector):
    extents = [
        2 * BYTE_WIDTH,
        2 * INNER,
        3 * CORE_WIDTH,
        BYTE_WIDTH,
        CORE_WIDTH - BYTE_WIDTH,
        8 * (INNER + 2 * STATE),
        2 * INNER,
        2 * MHEADS,
        2 * MHEADS,
    ]
    pieces = []
    offset = 0
    for extent in extents:
        pieces.append(vector[offset : offset + extent])
        offset += extent
    return (
        pieces[0].reshape(2, BYTE_WIDTH),
        pieces[1].reshape(2, INNER),
        pieces[2].reshape(3, CORE_WIDTH),
        pieces[3],
        pieces[4],
        pieces[5].reshape(2, 4, INNER + 2 * STATE),
        pieces[6].reshape(2, INNER),
        pieces[7].reshape(2, MHEADS),
        pieces[8].reshape(2, MHEADS),
    )


def route_prob(queries, key_rows):
    unit_query = queries * lax.rsqrt(jnp.sum(queries * queries, axis=-1, keepdims=True) + 1e-06)
    unit_key = key_rows * lax.rsqrt(jnp.sum(key_rows * key_rows, axis=-1, keepdims=True) + 1e-06)
    cosine = jnp.sum(unit_query[1:] * unit_key[:-1], axis=-1)
    return jnp.concatenate([jnp.ones((1,), jnp.float32), 0.5 * (1.0 - cosine)])


def span_maps(cut_marks):
    owner_slot = jnp.cumsum(cut_marks) - 1
    position_labels = jnp.arange(MAX_PIECES, dtype=jnp.int32)
    broadcast_back = (owner_slot[:, None] == position_labels[None, :]).astype(jnp.float32)
    select_items = broadcast_back.T * cut_marks[None, :].astype(jnp.float32)
    return (select_items, broadcast_back)


def merge_into_pieces(select_items, value_entries, blank_row):
    spans = jnp.dot(select_items, value_entries, precision=deepest_tier)
    return jnp.concatenate(
        [spans, jnp.broadcast_to(blank_row, (MAX_PIECES, CORE_WIDTH - BYTE_WIDTH))], axis=1
    )


def decay_products(confidence):
    rows = lax.broadcasted_iota(jnp.int32, (MAX_PIECES, MAX_PIECES), 0)
    columns = lax.broadcasted_iota(jnp.int32, (MAX_PIECES, MAX_PIECES), 1)
    products = jnp.where(rows > columns, 1.0 - confidence[:, None], 1.0)
    reach = 1
    while reach < MAX_PIECES:
        shifted = jnp.concatenate(
            [jnp.ones((reach, MAX_PIECES), jnp.float32), products[:-reach]], axis=0
        )
        products = products * shifted
        reach *= 2
    return jnp.where(rows >= columns, products, 0.0)


@jax.custom_vjp
def smooth_spans(piece_output, confidence):
    products = decay_products(confidence)
    return jnp.dot(products, confidence[:, None] * piece_output, precision=deepest_tier)


def smooth_keep(piece_output, confidence):
    products = decay_products(confidence)
    smoothed = jnp.dot(products, confidence[:, None] * piece_output, precision=deepest_tier)
    return smoothed, (piece_output, confidence, products, smoothed)


def smooth_pull(kept, slope):
    piece_output, confidence, products, smoothed = kept
    spread = lax.dot_general(
        products, slope, (((0,), (0,)), ((), ())), precision=deepest_tier
    )
    before = jnp.concatenate([jnp.zeros((1, smoothed.shape[1]), jnp.float32), smoothed[:-1]], axis=0)
    return (confidence[:, None] * spread, jnp.sum(spread * (piece_output - before), axis=-1))


smooth_spans.defvjp(smooth_keep, smooth_pull)


def link_layers(
    select_items,
    broadcast_back,
    cut_marks,
    latent_holder,
    closing_scale,
    cut_likelihood,
    shortcut_sum,
):
    piece_output = root_mean_rescale(latent_holder, closing_scale)[:, :BYTE_WIDTH]
    smoothed = smooth_spans(
        piece_output, jnp.dot(select_items, cut_likelihood, precision=deepest_tier)
    )
    confidence = jnp.where(cut_marks == 1, cut_likelihood, 1.0 - cut_likelihood)
    return shortcut_sum + confidence[:, None] * jnp.dot(
        broadcast_back, smoothed, precision=deepest_tier
    )


def adam_step(weight, grad, first, second, rate, decay):
    first_new = beta_one * first + (1.0 - beta_one) * grad
    second_new = beta_two * second + (1.0 - beta_two) * grad * grad
    ratio = (
        first_new
        / (1.0 - beta_one**STEP)
        / (jnp.sqrt(second_new / (1.0 - beta_two**STEP)) + adam_eps)
    )
    return (first_new, second_new, weight - rate * (ratio + decay * weight))


def lift_kernel(clip, gate, up, weight, first, second, *outputs):
    for side, grad in enumerate((gate, up)):
        updated = adam_step(
            weight[:, side, :],
            clip[0, 0] * grad[...],
            first[:, side, :],
            second[:, side, :],
            rate_main,
            weight_decay,
        )
        for output, value_entries in zip(outputs, updated):
            output[:, side, :] = value_entries


def lift_step(clip_factor, gate, up, weight, first, second):
    rows, columns = gate.shape
    block = 48 if rows % 48 == 0 else rows
    flat = pl.BlockSpec((block, columns), lambda part: (part, 0))
    paired = pl.BlockSpec((block, 2, columns), lambda part: (part, 0, 0))
    return pl.pallas_call(
        lift_kernel,
        grid=(rows // block,),
        out_shape=(jax.ShapeDtypeStruct(weight.shape, jnp.float32),) * 3,
        in_specs=[pl.BlockSpec(memory_space=pltpu.SMEM), flat, flat, paired, paired, paired],
        out_specs=(paired,) * 3,
        compiler_params=pltpu.CompilerParams(vmem_limit_bytes=32 * 2**20),
    )(clip_factor.reshape(1, 1), gate, up, weight, first, second)


def to_low(value_entries):
    return value_entries.astype(jnp.bfloat16)


def matmul_apply(left, right):
    return jnp.dot(left, right, preferred_element_type=jnp.float32)


def product_tn(left, right):
    return lax.dot_general(
        left, right, (((0,), (0,)), ((), ())), preferred_element_type=jnp.float32
    )


def product_nt(left, right):
    return lax.dot_general(
        left, right, (((1,), (1,)), ((), ())), preferred_element_type=jnp.float32
    )


def swap(value_entries, axis, mask):
    size = lax.axis_size(axis)
    return lax.ppermute(value_entries, axis, [(place, place ^ mask) for place in range(size)])


def bit_masks(size):
    masks = []
    mask = 1
    while mask < size:
        masks.append(mask)
        mask *= 2
    return masks


def after(value_entries, earlier):
    if not earlier:
        return value_entries
    return lax.optimization_barrier((value_entries,) + tuple(earlier))[0]


def spread_masks(over_tensor):
    dp_masks = bit_masks(lax.axis_size("dp"))
    masks = [("dp", mask) for mask in dp_masks[1:] + dp_masks[:1]]
    if over_tensor:
        masks += [("tensor", mask) for mask in reversed(bit_masks(lax.axis_size("tensor")))]
    return masks


class Summing:
    def __init__(self, grad, over_tensor):
        self.masks = list(reversed(spread_masks(over_tensor)))
        names = [("dp", mask) for mask in reversed(bit_masks(lax.axis_size("dp")))]
        if over_tensor:
            names += [("tensor", mask) for mask in reversed(bit_masks(lax.axis_size("tensor")))]
        self.names = names
        rows = grad.shape[0] // 2 ** len(names)
        self.addends = [(grad.reshape((2,) * len(names) + (rows,) + grad.shape[1:]), names)]
        self.pending = None

    def picked(self, other=None, token=None):
        result = []
        for array, names in self.addends:
            if token is not None:
                array = after(array, [token])
            for position in reversed(range(len(names))):
                axis, mask = names[position]
                own = (lax.axis_index(axis) // mask) % 2
                if names[position] == other:
                    array = take(array, position, 1 - own)
                elif names[position] not in self.names:
                    array = take(array, position, own)
            result.append(array)
        return result

    def operand(self):
        return to_low(total(self.picked(self.masks[0])))

    def accept(self):
        self.names = [name for name in self.names if name != self.masks[0]]
        self.masks = self.masks[1:]
        self.addends.append((self.pending, self.names))
        self.pending = None

    def begun_last(self):
        left = [mask for axis, mask in self.masks if axis == "dp" and mask > 1]
        return 0 < len(left) == len(self.masks) < len(bit_masks(lax.axis_size("dp"))) - 1

    def rest(self, token):
        kind = []
        for axis, mask in self.masks:
            if lane_name(axis, mask) not in kind:
                kind.append(lane_name(axis, mask))
        if len(self.addends) == 1 or kind[0] in ("core", "y"):
            array = self.addends[0][0]
            if len(self.addends) > 1:
                array = to_low(total(self.picked(token=token)))
            return [(array, tuple(name for name in BYTE_LANES if name in kind))], tuple(kind)
        arrays = []
        for array, names in self.addends:
            lanes_here = {lane_name(axis, mask) for axis, mask in names}
            arrays.append((array, tuple(name for name in BYTE_LANES if name in lanes_here)))
        return arrays, tuple(kind)

    def result(self, token=None):
        return total(self.picked(token=token))


def lane_name(axis, mask):
    if axis == "tensor":
        return ("core", "y")[mask - 1]
    return "x" if mask == 1 else "z"


def sum_slowly(job):
    while job.masks:
        axis, mask = job.masks[0]
        job.pending = swap(job.operand(), axis, mask)
        job.accept()
    return job.result()


class Conductor:
    def __init__(self):
        self.clock = 0.0
        self.jobs = []
        self.flights = []

    def add(self, job):
        self.jobs.append(job)
        return job

    def lane(self, job):
        axis, mask = job.masks[0]
        return (axis, mask if axis == "tensor" else min(mask, 2))

    def launch(self, limit, banned, value_entries):
        operands = []
        for job in self.jobs:
            if len(self.flights) >= limit:
                break
            if job.pending is not None or not job.masks:
                continue
            lane = self.lane(job)
            depth = {("dp", 1): 3, ("tensor", 1): 2}.get(lane, 1)
            if lane in banned or sum(flight[1] == lane for flight in self.flights) >= depth:
                continue
            axis, mask = job.masks[0]
            operand = job.operand()
            rate = 3.4 if (axis, mask) == ("tensor", 1) else 25.3
            if axis == "dp" and mask > 2:
                rate = 50.0
            operand = after(operand, [value_entries])
            operands.append(operand)
            job.pending = swap(operand, axis, mask)
            start = max([self.clock] + [flight[0] - 6.0 for flight in self.flights if flight[1] == lane])
            self.flights.append((start + 6.0 + rate * operand.size * 2e-6, lane, job))
        return after(value_entries, operands)

    def tick(self, value_entries, elapsed, banned=(), limit=5):
        self.clock += elapsed
        ended = [flight for flight in self.flights if flight[0] <= self.clock]
        if ended:
            value_entries = after(value_entries, [flight[2].pending for flight in ended])
            self.flights = [flight for flight in self.flights if flight[0] > self.clock]
            for flight in ended:
                flight[2].accept()
        return self.launch(limit, banned, value_entries)

    def close(self):
        for _, _, job in sorted(self.flights, key=lambda flight: flight[0]):
            job.accept()
        self.flights = []
        for job in self.jobs:
            while job.begun_last():
                axis, mask = job.masks[0]
                job.pending = swap(job.operand(), axis, mask)
                job.accept()


def flip(place, mask):
    result = place
    bit = 1
    while bit <= mask:
        if mask & bit:
            result = result + bit * (1 - 2 * ((place // bit) % 2))
        bit *= 2
    return result


def order_steps(jobs, depth=2):
    free, busy, flights, plan = {}, {}, [], []
    waiting = [0] * len(jobs)
    clock = 0.0
    while True:
        for job, steps in enumerate(jobs):
            step = waiting[job]
            if step < 0 or step >= len(steps):
                continue
            lane, cost = steps[step]
            if busy.get(lane, 0) >= depth:
                continue
            busy[lane] = busy.get(lane, 0) + 1
            free[lane] = max(free.get(lane, 0.0), clock) + cost
            flights.append((free[lane] + 1.5, job, step, lane))
            plan.append(("start", job, step))
            waiting[job] = -1 - step
        if not flights:
            return plan
        flight = min(flights)
        flights.remove(flight)
        clock, job, step, lane = flight
        busy[lane] -= 1
        plan.append(("wait", job, step))
        waiting[job] = step + 1


def link_cost(lane, elements):
    return elements * 2e-6 * {"core": 3.4, "y": 23.0, "x": 23.0, "z": 46.0}[lane]


def here():
    dp_place, tensor_place = lax.axis_index("dp"), lax.axis_index("tensor")
    return dp_place // 2, dp_place % 2, tensor_place // 2, tensor_place % 2


def partner(lane, mask, coordinates):
    z, x, y, core = coordinates
    if lane == "z":
        z = flip(z, mask)
    if lane == "x":
        x = 1 - x
    if lane == "y":
        y = 1 - y
    if lane == "core":
        core = 1 - core
    return (z * 2 + x, y * 2 + core)


def greet(line, depth_z, coordinates):
    z = coordinates[0]
    barrier = pltpu.get_barrier_semaphore()

    def tell(device):
        pl.semaphore_signal(
            barrier, inc=1, device_id=device, device_id_type=pl.DeviceIdType.MESH
        )

    if not line:
        others = peers("tensor", 4) + peers("dp", 2 * depth_z)
        for device in others:
            tell(device)
        pl.semaphore_wait(barrier, len(others))
        return

    for lane in ("x", "y", "core"):
        tell(partner(lane, 1, coordinates))

    @pl.when(z > 0)
    def _():
        tell(beside(-1, coordinates))

    @pl.when(z < depth_z - 1)
    def _():
        tell(beside(1, coordinates))

    ends = (z == 0).astype(jnp.int32) + (z == depth_z - 1).astype(jnp.int32)
    pl.semaphore_wait(barrier, 5 - ends)


def peers(axis, size):
    dp_place, tensor_place = lax.axis_index("dp"), lax.axis_index("tensor")
    if axis == "dp":
        return [(flip(dp_place, mask), tensor_place) for mask in range(1, size)]
    return [(dp_place, flip(tensor_place, mask)) for mask in range(1, size)]


def beside(way, coordinates):
    z, x, y, core = coordinates
    return ((z + way) * 2 + x, y * 2 + core)


def spread_kernel(plan, jobs, depth_z, *refs):
    count = (len(refs) - 3) // 2
    shards, wholes = refs[:count], refs[count : 2 * count]
    send_sems, receive_sems, own_sems = refs[2 * count :]
    coordinates = here()
    z = coordinates[0]
    greet(True, depth_z, coordinates)

    def spot(job, free, z_place):
        array, kind, first, size = jobs[job]
        index = [
            slice(None) if name in free else (z_place if name == "z" else place)
            for name, place in zip(("z", "x", "y", "core"), coordinates)
            if name in kind
        ]
        return wholes[array].at[tuple(index) + (slice(None), pl.ds(first, size))]

    def shard(job):
        array, _, first, size = jobs[job]
        return shards[array].at[:, pl.ds(first, size)]

    own = []
    for job in range(len(jobs)):
        own.append(pltpu.make_async_copy(shard(job), spot(job, (), z), own_sems.at[job]))
        own[-1].start()

    def copies(job, step, receiving):
        steps = lanes_of(jobs[job][1], depth_z)
        lane, reach = steps[step]
        free = [name for name, _ in steps[:step] if name != lane]
        base = job * (2 * depth_z + 1)
        pairs = []
        if lane == "z":
            for side, way in enumerate((1, -1)):
                number = base + 2 * (reach - 1) + side
                if receiving:
                    block = z - way * reach
                    condition = (block >= 0) & (block < depth_z)
                    target = spot(job, free, z if step == 0 else block)
                    source = target
                else:
                    block = z - way * (reach - 1)
                    condition = (block >= 0) & (block < depth_z)
                    condition &= (z + way >= 0) & (z + way < depth_z)
                    target = spot(job, free, block)
                    source = shard(job) if step == 0 else target
                copy = pltpu.make_async_remote_copy(
                    src_ref=source,
                    dst_ref=target,
                    send_sem=send_sems.at[number],
                    recv_sem=receive_sems.at[number],
                    device_id=beside(way, coordinates),
                    device_id_type=pl.DeviceIdType.MESH,
                )
                pairs.append((condition, copy))
            return pairs
        number = base + 2 * (depth_z - 1) + ("x", "y", "core").index(lane)
        target = spot(job, free, z)
        copy = pltpu.make_async_remote_copy(
            src_ref=shard(job) if step == 0 else target,
            dst_ref=target,
            send_sem=send_sems.at[number],
            recv_sem=receive_sems.at[number],
            device_id=partner(lane, 1, coordinates),
            device_id_type=pl.DeviceIdType.MESH,
        )
        return [(None, copy)]

    def perform(pairs, action):
        for condition, copy in pairs:
            if condition is None:
                getattr(copy, action)()
            else:
                pl.when(condition)(getattr(copy, action))

    copied = set()
    for action, job, step in plan:
        steps = lanes_of(jobs[job][1], depth_z)
        if action == "start":
            if steps[step][0] != steps[0][0] and job not in copied:
                own[job].wait()
                copied.add(job)
            perform(copies(job, step, False), "start")
        else:
            perform(copies(job, step, True), "wait_recv")
    for action, job, step in plan:
        if action == "start":
            perform(copies(job, step, False), "wait_send")


def lanes_of(kind, depth_z):
    steps = []
    for name in kind:
        steps += [(name, reach) for reach in range(1, depth_z if name == "z" else 2)]
    return steps


def spread_whole(shards, jobs, collective_id):
    depth_z = lax.axis_size("dp") // 2
    costs = []
    for array, kind, first, size in jobs:
        held, steps = shards[array].shape[0] * size, []
        for lane in kind:
            cost = 23.0 if lane != "core" else 3.4
            steps += [(lane, held * 2e-6 * cost)] * (depth_z - 1 if lane == "z" else 1)
            held *= depth_z if lane == "z" else 2
        costs.append(steps)
    plan = order_steps(costs)
    sizes = {"z": depth_z, "x": 2, "y": 2, "core": 2}
    kinds = {array: kind for array, kind, _, _ in jobs}
    shapes = [
        tuple(sizes[name] for name in ("z", "x", "y", "core") if name in kinds[array])
        + shard.shape
        for array, shard in enumerate(shards)
    ]
    numbers = len(jobs) * (2 * depth_z + 1)
    wholes = pl.pallas_call(
        partial(spread_kernel, plan, jobs, depth_z),
        out_shape=tuple(jax.ShapeDtypeStruct(shape, jnp.bfloat16) for shape in shapes),
        in_specs=[pl.BlockSpec(memory_space=pltpu.VMEM)] * len(shards),
        out_specs=(pl.BlockSpec(memory_space=pl.ANY),) * len(shards),
        scratch_shapes=[
            pltpu.SemaphoreType.DMA((numbers,)),
            pltpu.SemaphoreType.DMA((numbers,)),
            pltpu.SemaphoreType.DMA((len(jobs),)),
        ],
        compiler_params=pltpu.CompilerParams(
            collective_id=collective_id, has_side_effects=True, vmem_limit_bytes=60 * 2**20
        ),
    )(*shards)
    return [whole.reshape(-1, whole.shape[-1]) for whole in wholes]


BYTE_LANES = ("z", "x", "y", "core")
MAIN_LANES = ("z", "x")


def sum_kernel(plan, kinds, sources, depth_z, *refs):
    count = len(kinds)
    pieces_in = [[refs[number] for number, _ in parts] for parts in sources]
    total_in = sum(len(parts) for parts in sources)
    grads, extra = [parts[0] for parts in pieces_in], refs[total_in]
    outputs = refs[total_in + 1 : total_in + 1 + count]
    totals = refs[total_in + 1 + count]
    rest = list(refs[total_in + 2 + count :])
    coordinates = here()
    places = dict(zip(BYTE_LANES, coordinates))
    z = coordinates[0]
    mirrored = depth_z - 1 - z
    held, received, held_names, temporary = [], [], [], {}
    for job, kind in enumerate(kinds):
        held.append(rest.pop(0))
        received.append({lane: rest.pop(0) for lane in kind})
        held_names.append(names_held(kind, len(sources[job])))
    for key in temporary_shapes(kinds, sources, [ref.shape for ref in held]):
        temporary[key] = rest.pop(0)
    squares, arrivals, send_sems, receive_sems, own_sems, tile_sems = rest

    def slice_of(job, part):
        names = sources[job][part][1]
        spot = tuple(slice(None) if name in held_names[job] else places[name] for name in names)
        return pieces_in[job][part].at[spot]

    loads = []
    for job in range(count):
        loads.append(pltpu.make_async_copy(slice_of(job, 0), held[job], own_sems.at[job]))
        loads[-1].start()
    squares[...] = jnp.zeros_like(squares)
    greet(False, depth_z, coordinates)

    def prepare(job):
        loads[job].wait()
        for part in range(1, len(sources[job])):
            buffer = temporary[held[job].shape]
            copy = pltpu.make_async_copy(slice_of(job, part), buffer, own_sems.at[job])
            copy.start()
            copy.wait()
            lead, rows = held[job].shape[:-2], held[job].shape[-2]
            pieces = 1
            for size in lead:
                pieces *= size

            def piece(index, carry, buffer=buffer, lead=lead, rows=rows):
                spot, remainder = [], index
                for size in reversed(lead):
                    spot.insert(0, remainder % size)
                    remainder = remainder // size
                target, other = held[job].at[tuple(spot)], buffer.at[tuple(spot)]

                def row_step(number, inner):
                    part_rows = pl.ds(pl.multiple_of(number * 16, 16), 16)
                    target[part_rows, :] = to_low(
                        target[part_rows, :].astype(jnp.float32)
                        + other[part_rows, :].astype(jnp.float32)
                    )
                    return inner

                lax.fori_loop(0, rows // 16, row_step, 0)
                return carry

            lax.fori_loop(0, pieces, piece, 0)

    def chosen(job, step, lane_place):
        steps = lanes_of(kinds[job], depth_z)
        lane = steps[step][0]
        done = [name for name, _ in steps[:step] if name != lane]
        return [
            lane_place if name == lane else (places[name] if name in done else slice(None))
            for name in held_names[job]
        ]

    def slot(reach, side):
        shared = (depth_z - 2) // 2
        return reach - 1 if reach <= shared else shared + 2 * (reach - 1 - shared) + side

    def copies(job, step, receiving):
        kind = kinds[job]
        lane, reach = lanes_of(kind, depth_z)[step]
        base = job * (2 * depth_z + 1)
        if lane == "z":
            pairs = []
            for side, depth in enumerate((z, mirrored)):
                way = 1 - 2 * side
                aim = depth_z - reach + depth
                if side:
                    aim = depth_z - 1 - aim
                landing = received[job]["z"].at[slot(reach, side)]
                number = base + 2 * (reach - 1) + side
                source = landing if receiving else held[job].at[tuple(chosen(job, step, aim))]
                copy = pltpu.make_async_remote_copy(
                    src_ref=source,
                    dst_ref=landing,
                    send_sem=send_sems.at[number],
                    recv_sem=receive_sems.at[number],
                    device_id=beside(way, coordinates),
                    device_id_type=pl.DeviceIdType.MESH,
                )
                condition = (depth >= 1) & (depth <= reach) if receiving else depth <= reach - 1
                pairs.append((condition, copy))
            return pairs
        number = base + 2 * (depth_z - 1) + ("x", "y", "core").index(lane)
        if step == 0 and len(sources[job]) == 1:
            spot = tuple(
                1 - places[name] if name == lane else slice(None)
                for name in BYTE_LANES
                if name in kind
            )
            source = grads[job].at[spot]
        else:
            source = held[job].at[tuple(chosen(job, step, 1 - places[lane]))]
        copy = pltpu.make_async_remote_copy(
            src_ref=source,
            dst_ref=received[job][lane],
            send_sem=send_sems.at[number],
            recv_sem=receive_sems.at[number],
            device_id=partner(lane, 1, coordinates),
            device_id_type=pl.DeviceIdType.MESH,
        )
        return [(None, copy)]

    def add_pieces(job, step, lane_place, buffers, last):
        steps = lanes_of(kinds[job], depth_z)
        lane = steps[step][0]
        done = [name for name, _ in steps[:step] if name != lane]
        free = [name for name in BYTE_LANES if name in kinds[job] and name not in done + [lane]]
        sizes = [depth_z if name == "z" else 2 for name in free]
        pieces = 1
        for size in sizes:
            pieces *= size

        def piece(index, carry):
            spots, remainder = {}, index
            for name, size in reversed(list(zip(free, sizes))):
                spots[name] = remainder % size
                remainder = remainder // size
            mine = tuple(
                spots[name] if name in spots else (lane_place if name == lane else places[name])
                for name in held_names[job]
            )
            theirs = tuple(spots[name] for name in free)
            target = held[job].at[mine] if mine else held[job]
            arrived = [buffer.at[theirs] if theirs else buffer for buffer in buffers]
            rows, columns = target.shape[-2:]

            def row_step(number, inner):
                part = pl.ds(pl.multiple_of(number * 16, 16), 16)
                value = target[part, :].astype(jnp.float32)
                for other in arrived:
                    value = value + other[part, :].astype(jnp.float32)
                if last:
                    outputs[job][part, :] = value
                    square = jnp.zeros((16, 128), jnp.float32)
                    for first in range(0, columns, 128):
                        square = square + value[:, first : first + 128] * value[:, first : first + 128]
                    squares[...] += square
                else:
                    target[part, :] = to_low(value)
                return inner

            lax.fori_loop(0, rows // 16, row_step, 0)
            return carry

        if pieces == 1:
            piece(0, 0)
        else:
            lax.fori_loop(0, pieces, piece, 0)

    def accumulate(job, step):
        steps = lanes_of(kinds[job], depth_z)
        lane, reach = steps[step]
        last = step == len(steps) - 1
        if lane != "z":
            add_pieces(job, step, places[lane], [received[job][lane]], last)
            return
        buffers = [received[job]["z"].at[slot(reach, side)] for side in range(2)]
        if reach < depth_z - 1:
            for side, depth in enumerate((z, mirrored)):
                aim = depth_z - reach + depth - 1
                if side:
                    aim = depth_z - 1 - aim
                pl.when((depth >= 1) & (depth <= reach))(
                    partial(add_pieces, job, step, aim, [buffers[side]], False)
                )
            return
        ends = (z == 0) | (mirrored == 0)
        pl.when(jnp.logical_not(ends))(partial(add_pieces, job, step, z, buffers, last))
        pl.when(z == 0)(partial(add_pieces, job, step, z, buffers[1:], last))
        pl.when(mirrored == 0)(partial(add_pieces, job, step, z, buffers[:1], last))

    def perform(pairs, action):
        for condition, copy in pairs:
            if condition is None:
                getattr(copy, action)()
            else:
                pl.when(condition)(getattr(copy, action))

    loaded = set()
    for action, job, step in plan:
        lane = lanes_of(kinds[job], depth_z)[step][0]
        if job not in loaded and (action == "wait" or lane == "z" or len(sources[job]) > 1):
            prepare(job)
            loaded.add(job)
        if action == "start":
            perform(copies(job, step, False), "start")
        else:
            perform(copies(job, step, True), "wait_recv")
            accumulate(job, step)
    totals[...] = extra[...]
    totals[0:8, :] += squares[0:8, :] + squares[8:16, :]
    tiles = []
    for axis, size, first in (("tensor", 4, 0), ("dp", 2 * depth_z, 4)):
        spot = first + lax.axis_index(axis)
        arrivals[spot] = totals[...]
        for mask, device in enumerate(peers(axis, size), 1):
            tiles.append(
                pltpu.make_async_remote_copy(
                    src_ref=arrivals.at[spot],
                    dst_ref=arrivals.at[spot],
                    send_sem=tile_sems.at[2 * (first + mask)],
                    recv_sem=tile_sems.at[2 * (first + mask) + 1],
                    device_id=device,
                    device_id_type=pl.DeviceIdType.MESH,
                )
            )
            tiles[-1].start()
        for copy in tiles[1 - size :]:
            copy.wait_recv()
        result = arrivals[first]
        for place in range(1, size):
            result = result + arrivals[first + place]
        totals[...] = result
    for copy in tiles:
        copy.wait_send()
    for action, job, step in plan:
        if action == "start":
            perform(copies(job, step, False), "wait_send")


def names_held(kind, addends):
    return [
        name
        for name in BYTE_LANES
        if name in kind and (name == "z" or addends > 1 or name != kind[0])
    ]


def temporary_shapes(kinds, sources, shapes):
    return list(
        dict.fromkeys(
            tuple(shape) for shape, parts in zip(shapes, sources) if len(parts) > 1
        )
    )


def sum_whole(grads, kinds, extra, collective_id):
    depth_z = lax.axis_size("dp") // 2
    sizes = {"z": depth_z, "x": 2, "y": 2, "core": 2}
    jobs, arrays, shapes, scratch, sources, held_shapes = [], [], [], [], [], []
    for parts, kind in zip(grads, kinds):
        sources.append([])
        for array, names in parts:
            piece = array.shape[-2:]
            lead = tuple(sizes[name] for name in names)
            if array.ndim == 2:
                pieces = 1
                for size in lead:
                    pieces *= size
                piece = (array.shape[0] // pieces, array.shape[1])
            sources[-1].append((len(arrays), names))
            arrays.append(array.reshape(lead + piece))
        shapes.append(jax.ShapeDtypeStruct(piece, jnp.float32))
        steps, left = [], [name for name in BYTE_LANES if name in kind]
        held_shapes.append(tuple(sizes[name] for name in names_held(kind, len(parts))) + piece)
        scratch.append(pltpu.VMEM(held_shapes[-1], jnp.bfloat16))
        for lane in kind:
            left.remove(lane)
            rest = tuple(sizes[name] for name in left)
            extent = piece[0] * piece[1]
            for size in rest:
                extent *= size
            cost = 23.0 if lane != "core" else 3.4
            steps += [(lane, extent * 2e-6 * cost)] * (depth_z - 1 if lane == "z" else 1)
            lead = (2 * (depth_z - 1) - (depth_z - 2) // 2,) if lane == "z" else ()
            scratch.append(pltpu.VMEM(lead + rest + piece, jnp.bfloat16))
        jobs.append(steps)
    scratch += [
        pltpu.VMEM(shape, jnp.bfloat16)
        for shape in temporary_shapes(kinds, sources, held_shapes)
    ]
    plan = order_steps(jobs, 3)
    numbers = len(grads) * (2 * depth_z + 1)
    tile = jax.ShapeDtypeStruct(extra.shape, jnp.float32)
    places = 4 + 2 * depth_z
    return pl.pallas_call(
        partial(sum_kernel, plan, kinds, sources, depth_z),
        out_shape=tuple(shapes) + (tile,),
        in_specs=[pl.BlockSpec(memory_space=pl.ANY)] * len(arrays)
        + [pl.BlockSpec(memory_space=pltpu.VMEM)],
        out_specs=(pl.BlockSpec(memory_space=pltpu.VMEM),) * (len(grads) + 1),
        scratch_shapes=scratch
        + [
            pltpu.VMEM((16, 128), jnp.float32),
            pltpu.VMEM((places, 16, 128), jnp.float32),
            pltpu.SemaphoreType.DMA((numbers,)),
            pltpu.SemaphoreType.DMA((numbers,)),
            pltpu.SemaphoreType.DMA((len(grads),)),
            pltpu.SemaphoreType.DMA((2 * places,)),
        ],
        compiler_params=pltpu.CompilerParams(
            collective_id=collective_id, has_side_effects=True, vmem_limit_bytes=60 * 2**20
        ),
    )(*arrays, extra)


def take(value_entries, axis, index):
    return lax.dynamic_index_in_dim(value_entries, index, axis, keepdims=False)


def total(addends):
    result = addends[0].astype(jnp.float32)
    for addend in addends[1:]:
        result = result + addend.astype(jnp.float32)
    return result


def add_everywhere(value_entries):
    for axis in ("tensor", "dp"):
        for mask in bit_masks(lax.axis_size(axis)):
            value_entries = value_entries + swap(value_entries, axis, mask)
    return value_entries


def gather_rows(value_entries):
    pieces = [value_entries]
    for mask in reversed(bit_masks(lax.axis_size("tensor"))):
        pieces = pieces + [swap(piece, "tensor", mask) for piece in pieces]
    return jnp.concatenate(pieces, axis=0)


def total_lines(value_entries):
    size = lax.axis_size("tensor")
    rows = value_entries.shape[0] // size
    pieces = [to_low(value_entries[i * rows : (i + 1) * rows]) for i in range(size)]
    for mask in bit_masks(size):
        half = len(pieces) // 2
        pieces = [
            pieces[i].astype(jnp.float32)
            + swap(to_low(pieces[half + i]), "tensor", mask).astype(jnp.float32)
            for i in range(half)
        ]
    return pieces[0]


gather_grads = gather_rows
sum_grads = total_lines


def low_dot(left, right, left_dim, right_dim):
    return lax.dot_general(
        left, right, (((left_dim,), (right_dim,)), ((), ())), preferred_element_type=jnp.float32
    )


def sigmoid(value_entries):
    return 0.5 * jnp.tanh(0.5 * value_entries) + 0.5


def fold_rows(value_entries):
    return jnp.sum(value_entries.reshape(-1, 8, value_entries.shape[1]), axis=0)


def lower_ones():
    rows = lax.broadcasted_iota(jnp.int32, (ssd_block, ssd_block), 0)
    columns = lax.broadcasted_iota(jnp.int32, (ssd_block, ssd_block), 1)
    return (rows >= columns).astype(jnp.float32)


FORWARD_UNROLL = 8
BACKWARD_UNROLL = 4
PROJ_WIDE = 2 * INNER + 2 * STATE + 128


def step_terms(raw_steps, decay_refs):
    shifted = raw_steps + decay_refs[1:2, :]
    steps = softplus(shifted)
    rates = -jnp.exp(decay_refs[0:1, :])
    cumulative = jnp.dot(
        lower_ones(), steps * rates, precision=deepest_tier, preferred_element_type=jnp.float32
    )
    return shifted, steps, rates, cumulative


def head_tables():
    chosen = to_low(jnp.arange(INNER)[:, None] // HEADDIM == jnp.arange(ssd_block)[None, :])
    later = jnp.where(
        jnp.arange(ssd_block)[:, None] >= jnp.arange(ssd_block)[None, :], 0.0, -1e30
    )
    return chosen, later


def first_head():
    return lax.broadcasted_iota(jnp.int32, (ssd_block, ssd_block), 1) < HEADDIM


def both_heads(value_entries):
    mask = first_head()
    zeros = jnp.zeros_like(value_entries)
    return jnp.concatenate(
        [jnp.where(mask, value_entries, zeros), jnp.where(mask, zeros, value_entries)], axis=0
    )


def spread_heads(steps, cumulative, turned, wide, narrow):
    blank = jnp.zeros((ssd_block, ssd_block - MHEADS), jnp.float32)
    turned[...] = jnp.concatenate([cumulative, blank], axis=1).T
    mask = first_head()

    def over_lanes(value_entries, head):
        return jnp.broadcast_to(value_entries[:, head : head + 1], (ssd_block, ssd_block))

    for head in range(MHEADS):
        wide[head] = over_lanes(cumulative, head)
    for pair in range(MHEADS // 2):
        narrow[:, pair * ssd_block : (pair + 1) * ssd_block] = jnp.where(
            mask, over_lanes(steps, 2 * pair), over_lanes(steps, 2 * pair + 1)
        )


def gaps_of(wide, turned, later, head):
    return jnp.exp((wide[head] - turned[pl.ds(head, 1), :]) + later[...])


def quad_cumulative(wide, quad):
    mask = first_head()
    return jnp.concatenate(
        [
            jnp.where(mask, wide[4 * quad], wide[4 * quad + 1]),
            jnp.where(mask, wide[4 * quad + 2], wide[4 * quad + 3]),
        ],
        axis=1,
    )


def quad_lanes(quad, first=0):
    return pl.ds(pl.multiple_of(quad * 2 * ssd_block + first, ssd_block), 2 * ssd_block)


def lanes(block):
    return pl.ds(pl.multiple_of(block * ssd_block, ssd_block), ssd_block)


def convolve(padded_ref, taps_ref, columns):
    result = taps_ref[0:1, columns] * padded_ref[5 : 5 + ssd_block, columns]
    for tap in range(1, 4):
        result = result + taps_ref[tap : tap + 1, columns] * padded_ref[
            5 + tap : 5 + tap + ssd_block, columns
        ]
    return result


def middle_kernel(
    projected,
    taps,
    skip,
    decay,
    gain,
    later,
    middle,
    outcome,
    starts,
    padded,
    turned,
    wide,
    narrow,
    state,
    gated,
):
    chunk = pl.program_id(0)
    streams_extent = INNER + 2 * STATE

    @pl.when(chunk == 0)
    def _():
        padded[0:8, :] = jnp.zeros((8, streams_extent), jnp.float32)
        state[...] = jnp.zeros_like(state)

    @pl.when(chunk > 0)
    def _():
        padded[0:8, :] = padded[ssd_block : ssd_block + 8, :]

    padded[8 : 8 + ssd_block, :] = projected[:, INNER : INNER + streams_extent]
    _, steps, _, cumulative = step_terms(
        projected[:, INNER + streams_extent : INNER + streams_extent + MHEADS], decay
    )
    spread_heads(steps, cumulative, turned, wide, narrow)

    def active(columns):
        convolved = convolve(padded, taps, columns)
        return convolved * sigmoid(convolved)

    in_map = active(pl.ds(INNER, STATE))
    in_low = to_low(in_map)
    in_turned = to_low(in_map.T)
    out_low = to_low(active(pl.ds(INNER + STATE, STATE)))
    affinity = low_dot(out_low, in_low, 1, 1)

    def quad_step(quad, square_sum):
        columns = quad_lanes(quad)
        inputs = active(columns)
        weighted = inputs * narrow[:, columns]
        weighted_low = to_low(weighted)
        within = []
        for pair in range(2):
            head = 4 * quad + 2 * pair
            mixing = jnp.concatenate(
                [
                    to_low(affinity * gaps_of(wide, turned, later, head)),
                    to_low(affinity * gaps_of(wide, turned, later, head + 1)),
                ],
                axis=1,
            )
            part = weighted_low[:, pair * ssd_block : (pair + 1) * ssd_block]
            within.append(low_dot(mixing, both_heads(part), 1, 0))
        within = jnp.concatenate(within, axis=1)
        cumulative_here = quad_cumulative(wide, quad)
        last = cumulative_here[ssd_block - 1 :, :]
        held = state[:, columns]
        starts[0, :, columns] = held
        across = jnp.exp(cumulative_here) * low_dot(out_low, to_low(held), 1, 0)
        to_end = to_low(weighted * jnp.exp(last - cumulative_here))
        state[:, columns] = jnp.exp(last) * held + low_dot(in_turned, to_end, 1, 0)
        result = within + across + inputs * skip[:, columns]
        outcome[:, columns] = result
        gate = projected[:, columns]
        product = result * (gate * sigmoid(gate))
        gated[:, columns] = product
        return square_sum + product * product

    square_sum = lax.fori_loop(
        0,
        INNER // (2 * ssd_block),
        quad_step,
        jnp.zeros((ssd_block, 2 * ssd_block), jnp.float32),
        unroll=FORWARD_UNROLL,
    )
    scale = lax.rsqrt(jnp.sum(square_sum, axis=1, keepdims=True) * (1.0 / INNER) + norm_eps)

    def scale_step(quad, carry):
        columns = quad_lanes(quad)
        middle[:, columns] = to_low(gated[:, columns] * scale * gain[:, columns])
        return carry

    lax.fori_loop(0, INNER // (2 * ssd_block), scale_step, 0, unroll=2)


def middle_slope_kernel(
    projected,
    earlier,
    outcome,
    starts,
    slope,
    taps,
    skip,
    decay,
    gain,
    chosen,
    later,
    slope_projected,
    slope_taps,
    slope_skip,
    slope_gain,
    slope_decay,
    padded,
    turned,
    wide,
    narrow,
    slope_state,
    slope_conv,
    slope_affinity,
    slope_maps,
    slope_cumulative,
    slope_steps,
):
    chunk = pl.num_programs(0) - 1 - pl.program_id(0)
    streams_extent = INNER + 2 * STATE
    quads = INNER // (2 * ssd_block)

    @pl.when(pl.program_id(0) == 0)
    def _():
        slope_state[...] = jnp.zeros_like(slope_state)
        slope_conv[ssd_block : ssd_block + 8, :] = jnp.zeros((8, streams_extent), jnp.float32)
        slope_taps[...] = jnp.zeros_like(slope_taps)
        slope_skip[...] = jnp.zeros_like(slope_skip)
        slope_gain[...] = jnp.zeros_like(slope_gain)
        slope_decay[...] = jnp.zeros_like(slope_decay)

    @pl.when(pl.program_id(0) > 0)
    def _():
        slope_conv[ssd_block : ssd_block + 8, :] = slope_conv[0:8, :]

    @pl.when(chunk == 0)
    def _():
        padded[0:8, :] = jnp.zeros((8, streams_extent), jnp.float32)

    @pl.when(chunk > 0)
    def _():
        padded[0:8, :] = earlier[:, INNER : INNER + streams_extent]

    padded[8 : 8 + ssd_block, :] = projected[:, INNER : INNER + streams_extent]
    slope_affinity[...] = jnp.zeros_like(slope_affinity)
    slope_maps[...] = jnp.zeros_like(slope_maps)
    slope_cumulative[...] = jnp.zeros_like(slope_cumulative)
    slope_steps[...] = jnp.zeros_like(slope_steps)
    shifted, steps, rates, cumulative = step_terms(
        projected[:, INNER + streams_extent : INNER + streams_extent + MHEADS], decay
    )
    spread_heads(steps, cumulative, turned, wide, narrow)

    def silu_pair(value_entries):
        share = sigmoid(value_entries)
        return value_entries * share, share * (1.0 + value_entries * (1.0 - share))

    def pull_convolved(columns, target_columns, slope_block):
        slope_conv[0:ssd_block, columns] = slope_block
        result = taps[3:4, columns] * slope_block
        for tap in range(3):
            reach = 3 - tap
            result = result + taps[tap : tap + 1, columns] * slope_conv[
                reach : reach + ssd_block, columns
            ]
        for tap in range(4):
            slope_taps[tap, :, columns] += fold_rows(
                slope_block * padded[5 + tap : 5 + tap + ssd_block, columns]
            )
        slope_projected[:, target_columns] = to_low(result)

    maps = (pl.ds(INNER, STATE), pl.ds(INNER + STATE, STATE))
    in_map, in_pull = silu_pair(convolve(padded, taps, maps[0]))
    out_map, out_pull = silu_pair(convolve(padded, taps, maps[1]))
    in_low, out_low, out_turned = to_low(in_map), to_low(out_map), to_low(out_map.T)
    affinity = low_dot(out_low, in_low, 1, 1)
    mask = first_head()

    def sums_step(quad, sums):
        columns = quad_lanes(quad)
        gate = projected[:, columns]
        product = outcome[:, columns] * (gate * sigmoid(gate))
        return (
            sums[0] + product * product,
            sums[1] + product * (slope[:, columns] * gain[:, columns]),
        )

    blank = jnp.zeros((ssd_block, 2 * ssd_block), jnp.float32)
    squares, crossed = lax.fori_loop(0, quads, sums_step, (blank, blank), unroll=2)
    scale = lax.rsqrt(jnp.sum(squares, axis=1, keepdims=True) * (1.0 / INNER) + norm_eps)
    pulled = scale * scale * scale * (jnp.sum(crossed, axis=1, keepdims=True) * (1.0 / INNER))

    def quad_step(quad, carry):
        columns = quad_lanes(quad)
        gate, total_here = projected[:, columns], outcome[:, columns]
        gate_value, gate_pull = silu_pair(gate)
        product = total_here * gate_value
        slope_here = slope[:, columns]
        slope_gain[:, columns] += fold_rows(slope_here * product * scale)
        slope_product = scale * (slope_here * gain[:, columns]) - product * pulled
        slope_out = slope_product * gate_value
        slope_projected[:, columns] = to_low(slope_product * total_here * gate_pull)
        inputs, inputs_pull = silu_pair(convolve(padded, taps, columns))
        slope_skip[:, columns] += fold_rows(slope_out * inputs)
        skip_here = skip[:, columns]
        scanned = total_here - inputs * skip_here
        steps_here = narrow[:, columns]
        weighted = inputs * steps_here
        weighted_low = to_low(weighted)
        slope_low = to_low(slope_out)
        slope_within = []
        for pair in range(2):
            head = 4 * quad + 2 * pair
            here_low = slope_low[:, pair * ssd_block : (pair + 1) * ssd_block]
            part = weighted_low[:, pair * ssd_block : (pair + 1) * ssd_block]
            slope_mixing = low_dot(here_low, both_heads(part), 1, 1)
            mixing = []
            for side in range(2):
                gaps = gaps_of(wide, turned, later, head + side)
                mixing.append(to_low(affinity * gaps))
                slope_affinity[...] += (
                    slope_mixing[:, side * ssd_block : (side + 1) * ssd_block] * gaps
                )
            turned_back = low_dot(jnp.concatenate(mixing, axis=1), here_low, 0, 0)
            slope_within.append(
                jnp.where(mask, turned_back[:ssd_block], turned_back[ssd_block:])
            )
        slope_within = jnp.concatenate(slope_within, axis=1)
        cumulative_here = quad_cumulative(wide, quad)
        last = cumulative_here[ssd_block - 1 :, :]
        decayed = jnp.exp(last)
        held = starts[0, :, columns]
        slope_across = to_low(slope_out * jnp.exp(cumulative_here))
        slope_maps[1] += low_dot(slope_across, to_low(held), 1, 1)
        carried_state = slope_state[:, columns]
        carried_low = to_low(carried_state)
        to_end = jnp.exp(last - cumulative_here)
        ending = to_low(weighted * to_end)
        slope_ending = low_dot(in_low, carried_low, 1, 0)
        slope_maps[0] += low_dot(ending, carried_low, 1, 1)
        slope_state[:, columns] = decayed * carried_state + low_dot(out_turned, slope_across, 1, 0)
        slope_weighted = slope_within + slope_ending * to_end
        ending_slope = slope_ending * ending.astype(jnp.float32)
        ends = jnp.sum(ending_slope, axis=0, keepdims=True) + decayed * jnp.sum(
            carried_state * held, axis=0, keepdims=True
        )
        rows = lax.broadcasted_iota(jnp.int32, (ssd_block, 2 * ssd_block), 0)
        slope_gathered = (
            slope_low.astype(jnp.float32) * scanned
            - weighted_low.astype(jnp.float32) * slope_within
            - ending_slope
            + jnp.where(rows == ssd_block - 1, ends, 0.0)
        )
        high = to_low(slope_gathered)
        rest = to_low(slope_gathered - high.astype(jnp.float32))
        parts = [high, rest, to_low(slope_weighted * inputs)]
        sums = low_dot(jnp.concatenate(parts, axis=0), chosen[columns, :], 1, 0)
        slope_cumulative[...] += sums[:ssd_block] + sums[ssd_block : 2 * ssd_block]
        slope_steps[...] += sums[2 * ssd_block :]
        slope_inputs = slope_out * skip_here + slope_weighted * steps_here
        pull_convolved(columns, quad_lanes(quad, INNER), slope_inputs * inputs_pull)
        return carry

    lax.fori_loop(0, quads, quad_step, 0, unroll=BACKWARD_UNROLL)
    affinity_low = to_low(slope_affinity[...])
    slope_in = slope_maps[0] + low_dot(affinity_low, out_low, 0, 0)
    slope_out_map = slope_maps[1] + low_dot(affinity_low, in_low, 1, 0)
    pull_convolved(maps[0], pl.ds(2 * INNER, STATE), slope_in * in_pull)
    pull_convolved(maps[1], pl.ds(2 * INNER + STATE, STATE), slope_out_map * out_pull)
    slope_changes = lax.dot_general(
        lower_ones(),
        slope_cumulative[...],
        (((0,), (0,)), ((), ())),
        precision=deepest_tier,
        preferred_element_type=jnp.float32,
    )[:, :MHEADS]
    slope_step = slope_steps[:, :MHEADS] + slope_changes * rates
    slope_raw = slope_step * sigmoid(shifted)
    slope_decay[0] += fold_rows(slope_changes * steps) * rates
    slope_decay[1] += fold_rows(slope_raw)
    slope_projected[:, INNER + streams_extent :] = jnp.concatenate(
        [to_low(slope_raw), jnp.zeros((ssd_block, 128 - MHEADS), jnp.bfloat16)], axis=1
    )


def fixed(shape):
    return pl.BlockSpec(shape, lambda chunk: (0,) * len(shape))


def middle_forward(projected, smalls):
    conv_taps, skip_gain, a_log, dt_bias, gated_gain = smalls
    chosen, later = head_tables()
    extent, columns = projected.shape
    chunks = extent // ssd_block
    streams_extent = INNER + 2 * STATE
    return pl.pallas_call(
        middle_kernel,
        grid=(chunks,),
        out_shape=(
            jax.ShapeDtypeStruct((extent, INNER), jnp.bfloat16),
            jax.ShapeDtypeStruct((extent, INNER), jnp.float32),
            jax.ShapeDtypeStruct((chunks, STATE, INNER), jnp.float32),
        ),
        in_specs=[
            pl.BlockSpec((ssd_block, columns), lambda chunk: (chunk, 0)),
            fixed((4, streams_extent)),
            fixed((1, INNER)),
            fixed((2, MHEADS)),
            fixed((1, INNER)),
            fixed(later.shape),
        ],
        out_specs=(
            pl.BlockSpec((ssd_block, INNER), lambda chunk: (chunk, 0)),
            pl.BlockSpec((ssd_block, INNER), lambda chunk: (chunk, 0)),
            pl.BlockSpec((1, STATE, INNER), lambda chunk: (chunk, 0, 0)),
        ),
        scratch_shapes=[
            pltpu.VMEM((ssd_block + 8, streams_extent), jnp.float32),
            pltpu.VMEM((ssd_block, ssd_block), jnp.float32),
            pltpu.VMEM((MHEADS, ssd_block, ssd_block), jnp.float32),
            pltpu.VMEM((ssd_block, INNER), jnp.float32),
            pltpu.VMEM((STATE, INNER), jnp.float32),
            pltpu.VMEM((ssd_block, INNER), jnp.float32),
        ],
        compiler_params=pltpu.CompilerParams(vmem_limit_bytes=48 * 2**20),
        cost_estimate=pl.CostEstimate(
            flops=2 * 10**10, transcendentals=4 * 10**6, bytes_accessed=20 * 10**6
        ),
    )(
        projected,
        conv_taps,
        skip_gain.reshape(1, INNER),
        jnp.stack([a_log, dt_bias]),
        gated_gain.reshape(1, INNER),
        later,
    )


def middle_backward(projected, outcome, starts, slope, smalls):
    conv_taps, skip_gain, a_log, dt_bias, gated_gain = smalls
    chosen, later = head_tables()
    extent, columns = projected.shape
    chunks = extent // ssd_block
    streams_extent = INNER + 2 * STATE

    def back(chunk):
        return (chunks - 1 - chunk, 0)

    slope_projected, slope_taps, slope_skip, slope_gain, slope_decay = pl.pallas_call(
        middle_slope_kernel,
        grid=(chunks,),
        out_shape=(
            jax.ShapeDtypeStruct((extent, columns), jnp.bfloat16),
            jax.ShapeDtypeStruct((4, 8, streams_extent), jnp.float32),
            jax.ShapeDtypeStruct((8, INNER), jnp.float32),
            jax.ShapeDtypeStruct((8, INNER), jnp.float32),
            jax.ShapeDtypeStruct((2, 8, MHEADS), jnp.float32),
        ),
        in_specs=[
            pl.BlockSpec((ssd_block, columns), back),
            pl.BlockSpec(
                (8, columns),
                lambda chunk: (jnp.maximum((chunks - 1 - chunk) * (ssd_block // 8) - 1, 0), 0),
            ),
            pl.BlockSpec((ssd_block, INNER), back),
            pl.BlockSpec((1, STATE, INNER), lambda chunk: (chunks - 1 - chunk, 0, 0)),
            pl.BlockSpec((ssd_block, INNER), back),
            fixed((4, streams_extent)),
            fixed((1, INNER)),
            fixed((2, MHEADS)),
            fixed((1, INNER)),
            fixed(chosen.shape),
            fixed(later.shape),
        ],
        out_specs=(
            pl.BlockSpec((ssd_block, columns), back),
            fixed((4, 8, streams_extent)),
            fixed((8, INNER)),
            fixed((8, INNER)),
            fixed((2, 8, MHEADS)),
        ),
        scratch_shapes=[
            pltpu.VMEM((ssd_block + 8, streams_extent), jnp.float32),
            pltpu.VMEM((ssd_block, ssd_block), jnp.float32),
            pltpu.VMEM((MHEADS, ssd_block, ssd_block), jnp.float32),
            pltpu.VMEM((ssd_block, INNER), jnp.float32),
            pltpu.VMEM((STATE, INNER), jnp.float32),
            pltpu.VMEM((ssd_block + 8, streams_extent), jnp.float32),
            pltpu.VMEM((ssd_block, ssd_block), jnp.float32),
            pltpu.VMEM((2, ssd_block, STATE), jnp.float32),
            pltpu.VMEM((ssd_block, ssd_block), jnp.float32),
            pltpu.VMEM((ssd_block, ssd_block), jnp.float32),
        ],
        compiler_params=pltpu.CompilerParams(vmem_limit_bytes=48 * 2**20),
        cost_estimate=pl.CostEstimate(
            flops=5 * 10**10, transcendentals=8 * 10**6, bytes_accessed=30 * 10**6
        ),
    )(
        projected,
        projected,
        outcome,
        starts,
        slope,
        conv_taps,
        skip_gain.reshape(1, INNER),
        jnp.stack([a_log, dt_bias]),
        gated_gain.reshape(1, INNER),
        chosen,
        later,
    )
    slope_decay = jnp.sum(slope_decay, axis=1)
    return (
        slope_projected,
        (
            jnp.sum(slope_taps, axis=1),
            jnp.sum(slope_skip, axis=0),
            slope_decay[0],
            slope_decay[1],
            jnp.sum(slope_gain, axis=0),
        ),
    )


Y_LANE = (("tensor", 2),)


def mixer_forward(value_entries, w_in, exit_matrix, block_gain, smalls):
    rescaled_rows, rescale_grad = jax.vjp(root_mean_rescale, value_entries, block_gain)
    normed_low = to_low(rescaled_rows)
    projected = matmul_apply(normed_low, w_in)
    middle_low, outcome, starts = middle_forward(projected, smalls)
    return (
        value_entries + matmul_apply(middle_low, exit_matrix),
        (rescale_grad, normed_low, (projected, outcome, starts), middle_low),
    )


def mixer_backward(conductor, last, slope_emitted, kept, w_in, exit_matrix, smalls):
    rescale_grad, normed_low, middle_kept, middle_low = kept
    grad_low = to_low(slope_emitted)
    slope_exit_matrix = to_low(product_tn(middle_low, grad_low))
    job_out = conductor.add(Summing(slope_exit_matrix, True))
    slope_middle = product_nt(grad_low, exit_matrix)
    slope_middle = conductor.tick(after(slope_middle, [slope_exit_matrix]), 7.0)
    grad_proj, slope_smalls = middle_backward(*middle_kept, slope_middle, smalls)
    grad_proj = conductor.tick(grad_proj, 60.0 if last else 44.0, limit=0 if last else 5)
    grad_w_in = to_low(product_tn(normed_low, grad_proj))
    job_in = conductor.add(Summing(grad_w_in, True))
    grad_proj = conductor.tick(after(grad_proj, [grad_w_in]), 7.0, limit=0 if last else 5)
    grad_values, slope_scale = rescale_grad(product_nt(grad_proj, w_in))
    slope_value = conductor.tick(grad_values + slope_emitted, 10.0, Y_LANE, limit=0 if last else 5)
    return (slope_value, slope_scale, slope_smalls, (job_out, job_in))


def head_mask(head, extent):
    columns = lax.broadcasted_iota(jnp.int32, (1, extent), 1)
    inside = (columns >= head * HD) & (columns < (head + 1) * HD)
    return jnp.where(inside, 1.0, 0.0).astype(jnp.bfloat16)


def head_weights(queries, key_rows):
    scores = low_dot(queries, key_rows, 1, 1) * HD ** (-0.5)
    rows = lax.broadcasted_iota(jnp.int32, (MAX_PIECES, MAX_PIECES), 0)
    columns = lax.broadcasted_iota(jnp.int32, (MAX_PIECES, MAX_PIECES), 1)
    scores = jnp.where(rows >= columns, scores, -jnp.inf)
    exponents = jnp.exp(scores - jnp.max(scores, axis=-1, keepdims=True))
    return exponents / jnp.sum(exponents, axis=-1, keepdims=True)


def attend_kernel(triple, output):
    extent = output.shape[1]
    queries, key_rows = triple[:, :extent], triple[:, extent : 2 * extent]
    value_rows = triple[:, 2 * extent :]
    attended = jnp.zeros(output.shape, jnp.float32)
    for head in range(extent // HD):
        mask = head_mask(head, extent)
        weights = to_low(head_weights(queries * mask, key_rows))
        attended = attended + low_dot(weights, value_rows * mask, 1, 0)
    output[...] = to_low(attended)


def attend_slope_kernel(triple, slope, output):
    extent = slope.shape[1]
    queries, key_rows = triple[:, :extent], triple[:, extent : 2 * extent]
    value_rows = triple[:, 2 * extent :]
    slope_here = slope[...]
    slopes = [jnp.zeros(slope.shape, jnp.float32)] * 3
    for head in range(extent // HD):
        mask = head_mask(head, extent)
        weights = head_weights(queries * mask, key_rows)
        slope_masked = slope_here * mask
        slope_weights = low_dot(slope_masked, value_rows, 1, 1)
        slope_scores = to_low(
            weights
            * (slope_weights - jnp.sum(weights * slope_weights, axis=-1, keepdims=True))
        )
        slopes[0] = slopes[0] + low_dot(slope_scores, key_rows * mask, 1, 0)
        slopes[1] = slopes[1] + low_dot(slope_scores, queries * mask, 0, 0)
        slopes[2] = slopes[2] + low_dot(to_low(weights), slope_masked, 0, 0)
    output[:, :extent] = to_low(slopes[0] * HD ** (-0.5))
    output[:, extent : 2 * extent] = to_low(slopes[1] * HD ** (-0.5))
    output[:, 2 * extent :] = to_low(slopes[2])


def by_sequence(kernel, columns, *arrays):
    rows = arrays[0].shape[0]
    return pl.pallas_call(
        kernel,
        grid=(rows // MAX_PIECES,),
        out_shape=jax.ShapeDtypeStruct((rows, columns), jnp.bfloat16),
        in_specs=[
            pl.BlockSpec((MAX_PIECES, array.shape[1]), lambda group: (group, 0)) for array in arrays
        ],
        out_specs=pl.BlockSpec((MAX_PIECES, columns), lambda group: (group, 0)),
        compiler_params=pltpu.CompilerParams(vmem_limit_bytes=24 * 2**20),
        cost_estimate=pl.CostEstimate(
            flops=3 * 10**9, transcendentals=3 * 10**5, bytes_accessed=4 * 10**6
        ),
    )(*arrays)


def apply_heads(latent_holder, heed_scale, triple_matrix, exit_matrix):
    rescaled_rows, rescale_grad = jax.vjp(root_mean_rescale, latent_holder, heed_scale)
    rows_low = gather_rows(to_low(rescaled_rows))
    triple = to_low(matmul_apply(rows_low, triple_matrix))
    heads_output = by_sequence(attend_kernel, triple.shape[1] // 3, triple)
    outcome = latent_holder + total_lines(product_nt(heads_output, exit_matrix))
    return outcome, (rescale_grad, rows_low, triple, heads_output)


def apply_heads_grad(conductor, slope_emitted, kept, triple_matrix, exit_matrix):
    rescale_grad, rows_low, triple, heads_output = kept
    grad_rows = conductor.tick(gather_grads(to_low(slope_emitted)), 12.0, Y_LANE)
    slope_exit_matrix = to_low(product_tn(grad_rows, heads_output))
    grad_attended = to_low(matmul_apply(grad_rows, exit_matrix))
    grad_triple = by_sequence(attend_slope_kernel, triple.shape[1], triple, grad_attended)
    grad_triple = conductor.tick(after(grad_triple, [slope_exit_matrix]), 10.0, Y_LANE)
    slope_rescaled = sum_grads(product_nt(grad_triple, triple_matrix))
    slope_triple_matrix = to_low(product_tn(rows_low, grad_triple))
    job_exit = conductor.add(Summing(slope_exit_matrix, False))
    job_triple = conductor.add(Summing(slope_triple_matrix, False))
    slope_rescaled = conductor.tick(
        after(slope_rescaled, [slope_triple_matrix]), 10.0, Y_LANE
    )
    gradient_holder, slope_scale = rescale_grad(slope_rescaled)
    return (gradient_holder + slope_emitted, slope_scale, job_triple, job_exit)


def swiglu(both):
    half = both.shape[1] // 2
    return jax.nn.silu(both[:, :half]) * both[:, half:]


def perceptron_apply(latent_holder, perceptron_scale, lift_matrix, lower_matrix):
    rescaled_rows, rescale_grad = jax.vjp(root_mean_rescale, latent_holder, perceptron_scale)
    rows_low = gather_rows(to_low(rescaled_rows))
    latent_state, act_pull = jax.vjp(swiglu, matmul_apply(rows_low, lift_matrix))
    latent_merged = to_low(latent_state)
    outcome = latent_holder + total_lines(product_nt(latent_merged, lower_matrix))
    return (outcome, (rescale_grad, rows_low, act_pull, latent_merged))


def perceptron_grad(conductor, slope_emitted, kept, lift_matrix, lower_matrix):
    rescale_grad, rows_low, act_pull, latent_merged = kept
    grad_rows = conductor.tick(gather_grads(to_low(slope_emitted)), 13.0, Y_LANE)
    slope_lower_matrix = to_low(product_tn(grad_rows, latent_merged))
    job_lower = conductor.add(Summing(slope_lower_matrix, False))
    grad_rows = conductor.tick(after(grad_rows, [slope_lower_matrix]), 2.0, Y_LANE)
    (grad_both,) = act_pull(matmul_apply(grad_rows, lower_matrix))
    grad_both = conductor.tick(to_low(grad_both), 4.0, Y_LANE)
    slope_rescaled = sum_grads(product_nt(grad_both, lift_matrix))
    half = grad_both.shape[1] // 2
    slope_lifts = [
        to_low(product_tn(rows_low, grad_both[:, :half])),
        to_low(product_tn(rows_low, grad_both[:, half:])),
    ]
    slope_lifts = [conductor.add(Summing(slope, False)) for slope in slope_lifts]
    slope_rescaled = conductor.tick(slope_rescaled, 14.0, Y_LANE)
    gradient_holder, slope_scale = rescale_grad(slope_rescaled)
    return (gradient_holder + slope_emitted, slope_scale, job_lower, slope_lifts)


def body(
    byte_ids,
    targets,
    boundaries,
    lengths,
    tables,
    tables_first,
    tables_second,
    mamba_in,
    mamba_in_first,
    mamba_in_second,
    mamba_out,
    mamba_out_first,
    mamba_out_second,
    route_proj,
    route_proj_first,
    route_proj_second,
    small_params,
    small_params_first,
    small_params_second,
    heed_triple_matrix,
    attn_qkv_first,
    attn_qkv_second,
    heed_exit_matrix,
    attn_out_first,
    attn_out_second,
    lifting_matrix,
    mlp_gate_up_first,
    mlp_gate_up_second,
    lowering_matrix,
    mlp_down_first,
    mlp_down_second,
):
    devices = lax.axis_size("dp") * lax.axis_size("tensor")
    table_rows = tables.shape[1]
    small_here = small_params.shape[0]
    mixed_rows = 2 * table_rows
    length_pair = jnp.stack([lengths[0] // 16, lengths[0] % 16]).astype(jnp.bfloat16)
    tail = jnp.concatenate([to_low(small_params), length_pair])
    mixed = jnp.concatenate(
        [
            to_low(tables).reshape(mixed_rows, BYTE_WIDTH),
            jnp.pad(tail, (0, mixed_rows * 128 - tail.shape[0])).reshape(mixed_rows, 128),
        ],
        axis=1,
    )

    def wide_in(layer):
        low = to_low(mamba_in[layer])
        return jnp.pad(low, ((0, 0), (0, PROJ_WIDE - low.shape[1])))

    conductor = Conductor()
    exact_tiles = mamba_in.shape[1] % 16 == 0
    shards = [
        mixed,
        wide_in(0),
        to_low(mamba_out[0]),
        to_low(route_proj),
        to_low(heed_triple_matrix).reshape(heed_triple_matrix.shape[0], -1),
        to_low(heed_exit_matrix).T,
        to_low(lifting_matrix).reshape(lifting_matrix.shape[0], -1),
        to_low(lowering_matrix).T,
        wide_in(1),
        to_low(mamba_out[1]),
    ]
    kinds = [BYTE_LANES] * 4 + [MAIN_LANES] * 4 + [BYTE_LANES] * 2
    if exact_tiles:
        fan, late = MAIN_LANES, MAIN_LANES[::-1]
        in_first, in_last = 18 * 128, PROJ_WIDE - 18 * 128
        half_route = route_proj.shape[1] // 2
        half_lift = shards[6].shape[1] // 2
        jobs = [
            (3, BYTE_LANES, half_route, half_route),
            (9, BYTE_LANES, 0, BYTE_WIDTH),
            (8, BYTE_LANES, 0, in_first),
            (0, BYTE_LANES, 0, BYTE_WIDTH + 128),
            (1, BYTE_LANES, in_first, in_last),
            (2, BYTE_LANES, 0, BYTE_WIDTH),
            (8, BYTE_LANES, in_first, in_last),
            (4, fan, 0, shards[4].shape[1]),
            (1, BYTE_LANES, 0, in_first),
            (6, fan, half_lift, half_lift),
            (3, BYTE_LANES, 0, half_route),
            (7, fan, 0, shards[7].shape[1]),
            (5, late, 0, shards[5].shape[1]),
            (6, late, 0, half_lift),
        ]
        wholes = spread_whole(shards, jobs, 0)
    else:
        wholes = [
            lax.all_gather(
                shard, ("dp", "tensor") if kind == BYTE_LANES else "dp", axis=0, tiled=True
            )
            for shard, kind in zip(shards, kinds)
        ]
    mixed_whole = wholes[0]
    full_in, full_out, full_route = [wholes[1], wholes[8]], [wholes[2], wholes[9]], wholes[3]
    triple_whole, heed_exit_whole, lift_matrix_whole, lower_matrix_whole = wholes[4:8]
    mixed_whole = mixed_whole.reshape(devices, mixed_rows, BYTE_WIDTH + 128)
    full_tables = (
        mixed_whole[:, :, :BYTE_WIDTH]
        .reshape(devices, 2, table_rows, BYTE_WIDTH)
        .transpose(1, 0, 2, 3)
        .reshape(2, VOCAB, BYTE_WIDTH)
    )
    tails = mixed_whole[:, :, BYTE_WIDTH:].reshape(devices, -1)
    full_small = tails[:, :small_here].reshape(-1)
    pairs = tails[:, small_here : small_here + 2].astype(jnp.float32)
    byte_count = jnp.sum(pairs[:, 0] * 16.0 + pairs[:, 1])
    (
        block_gains,
        gated_gains,
        core_scales,
        head_gain,
        blank_row,
        conv_taps,
        skip_gains,
        a_logs,
        dt_biases,
    ) = unpack_small(full_small.astype(jnp.float32))
    layer_smalls = [
        (
            conv_taps[layer_index],
            skip_gains[layer_index],
            a_logs[layer_index],
            dt_biases[layer_index],
            gated_gains[layer_index],
        )
        for layer_index in range(2)
    ]
    cut_marks = boundaries[0]
    seq_len = byte_ids.shape[1]
    vocab_ids = jnp.arange(VOCAB, dtype=jnp.int32)
    onehot_in = (byte_ids[0][:, None] == vocab_ids[None, :]).astype(jnp.bfloat16)
    embedded = matmul_apply(onehot_in, full_tables[0])
    packer_output, kept_enc = mixer_forward(
        embedded, full_in[0], full_out[0], block_gains[0], layer_smalls[0]
    )
    encoded_low = to_low(packer_output)
    directed_rows = matmul_apply(encoded_low, full_route)
    cut_likelihood, prob_pull = jax.vjp(
        route_prob, directed_rows[:, :BYTE_WIDTH], directed_rows[:, BYTE_WIDTH : 2 * BYTE_WIDTH]
    )
    select_items, broadcast_back = span_maps(cut_marks)
    latent_holder, merge_transpose = jax.vjp(
        partial(merge_into_pieces, select_items), packer_output, blank_row
    )
    latent_holder, saved_heeding = apply_heads(
        latent_holder, core_scales[0], triple_whole, heed_exit_whole
    )
    latent_holder, saved_perceptron = perceptron_apply(
        latent_holder, core_scales[1], lift_matrix_whole, lower_matrix_whole
    )
    unpacked_bytes, link_layers_grad = jax.vjp(
        partial(link_layers, select_items, broadcast_back, cut_marks),
        latent_holder,
        core_scales[2],
        cut_likelihood,
        directed_rows[:, 2 * BYTE_WIDTH :],
    )
    final_out, kept_dec = mixer_forward(
        unpacked_bytes, full_in[1], full_out[1], block_gains[1], layer_smalls[1]
    )
    head_in, head_pull = jax.vjp(root_mean_rescale, final_out, head_gain)
    head_low = to_low(head_in)
    logits = product_nt(head_low, full_tables[1])
    maxima = jnp.max(logits, axis=-1, keepdims=True)
    log_total = maxima + jnp.log(jnp.sum(jnp.exp(logits - maxima), axis=-1, keepdims=True))
    onehot_out = (targets[0][:, None] == vocab_ids[None, :]).astype(jnp.float32)
    counted = (jnp.arange(seq_len, dtype=jnp.int32) < lengths[0]).astype(jnp.float32)[:, None]
    loss_local = jnp.sum((log_total - logits) * onehot_out * counted)
    grad_logits = to_low((jnp.exp(logits - log_total) - onehot_out) * counted / byte_count)
    grad_table_out = product_tn(grad_logits, head_low)
    grad_final, grad_head_gain = head_pull(matmul_apply(grad_logits, full_tables[1]))
    slope_unpacked, grad_block_dec, grad_small_dec, jobs_dec = mixer_backward(
        conductor, False, grad_final, kept_dec, full_in[1], full_out[1], layer_smalls[1]
    )
    gradient_holder, slope_closing_scale, slope_likelihood, slope_shortcut = link_layers_grad(
        slope_unpacked
    )
    gradient_holder, slope_perceptron_scale, job_lower, slope_lifts = perceptron_grad(
        conductor, conductor.tick(gradient_holder, 14.0, Y_LANE), saved_perceptron, lift_matrix_whole, lower_matrix_whole
    )
    gradient_holder, slope_heed_scale, *jobs_heads = apply_heads_grad(
        conductor, gradient_holder, saved_heeding, triple_whole, heed_exit_whole
    )
    gradient_merged, gradient_blank = merge_transpose(gradient_holder)
    grad_query, grad_key = prob_pull(slope_likelihood)
    grad_routed = to_low(jnp.concatenate([grad_query, grad_key, slope_shortcut], axis=1))
    grad_routed = after(grad_routed, [gradient_merged])
    grad_route = to_low(product_tn(encoded_low, grad_routed))
    job_route = Summing(grad_route, True)
    grad_routed = conductor.tick(after(grad_routed, [grad_route]), 7.0)
    grad_embedded, grad_block_enc, grad_small_enc, jobs_enc = mixer_backward(
        conductor,
        True,
        gradient_merged + product_nt(grad_routed, full_route),
        kept_enc,
        full_in[0],
        full_out[0],
        layer_smalls[0],
    )
    embedded_high = to_low(grad_embedded)
    embedded_rest = to_low(grad_embedded - embedded_high.astype(jnp.float32))
    grad_table_in = product_tn(onehot_in, embedded_high) + product_tn(onehot_in, embedded_rest)
    grad_small = jnp.concatenate(
        [
            piece.reshape(-1)
            for piece in (
                jnp.stack([grad_block_enc, grad_block_dec]),
                jnp.stack([grad_small_enc[4], grad_small_dec[4]]),
                jnp.stack([slope_heed_scale, slope_perceptron_scale, slope_closing_scale]),
                grad_head_gain,
                gradient_blank,
                jnp.stack([grad_small_enc[0], grad_small_dec[0]]),
                jnp.stack([grad_small_enc[1], grad_small_dec[1]]),
                jnp.stack([grad_small_enc[2], grad_small_dec[2]]),
                jnp.stack([grad_small_enc[3], grad_small_dec[3]]),
            )
        ]
    )
    width = mamba_in.shape[2]
    grad_mixed = jnp.concatenate(
        [
            jnp.concatenate(
                [
                    to_low(grad_table_in).reshape(devices, table_rows, BYTE_WIDTH),
                    to_low(grad_table_out).reshape(devices, table_rows, BYTE_WIDTH),
                ],
                axis=1,
            ),
            jnp.pad(
                to_low(grad_small).reshape(devices, small_here),
                ((0, 0), (0, mixed_rows * 128 - small_here)),
            ).reshape(devices, mixed_rows, 128),
        ],
        axis=2,
    )
    conductor.close()
    parts = [
        jobs_heads[1],
        slope_lifts[0],
        slope_lifts[1],
        jobs_heads[0],
        job_lower,
        jobs_dec[1],
        jobs_dec[0],
        jobs_enc[0],
        job_route,
        jobs_enc[1],
        Summing(grad_mixed.reshape(-1, BYTE_WIDTH + 128), True),
    ]
    sums = [None if part.masks else part.result(jobs_enc[1].addends[0][0]) for part in parts]
    open_parts = [number for number in (8, 9, 7, 10, 3, 0, 1, 2, 4, 5, 6) if parts[number].masks]
    rests = [parts[number].rest(jobs_enc[1].addends[0][0]) for number in open_parts]
    grads = [grad for grad, _ in rests]
    sum_kinds = [kind for _, kind in rests]
    if exact_tiles:
        early = sum((jnp.sum(part * part) for part in sums if part is not None), jnp.float32(0.0))
        extra = jnp.zeros((16, 128), jnp.float32).at[0, 0].set(early).at[8, 0].set(loss_local)
        *ends, totals = sum_whole(grads, sum_kinds, extra, 1)
        square_total, loss_sum = jnp.sum(totals[:8]), jnp.sum(totals[8:])
    else:
        ends = [sum_slowly(parts[number]) for number in open_parts]
    for number, end in zip(open_parts, ends):
        sums[number] = end
    reduced_wo = sums[0].T
    reduced_gate_up = jnp.stack([sums[1], sums[2]], axis=1)
    reduced_qkv = sums[3].reshape(heed_triple_matrix.shape)
    reduced_down = sums[4].T
    reduced_in_dec = sums[5][:, :width]
    reduced_out_dec, reduced_out_enc, reduced_route = sums[6:9]
    reduced_in_enc = sums[9][:, :width]
    reduced_mixed = sums[10]
    reduced_tables = reduced_mixed[:, :BYTE_WIDTH].reshape(2, table_rows, BYTE_WIDTH)
    reduced_small = reduced_mixed[:, BYTE_WIDTH:].reshape(-1)[:small_here]
    reduced_in = jnp.stack([reduced_in_enc, reduced_in_dec])
    reduced_out = jnp.stack([reduced_out_enc, reduced_out_dec])
    reduced = (
        reduced_tables,
        reduced_in,
        reduced_out,
        reduced_route,
        reduced_small,
        reduced_qkv,
        reduced_wo,
        reduced_gate_up,
        reduced_down,
    )
    if not exact_tiles:
        squares = sum((jnp.sum(grad * grad) for grad in reduced))
        totals = add_everywhere(jnp.stack([squares, loss_local]).reshape(1, 2))
        square_total, loss_sum = (totals[0, 0], totals[0, 1])
    grad_norm = jnp.sqrt(square_total)
    clip_factor = jnp.minimum(1.0, max_norm / (grad_norm + 1e-06))
    masters = (
        tables,
        mamba_in,
        mamba_out,
        route_proj,
        small_params,
        heed_triple_matrix,
        heed_exit_matrix,
        lifting_matrix,
        lowering_matrix,
    )
    firsts = (
        tables_first,
        mamba_in_first,
        mamba_out_first,
        route_proj_first,
        small_params_first,
        attn_qkv_first,
        attn_out_first,
        mlp_gate_up_first,
        mlp_down_first,
    )
    seconds = (
        tables_second,
        mamba_in_second,
        mamba_out_second,
        route_proj_second,
        small_params_second,
        attn_qkv_second,
        attn_out_second,
        mlp_gate_up_second,
        mlp_down_second,
    )
    rate_list = (
        rate_byte,
        rate_byte,
        rate_byte,
        rate_byte,
        rate_small,
        rate_main,
        rate_main,
        rate_main,
        rate_main,
    )
    decay_list = (
        weight_decay,
        weight_decay,
        weight_decay,
        weight_decay,
        0.0,
        weight_decay,
        weight_decay,
        weight_decay,
        weight_decay,
    )
    updated = [
        adam_step(
            masters[position],
            clip_factor * reduced[position],
            firsts[position],
            seconds[position],
            rate_list[position],
            decay_list[position],
        )
        for position in range(9)
    ]
    updated[7] = lift_step(
        clip_factor, sums[1], sums[2], lifting_matrix, mlp_gate_up_first, mlp_gate_up_second
    )
    return (loss_sum, byte_count, grad_norm) + tuple(
        (member for triple_out in updated for member in triple_out)
    )


def solution(mesh):
    return jax.shard_map(
        body,
        mesh=mesh,
        in_specs=(
            P(("dp", "tensor"), None),
            P(("dp", "tensor"), None),
            P(("dp", "tensor"), None),
            P(("dp", "tensor")),
            P(None, ("dp", "tensor"), None),
            P(None, ("dp", "tensor"), None),
            P(None, ("dp", "tensor"), None),
            P(None, ("dp", "tensor"), None),
            P(None, ("dp", "tensor"), None),
            P(None, ("dp", "tensor"), None),
            P(None, ("dp", "tensor"), None),
            P(None, ("dp", "tensor"), None),
            P(None, ("dp", "tensor"), None),
            P(("dp", "tensor"), None),
            P(("dp", "tensor"), None),
            P(("dp", "tensor"), None),
            P(("dp", "tensor")),
            P(("dp", "tensor")),
            P(("dp", "tensor")),
            P("dp", None, "tensor"),
            P("dp", None, "tensor"),
            P("dp", None, "tensor"),
            P("tensor", "dp"),
            P("tensor", "dp"),
            P("tensor", "dp"),
            P("dp", None, "tensor"),
            P("dp", None, "tensor"),
            P("dp", None, "tensor"),
            P("tensor", "dp"),
            P("tensor", "dp"),
            P("tensor", "dp"),
        ),
        out_specs=(
            P(),
            P(),
            P(),
            P(None, ("dp", "tensor"), None),
            P(None, ("dp", "tensor"), None),
            P(None, ("dp", "tensor"), None),
            P(None, ("dp", "tensor"), None),
            P(None, ("dp", "tensor"), None),
            P(None, ("dp", "tensor"), None),
            P(None, ("dp", "tensor"), None),
            P(None, ("dp", "tensor"), None),
            P(None, ("dp", "tensor"), None),
            P(("dp", "tensor"), None),
            P(("dp", "tensor"), None),
            P(("dp", "tensor"), None),
            P(("dp", "tensor")),
            P(("dp", "tensor")),
            P(("dp", "tensor")),
            P("dp", None, "tensor"),
            P("dp", None, "tensor"),
            P("dp", None, "tensor"),
            P("tensor", "dp"),
            P("tensor", "dp"),
            P("tensor", "dp"),
            P("dp", None, "tensor"),
            P("dp", None, "tensor"),
            P("dp", None, "tensor"),
            P("tensor", "dp"),
            P("tensor", "dp"),
            P("tensor", "dp"),
        ),
        check_vma=False,
    )
```
